32 devices in a mesh: req: 8 (over z, x), tp: 4 (over y, core).
Axes of the slice: x: 2, y: 2, z: 4, core: 2. Of those that a mesh axis runs over, the one named last changes fastest.
Arguments:
- tokens_new: bfloat16 [8, 16, 2, 1024], P('req'), may hold values from -6 to 6
- prefix_len: int32 [8], replicated, may hold values from 1 to 4096, as said below
- tail_len: int32 [8, 16], P('req'), may hold values from 1 to 512, as said below
- pool_home: int32 [256], replicated, may hold values from 0 to 7, as said below
- pool_page: int32 [256], replicated, may hold values from 0 to 31
- slot_page_cache: bfloat16 [256, 128, 2, 512], P('req', None, None, 'tp'), may hold values from -64 to 64
- tail_cache: bfloat16 [8, 16, 512, 2, 512], P('req', None, None, None, 'tp'), may hold values from -6 to 6
- routes: int32 [8, 16, 2, 8], P('req'), may hold values from 0 to 31, all different within a row; in each aligned block of 32 rows (0 to 31, 32 to 63, ..., all dimensions but the last counted through in order) at most 12 rows name the same one
- norm_gains: float32 [3, 1024], replicated, may hold values from 0.1 to 1.9
- query_weight: bfloat16 [1024, 1024], P(None, 'tp'), may hold values from -0.1875 to 0.1875
- key_value_weight: bfloat16 [1024, 2, 512], P(None, None, 'tp'), may hold values from -0.1875 to 0.1875
- out_weight: bfloat16 [1024, 1024], P('tp'), may hold values from -0.1875 to 0.1875
- router: bfloat16 [1024, 32], replicated, may hold values from -0.375 to 0.375
- expert_in: bfloat16 [32, 1024, 2, 512], P('req', None, None, 'tp'), as said below
- expert_out: bfloat16 [32, 512, 1024], P('req', 'tp'), as said below
- score_weight: float32 [1024], replicated, may hold values from -0.1875 to 0.1875
Outputs:
- layer_out: bfloat16 [8, 16, 2, 1024], P('req')
- row_score: float32 [8, 16, 2], P('req')
The draws below stay inside these ranges and needn't reach their ends.
Inputs may be any that keep to these rules, and one draw needn't show every extreme that they name: `prefix_len`: some request has exactly 4096 prefix positions. `tail_len`: some sample has exactly 512 tail positions. `pool_home`: entry s * 32 + v describes slot v of the pool of device s of req. Every page 0 to 31 of every request lies in exactly one slot, and one device's pool holds either exactly 4 pages of a request or none of them. `routes`: in the 32 rows of one device no expert is named more than 12 times. `expert_in`: expert table copy c equals copy c mod 32. `expert_out`: expert table copy c equals copy c mod 32.
All inputs are finite; a program needn't handle non-finite values.
Results may differ from the reference program's by a relative error of at most 0.017.
Values may be sent and summed in bfloat16 or wider, within the bound.
No kernel may reach another device: no remote copies, remote signals or barrier semaphores. Data moves between devices by JAX's collectives and lax.ppermute only.
A program may use at most 128 MiB of HBM per device.

```python
import math
import jax
import jax.numpy as jnp
import numpy as np
from jax import lax

MODEL_DIM = 1024
QUERY_HEADS = 16
KEY_VALUE_HEADS = 8
HEAD_DIM = 64
FF = 512
EXPERTS = 32
TOPK = 8
SAMPLE_COUNT = 16
NEW_TOKENS = 2
PAGE_POSITIONS = 128
MOST = 12
PLEN = 4096
TAIL_LENGTH = 512
PREFIX_PAGES = 32
PROMPT_COUNT = 8
KEY_VALUE_WIDTH = 512
EXP_SLOTS = 32
N_REQ = 8


def pool_layout(key):
    base_key = jax.random.fold_in(key, 7)
    group_key, slot_key, offset_key, page_key = jax.random.split(base_key, 4)
    home_order = jax.random.permutation(group_key, N_REQ).astype(jnp.int32)
    slot_order = jax.random.permutation(slot_key, PREFIX_PAGES).astype(jnp.int32)
    offset_order = jax.random.permutation(offset_key, N_REQ).astype(jnp.int32)
    page_keys = jax.random.split(page_key, N_REQ)
    page_orders = jax.vmap(lambda single: jax.random.permutation(single, PREFIX_PAGES))(page_keys).astype(jnp.int32)
    offsets = jnp.take(offset_order, slot_order % N_REQ)
    owners = jnp.arange(N_REQ, dtype=jnp.int32)[:, None]
    groups = (owners - offsets[None, :]) % N_REQ
    homes = jnp.take(home_order, groups)
    slot_column = jnp.broadcast_to(jnp.arange(PREFIX_PAGES, dtype=jnp.int32)[None, :], (N_REQ, PREFIX_PAGES))
    prefix_page_list = page_orders[groups, slot_column]
    return (homes.reshape(-1).astype(jnp.int32), prefix_page_list.reshape(-1).astype(jnp.int32))


def draw_pool_home(key, part):
    return pool_layout(key)[0]


def draw_pool_page(key, part):
    return pool_layout(key)[1]


def draw_prefix_len(key, part):
    length_key, spot_key = jax.random.split(jax.random.fold_in(key, 11))
    lengths = jax.random.randint(length_key, (PROMPT_COUNT,), 1, PLEN + 1)
    chosen = jax.random.randint(spot_key, (), 0, PROMPT_COUNT)
    return lengths.at[chosen].set(PLEN).astype(jnp.int32)


def draw_tail_len(key, part):
    length_key, spot_key = jax.random.split(jax.random.fold_in(key, 12))
    lengths = jax.random.randint(length_key, (PROMPT_COUNT * SAMPLE_COUNT,), 1, TAIL_LENGTH + 1)
    chosen = jax.random.randint(spot_key, (), 0, PROMPT_COUNT * SAMPLE_COUNT)
    return lengths.at[chosen].set(TAIL_LENGTH).reshape(PROMPT_COUNT, SAMPLE_COUNT).astype(jnp.int32)


def draw_slot_page_cache(key, part):
    value_key = jax.random.fold_in(jax.random.fold_in(key, 13), 0)
    shape = (N_REQ * PREFIX_PAGES, PAGE_POSITIONS, 2, KEY_VALUE_WIDTH)
    values = jax.random.normal(value_key, shape, jnp.float32)
    return jnp.clip(values, -64.0, 64.0).astype(jnp.bfloat16)


def draw_expert_in(key, part):
    values = jax.random.normal(jax.random.fold_in(key, 17), (EXPERTS, MODEL_DIM, 2, FF), jnp.float32)
    values = jnp.clip(values, -5.0, 5.0) * MODEL_DIM ** (-0.5)
    return jnp.tile(values, (EXP_SLOTS // EXPERTS, 1, 1, 1)).astype(jnp.bfloat16)


def draw_expert_out(key, part):
    values = jax.random.normal(jax.random.fold_in(key, 19), (EXPERTS, FF, MODEL_DIM), jnp.float32)
    values = jnp.clip(values, -5.0, 5.0) * FF ** (-0.5)
    return jnp.tile(values, (EXP_SLOTS // EXPERTS, 1, 1)).astype(jnp.bfloat16)


def levels(rng, dims, cuts, smallest, top_value):
    factor_of = 1.0
    for axis_at, blocks in cuts:
        heights = jax.random.uniform(jax.random.fold_in(jax.random.fold_in(rng, 6), axis_at), (blocks,), jnp.float32, smallest / len(cuts), top_value / len(cuts))
        factor_of = factor_of * jnp.repeat(jnp.exp(heights), dims[axis_at] // blocks).reshape((-1,) + (1,) * (len(dims) - 1 - axis_at))
    return factor_of


def shared_out(key, own, number, rows, count, top, limit, skew):
    sequence = jax.random.permutation(key, count)
    heavy_load, common = shares(count, rows * top, limit, skew, True), shares(count, rows * top, limit, skew, False)
    places = jnp.arange(count)

    def named(sizes, rotation):
        used = int((sizes > 0).sum())
        fixed = max(1, used // 4)
        passed = fixed + (places - fixed + rotation * (used - fixed)) % max(1, count - fixed)
        return jnp.zeros((count,), jnp.int32).at[sequence[jnp.where(places < fixed, places, passed)]].set(jnp.asarray(sizes, jnp.int32))

    sizes = jnp.where(number % 4 == 0, named(heavy_load, number // 4), named(common, number - number // 4 - 1))
    mixed = jax.random.permutation(jax.random.fold_in(own, 3), count)
    source_of, sink = mixed[0:count // 2 * 2:2], mixed[1:count // 2 * 2:2]
    margin = jnp.minimum(sizes[source_of] - 1, limit - sizes[sink]) // 2
    margin = jnp.where((source_of == sequence[0]) | (sink == sequence[0]) | (sizes[sink] == 0), 0, jnp.maximum(margin, 0))
    passed = jax.random.randint(jax.random.fold_in(own, 4), (count // 2,), 0, 1 << 20) % (margin + 1)
    sizes = sizes.at[source_of].add(-passed).at[sink].add(passed)
    members = jnp.searchsorted(jnp.cumsum(sizes), jnp.arange(rows * top), side="right").astype(jnp.int32)
    grid = members.reshape(top, rows).T
    grid = grid[jax.random.permutation(jax.random.fold_in(own, 1), rows)]
    rotation = jax.random.randint(jax.random.fold_in(own, 2), (rows, 1), 0, top)
    return jnp.take_along_axis(grid, (jnp.arange(top)[None, :] + rotation) % top, axis=1)


def shares(number_of, total, reach, lean, full):
    loads = [(1 << 20) // math.isqrt(standing ** lean) + 1 for standing in range(1, number_of + 1)]
    largest = reach if full else min(reach, max(-(-total // number_of), total * loads[0] // sum(loads)))
    least = 1 if total - largest >= number_of - 1 else 0
    given, spare = [largest] + [least] * (number_of - 1), total - largest - least * (number_of - 1)
    while spare > 0:
        movable = [i for i in range(1, number_of) if given[i] < largest] or [i for i in range(1, number_of) if given[i] < reach]
        pool, budget = sum([loads[i] for i in movable]), spare
        for i in movable:
            extra = min(reach - given[i], max(1, budget * loads[i] // pool), spare)
            given[i] = given[i] + extra
            spare = spare - extra
    return np.array(given)


def scatter_about(own_key, dims, scale, limit, cuts=(), kind=jnp.bfloat16):
    loudness = levels(own_key, dims, cuts, -0.22, 0.18) if cuts else 1.0
    drawn = jax.random.normal(own_key, dims, jnp.float32) * scale * loudness
    return jnp.minimum(jnp.maximum(drawn, -limit), limit).astype(kind)


def setup_inputs(seed: int = 0) -> dict:
    streams_of = jax.random.split(jax.random.key(seed), 17)
    tokens_new = scatter_about(streams_of[0], (PROMPT_COUNT, SAMPLE_COUNT, NEW_TOKENS, MODEL_DIM), 1.0, 6.0, ((0, 8),))
    prefix_len = draw_prefix_len(jax.random.fold_in(streams_of[16], 71), 0)
    tail_len = draw_tail_len(jax.random.fold_in(streams_of[16], 71), 0)
    pool_home = draw_pool_home(jax.random.fold_in(streams_of[16], 71), 0)
    pool_page = draw_pool_page(jax.random.fold_in(streams_of[16], 71), 0)
    slot_page_cache = draw_slot_page_cache(jax.random.fold_in(streams_of[16], 71), 0)
    tail_cache = scatter_about(streams_of[6], (PROMPT_COUNT, SAMPLE_COUNT, TAIL_LENGTH, 2, KEY_VALUE_WIDTH), 1.0, 6.0, ((0, 8), (4, 4)))
    routes_keys = jax.random.split(jax.random.fold_in(streams_of[7], 1), PROMPT_COUNT * SAMPLE_COUNT * NEW_TOKENS // (SAMPLE_COUNT * NEW_TOKENS))
    routes_turns = jax.random.permutation(jax.random.fold_in(streams_of[7], 3), PROMPT_COUNT * SAMPLE_COUNT * NEW_TOKENS // (SAMPLE_COUNT * NEW_TOKENS))
    routes = jax.vmap(lambda own, number: shared_out(jax.random.fold_in(streams_of[7], 2), own, number, SAMPLE_COUNT * NEW_TOKENS, EXPERTS, TOPK, MOST, 2))(routes_keys, routes_turns).reshape((PROMPT_COUNT, SAMPLE_COUNT, NEW_TOKENS, TOPK))
    norm_gains = jnp.clip(1.0 + 0.18 * jax.random.normal(streams_of[8], (3, MODEL_DIM), jnp.float32), 0.1, 1.9)
    query_weight = scatter_about(streams_of[9], (MODEL_DIM, QUERY_HEADS * HEAD_DIM), MODEL_DIM ** -0.5, 0.1875, ((1, 4),))
    key_value_weight = scatter_about(streams_of[10], (MODEL_DIM, 2, KEY_VALUE_WIDTH), MODEL_DIM ** -0.5, 0.1875, ((2, 4),))
    out_weight = scatter_about(streams_of[11], (QUERY_HEADS * HEAD_DIM, MODEL_DIM), (QUERY_HEADS * HEAD_DIM) ** -0.5, 0.1875, ((0, 4),))
    router = scatter_about(streams_of[12], (MODEL_DIM, EXPERTS), (MODEL_DIM // 4) ** -0.5, 0.375)
    expert_in = draw_expert_in(jax.random.fold_in(streams_of[16], 71), 0)
    expert_out = draw_expert_out(jax.random.fold_in(streams_of[16], 71), 0)
    score_weight = scatter_about(streams_of[15], (MODEL_DIM,), MODEL_DIM ** -0.5, 0.1875, (), jnp.float32)
    return dict(tokens_new=tokens_new, prefix_len=prefix_len, tail_len=tail_len, pool_home=pool_home, pool_page=pool_page, slot_page_cache=slot_page_cache, tail_cache=tail_cache, routes=routes, norm_gains=norm_gains, query_weight=query_weight, key_value_weight=key_value_weight, out_weight=out_weight, router=router, expert_in=expert_in, expert_out=expert_out, score_weight=score_weight)


EPSILON = 1e-05
ROPE_BASE = 10000.0
LOWEST = -1e+30

def rms_scale(values, gain_row):
    widened = values.astype(jnp.float32)
    return widened * lax.rsqrt(lax.optimization_barrier(jnp.mean(widened * widened, axis=-1, keepdims=True)) + EPSILON) * gain_row

def apply_rotary(vectors, token_positions):
    half_width = vectors.shape[-1] // 2
    frequency = ROPE_BASE ** (-jnp.arange(half_width, dtype=jnp.float32) / half_width)
    angles = token_positions.astype(jnp.float32)[..., None] * frequency
    cosine = jnp.cos(angles)[..., None, :]
    sine_part = jnp.sin(angles)[..., None, :]
    leading = vectors[..., :half_width]
    trailing = vectors[..., half_width:]
    return jnp.concatenate([leading * cosine - trailing * sine_part, trailing * cosine + leading * sine_part], axis=-1)

def block_stats(scores, visible):
    block_top = lax.optimization_barrier(jnp.max(jnp.where(visible, scores, LOWEST), axis=-1))
    weights = jnp.where(visible, jnp.exp(jnp.where(visible, scores - block_top[..., None], 0.0)), 0.0)
    return (block_top, lax.optimization_barrier(jnp.sum(weights, axis=-1)), weights)

def rounded(values):
    return lax.optimization_barrier(values.astype(jnp.bfloat16)).astype(jnp.float32)

def attend(query_rows, fresh_keys, fresh_values, prefix_page_list, page_ids, prefix_count, sample_tails, tail_count):
    score_scale = HEAD_DIM ** (-0.5)
    query_wide = query_rows.astype(jnp.float32)
    page_keys = prefix_page_list[:, :, 0].astype(jnp.float32)
    page_values = prefix_page_list[:, :, 1].astype(jnp.float32)
    page_scores = jnp.einsum('sikgd,btkd->bsikgt', query_wide, page_keys) * score_scale
    page_spots = page_ids[:, None] * PAGE_POSITIONS + jnp.arange(PAGE_POSITIONS, dtype=jnp.int32)[None, :]
    page_seen = ((page_spots < prefix_count) & (page_ids[:, None] >= 0))[:, None, None, None, None, :]
    page_top, page_total, page_weights = block_stats(page_scores, page_seen)
    page_numer = jnp.einsum('bsikgt,btkd->bsikgd', rounded(page_weights), page_values)
    tail_block_list = sample_tails.reshape(SAMPLE_COUNT, TAIL_LENGTH // PAGE_POSITIONS, PAGE_POSITIONS, 2, KEY_VALUE_HEADS, HEAD_DIM).astype(jnp.float32)
    tail_scores = jnp.einsum('sikgd,sbtkd->sbikgt', query_wide, tail_block_list[:, :, :, 0]) * score_scale
    tail_spots = jnp.arange(TAIL_LENGTH, dtype=jnp.int32).reshape(TAIL_LENGTH // PAGE_POSITIONS, PAGE_POSITIONS)
    tail_seen = (tail_spots[None] < tail_count[:, None, None])[:, :, None, None, None, :]
    tail_top, tail_total, tail_weights = block_stats(tail_scores, tail_seen)
    tail_numer = jnp.einsum('sbikgt,sbtkd->sbikgd', rounded(tail_weights), tail_block_list[:, :, :, 1])
    fresh_scores = jnp.einsum('sikgd,sjkd->sikgj', query_wide, fresh_keys.astype(jnp.float32)) * score_scale
    fresh_seen = (jnp.arange(NEW_TOKENS)[None, :] <= jnp.arange(NEW_TOKENS)[:, None])[None, :, None, None, :]
    fresh_top, fresh_total, fresh_weights = block_stats(fresh_scores, fresh_seen)
    fresh_numer = jnp.einsum('sikgj,sjkd->sikgd', rounded(fresh_weights), fresh_values.astype(jnp.float32))
    overall = jnp.maximum(jnp.maximum(lax.optimization_barrier(jnp.max(page_top, axis=0)), lax.optimization_barrier(jnp.max(tail_top, axis=1))), fresh_top)
    page_factor = jnp.exp(page_top - overall[None])
    tail_factor = jnp.exp(tail_top - overall[:, None])
    fresh_factor = jnp.exp(fresh_top - overall)
    denominator = lax.optimization_barrier(jnp.sum(page_factor * page_total, axis=0)) + lax.optimization_barrier(jnp.sum(tail_factor * tail_total, axis=1)) + fresh_factor * fresh_total
    numerator = lax.optimization_barrier(jnp.sum(page_factor[..., None] * page_numer, axis=0)) + lax.optimization_barrier(jnp.sum(tail_factor[..., None] * tail_numer, axis=1)) + fresh_factor[..., None] * fresh_numer
    return numerator / denominator[..., None]

def reference(tokens_new, prefix_len, tail_len, pool_home, pool_page, slot_page_cache, tail_cache, routes, norm_gains, query_weight, key_value_weight, out_weight, router, expert_in, expert_out, score_weight):
    row_count = PROMPT_COUNT * SAMPLE_COUNT * NEW_TOKENS
    query_group_width = QUERY_HEADS // KEY_VALUE_HEADS
    flat_tokens = tokens_new.reshape(row_count, MODEL_DIM)
    normalized_input = rms_scale(flat_tokens, norm_gains[0]).astype(jnp.bfloat16)
    query_vectors = jnp.dot(normalized_input, query_weight, preferred_element_type=jnp.float32).reshape(PROMPT_COUNT, SAMPLE_COUNT, NEW_TOKENS, QUERY_HEADS, HEAD_DIM)
    key_value_rows = jnp.dot(normalized_input, key_value_weight.reshape(MODEL_DIM, 2 * KEY_VALUE_WIDTH), preferred_element_type=jnp.float32).reshape(PROMPT_COUNT, SAMPLE_COUNT, NEW_TOKENS, 2, KEY_VALUE_HEADS, HEAD_DIM)
    token_positions = prefix_len[:, None, None] + tail_len[:, :, None] + jnp.arange(NEW_TOKENS, dtype=jnp.int32)[None, None, :]
    rotated_query = apply_rotary(query_vectors, token_positions).astype(jnp.bfloat16).reshape(PROMPT_COUNT, SAMPLE_COUNT, NEW_TOKENS, KEY_VALUE_HEADS, query_group_width, HEAD_DIM)
    key_rot = apply_rotary(key_value_rows[:, :, :, 0], token_positions).astype(jnp.bfloat16)
    value_new = key_value_rows[:, :, :, 1].astype(jnp.bfloat16)

    def one_prompt(prompt):
        score_ranking = jnp.argsort(jnp.where(pool_home == prompt, pool_page, PREFIX_PAGES), stable=True)[:PREFIX_PAGES].astype(jnp.int32)
        prefix_page_list = jnp.take(slot_page_cache, score_ranking, axis=0).reshape(PREFIX_PAGES, PAGE_POSITIONS, 2, KEY_VALUE_HEADS, HEAD_DIM)
        page_ids = jnp.take(pool_page, score_ranking)
        return attend(rotated_query[prompt], key_rot[prompt], value_new[prompt], prefix_page_list, page_ids, prefix_len[prompt], tail_cache[prompt], tail_len[prompt])
    attention = lax.map(one_prompt, jnp.arange(PROMPT_COUNT, dtype=jnp.int32))
    attn_rows = attention.reshape(row_count, QUERY_HEADS * HEAD_DIM).astype(jnp.bfloat16)
    attn_out = jnp.dot(attn_rows, out_weight, preferred_element_type=jnp.float32)
    residual = (flat_tokens.astype(jnp.float32) + attn_out).astype(jnp.bfloat16)
    normed_moe = rms_scale(residual, norm_gains[1]).astype(jnp.bfloat16)
    logits = jnp.dot(normed_moe, router, preferred_element_type=jnp.float32)
    routing = routes.reshape(row_count, TOPK)
    gate_values = jax.nn.softmax(jnp.take_along_axis(logits, routing, axis=1), axis=-1)
    pair_expert = routing.reshape(-1)
    pair_gate = gate_values.reshape(-1)
    pair_token = jnp.arange(row_count * TOPK, dtype=jnp.int32) // TOPK
    capacity = N_REQ * MOST

    def one_expert(expert):
        score_ranking = jnp.argsort((pair_expert != expert).astype(jnp.int32), stable=True)[:capacity].astype(jnp.int32)
        chosen = jnp.take(pair_token, score_ranking)
        inputs = jnp.take(normed_moe, chosen, axis=0)
        gate_up = jnp.dot(inputs, expert_in[expert].reshape(MODEL_DIM, 2 * FF), preferred_element_type=jnp.float32).reshape(capacity, 2, FF)
        hidden = (jax.nn.silu(gate_up[:, 0]) * gate_up[:, 1]).astype(jnp.bfloat16)
        result = jnp.dot(hidden, expert_out[expert], preferred_element_type=jnp.float32)
        weight = jnp.where(jnp.take(pair_expert, score_ranking) == expert, jnp.take(pair_gate, score_ranking), 0.0)
        return (result * weight[:, None], chosen)
    results, chosen_rows = lax.map(one_expert, jnp.arange(EXPERTS, dtype=jnp.int32))
    expert_mix = jnp.zeros((row_count, MODEL_DIM), jnp.float32).at[chosen_rows.reshape(-1)].add(results.reshape(-1, MODEL_DIM))
    layer_out = (residual.astype(jnp.float32) + expert_mix).astype(jnp.bfloat16)
    final_norm = rms_scale(layer_out, norm_gains[2])
    row_score = lax.optimization_barrier(jnp.sum(final_norm * score_weight, axis=-1))
    return (layer_out.reshape(PROMPT_COUNT, SAMPLE_COUNT, NEW_TOKENS, MODEL_DIM), row_score.reshape(PROMPT_COUNT, SAMPLE_COUNT, NEW_TOKENS))
```

```python
import functools

import jax
import jax.numpy as jnp
from jax import lax
from jax.experimental import pallas as pl
from jax.experimental.pallas import tpu as pltpu
from jax.sharding import PartitionSpec as P

HEAD_DIM = 64
LANES = 128
EPSILON = 1e-05
ROPE_BASE = 10000.0
LOWEST = -1e30
FLOOR = -1e28
F32 = jnp.float32
BF16 = jnp.bfloat16
VMEM_LIMIT = 48 * 1024 * 1024

VMEM = pl.BlockSpec(memory_space=pltpu.VMEM)
SMEM = pl.BlockSpec(memory_space=pltpu.SMEM)


def params():
    return pltpu.CompilerParams(vmem_limit_bytes=VMEM_LIMIT)


def cost(flops, moved):
    return pl.CostEstimate(flops=int(flops), bytes_accessed=int(moved), transcendentals=0)


def dot(left, right):
    return jnp.dot(left, right, preferred_element_type=F32)


def dot_t(left, right):
    return lax.dot_general(left, right, (((1,), (1,)), ((), ())), preferred_element_type=F32)


def lane_iota(shape):
    return lax.broadcasted_iota(jnp.int32, shape, len(shape) - 1)


def normalize(x, gain):
    return x * lax.rsqrt(jnp.mean(x * x, axis=-1, keepdims=True) + EPSILON) * gain


def rotate(x, cosine, sine):
    lanes = lane_iota(x.shape)
    partner = jnp.where(lanes % HEAD_DIM < HEAD_DIM // 2, pltpu.roll(x, 96, 1), pltpu.roll(x, 32, 1))
    return x * cosine + partner * sine


def by_head(packed, low):
    zero = jnp.zeros_like(packed)
    return jnp.concatenate([jnp.where(low, packed, zero), jnp.where(low, zero, packed)], axis=0)


def swap_halves(first, second):
    low = lane_iota(first.shape) < HEAD_DIM
    return (
        jnp.where(low, first, pltpu.roll(second, HEAD_DIM, 1)),
        jnp.where(low, pltpu.roll(first, HEAD_DIM, 1), second),
    )


def query_kernel(part_rows, tokens, gains, weight, cosine, sine, query, normed):
    rows = normalize(tokens[...].astype(F32), gains[0:1, :]).astype(BF16)
    normed[...] = rows
    flat = dot(rows, weight[...])
    pieces = []
    for group in swap_halves(flat[:, :LANES], flat[:, LANES:]):
        pieces.append(rotate(group, cosine[...], sine[...]).astype(BF16).astype(F32) * 0.125)
    parts = tokens.shape[0] // part_rows
    ordered = []
    for part in range(parts):
        for piece in pieces:
            ordered.append(piece[part * part_rows : (part + 1) * part_rows])
    query[...] = jnp.concatenate(ordered, axis=0).astype(BF16)


def tail_kernel(
    fresh_count, lengths, query, normed, weight, cosine, sine, cache, numer, top, total
):
    tokens = normed.shape[0]
    samples = cache.shape[0]
    width = cache.shape[1]
    parts = query.shape[0] // 16
    per_part = samples // parts
    spread = (
        lax.broadcasted_iota(jnp.int32, (LANES, 2 * LANES), 1)
        == 2 * lax.broadcasted_iota(jnp.int32, (LANES, 2 * LANES), 0)
    ).astype(BF16)
    rows = normed[...]
    widened = jnp.concatenate(
        [dot(rows[:, c : c + LANES], spread) for c in range(0, rows.shape[1], LANES)], axis=1
    )
    both = jnp.concatenate([widened, pltpu.roll(widened, 1, 1)], axis=0).astype(BF16)
    made = dot(both, weight[...])
    key_new = rotate(made[:tokens], cosine[...], sine[...]).astype(BF16)
    value_new = made[tokens:].astype(BF16)
    low = lane_iota((16, LANES)) < HEAD_DIM
    row_id = lax.broadcasted_iota(jnp.int32, (32, 1), 0)
    row_sample = (row_id % 8) // fresh_count
    row_fresh = row_id % fresh_count
    column = lane_iota((32, width))
    even = column % 2 == 0
    token_id = lane_iota((32, tokens))
    for part in range(parts):
        wide = by_head(query[part * 16 : (part + 1) * 16, :], low)
        scores = None
        length = jnp.zeros((32, 1), jnp.int32)
        for a in range(per_part):
            sample = part * per_part + a
            one = dot_t(wide, cache[sample])
            scores = one if a == 0 else jnp.where(row_sample == a, one, scores)
            length = jnp.where(row_sample == a, lengths[0, sample], length)
        scores = jnp.where(even & (column < 2 * length), scores, LOWEST)
        fresh = dot_t(wide, key_new)
        own_sample = row_sample + part * per_part
        fresh_seen = (token_id // fresh_count == own_sample) & (token_id % fresh_count <= row_fresh)
        fresh = jnp.where(fresh_seen, fresh, LOWEST)
        peak = jnp.maximum(
            jnp.max(scores, axis=1, keepdims=True), jnp.max(fresh, axis=1, keepdims=True)
        )
        weights = jnp.exp(scores - peak)
        fresh_weights = jnp.exp(fresh - peak)
        amount = jnp.sum(weights, axis=1, keepdims=True) + jnp.sum(
            fresh_weights, axis=1, keepdims=True
        )
        shifted = pltpu.roll(weights, 1, 1).astype(BF16)
        mixed = None
        for a in range(per_part):
            one = dot(shifted, cache[part * per_part + a])
            mixed = one if a == 0 else jnp.where(row_sample == a, one, mixed)
        mixed = mixed + dot(fresh_weights.astype(BF16), value_new)
        place = slice(part * 16, (part + 1) * 16)
        numer[place, :] = jnp.where(low, mixed[:16], mixed[16:])
        top[place, :] = jnp.where(low, peak[:16], peak[16:])
        total[place, :] = jnp.where(low, amount[:16], amount[16:])


def page_kernel(
    slot_cap,
    parts,
    place,
    homes,
    pages,
    lengths,
    query,
    cache,
    tail_numer,
    tail_top,
    tail_total,
    out,
    slots,
    counts,
):
    requests = query.shape[0]
    pool = cache.shape[0]
    width = cache.shape[1]
    rows = parts * 16
    page_size = width // 2
    me = place[0]
    base = me * pool

    def clear(r, carry):
        counts[r] = 0
        for j in range(slot_cap):
            slots[r * slot_cap + j] = -1
        return carry

    lax.fori_loop(0, requests, clear, 0)

    def assign(v, carry):
        r = homes[base + v]
        rank = counts[r]
        slots[r * slot_cap + rank] = v
        counts[r] = rank + 1
        return carry

    lax.fori_loop(0, pool, assign, 0)

    low = lane_iota((rows, LANES)) < HEAD_DIM
    column = lane_iota((2 * rows, width))
    even = column % 2 == 0
    section = (lane_iota((rows, LANES)) % HEAD_DIM) // 16

    def emit(r, numer, top, total):
        high = total.astype(BF16).astype(F32)
        stats = jnp.where(section == 0, top, jnp.where(section == 1, high, total - high))
        numer = numer.astype(BF16)
        stats = stats.astype(BF16)
        for part in range(parts):
            out[r * parts + part, 0:16, :] = numer[part * 16 : (part + 1) * 16]
            out[r * parts + part, 16:32, :] = stats[part * 16 : (part + 1) * 16]

    def one_request(r, carry):
        wide = by_head(query[r, 0:rows, :], low)
        scores = []
        found = []
        for j in range(slot_cap):
            slot = slots[r * slot_cap + j]
            safe = jnp.maximum(slot, 0)
            found.append(safe)
            limit = jnp.where(slot >= 0, 2 * (lengths[r] - pages[base + safe] * page_size), 0)
            one = dot_t(wide, cache[safe])
            scores.append(jnp.where(even & (column < limit), one, LOWEST))
        peak = functools.reduce(jnp.maximum, scores)
        peak = jnp.maximum(jnp.max(peak, axis=1, keepdims=True), FLOOR).astype(BF16).astype(F32)
        amount = None
        mixed = None
        for j in range(slot_cap):
            weights = jnp.exp(scores[j] - peak)
            amount = weights if j == 0 else amount + weights
            one = dot(pltpu.roll(weights, 1, 1).astype(BF16), cache[found[j]])
            mixed = one if j == 0 else mixed + one
        amount = jnp.sum(amount, axis=1, keepdims=True)
        numer = jnp.where(low, mixed[:rows], mixed[rows:])
        top = jnp.where(low, peak[:rows], peak[rows:])
        total = jnp.where(low, amount[:rows], amount[rows:])

        @pl.when(r != me)
        def _():
            emit(r, numer, top, total)

        @pl.when(r == me)
        def _():
            joint = jnp.maximum(top, tail_top[...]).astype(BF16).astype(F32)
            here = jnp.exp(top - joint)
            there = jnp.exp(tail_top[...] - joint)
            emit(
                r,
                numer * here + tail_numer[...] * there,
                joint,
                total * here + tail_total[...] * there,
            )

        return carry

    lax.fori_loop(0, requests, one_request, 0)


def merge_kernel(place, arrived, tokens, gains, weight, out, residual):
    parts = arrived.shape[1]
    low = lane_iota((1, 16, LANES)) < HEAD_DIM
    blocks = []
    for t in range(parts):
        stats = arrived[:, t, 16:32, :].astype(F32)
        numer = arrived[:, t, 0:16, :].astype(F32)

        def pick(lane):
            return jnp.where(
                low, stats[:, :, lane : lane + 1], stats[:, :, HEAD_DIM + lane : HEAD_DIM + lane + 1]
            )

        top = pick(0)
        total = pick(16) + pick(32)
        factor = jnp.exp(top - jnp.max(top, axis=0, keepdims=True))
        attended = jnp.sum(factor * numer, axis=0) / jnp.sum(factor * total, axis=0)
        blocks.extend(swap_halves(attended[0:8], attended[8:16]))
    attended = jnp.concatenate(blocks, axis=1).astype(BF16)
    projected = dot(attended, weight[...])
    rows = (tokens[place[1]].astype(F32) + projected).astype(BF16).astype(F32)
    residual[...] = rows
    normed = normalize(rows, gains[1:2, :])
    half = normed.shape[1] // 2
    message = jnp.concatenate([normed[:, :half], normed[:, half:]], axis=0).astype(BF16)
    for n in range(out.shape[0]):
        out[n] = message


def prepare_kernel(source, out, wide):
    depth = source.shape[1] // 2
    wide[...] = source[0].astype(F32)
    out[:, :LANES] = wide[pl.ds(0, depth, stride=2), :].astype(BF16)
    out[:, LANES:] = wide[pl.ds(1, depth, stride=2), :].astype(BF16)


def expert_kernel(copies, part_rows, place, arrived, packed, router, first, second, out):
    count = arrived.shape[0]
    half = arrived.shape[2]
    block = pl.program_id(0)
    requests = packed.shape[0]
    parts = count // requests
    local = first.shape[1] // (2 * LANES)
    expert_count = router.shape[0]
    states = arrived[...].astype(F32)
    states = jnp.concatenate(
        [
            states[:, :part_rows].reshape(count * part_rows, half),
            states[:, part_rows:].reshape(count * part_rows, half),
        ],
        axis=1,
    ).astype(BF16)
    logits = dot_t(states, router[...])
    masks = []
    for r in range(requests):
        row = packed[r].astype(F32)[:part_rows]
        for t in range(parts):
            moved = row if t == 0 else pltpu.roll(row, LANES - t * expert_count, 1)
            masks.append(moved[:, :expert_count])
    mask = jnp.concatenate(masks, axis=0)
    chosen = jnp.where(mask > 0.5, logits, LOWEST)
    shares = jnp.exp(chosen - jnp.max(chosen, axis=1, keepdims=True))
    gates = shares / jnp.sum(shares, axis=1, keepdims=True)
    hidden_all = dot(states, first[...])
    lanes = lane_iota(gates.shape)
    row_request = block * requests + lax.broadcasted_iota(
        jnp.int32, (gates.shape[0], 1), 0
    ) // (parts * part_rows)
    pieces = []
    for e in range(local):
        slot = place[0] * local + e
        gate = jnp.sum(
            jnp.where(lanes == slot % expert_count, gates, 0.0), axis=1, keepdims=True
        )
        if copies > 1:
            gate = jnp.where(row_request % copies == slot // expert_count, gate, 0.0)
        value = hidden_all[:, e * 2 * LANES : e * 2 * LANES + LANES]
        other = hidden_all[:, e * 2 * LANES + LANES : (e + 1) * 2 * LANES]
        hidden = (value / (1.0 + jnp.exp(-value)) * other).astype(BF16).astype(F32)
        pieces.append((hidden * gate).astype(BF16))
    mixed = dot(jnp.concatenate(pieces, axis=1), second[...])
    out[...] = jnp.concatenate(
        [
            mixed[:, :half].reshape(count, part_rows, half),
            mixed[:, half:].reshape(count, part_rows, half),
        ],
        axis=1,
    ).astype(BF16)


def finish_kernel(arrived, residual, out):
    mixed = jnp.sum(arrived[...].astype(F32), axis=0)
    rows = mixed.shape[0] // 2
    half = mixed.shape[1]
    kept = residual[...]
    message = jnp.concatenate([kept[:, :half], kept[:, half:]], axis=0) + mixed
    message = message.astype(BF16)
    for n in range(out.shape[0]):
        out[n] = message


def score_kernel(arrived, gains, weight, layer, score):
    parts, double, half = arrived.shape
    rows = double // 2
    states = arrived[...].astype(F32)
    states = jnp.concatenate(
        [
            states[:, :rows].reshape(parts * rows, half),
            states[:, rows:].reshape(parts * rows, half),
        ],
        axis=1,
    )
    layer[...] = states.astype(BF16)
    final = normalize(states, gains[2:3, :])
    score[...] = jnp.sum(final * weight[...], axis=1, keepdims=True)


def shards(
    tokens_new,
    prefix_len,
    tail_len,
    pool_home,
    pool_page,
    slot_page_cache,
    tail_cache,
    routes,
    norm_gains,
    query_weight,
    key_value_weight,
    out_weight,
    router,
    expert_in,
    expert_out,
    score_weight,
):
    req_count = lax.axis_size("req")
    parts = lax.axis_size("tp")
    device = lax.axis_index("req")
    place = jnp.stack([device, lax.axis_index("tp")]).astype(jnp.int32)
    _, samples, fresh_count, model = tokens_new.shape
    tokens = samples * fresh_count
    part_rows = tokens // parts
    pool = slot_page_cache.shape[0]
    page_size = slot_page_cache.shape[1]
    slot_cap = max(1, pool // req_count)
    tail_count = tail_cache.shape[2]
    local = expert_in.shape[0]
    expert_count = router.shape[1]
    copies = local * req_count // expert_count
    everyone = req_count * parts
    rows = 2 * tokens

    flat_tokens = tokens_new.reshape(tokens, model)
    out_full = lax.all_gather(out_weight, "tp", axis=0, tiled=True)

    frequency = ROPE_BASE ** (-jnp.arange(HEAD_DIM // 2, dtype=F32) / (HEAD_DIM // 2))
    positions = (
        jnp.take(prefix_len, device)
        + tail_len[0][:, None]
        + jnp.arange(fresh_count, dtype=jnp.int32)[None, :]
    ).reshape(tokens)
    angles = positions.astype(F32)[:, None] * frequency[None, :]
    cosine = jnp.cos(angles)
    sine = jnp.sin(angles)
    cosine = jnp.concatenate([cosine] * 4, axis=1)
    sine = jnp.concatenate([-sine, sine, -sine, sine], axis=1)

    query, normed = pl.pallas_call(
        functools.partial(query_kernel, part_rows),
        out_shape=(
            jax.ShapeDtypeStruct((rows, LANES), BF16),
            jax.ShapeDtypeStruct((tokens, model), BF16),
        ),
        in_specs=[VMEM] * 5,
        out_specs=(VMEM, VMEM),
        compiler_params=params(),
        name="query",
    )(flat_tokens, norm_gains, query_weight, cosine, sine)

    named = (
        routes.reshape(tokens, -1)[:, :, None]
        == jnp.arange(expert_count, dtype=jnp.int32)[None, None, :]
    )
    named = jnp.any(named, axis=1).astype(BF16)
    named = named.reshape(parts, part_rows, expert_count).transpose(1, 0, 2)
    named = named.reshape(part_rows, parts * expert_count)
    named = jnp.pad(named, ((0, 16 - part_rows), (0, 0)))
    first_message = jnp.concatenate([query, named], axis=0)
    first_all = lax.all_to_all(
        jnp.broadcast_to(first_message[None], (req_count,) + first_message.shape),
        "req",
        split_axis=0,
        concat_axis=0,
        tiled=True,
    )

    tail_numer, tail_top, tail_total = pl.pallas_call(
        functools.partial(tail_kernel, fresh_count),
        out_shape=(jax.ShapeDtypeStruct((rows, LANES), F32),) * 3,
        in_specs=[SMEM] + [VMEM] * 6,
        out_specs=(VMEM,) * 3,
        compiler_params=params(),
        cost_estimate=cost(2e9, 5e6),
        name="tail",
    )(
        tail_len,
        query,
        normed,
        key_value_weight.reshape(2 * model, LANES),
        cosine,
        sine,
        tail_cache.reshape(samples, 2 * tail_count, LANES),
    )

    first_weights = pl.pallas_call(
        prepare_kernel,
        grid=(local,),
        out_shape=jax.ShapeDtypeStruct((model, local * 2 * LANES), BF16),
        in_specs=[pl.BlockSpec((1, 2 * model, LANES), lambda e: (e, 0, 0))],
        out_specs=pl.BlockSpec((model, 2 * LANES), lambda e: (0, e)),
        scratch_shapes=[pltpu.VMEM((2 * model, LANES), F32)],
        compiler_params=params(),
        cost_estimate=cost(1e6, 8e6),
        name="prepare",
    )(expert_in.reshape(local, 2 * model, LANES))

    partial = pl.pallas_call(
        functools.partial(page_kernel, slot_cap, parts),
        out_shape=jax.ShapeDtypeStruct((everyone, 32, LANES), BF16),
        in_specs=[SMEM] * 4 + [VMEM] * 5,
        out_specs=VMEM,
        scratch_shapes=[
            pltpu.SMEM((req_count * slot_cap,), jnp.int32),
            pltpu.SMEM((req_count,), jnp.int32),
        ],
        compiler_params=params(),
        cost_estimate=cost(2e9, 5e6),
        name="pages",
    )(
        place,
        pool_home,
        pool_page,
        prefix_len,
        first_all,
        slot_page_cache.reshape(pool, 2 * page_size, LANES),
        tail_numer,
        tail_top,
        tail_total,
    )
    partial = lax.all_to_all(partial, ("req", "tp"), split_axis=0, concat_axis=0, tiled=True)

    half = model // 2
    message, residual = pl.pallas_call(
        merge_kernel,
        out_shape=(
            jax.ShapeDtypeStruct((everyone, 2 * part_rows, half), BF16),
            jax.ShapeDtypeStruct((part_rows, model), F32),
        ),
        in_specs=[SMEM] + [VMEM] * 4,
        out_specs=(VMEM, VMEM),
        compiler_params=params(),
        name="merge",
    )(
        place,
        partial.reshape(req_count, parts, 32, LANES),
        flat_tokens.reshape(parts, part_rows, model),
        norm_gains,
        out_full,
    )
    states = lax.all_to_all(message, ("req", "tp"), split_axis=0, concat_axis=0, tiled=True)

    group = min(req_count, 8)
    mixed = pl.pallas_call(
        functools.partial(expert_kernel, copies, part_rows),
        grid=(req_count // group,),
        out_shape=jax.ShapeDtypeStruct((everyone, 2 * part_rows, half), BF16),
        in_specs=[
            SMEM,
            pl.BlockSpec((group * parts, 2 * part_rows, half), lambda b: (b, 0, 0)),
            pl.BlockSpec((group, 16, LANES), lambda b: (b, rows // 16, 0)),
            VMEM,
            VMEM,
            VMEM,
        ],
        out_specs=pl.BlockSpec((group * parts, 2 * part_rows, half), lambda b: (b, 0, 0)),
        compiler_params=params(),
        name="experts",
    )(
        place,
        states,
        first_all,
        router.T,
        first_weights,
        expert_out.reshape(local * LANES, model),
    )
    mixed = lax.all_to_all(mixed, ("req", "tp"), split_axis=0, concat_axis=0, tiled=True)

    finished = pl.pallas_call(
        finish_kernel,
        out_shape=jax.ShapeDtypeStruct((parts, 2 * part_rows, half), BF16),
        in_specs=[VMEM, VMEM],
        out_specs=VMEM,
        compiler_params=params(),
        name="finish",
    )(mixed, residual)
    finished = lax.all_to_all(finished, "tp", split_axis=0, concat_axis=0, tiled=True)

    layer, score = pl.pallas_call(
        score_kernel,
        out_shape=(
            jax.ShapeDtypeStruct((tokens, model), BF16),
            jax.ShapeDtypeStruct((tokens, 1), F32),
        ),
        in_specs=[VMEM] * 3,
        out_specs=(VMEM, VMEM),
        compiler_params=params(),
        name="score",
    )(finished, norm_gains, score_weight.reshape(1, model))
    return (
        layer.reshape(1, samples, fresh_count, model),
        score.reshape(1, samples, fresh_count),
    )


def solution(mesh):
    placed = (
        P("req", None, None, None),
        P(),
        P("req", None),
        P(),
        P(),
        P("req", None, None, "tp"),
        P("req", None, None, None, "tp"),
        P("req", None, None, None),
        P(),
        P(None, "tp"),
        P(None, None, "tp"),
        P("tp", None),
        P(),
        P("req", None, None, "tp"),
        P("req", "tp", None),
        P(),
    )
    return jax.shard_map(
        shards,
        mesh=mesh,
        in_specs=placed,
        out_specs=(P("req", None, None, None), P("req", None, None)),
        check_vma=False,
    )
```

```python
import functools

import jax
import jax.numpy as jnp
import numpy as np
from jax import lax
from jax.experimental import pallas as pl
from jax.experimental.pallas import tpu as pltpu
from jax.sharding import PartitionSpec as P

HEAD_DIM = 64
LANES = 128
EPSILON = 1e-05
ROPE_BASE = 10000.0
LOWEST = -1e30
FLOOR = -1e28
F32 = jnp.float32
BF16 = jnp.bfloat16
MIB = 1024 * 1024

VMEM = pl.BlockSpec(memory_space=pltpu.VMEM)
SMEM = pl.BlockSpec(memory_space=pltpu.SMEM)
HBM = pl.BlockSpec(memory_space=pltpu.HBM)


def params(mib):
    return pltpu.CompilerParams(vmem_limit_bytes=mib * MIB)


def cost(flops, moved):
    return pl.CostEstimate(flops=int(flops), bytes_accessed=int(moved), transcendentals=0)


def dot(left, right):
    return jnp.dot(left, right, preferred_element_type=F32)


def dot_t(left, right):
    return lax.dot_general(left, right, (((1,), (1,)), ((), ())), preferred_element_type=F32)


def lane_iota(shape):
    return lax.broadcasted_iota(jnp.int32, shape, len(shape) - 1)


def normalize(x, gain):
    return x * lax.rsqrt(jnp.mean(x * x, axis=-1, keepdims=True) + EPSILON) * gain


def rotate(x, cosine, sine):
    lanes = lane_iota(x.shape)
    partner = jnp.where(lanes % HEAD_DIM < HEAD_DIM // 2, pltpu.roll(x, 96, 1), pltpu.roll(x, 32, 1))
    return x * cosine + partner * sine


def by_head(packed, low):
    zero = jnp.zeros_like(packed)
    return jnp.concatenate([jnp.where(low, packed, zero), jnp.where(low, zero, packed)], axis=0)


def swap_halves(first, second):
    low = lane_iota(first.shape) < HEAD_DIM
    return (
        jnp.where(low, first, pltpu.roll(second, HEAD_DIM, 1)),
        jnp.where(low, pltpu.roll(first, HEAD_DIM, 1), second),
    )


def query_kernel(
    fresh_count,
    place,
    prefix,
    lengths,
    tokens,
    named,
    gains,
    frequency,
    weight,
    message,
    flat,
    normed,
    cosine,
    sine,
    wide,
    ordered,
):
    count, model = normed.shape
    samples = count // fresh_count
    parts, part_rows, _ = flat.shape
    blocks = model // LANES
    wide[...] = tokens[...].astype(F32)
    for c in range(blocks):
        for i in range(fresh_count):
            ordered[c, pl.ds(i, samples, stride=fresh_count), :] = wide[
                pl.ds(fresh_count * c + i, samples, stride=fresh_count * blocks), :
            ]
    states = jnp.concatenate([ordered[c] for c in range(blocks)], axis=1)
    for part in range(parts):
        flat[part] = states[part * part_rows : (part + 1) * part_rows].astype(BF16)
    rows = normalize(states, gains[0:1, :]).astype(BF16)
    normed[...] = rows
    row_id = lax.broadcasted_iota(jnp.int32, (count, 1), 0)
    position = row_id % fresh_count + prefix[place[0]]
    for sample in range(samples):
        position = position + jnp.where(row_id // fresh_count == sample, lengths[0, sample], 0)
    angles = position.astype(F32) * frequency[...]
    cosine[...] = jnp.cos(angles)
    turn = jnp.sin(angles)
    sine[...] = jnp.where(lane_iota(turn.shape) % HEAD_DIM < HEAD_DIM // 2, -turn, turn)
    made = dot(rows, weight[...])
    pieces = []
    for group in swap_halves(made[:, :LANES], made[:, LANES:]):
        pieces.append(rotate(group, cosine[...], sine[...]).astype(BF16).astype(F32) * 0.125)
    packed = []
    for part in range(parts):
        for piece in pieces:
            packed.append(piece[part * part_rows : (part + 1) * part_rows])
    routed = named[...].astype(F32)
    packed.append(
        jnp.concatenate(
            [routed, jnp.zeros((routed.shape[0], LANES - routed.shape[1]), F32)], axis=1
        )
    )
    packed = jnp.concatenate(packed, axis=0).astype(BF16)
    for n in range(message.shape[0]):
        message[n] = packed


def split_pages_kernel(source, out, wide):
    count, double, _ = source.shape
    half = double // 2
    wide[...] = source[...].astype(F32).reshape(count * double, LANES)
    keys = wide[pl.ds(0, count * half, stride=2), :].astype(BF16)
    values = wide[pl.ds(1, count * half, stride=2), :].astype(BF16)
    out[:, :half, :] = keys.reshape(count, half, LANES)
    out[:, half:, :] = values.reshape(count, half, LANES)


def tail_kernel(
    fresh_count, lengths, query, normed, weight, cosine, sine, cache, numer, top, total
):
    tokens = normed.shape[0]
    samples = cache.shape[0]
    width = cache.shape[1]
    parts = 2 * tokens // 16
    per_part = samples // parts
    spread = (
        lax.broadcasted_iota(jnp.int32, (LANES, 2 * LANES), 1)
        == 2 * lax.broadcasted_iota(jnp.int32, (LANES, 2 * LANES), 0)
    ).astype(BF16)
    rows = normed[...]
    widened = jnp.concatenate(
        [dot(rows[:, c : c + LANES], spread) for c in range(0, rows.shape[1], LANES)], axis=1
    )
    both = jnp.concatenate([widened, pltpu.roll(widened, 1, 1)], axis=0).astype(BF16)
    made = dot(both, weight[...])
    key_new = rotate(made[:tokens], cosine[...], sine[...]).astype(BF16)
    value_new = made[tokens:].astype(BF16)
    low = lane_iota((16, LANES)) < HEAD_DIM
    row_id = lax.broadcasted_iota(jnp.int32, (32, 1), 0)
    row_sample = (row_id % 8) // fresh_count
    row_fresh = row_id % fresh_count
    column = lane_iota((32, width))
    even = column % 2 == 0
    token_id = lane_iota((32, tokens))
    for part in range(parts):
        wide = by_head(query[0, part * 16 : (part + 1) * 16, :], low)
        scores = None
        length = jnp.zeros((32, 1), jnp.int32)
        for a in range(per_part):
            sample = part * per_part + a
            one = dot_t(wide, cache[sample])
            scores = one if a == 0 else jnp.where(row_sample == a, one, scores)
            length = jnp.where(row_sample == a, lengths[0, sample], length)
        scores = jnp.where(even & (column < 2 * length), scores, LOWEST)
        fresh = dot_t(wide, key_new)
        own_sample = row_sample + part * per_part
        fresh_seen = (token_id // fresh_count == own_sample) & (token_id % fresh_count <= row_fresh)
        fresh = jnp.where(fresh_seen, fresh, LOWEST)
        peak = jnp.maximum(
            jnp.max(scores, axis=1, keepdims=True), jnp.max(fresh, axis=1, keepdims=True)
        )
        weights = jnp.exp(scores - peak)
        fresh_weights = jnp.exp(fresh - peak)
        amount = jnp.sum(weights, axis=1, keepdims=True) + jnp.sum(
            fresh_weights, axis=1, keepdims=True
        )
        shifted = pltpu.roll(weights, 1, 1).astype(BF16)
        mixed = None
        for a in range(per_part):
            one = dot(shifted, cache[part * per_part + a])
            mixed = one if a == 0 else jnp.where(row_sample == a, one, mixed)
        mixed = mixed + dot(fresh_weights.astype(BF16), value_new)
        place = slice(part * 16, (part + 1) * 16)
        numer[place, :] = jnp.where(low, mixed[:16], mixed[16:])
        top[place, :] = jnp.where(low, peak[:16], peak[16:])
        total[place, :] = jnp.where(low, amount[:16], amount[16:])


def page_kernel(
    slot_cap,
    parts,
    place,
    homes,
    pages,
    lengths,
    query,
    cache,
    tail_numer,
    tail_top,
    tail_total,
    out,
    slots,
    counts,
):
    requests = query.shape[0]
    pool = cache.shape[0]
    width = cache.shape[1]
    rows = parts * 16
    page_size = width // 2
    me = place[0]
    base = me * pool

    def clear(r, carry):
        counts[r] = 0
        for j in range(slot_cap):
            slots[r * slot_cap + j] = -1
        return carry

    lax.fori_loop(0, requests, clear, 0)

    def assign(v, carry):
        r = homes[base + v]
        rank = counts[r]
        slots[r * slot_cap + rank] = v
        counts[r] = rank + 1
        return carry

    lax.fori_loop(0, pool, assign, 0)

    low = lane_iota((rows, LANES)) < HEAD_DIM
    column = lane_iota((2 * rows, page_size))
    section = (lane_iota((rows, LANES)) % HEAD_DIM) // 16

    def emit(r, numer, top, total):
        high = total.astype(BF16).astype(F32)
        stats = jnp.where(section == 0, top, jnp.where(section == 1, high, total - high))
        numer = numer.astype(BF16)
        stats = stats.astype(BF16)
        for part in range(parts):
            out[r * parts + part, 0:16, :] = numer[part * 16 : (part + 1) * 16]
            out[r * parts + part, 16:32, :] = stats[part * 16 : (part + 1) * 16]

    def one_request(r, carry):
        wide = by_head(query[r, 0:rows, :], low)
        scores = []
        found = []
        for j in range(slot_cap):
            slot = slots[r * slot_cap + j]
            safe = jnp.maximum(slot, 0)
            found.append(safe)
            limit = jnp.where(slot >= 0, lengths[r] - pages[base + safe] * page_size, 0)
            one = dot_t(wide, cache[safe, :page_size, :])
            scores.append(jnp.where(column < limit, one, LOWEST))
        peak = functools.reduce(jnp.maximum, scores)
        peak = jnp.maximum(jnp.max(peak, axis=1, keepdims=True), FLOOR).astype(BF16).astype(F32)
        amount = None
        mixed = None
        for j in range(slot_cap):
            weights = jnp.exp(scores[j] - peak)
            amount = weights if j == 0 else amount + weights
            one = dot(weights.astype(BF16), cache[found[j], page_size:, :])
            mixed = one if j == 0 else mixed + one
        amount = jnp.sum(amount, axis=1, keepdims=True)
        numer = jnp.where(low, mixed[:rows], mixed[rows:])
        top = jnp.where(low, peak[:rows], peak[rows:])
        total = jnp.where(low, amount[:rows], amount[rows:])

        @pl.when(r != me)
        def _():
            emit(r, numer, top, total)

        @pl.when(r == me)
        def _():
            joint = jnp.maximum(top, tail_top[...]).astype(BF16).astype(F32)
            here = jnp.exp(top - joint)
            there = jnp.exp(tail_top[...] - joint)
            emit(
                r,
                numer * here + tail_numer[...] * there,
                joint,
                total * here + tail_total[...] * there,
            )

        return carry

    lax.fori_loop(0, requests, one_request, 0)


def merge_kernel(place, arrived, tokens, gains, source, out, residual, weight, done):
    loading = pltpu.make_async_copy(source, weight, done)
    loading.start()
    parts = arrived.shape[1]
    low = lane_iota((1, 16, LANES)) < HEAD_DIM
    blocks = []
    for t in range(parts):
        stats = arrived[:, t, 16:32, :].astype(F32)
        numer = arrived[:, t, 0:16, :].astype(F32)

        def pick(lane):
            return jnp.where(
                low, stats[:, :, lane : lane + 1], stats[:, :, HEAD_DIM + lane : HEAD_DIM + lane + 1]
            )

        top = pick(0)
        total = pick(16) + pick(32)
        factor = jnp.exp(top - jnp.max(top, axis=0, keepdims=True))
        attended = jnp.sum(factor * numer, axis=0) / jnp.sum(factor * total, axis=0)
        blocks.extend(swap_halves(attended[0:8], attended[8:16]))
    attended = jnp.concatenate(blocks, axis=1).astype(BF16)
    loading.wait()
    projected = dot(attended, weight[...])
    rows = (tokens[place[1]].astype(F32) + projected).astype(BF16).astype(F32)
    residual[...] = rows
    normed = normalize(rows, gains[1:2, :])
    half = normed.shape[1] // 2
    message = jnp.concatenate([normed[:, :half], normed[:, half:]], axis=0).astype(BF16)
    for n in range(out.shape[0]):
        out[n] = message


def prepare_kernel(source, out, wide):
    depth = source.shape[1] // 2
    wide[...] = source[0].astype(F32)
    out[:, :LANES] = wide[pl.ds(0, depth, stride=2), :].astype(BF16)
    out[:, LANES:] = wide[pl.ds(1, depth, stride=2), :].astype(BF16)


def names_kernel(part_rows, fresh_count, place, packed, out):
    requests, span, _ = packed.shape
    experts = out.shape[1]
    halves = out.shape[0] // (requests * part_rows)
    top = span // fresh_count
    row = lax.broadcasted_iota(jnp.int32, (halves * part_rows, LANES), 0)
    token = (row // part_rows) * 2 * part_rows + (place[1] % 2) * part_rows + row % part_rows
    pick = (lane_iota(row.shape) == token // fresh_count).astype(BF16)
    found = jnp.concatenate([dot_t(pick, packed[r]) for r in range(requests)], axis=0)
    fresh = lax.broadcasted_iota(jnp.int32, (found.shape[0], 1), 0) % fresh_count
    chosen = found[:, :top]
    for i in range(1, fresh_count):
        chosen = jnp.where(fresh == i, found[:, i * top : (i + 1) * top], chosen)
    lanes = lane_iota(out.shape).astype(F32)
    mask = jnp.zeros(out.shape, F32)
    for k in range(top):
        mask = jnp.where(chosen[:, k : k + 1] == lanes, 1.0, mask)
    out[...] = mask


def expert_kernel(
    copies, part_rows, place, arrived, mask, router, first, first_other, second, second_other, out
):
    count = arrived.shape[0]
    half = arrived.shape[2]
    block = pl.program_id(0)
    local = first.shape[1] // (2 * LANES)
    expert_count = router.shape[0]
    states = arrived[...].astype(F32)
    states = jnp.concatenate(
        [
            states[:, :part_rows].reshape(count * part_rows, half),
            states[:, part_rows:].reshape(count * part_rows, half),
        ],
        axis=1,
    ).astype(BF16)
    logits = dot_t(states, router[...])
    chosen = jnp.where(mask[...] > 0.5, logits, LOWEST)
    shares = jnp.exp(chosen - jnp.max(chosen, axis=1, keepdims=True))
    gates = shares / jnp.sum(shares, axis=1, keepdims=True)
    lanes = lane_iota(gates.shape)
    row_request = (
        block * count + lax.broadcasted_iota(jnp.int32, (gates.shape[0], 1), 0) // part_rows
    ) // 2
    weights = []
    for e in range(local):
        slot = place[0] * local + e
        gate = jnp.sum(
            jnp.where(lanes == slot % expert_count, gates, 0.0), axis=1, keepdims=True
        )
        if copies > 1:
            gate = jnp.where(row_request % copies == slot // expert_count, gate, 0.0)
        weights.append(gate)
    mixed = None
    for up, down in ((first, second), (first_other, second_other)):
        wide = dot(states, up[...])
        pieces = []
        for e in range(local):
            value = wide[:, e * 2 * LANES : e * 2 * LANES + LANES]
            other = wide[:, e * 2 * LANES + LANES : (e + 1) * 2 * LANES]
            hidden = (value / (1.0 + jnp.exp(-value)) * other).astype(BF16).astype(F32)
            pieces.append((hidden * weights[e]).astype(BF16))
        part = dot(jnp.concatenate(pieces, axis=1), down[...])
        mixed = part if mixed is None else mixed + part
    out[...] = jnp.concatenate(
        [
            mixed[:, :half].reshape(count, part_rows, half),
            mixed[:, half:].reshape(count, part_rows, half),
        ],
        axis=1,
    ).astype(BF16)


def finish_kernel(arrived, residual, out):
    mixed = jnp.sum(arrived[...].astype(F32), axis=0)
    half = mixed.shape[1]
    kept = residual[...]
    message = jnp.concatenate([kept[:, :half], kept[:, half:]], axis=0) + mixed
    out[...] = message.astype(BF16)


def score_kernel(fresh_count, place, *refs):
    *arrived, gains, weight, layer, score, ordered, wide = refs
    double, half = arrived[0].shape
    rows = double // 2
    blocks, tokens, _ = ordered.shape
    samples = tokens // fresh_count
    for step, block in enumerate(arrived):
        state = block[...].astype(F32)
        spot = pl.ds(pl.multiple_of((place[1] ^ step) * rows, rows), rows)
        for c in range(blocks // 2):
            ordered[c, spot, :] = state[:rows, c * LANES : (c + 1) * LANES]
            ordered[blocks // 2 + c, spot, :] = state[rows:, c * LANES : (c + 1) * LANES]
    for c in range(blocks):
        for i in range(fresh_count):
            wide[pl.ds(fresh_count * c + i, samples, stride=fresh_count * blocks), :] = ordered[
                c, pl.ds(i, samples, stride=fresh_count), :
            ]
    layer[...] = wide[...].astype(BF16)
    states = jnp.concatenate([ordered[c] for c in range(blocks)], axis=1)
    final = normalize(states, gains[2:3, :])
    scored = jnp.sum(final * weight[...], axis=1, keepdims=True)
    row = lax.broadcasted_iota(jnp.int32, (tokens, samples), 0)
    here = row // fresh_count == lane_iota(row.shape)
    for i in range(fresh_count):
        score[i : i + 1, :] = jnp.sum(
            jnp.where(here & (row % fresh_count == i), scored, 0.0), axis=0, keepdims=True
        )


def shards(
    tokens_new,
    prefix_len,
    tail_len,
    pool_home,
    pool_page,
    slot_page_cache,
    tail_cache,
    routes,
    norm_gains,
    query_weight,
    key_value_weight,
    out_weight,
    router,
    expert_in,
    expert_out,
    score_weight,
):
    req_count = lax.axis_size("req")
    pairs = lax.axis_size("tp_pair")
    parts = 2 * pairs
    device = lax.axis_index("req")
    place = jnp.stack([device, lax.axis_index("tp_pair") * 2 + lax.axis_index("tp_side")])
    place = place.astype(jnp.int32)
    _, samples, fresh_count, model = tokens_new.shape
    tokens = samples * fresh_count
    part_rows = tokens // parts
    pool = slot_page_cache.shape[0]
    page_size = slot_page_cache.shape[1]
    slot_cap = max(1, pool // req_count)
    tail_count = tail_cache.shape[2]
    local = expert_in.shape[0]
    expert_count = router.shape[1]
    copies = local * req_count // expert_count
    everyone = req_count * parts
    rows = 2 * tokens
    blocks = model // LANES
    top = routes.shape[3]
    half = model // 2
    team = req_count * pairs

    swap = [(0, 1), (1, 0)]
    first_raw = expert_in.reshape(local, 2 * model, LANES)
    second_raw = expert_out.reshape(local * LANES, model)
    first_other = lax.ppermute(first_raw, "tp_side", swap)
    second_other = lax.ppermute(second_raw, "tp_side", swap)
    out_full = lax.all_gather(out_weight, ("tp_pair", "tp_side"), axis=0, tiled=True)

    token_bytes = tokens_new.reshape(samples, fresh_count, blocks, LANES)
    token_bytes = token_bytes.transpose(0, 2, 1, 3).reshape(tokens * blocks, LANES)
    route_bytes = routes[0].transpose(1, 2, 0).reshape(fresh_count * top, samples)
    frequency = ROPE_BASE ** (-np.arange(HEAD_DIM // 2, dtype=np.float64) / (HEAD_DIM // 2))
    frequency = jnp.asarray(np.tile(frequency, 4)[None, :].astype(np.float32))

    message, flat, normed, cosine, sine = pl.pallas_call(
        functools.partial(query_kernel, fresh_count),
        out_shape=(
            jax.ShapeDtypeStruct((req_count, rows + fresh_count * top, LANES), BF16),
            jax.ShapeDtypeStruct((parts, part_rows, model), BF16),
            jax.ShapeDtypeStruct((tokens, model), BF16),
            jax.ShapeDtypeStruct((tokens, LANES), F32),
            jax.ShapeDtypeStruct((tokens, LANES), F32),
        ),
        in_specs=[SMEM] * 3 + [VMEM] * 5,
        out_specs=(VMEM,) * 5,
        scratch_shapes=[
            pltpu.VMEM((tokens * blocks, LANES), F32),
            pltpu.VMEM((blocks, tokens, LANES), F32),
        ],
        compiler_params=params(8),
        name="query",
    )(place, prefix_len, tail_len, token_bytes, route_bytes, norm_gains, frequency, query_weight)

    first_all = lax.all_to_all(message, "req", split_axis=0, concat_axis=0, tiled=True)

    tail_numer, tail_top, tail_total = pl.pallas_call(
        functools.partial(tail_kernel, fresh_count),
        out_shape=(jax.ShapeDtypeStruct((rows, LANES), F32),) * 3,
        in_specs=[SMEM] + [VMEM] * 6,
        out_specs=(VMEM,) * 3,
        compiler_params=params(12),
        cost_estimate=cost(2e9, 5e6),
        name="tail",
    )(
        tail_len,
        message,
        normed,
        key_value_weight.reshape(2 * model, LANES),
        cosine,
        sine,
        tail_cache.reshape(samples, 2 * tail_count, LANES),
    )

    step = 8 if pool % 8 == 0 else 1
    split_pages = pl.pallas_call(
        split_pages_kernel,
        grid=(pool // step,),
        out_shape=jax.ShapeDtypeStruct((pool, 2 * page_size, LANES), BF16),
        in_specs=[pl.BlockSpec((step, 2 * page_size, LANES), lambda v: (v, 0, 0))],
        out_specs=pl.BlockSpec((step, 2 * page_size, LANES), lambda v: (v, 0, 0)),
        scratch_shapes=[pltpu.VMEM((step * 2 * page_size, LANES), F32)],
        compiler_params=params(8),
        cost_estimate=cost(1e6, 4e6),
        name="split_pages",
    )(slot_page_cache.reshape(pool, 2 * page_size, LANES))

    partial = pl.pallas_call(
        functools.partial(page_kernel, slot_cap, parts),
        out_shape=jax.ShapeDtypeStruct((everyone, 32, LANES), BF16),
        in_specs=[SMEM] * 4 + [VMEM] * 5,
        out_specs=VMEM,
        scratch_shapes=[
            pltpu.SMEM((req_count * slot_cap,), jnp.int32),
            pltpu.SMEM((req_count,), jnp.int32),
        ],
        compiler_params=params(12),
        cost_estimate=cost(2e9, 5e6),
        name="pages",
    )(
        place,
        pool_home,
        pool_page,
        prefix_len,
        first_all,
        split_pages,
        tail_numer,
        tail_top,
        tail_total,
    )
    partial = lax.all_to_all(
        partial, ("req", "tp_pair", "tp_side"), split_axis=0, concat_axis=0, tiled=True
    )

    def prepared(source, name):
        return pl.pallas_call(
            prepare_kernel,
            grid=(local,),
            out_shape=jax.ShapeDtypeStruct((model, local * 2 * LANES), BF16),
            in_specs=[pl.BlockSpec((1, 2 * model, LANES), lambda e: (e, 0, 0))],
            out_specs=pl.BlockSpec((model, 2 * LANES), lambda e: (0, e)),
            scratch_shapes=[pltpu.VMEM((2 * model, LANES), F32)],
            compiler_params=params(8),
            cost_estimate=cost(1e6, 4e6),
            name=name,
        )(source)

    first_own = prepared(first_raw, "prepare_own")
    first_swapped = prepared(first_other, "prepare_swapped")
    mask = pl.pallas_call(
        functools.partial(names_kernel, part_rows, fresh_count),
        grid=(1,),
        out_shape=jax.ShapeDtypeStruct((team * part_rows, expert_count), F32),
        in_specs=[
            SMEM,
            pl.BlockSpec(
                (req_count, fresh_count * top, LANES),
                lambda b: (0, rows // (fresh_count * top), 0),
            ),
        ],
        out_specs=pl.BlockSpec((team * part_rows, expert_count), lambda b: (0, 0)),
        compiler_params=params(8),
        cost_estimate=cost(1e6, 1e6),
        name="names",
    )(place, first_all)

    message, residual = pl.pallas_call(
        merge_kernel,
        out_shape=(
            jax.ShapeDtypeStruct((team, 2 * part_rows, half), BF16),
            jax.ShapeDtypeStruct((part_rows, model), F32),
        ),
        in_specs=[SMEM] + [VMEM] * 3 + [HBM],
        out_specs=(VMEM, VMEM),
        scratch_shapes=[pltpu.VMEM((model, model), BF16), pltpu.SemaphoreType.DMA(())],
        compiler_params=params(16),
        name="merge",
    )(place, partial.reshape(req_count, parts, 32, LANES), flat, norm_gains, out_full)
    states = lax.all_to_all(message, ("req", "tp_pair"), split_axis=0, concat_axis=0, tiled=True)

    group = min(req_count, 8) * pairs
    mixed = pl.pallas_call(
        functools.partial(expert_kernel, copies, part_rows),
        grid=(team // group,),
        out_shape=jax.ShapeDtypeStruct((team, 2 * part_rows, half), BF16),
        in_specs=[
            SMEM,
            pl.BlockSpec((group, 2 * part_rows, half), lambda b: (b, 0, 0)),
            pl.BlockSpec((group * part_rows, expert_count), lambda b: (b, 0)),
        ]
        + [VMEM] * 5,
        out_specs=pl.BlockSpec((group, 2 * part_rows, half), lambda b: (b, 0, 0)),
        compiler_params=params(16),
        name="experts",
    )(
        place,
        states,
        mask,
        router.T,
        first_own,
        first_swapped,
        second_raw,
        second_other,
    )
    mixed = lax.all_to_all(mixed, ("req", "tp_pair"), split_axis=0, concat_axis=0, tiled=True)

    finished = pl.pallas_call(
        finish_kernel,
        out_shape=jax.ShapeDtypeStruct((2 * part_rows, half), BF16),
        in_specs=[VMEM, VMEM],
        out_specs=VMEM,
        compiler_params=params(8),
        name="finish",
    )(mixed, residual)
    whole = ("tp_pair", "tp_side")
    gathered = [finished]
    for flip in range(1, parts):
        gathered.append(lax.ppermute(finished, whole, [(t, t ^ flip) for t in range(parts)]))

    layer, score = pl.pallas_call(
        functools.partial(score_kernel, fresh_count),
        out_shape=(
            jax.ShapeDtypeStruct((tokens * blocks, LANES), BF16),
            jax.ShapeDtypeStruct((fresh_count, samples), F32),
        ),
        in_specs=[SMEM] + [VMEM] * (parts + 2),
        out_specs=(VMEM, VMEM),
        scratch_shapes=[
            pltpu.VMEM((blocks, tokens, LANES), F32),
            pltpu.VMEM((tokens * blocks, LANES), F32),
        ],
        compiler_params=params(8),
        name="score",
    )(place, *gathered, norm_gains, score_weight.reshape(1, model))
    layer = layer.reshape(samples, blocks, fresh_count, LANES).transpose(0, 2, 1, 3)
    return (
        layer.reshape(1, samples, fresh_count, model),
        score.T.reshape(1, samples, fresh_count),
    )


def solution(mesh):
    tp = ("tp_pair", "tp_side")
    req_count, parts = mesh.devices.shape
    mesh = jax.sharding.Mesh(
        mesh.devices.reshape(req_count, parts // 2, 2), ("req", "tp_pair", "tp_side")
    )
    placed = (
        P("req", None, None, None),
        P(),
        P("req", None),
        P(),
        P(),
        P("req", None, None, tp),
        P("req", None, None, None, tp),
        P("req", None, None, None),
        P(),
        P(None, tp),
        P(None, None, tp),
        P(tp, None),
        P(),
        P("req", None, None, tp),
        P("req", tp, None),
        P(),
    )
    return jax.shard_map(
        shards,
        mesh=mesh,
        in_specs=placed,
        out_specs=(P("req", None, None, None), P("req", None, None)),
        check_vma=False,
    )
```

```python
import functools
import math

import jax
import jax.numpy as jnp
from jax import lax
from jax.experimental import pallas as pl
from jax.experimental.pallas import tpu as pltpu
from jax.sharding import PartitionSpec as P

HEAD_DIM = 64
LANES = 128
EPSILON = 1e-05
ROPE_BASE = 10000.0
LOWEST = -1e30
FLOOR = -1e28
F32 = jnp.float32
BF16 = jnp.bfloat16
MIB = 1024 * 1024
HOLD_MIB = 56

VMEM = pl.BlockSpec(memory_space=pltpu.VMEM)
SMEM = pl.BlockSpec(memory_space=pltpu.SMEM)
HBM = pl.BlockSpec(memory_space=pltpu.HBM)
ANY = pl.BlockSpec(memory_space=pl.ANY)


def params(mib):
    return pltpu.CompilerParams(vmem_limit_bytes=mib * MIB)


def cost(flops, moved):
    return pl.CostEstimate(flops=int(flops), bytes_accessed=int(moved), transcendentals=0)


def dot(left, right):
    return jnp.dot(left, right, preferred_element_type=F32)


def dot_t(left, right):
    return lax.dot_general(left, right, (((1,), (1,)), ((), ())), preferred_element_type=F32)


def lane_iota(shape):
    return lax.broadcasted_iota(jnp.int32, shape, len(shape) - 1)


def normalize(x, gain):
    return x * lax.rsqrt(jnp.mean(x * x, axis=-1, keepdims=True) + EPSILON) * gain


def rotate(x, cosine, sine):
    lanes = lane_iota(x.shape)
    partner = jnp.where(lanes % HEAD_DIM < HEAD_DIM // 2, pltpu.roll(x, 96, 1), pltpu.roll(x, 32, 1))
    return x * cosine + partner * sine


def by_head(packed, low):
    zero = jnp.zeros_like(packed)
    return jnp.concatenate([jnp.where(low, packed, zero), jnp.where(low, zero, packed)], axis=0)


def swap_halves(first, second):
    low = lane_iota(first.shape) < HEAD_DIM
    return (
        jnp.where(low, first, pltpu.roll(second, HEAD_DIM, 1)),
        jnp.where(low, pltpu.roll(first, HEAD_DIM, 1), second),
    )


def query_kernel(
    fresh_count,
    place,
    prefix_far,
    lengths_far,
    tokens_far,
    named_far,
    gains_far,
    weight_far,
    message,
    flat,
    normed,
    cosine,
    sine,
    gains,
    prefix,
    lengths,
    tokens,
    named,
    weight,
    wide,
    ordered,
    done,
):
    loads = []
    for k, (far, near) in enumerate(
        (
            (tokens_far, tokens),
            (gains_far, gains),
            (lengths_far, lengths),
            (prefix_far, prefix),
            (weight_far, weight),
            (named_far, named),
        )
    ):
        loads.append(pltpu.make_async_copy(far, near, done.at[k]))
        loads[-1].start()
    count, model = normed.shape
    samples = count // fresh_count
    parts, part_rows, _ = flat.shape
    blocks = model // LANES
    loads[0].wait()
    wide[...] = tokens[...].astype(F32)
    for c in range(blocks):
        for i in range(fresh_count):
            ordered[c, pl.ds(i, samples, stride=fresh_count), :] = wide[
                pl.ds(fresh_count * c + i, samples, stride=fresh_count * blocks), :
            ]
    states = jnp.concatenate([ordered[c] for c in range(blocks)], axis=1)
    for part in range(parts):
        flat[part] = states[part * part_rows : (part + 1) * part_rows].astype(BF16)
    loads[1].wait()
    rows = normalize(states, gains[0:1, :]).astype(BF16)
    normed[...] = rows
    loads[2].wait()
    loads[3].wait()
    row_id = lax.broadcasted_iota(jnp.int32, (count, 1), 0)
    position = row_id % fresh_count + prefix[place[0]]
    for sample in range(samples):
        position = position + jnp.where(row_id // fresh_count == sample, lengths[0, sample], 0)
    within = lane_iota((1, LANES)) % HEAD_DIM
    pair = (within % (HEAD_DIM // 2)).astype(F32)
    frequency = jnp.exp(pair * (-math.log(ROPE_BASE) / (HEAD_DIM // 2)))
    angles = position.astype(F32) * frequency
    cosine[...] = jnp.cos(angles)
    turn = jnp.sin(angles)
    sine[...] = jnp.where(within < HEAD_DIM // 2, -turn, turn)
    loads[4].wait()
    made = dot(rows, weight[...])
    pieces = []
    for group in swap_halves(made[:, :LANES], made[:, LANES:]):
        pieces.append(rotate(group, cosine[...], sine[...]).astype(BF16).astype(F32) * 0.125)
    packed = []
    for part in range(parts):
        for piece in pieces:
            packed.append(piece[part * part_rows : (part + 1) * part_rows])
    loads[5].wait()
    routed = named[...].astype(F32)
    packed.append(
        jnp.concatenate(
            [routed, jnp.zeros((routed.shape[0], LANES - routed.shape[1]), F32)], axis=1
        )
    )
    packed = jnp.concatenate(packed, axis=0).astype(BF16)
    message[...] = packed


def split_pages_kernel(source, out, wide):
    count, double, _ = source.shape
    half = double // 2
    wide[...] = source[...].astype(F32).reshape(count * double, LANES)
    keys = wide[pl.ds(0, count * half, stride=2), :].astype(BF16)
    values = wide[pl.ds(1, count * half, stride=2), :].astype(BF16)
    out[:, :half, :] = keys.reshape(count, half, LANES)
    out[:, half:, :] = values.reshape(count, half, LANES)


def statistics(top, total):
    section = (lane_iota(top.shape) % HEAD_DIM) // 16
    high = total.astype(BF16).astype(F32)
    return jnp.where(section == 0, top, jnp.where(section == 1, high, total - high)).astype(BF16)


def tail_kernel(
    fresh_count,
    place,
    lengths,
    query,
    normed,
    cosine,
    sine,
    after,
    weight_far,
    cache_far,
    project_far,
    *refs,
):
    del after
    parts = len(refs) - 6
    outs = refs[:parts]
    project, weight, cache, staged, load, done = refs[parts:]
    loads = [
        pltpu.make_async_copy(weight_far, weight, load.at[0]),
        pltpu.make_async_copy(project_far, project, load.at[1]),
    ]
    tokens = normed.shape[0]
    samples, width, _ = cache.shape
    per_part = samples // parts
    for part in range(parts):
        span = pl.ds(part * per_part, per_part)
        loads.append(pltpu.make_async_copy(cache_far.at[span], cache.at[span], done.at[part]))
    for copy in loads:
        copy.start()
    spread = (
        lax.broadcasted_iota(jnp.int32, (LANES, 2 * LANES), 1)
        == 2 * lax.broadcasted_iota(jnp.int32, (LANES, 2 * LANES), 0)
    ).astype(BF16)
    rows = normed[...]
    widened = jnp.concatenate(
        [dot(rows[:, c : c + LANES], spread) for c in range(0, rows.shape[1], LANES)], axis=1
    )
    both = jnp.concatenate([widened, pltpu.roll(widened, 1, 1)], axis=0).astype(BF16)
    loads[0].wait()
    made = dot(both, weight[...])
    key_new = rotate(made[:tokens], cosine[...], sine[...]).astype(BF16)
    value_new = made[tokens:].astype(BF16)
    low = lane_iota((16, LANES)) < HEAD_DIM
    row_id = lax.broadcasted_iota(jnp.int32, (32, 1), 0)
    row_sample = (row_id % 8) // fresh_count
    row_fresh = row_id % fresh_count
    column = lane_iota((32, width))
    even = column % 2 == 0
    token_id = lane_iota((32, tokens))
    for part in range(parts):
        loads[2 + part].wait()
        wide = by_head(query[part * 16 : (part + 1) * 16, :], low)
        scores = None
        length = jnp.zeros((32, 1), jnp.int32)
        for a in range(per_part):
            sample = part * per_part + a
            one = dot_t(wide, cache[sample])
            scores = one if a == 0 else jnp.where(row_sample == a, one, scores)
            length = jnp.where(row_sample == a, lengths[0, sample], length)
        scores = jnp.where(even & (column < 2 * length), scores, LOWEST)
        fresh = dot_t(wide, key_new)
        own_sample = row_sample + part * per_part
        fresh_seen = (token_id // fresh_count == own_sample) & (token_id % fresh_count <= row_fresh)
        fresh = jnp.where(fresh_seen, fresh, LOWEST)
        peak = jnp.maximum(
            jnp.max(scores, axis=1, keepdims=True), jnp.max(fresh, axis=1, keepdims=True)
        )
        peak = peak.astype(BF16).astype(F32)
        weights = jnp.exp(scores - peak)
        fresh_weights = jnp.exp(fresh - peak)
        amount = jnp.sum(weights, axis=1, keepdims=True) + jnp.sum(
            fresh_weights, axis=1, keepdims=True
        )
        shifted = pltpu.roll(weights, 1, 1).astype(BF16)
        mixed = None
        for a in range(per_part):
            one = dot(shifted, cache[part * per_part + a])
            mixed = one if a == 0 else jnp.where(row_sample == a, one, mixed)
        mixed = mixed + dot(fresh_weights.astype(BF16), value_new)
        staged[part, 0:16, :] = jnp.where(low, mixed[:16], mixed[16:]).astype(BF16)
        staged[part, 16:32, :] = statistics(
            jnp.where(low, peak[:16], peak[16:]), jnp.where(low, amount[:16], amount[16:])
        )
    for flip in range(parts):
        outs[flip][...] = staged[place[1] ^ flip]
    loads[1].wait()


def page_kernel(slot_cap, parts, place, homes, pages, lengths, cache, *refs):
    *blocks, out, named, query, slots, counts = refs
    requests = query.shape[0]
    if len(blocks) == 1:
        query[...] = blocks[0][...]
    else:
        for step, block in enumerate(blocks):
            query[lax.rem(place[0] - step + requests, requests)] = block[...]
    named[...] = query[:, parts * 16 :, :]
    pool = cache.shape[0]
    page_size = cache.shape[1] // 2
    rows = parts * 16
    base = place[0] * pool

    def clear(r, carry):
        counts[r] = 0
        for j in range(slot_cap):
            slots[r * slot_cap + j] = -1
        return carry

    lax.fori_loop(0, requests, clear, 0)

    def assign(v, carry):
        r = homes[base + v]
        rank = counts[r]
        slots[r * slot_cap + rank] = v
        counts[r] = rank + 1
        return carry

    lax.fori_loop(0, pool, assign, 0)

    low = lane_iota((rows, LANES)) < HEAD_DIM
    column = lane_iota((2 * rows, page_size))

    def one_request(r):
        wide = by_head(query[r, 0:rows, :], low)
        scores = []
        found = []
        for j in range(slot_cap):
            slot = slots[r * slot_cap + j]
            safe = jnp.maximum(slot, 0)
            found.append(safe)
            limit = jnp.where(slot >= 0, lengths[r] - pages[base + safe] * page_size, 0)
            one = dot_t(wide, cache[safe, :page_size, :])
            scores.append(jnp.where(column < limit, one, LOWEST))
        peak = functools.reduce(jnp.maximum, scores)
        peak = jnp.maximum(jnp.max(peak, axis=1, keepdims=True), FLOOR).astype(BF16).astype(F32)
        amount = None
        mixed = None
        for j in range(slot_cap):
            weights = jnp.exp(scores[j] - peak)
            amount = weights if j == 0 else amount + weights
            one = dot(weights.astype(BF16), cache[found[j], page_size:, :])
            mixed = one if j == 0 else mixed + one
        amount = jnp.sum(amount, axis=1, keepdims=True)
        numer = jnp.where(low, mixed[:rows], mixed[rows:]).astype(BF16)
        stats = statistics(
            jnp.where(low, peak[:rows], peak[rows:]), jnp.where(low, amount[:rows], amount[rows:])
        )
        for part in range(parts):
            out[r * parts + part, 0:16, :] = numer[part * 16 : (part + 1) * 16]
            out[r * parts + part, 16:32, :] = stats[part * 16 : (part + 1) * 16]

    step = 8 if requests % 8 == 0 else 1

    def several(g, carry):
        for k in range(step):
            one_request(g * step + k)
        return carry

    if requests == step:
        several(0, 0)
    else:
        lax.fori_loop(0, requests // step, several, 0)


def merge_kernel(place, arrived, tokens, gains, *refs):
    parts = arrived.shape[1]
    tails = refs[:parts]
    weights = refs[parts : 2 * parts]
    out, residual, staged, columns = refs[2 * parts :]
    low = lane_iota((16, LANES)) < HEAD_DIM
    for flip in range(parts):
        staged[place[1] ^ flip] = tails[flip][...].astype(F32)

    def pick(stats, lane):
        return jnp.where(
            low[None], stats[:, :, lane : lane + 1], stats[:, :, HEAD_DIM + lane : HEAD_DIM + lane + 1]
        )

    for t in range(parts):
        block = jnp.concatenate([arrived[:, t].astype(F32), staged[t][None]], axis=0)
        numer = block[:, :16]
        stats = block[:, 16:]
        top = pick(stats, 0)
        total = pick(stats, 16) + pick(stats, 32)
        factor = jnp.exp(top - jnp.max(top, axis=0, keepdims=True))
        attended = jnp.sum(factor * numer, axis=0) / jnp.sum(factor * total, axis=0)
        columns[t] = jnp.concatenate(swap_halves(attended[0:8], attended[8:16]), axis=1)
    projected = None
    for flip in range(parts):
        one = dot(columns[place[1] ^ flip].astype(BF16), weights[flip][...])
        projected = one if projected is None else projected + one
    rows = (tokens[place[1]].astype(F32) + projected).astype(BF16).astype(F32)
    residual[...] = rows
    normed = normalize(rows, gains[1:2, :])
    half = normed.shape[1] // 2
    message = jnp.concatenate([normed[:, :half], normed[:, half:]], axis=0).astype(BF16)
    for n in range(out.shape[0]):
        out[n] = message


def prepare_kernel(
    first_far, second_far, router_far, other, first, swapped, second, router, near, wide, done
):
    local, double, _ = near.shape
    depth = double // 2
    loads = [
        pltpu.make_async_copy(second_far, second, done.at[0]),
        pltpu.make_async_copy(router_far, router, done.at[1]),
    ]
    first_load = pltpu.make_async_copy(first_far, near, done.at[2])
    first_load.start()
    for copy in loads:
        copy.start()

    def separate(source, out, e):
        wide[...] = source[e].astype(F32)
        out[e, :, :LANES] = wide[pl.ds(0, depth, stride=2), :].astype(BF16)
        out[e, :, LANES:] = wide[pl.ds(1, depth, stride=2), :].astype(BF16)

    def from_other(e, carry):
        separate(other, swapped, e)
        return carry

    def from_own(e, carry):
        separate(near, first, e)
        return carry

    lax.fori_loop(0, local, from_other, 0)
    first_load.wait()
    lax.fori_loop(0, local, from_own, 0)
    for copy in loads:
        copy.wait()


def names_kernel(part_rows, fresh_count, place, packed, out):
    requests, span, _ = packed.shape
    experts = out.shape[1]
    halves = out.shape[0] // (requests * part_rows)
    top = span // fresh_count
    row = lax.broadcasted_iota(jnp.int32, (halves * part_rows, LANES), 0)
    token = (row // part_rows) * 2 * part_rows + (place[1] % 2) * part_rows + row % part_rows
    pick = (lane_iota(row.shape) == token // fresh_count).astype(BF16)
    found = jnp.concatenate([dot_t(pick, packed[r]) for r in range(requests)], axis=0)
    fresh = lax.broadcasted_iota(jnp.int32, (found.shape[0], 1), 0) % fresh_count
    chosen = found[:, :top]
    for i in range(1, fresh_count):
        chosen = jnp.where(fresh == i, found[:, i * top : (i + 1) * top], chosen)
    lanes = lane_iota(out.shape).astype(F32)
    mask = jnp.zeros(out.shape, F32)
    for k in range(top):
        mask = jnp.where(chosen[:, k : k + 1] == lanes, 1.0, mask)
    out[...] = mask


def expert_kernel(
    copies, part_rows, place, arrived, mask, router, first, first_other, second, second_other, out
):
    count = arrived.shape[0]
    half = arrived.shape[2]
    block = pl.program_id(0)
    local = first.shape[0]
    expert_count = router.shape[0]
    states = arrived[...].astype(F32)
    states = jnp.concatenate(
        [
            states[:, :part_rows].reshape(count * part_rows, half),
            states[:, part_rows:].reshape(count * part_rows, half),
        ],
        axis=1,
    ).astype(BF16)
    logits = dot_t(states, router[...])
    chosen = jnp.where(mask[...] > 0.5, logits, LOWEST)
    shares = jnp.exp(chosen - jnp.max(chosen, axis=1, keepdims=True))
    gates = shares / jnp.sum(shares, axis=1, keepdims=True)
    lanes = lane_iota(gates.shape)
    row_request = (
        block * count + lax.broadcasted_iota(jnp.int32, (gates.shape[0], 1), 0) // part_rows
    ) // 2
    weights = []
    for e in range(local):
        slot = place[0] * local + e
        gate = jnp.sum(
            jnp.where(lanes == slot % expert_count, gates, 0.0), axis=1, keepdims=True
        )
        if copies > 1:
            gate = jnp.where(row_request % copies == slot // expert_count, gate, 0.0)
        weights.append(gate)
    mixed = None
    for up, down in ((first, second), (first_other, second_other)):
        pieces = []
        for e in range(local):
            wide = dot(states, up[e])
            value = wide[:, :LANES]
            other = wide[:, LANES:]
            hidden = (value / (1.0 + jnp.exp(-value)) * other).astype(BF16).astype(F32)
            pieces.append((hidden * weights[e]).astype(BF16))
        part = dot(jnp.concatenate(pieces, axis=1), down[...])
        mixed = part if mixed is None else mixed + part
    out[...] = jnp.concatenate(
        [
            mixed[:, :half].reshape(count, part_rows, half),
            mixed[:, half:].reshape(count, part_rows, half),
        ],
        axis=1,
    ).astype(BF16)


def finish_kernel(arrived, residual, out):
    mixed = jnp.sum(arrived[...].astype(F32), axis=0)
    half = mixed.shape[1]
    kept = residual[...]
    message = jnp.concatenate([kept[:, :half], kept[:, half:]], axis=0) + mixed
    out[...] = message.astype(BF16)


def score_kernel(fresh_count, place, *refs):
    *arrived, gains, weight, layer, score, ordered, wide = refs
    double, half = arrived[0].shape
    rows = double // 2
    blocks, tokens, _ = ordered.shape
    samples = tokens // fresh_count
    for step, block in enumerate(arrived):
        state = block[...].astype(F32)
        spot = pl.ds(pl.multiple_of((place[1] ^ step) * rows, rows), rows)
        for c in range(blocks // 2):
            ordered[c, spot, :] = state[:rows, c * LANES : (c + 1) * LANES]
            ordered[blocks // 2 + c, spot, :] = state[rows:, c * LANES : (c + 1) * LANES]
    for c in range(blocks):
        for i in range(fresh_count):
            wide[pl.ds(fresh_count * c + i, samples, stride=fresh_count * blocks), :] = ordered[
                c, pl.ds(i, samples, stride=fresh_count), :
            ]
    layer[...] = wide[...].astype(BF16)
    states = jnp.concatenate([ordered[c] for c in range(blocks)], axis=1)
    final = normalize(states, gains[2:3, :])
    scored = jnp.sum(final * weight[...], axis=1, keepdims=True)
    row = lax.broadcasted_iota(jnp.int32, (tokens, samples), 0)
    here = row // fresh_count == lane_iota(row.shape)
    for i in range(fresh_count):
        score[i : i + 1, :] = jnp.sum(
            jnp.where(here & (row % fresh_count == i), scored, 0.0), axis=0, keepdims=True
        )


def shards(
    tokens_new,
    prefix_len,
    tail_len,
    pool_home,
    pool_page,
    slot_page_cache,
    tail_cache,
    routes,
    norm_gains,
    query_weight,
    key_value_weight,
    out_weight,
    router,
    expert_in,
    expert_out,
    score_weight,
):
    req_count = lax.axis_size("req")
    pairs = lax.axis_size("tp_pair")
    parts = 2 * pairs
    device = lax.axis_index("req")
    place = jnp.stack([device, lax.axis_index("tp_pair") * 2 + lax.axis_index("tp_side")])
    place = place.astype(jnp.int32)
    _, samples, fresh_count, model = tokens_new.shape
    tokens = samples * fresh_count
    part_rows = tokens // parts
    pool = slot_page_cache.shape[0]
    page_size = slot_page_cache.shape[1]
    slot_cap = max(1, pool // req_count)
    tail_count = tail_cache.shape[2]
    local = expert_in.shape[0]
    expert_count = router.shape[1]
    copies = local * req_count // expert_count
    everyone = req_count * parts
    rows = 2 * tokens
    blocks = model // LANES
    top = routes.shape[3]
    half = model // 2
    team = req_count * pairs

    whole = ("tp_pair", "tp_side")
    flips = [[(t, t ^ flip) for t in range(parts)] for flip in range(parts)]
    first_raw = expert_in.reshape(local, 2 * model, LANES)
    second_raw = expert_out.reshape(local * LANES, model)

    across = [lax.ppermute(out_weight, whole, flips[flip]) for flip in range(2, parts, 2)]

    token_bytes = tokens_new.reshape(samples, fresh_count, blocks, LANES)
    token_bytes = token_bytes.transpose(0, 2, 1, 3).reshape(tokens * blocks, LANES)
    route_bytes = routes[0].transpose(1, 2, 0).reshape(fresh_count * top, samples)

    message, flat, normed, cosine, sine, gains = pl.pallas_call(
        functools.partial(query_kernel, fresh_count),
        out_shape=(
            jax.ShapeDtypeStruct((rows + fresh_count * top, LANES), BF16),
            jax.ShapeDtypeStruct((parts, part_rows, model), BF16),
            jax.ShapeDtypeStruct((tokens, model), BF16),
            jax.ShapeDtypeStruct((tokens, LANES), F32),
            jax.ShapeDtypeStruct((tokens, LANES), F32),
            jax.ShapeDtypeStruct(norm_gains.shape, F32),
        ),
        in_specs=[SMEM] + [HBM] * 6,
        out_specs=(VMEM,) * 6,
        scratch_shapes=[
            pltpu.SMEM(prefix_len.shape, jnp.int32),
            pltpu.SMEM(tail_len.shape, jnp.int32),
            pltpu.VMEM(token_bytes.shape, BF16),
            pltpu.VMEM(route_bytes.shape, jnp.int32),
            pltpu.VMEM(query_weight.shape, BF16),
            pltpu.VMEM((tokens * blocks, LANES), F32),
            pltpu.VMEM((blocks, tokens, LANES), F32),
            pltpu.SemaphoreType.DMA((6,)),
        ],
        compiler_params=params(HOLD_MIB),
        name="query",
    )(place, prefix_len, tail_len, token_bytes, route_bytes, norm_gains, query_weight)

    if req_count <= 8:
        first_all = [message] + [
            lax.ppermute(message, "req", [(d, (d + step) % req_count) for d in range(req_count)])
            for step in range(1, req_count)
        ]
    else:
        copies_out = jnp.broadcast_to(message[None], (req_count,) + message.shape)
        first_all = [
            lax.all_to_all(copies_out, "req", split_axis=0, concat_axis=0, tiled=True)
        ]

    step = 8 if pool % 8 == 0 else 1
    split_pages = pl.pallas_call(
        split_pages_kernel,
        grid=(pool // step,),
        out_shape=jax.ShapeDtypeStruct((pool, 2 * page_size, LANES), BF16),
        in_specs=[pl.BlockSpec((step, 2 * page_size, LANES), lambda v: (v, 0, 0))],
        out_specs=pl.BlockSpec((step, 2 * page_size, LANES), lambda v: (v, 0, 0)),
        scratch_shapes=[pltpu.VMEM((step * 2 * page_size, LANES), F32)],
        compiler_params=params(8),
        cost_estimate=cost(1e6, 4e6),
        name="split_pages",
    )(slot_page_cache.reshape(pool, 2 * page_size, LANES))

    partial, named = pl.pallas_call(
        functools.partial(page_kernel, slot_cap, parts),
        out_shape=(
            jax.ShapeDtypeStruct((everyone, 32, LANES), BF16),
            jax.ShapeDtypeStruct((req_count, fresh_count * top, LANES), BF16),
        ),
        in_specs=[SMEM] * 4 + [VMEM] * (1 + len(first_all)),
        out_specs=(VMEM, VMEM),
        scratch_shapes=[
            pltpu.VMEM((req_count,) + message.shape, BF16),
            pltpu.SMEM((req_count * slot_cap,), jnp.int32),
            pltpu.SMEM((req_count,), jnp.int32),
        ],
        compiler_params=params(12),
        cost_estimate=cost(2e9, 5e6),
        name="pages",
    )(place, pool_home, pool_page, prefix_len, split_pages, *first_all)
    arrived = lax.all_to_all(
        partial, ("req",) + whole, split_axis=0, concat_axis=0, tiled=True
    )

    projects = [lax.ppermute(out_weight, whole, flips[1])]
    for block in across:
        block, _ = lax.optimization_barrier((block, partial))
        projects += [block, lax.ppermute(block, whole, flips[1])]

    *tails, project = pl.pallas_call(
        functools.partial(tail_kernel, fresh_count),
        out_shape=(jax.ShapeDtypeStruct((32, LANES), BF16),) * parts
        + (jax.ShapeDtypeStruct(out_weight.shape, BF16),),
        in_specs=[SMEM] * 2 + [VMEM] * 4 + [ANY] + [HBM] * 3,
        out_specs=(VMEM,) * (parts + 1),
        scratch_shapes=[
            pltpu.VMEM((2 * model, LANES), BF16),
            pltpu.VMEM((samples, 2 * tail_count, LANES), BF16),
            pltpu.VMEM((parts, 32, LANES), BF16),
            pltpu.SemaphoreType.DMA((2,)),
            pltpu.SemaphoreType.DMA((parts,)),
        ],
        compiler_params=params(16),
        cost_estimate=cost(2e9, 5e6),
        name="tail",
    )(
        place,
        tail_len,
        message,
        normed,
        cosine,
        sine,
        partial,
        key_value_weight.reshape(2 * model, LANES),
        tail_cache.reshape(samples, 2 * tail_count, LANES),
        out_weight,
    )
    tails = [tails[0]] + [
        lax.ppermute(tails[flip], whole, flips[flip]) for flip in range(1, parts)
    ]
    projects = [project] + projects
    first_other = lax.ppermute(first_raw, whole, flips[1])
    second_other = lax.ppermute(second_raw, whole, flips[1])

    mask = pl.pallas_call(
        functools.partial(names_kernel, part_rows, fresh_count),
        out_shape=jax.ShapeDtypeStruct((team * part_rows, expert_count), F32),
        in_specs=[SMEM, VMEM],
        out_specs=VMEM,
        compiler_params=params(8),
        cost_estimate=cost(1e6, 1e6),
        name="names",
    )(place, named)

    message, residual = pl.pallas_call(
        merge_kernel,
        out_shape=(
            jax.ShapeDtypeStruct((team, 2 * part_rows, half), BF16),
            jax.ShapeDtypeStruct((part_rows, model), F32),
        ),
        in_specs=[SMEM] + [VMEM] * (3 + 2 * parts),
        out_specs=(VMEM, VMEM),
        scratch_shapes=[
            pltpu.VMEM((parts, 32, LANES), F32),
            pltpu.VMEM((parts, part_rows, model // parts), F32),
        ],
        compiler_params=params(12),
        name="merge",
    )(place, arrived.reshape(req_count, parts, 32, LANES), flat, gains, *tails, *projects)

    first_own, first_swapped, second_own, router_near = pl.pallas_call(
        prepare_kernel,
        out_shape=(
            jax.ShapeDtypeStruct((local, model, 2 * LANES), BF16),
            jax.ShapeDtypeStruct((local, model, 2 * LANES), BF16),
            jax.ShapeDtypeStruct(second_raw.shape, BF16),
            jax.ShapeDtypeStruct((expert_count, model), BF16),
        ),
        in_specs=[HBM] * 3 + [VMEM],
        out_specs=(VMEM,) * 4,
        scratch_shapes=[
            pltpu.VMEM(first_raw.shape, BF16),
            pltpu.VMEM((2 * model, LANES), F32),
            pltpu.SemaphoreType.DMA((3,)),
        ],
        compiler_params=params(12),
        cost_estimate=cost(2e9, 8e6),
        name="prepare",
    )(first_raw, second_raw, router.T, first_other)

    states = lax.all_to_all(message, ("req", "tp_pair"), split_axis=0, concat_axis=0, tiled=True)

    group = min(req_count, 8) * pairs
    mixed = pl.pallas_call(
        functools.partial(expert_kernel, copies, part_rows),
        grid=(team // group,),
        out_shape=jax.ShapeDtypeStruct((team, 2 * part_rows, half), BF16),
        in_specs=[
            SMEM,
            pl.BlockSpec((group, 2 * part_rows, half), lambda b: (b, 0, 0)),
            pl.BlockSpec((group * part_rows, expert_count), lambda b: (b, 0)),
        ]
        + [VMEM] * 5,
        out_specs=pl.BlockSpec((group, 2 * part_rows, half), lambda b: (b, 0, 0)),
        compiler_params=params(16),
        name="experts",
    )(
        place,
        states,
        mask,
        router_near,
        first_own,
        first_swapped,
        second_own,
        second_other,
    )
    mixed = lax.all_to_all(mixed, ("req", "tp_pair"), split_axis=0, concat_axis=0, tiled=True)

    finished = pl.pallas_call(
        finish_kernel,
        out_shape=jax.ShapeDtypeStruct((2 * part_rows, half), BF16),
        in_specs=[VMEM, VMEM],
        out_specs=VMEM,
        compiler_params=params(8),
        name="finish",
    )(mixed, residual)
    gathered = [finished] + [
        lax.ppermute(finished, whole, flips[flip]) for flip in range(1, parts)
    ]

    layer, score = pl.pallas_call(
        functools.partial(score_kernel, fresh_count),
        out_shape=(
            jax.ShapeDtypeStruct((tokens * blocks, LANES), BF16),
            jax.ShapeDtypeStruct((fresh_count, samples), F32),
        ),
        in_specs=[SMEM] + [VMEM] * (parts + 2),
        out_specs=(VMEM, VMEM),
        scratch_shapes=[
            pltpu.VMEM((blocks, tokens, LANES), F32),
            pltpu.VMEM((tokens * blocks, LANES), F32),
        ],
        compiler_params=params(8),
        name="score",
    )(place, *gathered, gains, score_weight.reshape(1, model))
    layer = layer.reshape(samples, blocks, fresh_count, LANES).transpose(0, 2, 1, 3)
    return (
        layer.reshape(1, samples, fresh_count, model),
        score.T.reshape(1, samples, fresh_count),
    )


def solution(mesh):
    tp = ("tp_pair", "tp_side")
    req_count, parts = mesh.devices.shape
    mesh = jax.sharding.Mesh(
        mesh.devices.reshape(req_count, parts // 2, 2), ("req", "tp_pair", "tp_side")
    )
    placed = (
        P("req", None, None, None),
        P(),
        P("req", None),
        P(),
        P(),
        P("req", None, None, tp),
        P("req", None, None, None, tp),
        P("req", None, None, None),
        P(),
        P(None, tp),
        P(None, None, tp),
        P(tp, None),
        P(),
        P("req", None, None, tp),
        P("req", tp, None),
        P(),
    )
    return jax.shard_map(
        shards,
        mesh=mesh,
        in_specs=placed,
        out_specs=(P("req", None, None, None), P("req", None, None)),
        check_vma=False,
    )
```

```python
import functools
import math

import jax
import jax.numpy as jnp
from jax import lax
from jax.experimental import pallas as pl
from jax.experimental.pallas import tpu as pltpu
from jax.sharding import PartitionSpec as P

HEAD_DIM = 64
LANES = 128
EPSILON = 1e-05
ROPE_BASE = 10000.0
LOWEST = -1e30
FLOOR = -1e28
F32 = jnp.float32
BF16 = jnp.bfloat16
MIB = 1024 * 1024
HOLD_MIB = 56

VMEM = pl.BlockSpec(memory_space=pltpu.VMEM)
SMEM = pl.BlockSpec(memory_space=pltpu.SMEM)
HBM = pl.BlockSpec(memory_space=pltpu.HBM)
ANY = pl.BlockSpec(memory_space=pl.ANY)


def params(mib):
    return pltpu.CompilerParams(vmem_limit_bytes=mib * MIB)


def cost(flops, moved):
    return pl.CostEstimate(flops=int(flops), bytes_accessed=int(moved), transcendentals=0)


def dot(left, right):
    return jnp.dot(left, right, preferred_element_type=F32)


def dot_t(left, right):
    return lax.dot_general(left, right, (((1,), (1,)), ((), ())), preferred_element_type=F32)


def my_part():
    return lax.axis_index("tp_pair") * 2 + lax.axis_index("tp_side")


def load_all(pairs, done):
    copies = [pltpu.make_async_copy(far, near, done.at[k]) for k, (far, near) in enumerate(pairs)]
    for copy in copies:
        copy.start()
    return copies


def lane_iota(shape):
    return lax.broadcasted_iota(jnp.int32, shape, len(shape) - 1)


def normalize(x, gain):
    return x * lax.rsqrt(jnp.mean(x * x, axis=-1, keepdims=True) + EPSILON) * gain


def rotate(x, cosine, sine):
    lanes = lane_iota(x.shape)
    partner = jnp.where(lanes % HEAD_DIM < HEAD_DIM // 2, pltpu.roll(x, 96, 1), pltpu.roll(x, 32, 1))
    return x * cosine + partner * sine


def by_head(packed, low):
    zero = jnp.zeros_like(packed)
    return jnp.concatenate([jnp.where(low, packed, zero), jnp.where(low, zero, packed)], axis=0)


def swap_halves(first, second):
    low = lane_iota(first.shape) < HEAD_DIM
    return (
        jnp.where(low, first, pltpu.roll(second, HEAD_DIM, 1)),
        jnp.where(low, pltpu.roll(first, HEAD_DIM, 1), second),
    )


def query_kernel(
    fresh_count,
    prefix_far,
    lengths_far,
    tokens_far,
    named_far,
    gains_far,
    weight_far,
    message,
    flat,
    normed,
    cosine,
    sine,
    prefix,
    lengths,
    tokens,
    named,
    gains,
    weight,
    wide,
    ordered,
    done,
):
    loads = load_all(
        (
            (tokens_far, tokens),
            (gains_far, gains),
            (lengths_far, lengths),
            (prefix_far, prefix),
            (weight_far, weight),
            (named_far, named),
        ),
        done,
    )
    count, model = normed.shape
    samples = count // fresh_count
    parts, part_rows, _ = flat.shape
    blocks = model // LANES
    loads[0].wait()
    wide[...] = tokens[...].astype(F32)
    for c in range(blocks):
        for i in range(fresh_count):
            ordered[c, pl.ds(i, samples, stride=fresh_count), :] = wide[
                pl.ds(fresh_count * c + i, samples, stride=fresh_count * blocks), :
            ]
    states = jnp.concatenate([ordered[c] for c in range(blocks)], axis=1)
    for part in range(parts):
        flat[part] = states[part * part_rows : (part + 1) * part_rows].astype(BF16)
    loads[1].wait()
    rows = normalize(states, gains[0:1, :]).astype(BF16)
    normed[...] = rows
    loads[2].wait()
    loads[3].wait()
    row_id = lax.broadcasted_iota(jnp.int32, (count, 1), 0)
    position = row_id % fresh_count + prefix[lax.axis_index("req")]
    for sample in range(samples):
        position = position + jnp.where(row_id // fresh_count == sample, lengths[0, sample], 0)
    within = lane_iota((1, LANES)) % HEAD_DIM
    pair = (within % (HEAD_DIM // 2)).astype(F32)
    frequency = jnp.exp(pair * (-math.log(ROPE_BASE) / (HEAD_DIM // 2)))
    angles = position.astype(F32) * frequency
    cosine[...] = jnp.cos(angles)
    turn = jnp.sin(angles)
    sine[...] = jnp.where(within < HEAD_DIM // 2, -turn, turn)
    loads[4].wait()
    made = dot(rows, weight[...])
    pieces = []
    for group in swap_halves(made[:, :LANES], made[:, LANES:]):
        pieces.append(rotate(group, cosine[...], sine[...]).astype(BF16).astype(F32) * 0.125)
    packed = []
    for part in range(parts):
        for piece in pieces:
            packed.append(piece[part * part_rows : (part + 1) * part_rows])
    loads[5].wait()
    routed = named[...].astype(F32)
    packed.append(
        jnp.concatenate(
            [routed, jnp.zeros((routed.shape[0], LANES - routed.shape[1]), F32)], axis=1
        )
    )
    packed = jnp.concatenate(packed, axis=0).astype(BF16)
    for n in range(message.shape[0]):
        message[n] = packed


def split_pages_kernel(source, out, wide):
    count, double, _ = source.shape
    half = double // 2
    wide[...] = source[...].astype(F32).reshape(count * double, LANES)
    keys = wide[pl.ds(0, count * half, stride=2), :].astype(BF16)
    values = wide[pl.ds(1, count * half, stride=2), :].astype(BF16)
    out[:, :half, :] = keys.reshape(count, half, LANES)
    out[:, half:, :] = values.reshape(count, half, LANES)


def statistics(top, total):
    section = (lane_iota(top.shape) % HEAD_DIM) // 16
    high = total.astype(BF16).astype(F32)
    return jnp.where(section == 0, top, jnp.where(section == 1, high, total - high)).astype(BF16)


def tail_kernel(
    fresh_count,
    lengths_far,
    query_far,
    normed_far,
    cosine_far,
    sine_far,
    weight_far,
    cache_far,
    out,
    lengths,
    query,
    normed,
    cosine,
    sine,
    weight,
    cache,
    load,
    done,
):
    tokens = normed.shape[0]
    samples, width, _ = cache.shape
    parts = out.shape[0]
    per_part = samples // parts
    loads = load_all(
        (
            (normed_far, normed),
            (weight_far, weight),
            (cosine_far, cosine),
            (sine_far, sine),
            (query_far.at[0], query),
            (lengths_far, lengths),
        ),
        load,
    )
    spans = [pl.ds(part * per_part, per_part) for part in range(parts)]
    blocks = load_all([(cache_far.at[span], cache.at[span]) for span in spans], done)
    spread = (
        lax.broadcasted_iota(jnp.int32, (LANES, 2 * LANES), 1)
        == 2 * lax.broadcasted_iota(jnp.int32, (LANES, 2 * LANES), 0)
    ).astype(BF16)
    loads[0].wait()
    rows = normed[...]
    widened = jnp.concatenate(
        [dot(rows[:, c : c + LANES], spread) for c in range(0, rows.shape[1], LANES)], axis=1
    )
    both = jnp.concatenate([widened, pltpu.roll(widened, 1, 1)], axis=0).astype(BF16)
    for copy in loads[1:]:
        copy.wait()
    made = dot(both, weight[...])
    key_new = rotate(made[:tokens], cosine[...], sine[...]).astype(BF16)
    value_new = made[tokens:].astype(BF16)
    low = lane_iota((16, LANES)) < HEAD_DIM
    row_id = lax.broadcasted_iota(jnp.int32, (32, 1), 0)
    row_sample = (row_id % 8) // fresh_count
    row_fresh = row_id % fresh_count
    column = lane_iota((32, width))
    even = column % 2 == 0
    token_id = lane_iota((32, tokens))
    for part in range(parts):
        blocks[part].wait()
        wide = by_head(query[part * 16 : (part + 1) * 16, :], low)
        scores = None
        length = jnp.zeros((32, 1), jnp.int32)
        for a in range(per_part):
            sample = part * per_part + a
            one = dot_t(wide, cache[sample])
            scores = one if a == 0 else jnp.where(row_sample == a, one, scores)
            length = jnp.where(row_sample == a, lengths[0, sample], length)
        scores = jnp.where(even & (column < 2 * length), scores, LOWEST)
        fresh = dot_t(wide, key_new)
        own_sample = row_sample + part * per_part
        fresh_seen = (token_id // fresh_count == own_sample) & (token_id % fresh_count <= row_fresh)
        fresh = jnp.where(fresh_seen, fresh, LOWEST)
        peak = jnp.maximum(
            jnp.max(scores, axis=1, keepdims=True), jnp.max(fresh, axis=1, keepdims=True)
        )
        peak = peak.astype(BF16).astype(F32)
        weights = jnp.exp(scores - peak)
        fresh_weights = jnp.exp(fresh - peak)
        amount = jnp.sum(weights, axis=1, keepdims=True) + jnp.sum(
            fresh_weights, axis=1, keepdims=True
        )
        shifted = pltpu.roll(weights, 1, 1).astype(BF16)
        mixed = None
        for a in range(per_part):
            one = dot(shifted, cache[part * per_part + a])
            mixed = one if a == 0 else jnp.where(row_sample == a, one, mixed)
        mixed = mixed + dot(fresh_weights.astype(BF16), value_new)
        out[part, 0:16, :] = jnp.where(low, mixed[:16], mixed[16:]).astype(BF16)
        out[part, 16:32, :] = statistics(
            jnp.where(low, peak[:16], peak[16:]), jnp.where(low, amount[:16], amount[16:])
        )


def spread_stats(stats):
    low = lane_iota(stats.shape) < HEAD_DIM

    def pick(lane):
        return jnp.where(
            low, stats[..., lane : lane + 1], stats[..., HEAD_DIM + lane : HEAD_DIM + lane + 1]
        )

    return pick(0), pick(16) + pick(32)


def page_kernel(slot_cap, homes, pages, lengths, query, cache, tail, out, slots, counts):
    requests = query.shape[0]
    parts = tail.shape[0]
    pool = cache.shape[0]
    page_size = cache.shape[1] // 2
    rows = parts * 16
    me = lax.axis_index("req")
    base = me * pool
    tail_numer = jnp.concatenate([tail[p, 0:16, :] for p in range(parts)], axis=0).astype(F32)
    tail_stats = jnp.concatenate([tail[p, 16:32, :] for p in range(parts)], axis=0).astype(F32)
    tail_top, tail_total = spread_stats(tail_stats)

    def clear(r, carry):
        counts[r] = 0
        for j in range(slot_cap):
            slots[r * slot_cap + j] = -1
        return carry

    lax.fori_loop(0, requests, clear, 0)

    def assign(v, carry):
        r = homes[base + v]
        rank = counts[r]
        slots[r * slot_cap + rank] = v
        counts[r] = rank + 1
        return carry

    lax.fori_loop(0, pool, assign, 0)

    low = lane_iota((rows, LANES)) < HEAD_DIM
    column = lane_iota((2 * rows, page_size))

    def one_request(r):
        wide = by_head(query[r, 0:rows, :], low)
        scores = []
        found = []
        for j in range(slot_cap):
            slot = slots[r * slot_cap + j]
            safe = jnp.maximum(slot, 0)
            found.append(safe)
            limit = jnp.where(slot >= 0, lengths[r] - pages[base + safe] * page_size, 0)
            one = dot_t(wide, cache[safe, :page_size, :])
            scores.append(jnp.where(column < limit, one, LOWEST))
        peak = functools.reduce(jnp.maximum, scores)
        peak = jnp.maximum(jnp.max(peak, axis=1, keepdims=True), FLOOR).astype(BF16).astype(F32)
        amount = None
        mixed = None
        for j in range(slot_cap):
            weights = jnp.exp(scores[j] - peak)
            amount = weights if j == 0 else amount + weights
            one = dot(weights.astype(BF16), cache[found[j], page_size:, :])
            mixed = one if j == 0 else mixed + one
        amount = jnp.sum(amount, axis=1, keepdims=True)
        own = r == me
        top = jnp.where(low, peak[:rows], peak[rows:])
        joint = jnp.maximum(top, jnp.where(own, tail_top, FLOOR))
        here = jnp.exp(top - joint)
        there = jnp.where(own, jnp.exp(tail_top - joint), 0.0)
        numer = jnp.where(low, mixed[:rows], mixed[rows:]) * here + tail_numer * there
        total = jnp.where(low, amount[:rows], amount[rows:]) * here + tail_total * there
        numer = numer.astype(BF16)
        stats = statistics(joint, total)
        for part in range(parts):
            out[r * parts + part, 0:16, :] = numer[part * 16 : (part + 1) * 16]
            out[r * parts + part, 16:32, :] = stats[part * 16 : (part + 1) * 16]

    step = 8 if requests % 8 == 0 else 1

    def several(g, carry):
        for k in range(step):
            one_request(g * step + k)
        return carry

    if requests == step:
        several(0, 0)
    else:
        lax.fori_loop(0, requests // step, several, 0)


def merge_kernel(arrived, tokens, gains, *refs):
    parts = arrived.shape[1]
    weights = refs[:parts]
    out, residual, columns = refs[parts:]
    part = my_part()
    for t in range(parts):
        numer = arrived[:, t, 0:16, :].astype(F32)
        top, total = spread_stats(arrived[:, t, 16:32, :].astype(F32))
        factor = jnp.exp(top - jnp.max(top, axis=0, keepdims=True))
        attended = jnp.sum(factor * numer, axis=0) / jnp.sum(factor * total, axis=0)
        columns[t] = jnp.concatenate(swap_halves(attended[0:8], attended[8:16]), axis=1)
    projected = None
    for flip in range(parts):
        one = dot(columns[part ^ flip].astype(BF16), weights[flip][...])
        projected = one if projected is None else projected + one
    rows = (tokens[part].astype(F32) + projected).astype(BF16).astype(F32)
    residual[...] = rows
    normed = normalize(rows, gains[1:2, :])
    half = normed.shape[1] // 2
    message = jnp.concatenate([normed[:, :half], normed[:, half:]], axis=0).astype(BF16)
    for n in range(out.shape[0]):
        out[n] = message


def prepare_kernel(first_far, other_far, first, swapped, near, other, wide, done):
    local, double, _ = near.shape
    depth = double // 2
    loads = load_all(((first_far, near), (other_far, other)), done)

    def separate(source, out, e):
        buffer = wide.at[e % 2]
        buffer[...] = source[e].astype(F32)
        out[e, :, :LANES] = buffer[pl.ds(0, depth, stride=2), :].astype(BF16)
        out[e, :, LANES:] = buffer[pl.ds(1, depth, stride=2), :].astype(BF16)

    loads[0].wait()
    for e in range(local):
        separate(near, first, e)
    loads[1].wait()
    for e in range(local):
        separate(other, swapped, e)


def names_kernel(part_rows, fresh_count, packed, out):
    requests, span, _ = packed.shape
    experts = out.shape[1]
    halves = out.shape[0] // (requests * part_rows)
    top = span // fresh_count
    row = lax.broadcasted_iota(jnp.int32, (halves * part_rows, LANES), 0)
    token = (row // part_rows) * 2 * part_rows + lax.axis_index("tp_side") * part_rows + row % part_rows
    pick = (lane_iota(row.shape) == token // fresh_count).astype(BF16)
    found = jnp.concatenate([dot_t(pick, packed[r]) for r in range(requests)], axis=0)
    fresh = lax.broadcasted_iota(jnp.int32, (found.shape[0], 1), 0) % fresh_count
    chosen = found[:, :top]
    for i in range(1, fresh_count):
        chosen = jnp.where(fresh == i, found[:, i * top : (i + 1) * top], chosen)
    lanes = lane_iota(out.shape).astype(F32)
    mask = jnp.zeros(out.shape, F32)
    for k in range(top):
        mask = jnp.where(chosen[:, k : k + 1] == lanes, 1.0, mask)
    out[...] = mask


def expert_kernel(
    copies,
    part_rows,
    group,
    arrived_far,
    mask_far,
    router_far,
    first_far,
    first_other_far,
    second_far,
    second_other_far,
    out,
    arrived,
    mask,
    router,
    first,
    first_other,
    second,
    second_other,
    done,
):
    loads = load_all(
        (
            (arrived_far, arrived),
            (router_far, router),
            (mask_far, mask),
            (first_far, first),
            (second_far, second),
            (first_other_far, first_other),
            (second_other_far, second_other),
        ),
        done,
    )
    team, _, half = arrived.shape
    local = first.shape[0]
    expert_count = router.shape[0]
    count = group * part_rows
    me = lax.axis_index("req")

    def one_block(block, waiting):
        def arrive(*which):
            if waiting:
                for k in which:
                    loads[k].wait()

        here = pl.ds(block * group, group)
        arrive(0)
        states = arrived[here].astype(F32)
        states = jnp.concatenate(
            [
                states[:, :part_rows].reshape(count, half),
                states[:, part_rows:].reshape(count, half),
            ],
            axis=1,
        ).astype(BF16)
        arrive(1, 2)
        logits = dot_t(states, router[...])
        span = pl.ds(pl.multiple_of(block * count, count), count)
        chosen = jnp.where(mask[span, :] > 0.5, logits, LOWEST)
        shares = jnp.exp(chosen - jnp.max(chosen, axis=1, keepdims=True))
        gates = shares / jnp.sum(shares, axis=1, keepdims=True)
        lanes = lane_iota(gates.shape)
        row = lax.broadcasted_iota(jnp.int32, (count, 1), 0)
        row_request = (block * group + row // part_rows) // 2
        weights = []
        for e in range(local):
            slot = me * local + e
            gate = jnp.sum(
                jnp.where(lanes == lax.rem(slot, expert_count), gates, 0.0), axis=1, keepdims=True
            )
            if copies > 1:
                copy = lax.div(slot, expert_count)
                gate = jnp.where(lax.rem(row_request, copies) == copy, gate, 0.0)
            weights.append(gate)
        mixed = None
        for step, (up, down) in enumerate(((first, second), (first_other, second_other))):
            arrive(3 + 2 * step)
            pieces = []
            for e in range(local):
                wide = dot(states, up[e])
                value = wide[:, :LANES]
                other = wide[:, LANES:]
                hidden = (value / (1.0 + jnp.exp(-value)) * other).astype(BF16).astype(F32)
                pieces.append((hidden * weights[e]).astype(BF16))
            arrive(4 + 2 * step)
            part = dot(jnp.concatenate(pieces, axis=1), down[...])
            mixed = part if mixed is None else mixed + part
        out[here] = jnp.concatenate(
            [
                mixed[:, :half].reshape(group, part_rows, half),
                mixed[:, half:].reshape(group, part_rows, half),
            ],
            axis=1,
        ).astype(BF16)

    if team == group:
        one_block(0, True)
    else:
        for copy in loads:
            copy.wait()

        def body(block, carry):
            one_block(block, False)
            return carry

        lax.fori_loop(0, team // group, body, 0)


def finish_kernel(arrived, residual, out):
    mixed = jnp.sum(arrived[...].astype(F32), axis=0)
    half = mixed.shape[1]
    kept = residual[...]
    message = jnp.concatenate([kept[:, :half], kept[:, half:]], axis=0) + mixed
    out[...] = message.astype(BF16)


def score_kernel(fresh_count, *refs):
    *arrived, gains, weight, layer, score, ordered, wide = refs
    double, half = arrived[0].shape
    rows = double // 2
    blocks, tokens, _ = ordered.shape
    samples = tokens // fresh_count
    for step, block in enumerate(arrived):
        state = block[...].astype(F32)
        spot = pl.ds(pl.multiple_of((my_part() ^ step) * rows, rows), rows)
        for c in range(blocks // 2):
            ordered[c, spot, :] = state[:rows, c * LANES : (c + 1) * LANES]
            ordered[blocks // 2 + c, spot, :] = state[rows:, c * LANES : (c + 1) * LANES]
    for c in range(blocks):
        for i in range(fresh_count):
            wide[pl.ds(fresh_count * c + i, samples, stride=fresh_count * blocks), :] = ordered[
                c, pl.ds(i, samples, stride=fresh_count), :
            ]
    layer[...] = wide[...].astype(BF16)
    states = jnp.concatenate([ordered[c] for c in range(blocks)], axis=1)
    final = normalize(states, gains[2:3, :])
    scored = jnp.sum(final * weight[...], axis=1, keepdims=True)
    row = lax.broadcasted_iota(jnp.int32, (tokens, samples), 0)
    here = row // fresh_count == lane_iota(row.shape)
    for i in range(fresh_count):
        score[i : i + 1, :] = jnp.sum(
            jnp.where(here & (row % fresh_count == i), scored, 0.0), axis=0, keepdims=True
        )


def shards(
    tokens_new,
    prefix_len,
    tail_len,
    pool_home,
    pool_page,
    slot_page_cache,
    tail_cache,
    routes,
    norm_gains,
    query_weight,
    key_value_weight,
    out_weight,
    router,
    expert_in,
    expert_out,
    score_weight,
):
    req_count = lax.axis_size("req")
    pairs = lax.axis_size("tp_pair")
    parts = 2 * pairs
    _, samples, fresh_count, model = tokens_new.shape
    tokens = samples * fresh_count
    part_rows = tokens // parts
    pool = slot_page_cache.shape[0]
    page_size = slot_page_cache.shape[1]
    slot_cap = max(1, pool // req_count)
    tail_count = tail_cache.shape[2]
    local = expert_in.shape[0]
    expert_count = router.shape[1]
    copies = local * req_count // expert_count
    everyone = req_count * parts
    rows = 2 * tokens
    blocks = model // LANES
    top = routes.shape[3]
    half = model // 2
    team = req_count * pairs

    whole = ("tp_pair", "tp_side")
    flips = [[(t, t ^ flip) for t in range(parts)] for flip in range(parts)]
    first_raw = expert_in.reshape(local, 2 * model, LANES)
    second_raw = expert_out.reshape(local * LANES, model)

    across = [lax.ppermute(out_weight, whole, flips[flip]) for flip in range(2, parts, 2)]

    token_bytes = tokens_new.reshape(samples, fresh_count, blocks, LANES)
    token_bytes = token_bytes.transpose(0, 2, 1, 3).reshape(tokens * blocks, LANES)
    route_bytes = routes[0].transpose(1, 2, 0).reshape(fresh_count * top, samples)

    message, flat, normed, cosine, sine = pl.pallas_call(
        functools.partial(query_kernel, fresh_count),
        out_shape=(
            jax.ShapeDtypeStruct((req_count, rows + fresh_count * top, LANES), BF16),
            jax.ShapeDtypeStruct((parts, part_rows, model), BF16),
            jax.ShapeDtypeStruct((tokens, model), BF16),
            jax.ShapeDtypeStruct((tokens, LANES), F32),
            jax.ShapeDtypeStruct((tokens, LANES), F32),
        ),
        in_specs=[HBM] * 6,
        out_specs=(VMEM,) * 5,
        scratch_shapes=[
            pltpu.SMEM(prefix_len.shape, jnp.int32),
            pltpu.SMEM(tail_len.shape, jnp.int32),
            pltpu.VMEM(token_bytes.shape, BF16),
            pltpu.VMEM(route_bytes.shape, jnp.int32),
            pltpu.VMEM(norm_gains.shape, F32),
            pltpu.VMEM(query_weight.shape, BF16),
            pltpu.VMEM((tokens * blocks, LANES), F32),
            pltpu.VMEM((blocks, tokens, LANES), F32),
            pltpu.SemaphoreType.DMA((6,)),
        ],
        compiler_params=params(HOLD_MIB),
        name="query",
    )(prefix_len, tail_len, token_bytes, route_bytes, norm_gains, query_weight)

    first_all = lax.all_to_all(message, "req", split_axis=0, concat_axis=0, tiled=True)

    key_value_rows = key_value_weight.reshape(2 * model, LANES)
    tail_rows = tail_cache.reshape(samples, 2 * tail_count, LANES)
    tail = pl.pallas_call(
        functools.partial(tail_kernel, fresh_count),
        out_shape=jax.ShapeDtypeStruct((parts, 32, LANES), BF16),
        in_specs=[HBM] * 7,
        out_specs=VMEM,
        scratch_shapes=[
            pltpu.SMEM(tail_len.shape, jnp.int32),
            pltpu.VMEM(message.shape[1:], BF16),
            pltpu.VMEM(normed.shape, BF16),
            pltpu.VMEM(cosine.shape, F32),
            pltpu.VMEM(sine.shape, F32),
            pltpu.VMEM(key_value_rows.shape, BF16),
            pltpu.VMEM(tail_rows.shape, BF16),
            pltpu.SemaphoreType.DMA((6,)),
            pltpu.SemaphoreType.DMA((parts,)),
        ],
        compiler_params=params(HOLD_MIB),
        cost_estimate=cost(2e9, 5e6),
        name="tail",
    )(tail_len, message, normed, cosine, sine, key_value_rows, tail_rows)
    page_rows, tail = lax.optimization_barrier(
        (slot_page_cache.reshape(pool, 2 * page_size, LANES), tail)
    )

    step = 8 if pool % 8 == 0 else 1
    split_pages = pl.pallas_call(
        split_pages_kernel,
        grid=(pool // step,),
        out_shape=jax.ShapeDtypeStruct((pool, 2 * page_size, LANES), BF16),
        in_specs=[pl.BlockSpec((step, 2 * page_size, LANES), lambda v: (v, 0, 0))],
        out_specs=pl.BlockSpec((step, 2 * page_size, LANES), lambda v: (v, 0, 0)),
        scratch_shapes=[pltpu.VMEM((step * 2 * page_size, LANES), F32)],
        compiler_params=params(8),
        cost_estimate=cost(1e6, 4e6),
        name="split_pages",
    )(page_rows)

    partial = pl.pallas_call(
        functools.partial(page_kernel, slot_cap),
        out_shape=jax.ShapeDtypeStruct((everyone, 32, LANES), BF16),
        in_specs=[SMEM] * 3 + [VMEM] * 3,
        out_specs=VMEM,
        scratch_shapes=[
            pltpu.SMEM((req_count * slot_cap,), jnp.int32),
            pltpu.SMEM((req_count,), jnp.int32),
        ],
        compiler_params=params(12),
        cost_estimate=cost(2e9, 5e6),
        name="pages",
    )(pool_home, pool_page, prefix_len, first_all, split_pages, tail)
    arrived = lax.all_to_all(partial, ("req",) + whole, split_axis=0, concat_axis=0, tiled=True)

    projects = [out_weight, lax.ppermute(out_weight, whole, flips[1])]
    for block in across:
        block, _ = lax.optimization_barrier((block, partial))
        projects += [block, lax.ppermute(block, whole, flips[1])]
    first_other = lax.ppermute(first_raw, whole, flips[1])
    second_other = lax.ppermute(second_raw, whole, flips[1])

    first_raw, first_other, _ = lax.optimization_barrier((first_raw, first_other, partial))
    first_own, first_swapped = pl.pallas_call(
        prepare_kernel,
        out_shape=(jax.ShapeDtypeStruct((local, model, 2 * LANES), BF16),) * 2,
        in_specs=[HBM] * 2,
        out_specs=(VMEM,) * 2,
        scratch_shapes=[
            pltpu.VMEM(first_raw.shape, BF16),
            pltpu.VMEM(first_raw.shape, BF16),
            pltpu.VMEM((2, 2 * model, LANES), F32),
            pltpu.SemaphoreType.DMA((2,)),
        ],
        compiler_params=params(HOLD_MIB),
        cost_estimate=cost(2e9, 8e6),
        name="prepare",
    )(first_raw, first_other)
    mask = pl.pallas_call(
        functools.partial(names_kernel, part_rows, fresh_count),
        grid=(1,),
        out_shape=jax.ShapeDtypeStruct((team * part_rows, expert_count), F32),
        in_specs=[
            pl.BlockSpec(
                (req_count, fresh_count * top, LANES),
                lambda b: (0, rows // (fresh_count * top), 0),
            ),
        ],
        out_specs=pl.BlockSpec((team * part_rows, expert_count), lambda b: (0, 0)),
        compiler_params=params(8),
        cost_estimate=cost(1e6, 1e6),
        name="names",
    )(first_all)
    arrived, first_own, first_swapped, mask, second_other = lax.optimization_barrier(
        (arrived, first_own, first_swapped, mask, second_other)
    )

    message, residual = pl.pallas_call(
        merge_kernel,
        out_shape=(
            jax.ShapeDtypeStruct((team, 2 * part_rows, half), BF16),
            jax.ShapeDtypeStruct((part_rows, model), F32),
        ),
        in_specs=[VMEM] * (3 + parts),
        out_specs=(VMEM, VMEM),
        scratch_shapes=[pltpu.VMEM((parts, part_rows, model // parts), F32)],
        compiler_params=params(12),
        name="merge",
    )(arrived.reshape(req_count, parts, 32, LANES), flat, norm_gains, *projects)
    states = lax.all_to_all(message, ("req", "tp_pair"), split_axis=0, concat_axis=0, tiled=True)

    expert_inputs = (
        states,
        mask,
        router.T,
        first_own,
        first_swapped,
        second_raw,
        second_other,
    )
    mixed = pl.pallas_call(
        functools.partial(expert_kernel, copies, part_rows, min(req_count, 8) * pairs),
        out_shape=jax.ShapeDtypeStruct((team, 2 * part_rows, half), BF16),
        in_specs=[HBM] * 7,
        out_specs=VMEM,
        scratch_shapes=[pltpu.VMEM(array.shape, array.dtype) for array in expert_inputs]
        + [pltpu.SemaphoreType.DMA((7,))],
        compiler_params=params(HOLD_MIB),
        name="experts",
    )(*expert_inputs)
    mixed = lax.all_to_all(mixed, ("req", "tp_pair"), split_axis=0, concat_axis=0, tiled=True)

    finished = pl.pallas_call(
        finish_kernel,
        out_shape=jax.ShapeDtypeStruct((2 * part_rows, half), BF16),
        in_specs=[VMEM, VMEM],
        out_specs=VMEM,
        compiler_params=params(8),
        name="finish",
    )(mixed, residual)
    gathered = [finished] + [
        lax.ppermute(finished, whole, flips[flip]) for flip in range(1, parts)
    ]

    layer, score = pl.pallas_call(
        functools.partial(score_kernel, fresh_count),
        out_shape=(
            jax.ShapeDtypeStruct((tokens * blocks, LANES), BF16),
            jax.ShapeDtypeStruct((fresh_count, samples), F32),
        ),
        in_specs=[VMEM] * (parts + 2),
        out_specs=(VMEM, VMEM),
        scratch_shapes=[
            pltpu.VMEM((blocks, tokens, LANES), F32),
            pltpu.VMEM((tokens * blocks, LANES), F32),
        ],
        compiler_params=params(8),
        name="score",
    )(*gathered, norm_gains, score_weight.reshape(1, model))
    layer = layer.reshape(samples, blocks, fresh_count, LANES).transpose(0, 2, 1, 3)
    return (
        layer.reshape(1, samples, fresh_count, model),
        score.T.reshape(1, samples, fresh_count),
    )


def solution(mesh):
    tp = ("tp_pair", "tp_side")
    req_count, parts = mesh.devices.shape
    mesh = jax.sharding.Mesh(
        mesh.devices.reshape(req_count, parts // 2, 2), ("req", "tp_pair", "tp_side")
    )
    placed = (
        P("req", None, None, None),
        P(),
        P("req", None),
        P(),
        P(),
        P("req", None, None, tp),
        P("req", None, None, None, tp),
        P("req", None, None, None),
        P(),
        P(None, tp),
        P(None, None, tp),
        P(tp, None),
        P(),
        P("req", None, None, tp),
        P("req", tp, None),
        P(),
    )
    return jax.shard_map(
        shards,
        mesh=mesh,
        in_specs=placed,
        out_specs=(P("req", None, None, None), P("req", None, None)),
        check_vma=False,
    )
```

```python
import functools
import math

import jax
import jax.numpy as jnp
from jax import lax
from jax.experimental import pallas as pl
from jax.experimental.pallas import tpu as pltpu
from jax.sharding import PartitionSpec as P

HEAD_DIM = 64
LANES = 128
EPSILON = 1e-05
ROPE_BASE = 10000.0
LOWEST = -1e30
FLOOR = -1e28
F32 = jnp.float32
BF16 = jnp.bfloat16
MIB = 1024 * 1024
HOLD_MIB = 56

VMEM = pl.BlockSpec(memory_space=pltpu.VMEM)
SMEM = pl.BlockSpec(memory_space=pltpu.SMEM)
HBM = pl.BlockSpec(memory_space=pltpu.HBM)
ANY = pl.BlockSpec(memory_space=pl.ANY)


def params(mib):
    return pltpu.CompilerParams(vmem_limit_bytes=mib * MIB)


def cost(flops, moved):
    return pl.CostEstimate(flops=int(flops), bytes_accessed=int(moved), transcendentals=0)


def dot(left, right):
    return jnp.dot(left, right, preferred_element_type=F32)


def dot_t(left, right):
    return lax.dot_general(left, right, (((1,), (1,)), ((), ())), preferred_element_type=F32)


def my_part():
    return lax.axis_index("tp_pair") * 2 + lax.axis_index("tp_side")


def load_all(pairs, done):
    copies = [pltpu.make_async_copy(far, near, done.at[k]) for k, (far, near) in enumerate(pairs)]
    for copy in copies:
        copy.start()
    return copies


def lane_iota(shape):
    return lax.broadcasted_iota(jnp.int32, shape, len(shape) - 1)


def normalize(x, gain):
    return x * lax.rsqrt(jnp.mean(x * x, axis=-1, keepdims=True) + EPSILON) * gain


def rotate(x, cosine, sine):
    lanes = lane_iota(x.shape)
    partner = jnp.where(lanes % HEAD_DIM < HEAD_DIM // 2, pltpu.roll(x, 96, 1), pltpu.roll(x, 32, 1))
    return x * cosine + partner * sine


def by_head(packed, low):
    zero = jnp.zeros_like(packed)
    return jnp.concatenate([jnp.where(low, packed, zero), jnp.where(low, zero, packed)], axis=0)


def swap_halves(first, second):
    low = lane_iota(first.shape) < HEAD_DIM
    return (
        jnp.where(low, first, pltpu.roll(second, HEAD_DIM, 1)),
        jnp.where(low, pltpu.roll(first, HEAD_DIM, 1), second),
    )


def query_kernel(
    fresh_count,
    prefix_far,
    lengths_far,
    tokens_far,
    named_far,
    gains_far,
    weight_far,
    message,
    flat,
    normed,
    cosine,
    sine,
    prefix,
    lengths,
    tokens,
    named,
    gains,
    weight,
    wide,
    ordered,
    done,
):
    loads = load_all(
        (
            (tokens_far, tokens),
            (gains_far, gains),
            (lengths_far, lengths),
            (prefix_far, prefix),
            (weight_far, weight),
            (named_far, named),
        ),
        done,
    )
    count, model = normed.shape
    samples = count // fresh_count
    parts, part_rows, _ = flat.shape
    blocks = model // LANES
    loads[0].wait()
    wide[...] = tokens[...].astype(F32)
    for c in range(blocks):
        for i in range(fresh_count):
            ordered[c, pl.ds(i, samples, stride=fresh_count), :] = wide[
                pl.ds(fresh_count * c + i, samples, stride=fresh_count * blocks), :
            ]
    states = jnp.concatenate([ordered[c] for c in range(blocks)], axis=1)
    for part in range(parts):
        flat[part] = states[part * part_rows : (part + 1) * part_rows].astype(BF16)
    loads[1].wait()
    rows = normalize(states, gains[0:1, :]).astype(BF16)
    normed[...] = rows
    loads[2].wait()
    loads[3].wait()
    row_id = lax.broadcasted_iota(jnp.int32, (count, 1), 0)
    position = row_id % fresh_count + prefix[lax.axis_index("req")]
    for sample in range(samples):
        position = position + jnp.where(row_id // fresh_count == sample, lengths[0, sample], 0)
    within = lane_iota((1, LANES)) % HEAD_DIM
    pair = (within % (HEAD_DIM // 2)).astype(F32)
    frequency = jnp.exp(pair * (-math.log(ROPE_BASE) / (HEAD_DIM // 2)))
    angles = position.astype(F32) * frequency
    cosine[...] = jnp.cos(angles)
    turn = jnp.sin(angles)
    sine[...] = jnp.where(within < HEAD_DIM // 2, -turn, turn)
    loads[4].wait()
    made = dot(rows, weight[...])
    pieces = []
    for group in swap_halves(made[:, :LANES], made[:, LANES:]):
        pieces.append(rotate(group, cosine[...], sine[...]).astype(BF16).astype(F32) * 0.125)
    packed = []
    for part in range(parts):
        for piece in pieces:
            packed.append(piece[part * part_rows : (part + 1) * part_rows])
    loads[5].wait()
    routed = named[...].astype(F32)
    packed.append(
        jnp.concatenate(
            [routed, jnp.zeros((routed.shape[0], LANES - routed.shape[1]), F32)], axis=1
        )
    )
    packed = jnp.concatenate(packed, axis=0).astype(BF16)
    for n in range(message.shape[0]):
        message[n] = packed


def split_pages_kernel(source, out, wide):
    count, double, _ = source.shape
    half = double // 2
    wide[...] = source[...].astype(F32).reshape(count * double, LANES)
    keys = wide[pl.ds(0, count * half, stride=2), :].astype(BF16)
    values = wide[pl.ds(1, count * half, stride=2), :].astype(BF16)
    out[:, :half, :] = keys.reshape(count, half, LANES)
    out[:, half:, :] = values.reshape(count, half, LANES)


def pack_message(numer, top, total):
    high = total.astype(BF16).astype(F32)
    section = (lane_iota((8, LANES)) % HEAD_DIM) // 8
    stats = jnp.zeros((8, LANES), F32)
    for group in range(2):
        span = slice(group * 8, (group + 1) * 8)
        for k, kind in enumerate((top, high, total - high)):
            stats = jnp.where(section == 3 * group + k, kind[span], stats)
    return jnp.concatenate([numer, stats], axis=0).astype(BF16)


def unpack_message(block):
    block = block.astype(F32)
    stats = block[..., 16:24, :]
    low = lane_iota(stats.shape) < HEAD_DIM

    def pick(section):
        lane = section * 8
        return jnp.where(
            low, stats[..., lane : lane + 1], stats[..., HEAD_DIM + lane : HEAD_DIM + lane + 1]
        )

    top = jnp.concatenate([pick(0), pick(3)], axis=-2)
    total = jnp.concatenate([pick(1) + pick(2), pick(4) + pick(5)], axis=-2)
    return block[..., 0:16, :], top, total


def tail_kernel(
    fresh_count,
    lengths_far,
    query_far,
    normed_far,
    cosine_far,
    sine_far,
    weight_far,
    cache_far,
    out,
    lengths,
    query,
    normed,
    cosine,
    sine,
    weight,
    cache,
    load,
    done,
):
    tokens = normed.shape[0]
    samples, width, _ = cache.shape
    parts = out.shape[0]
    per_part = samples // parts
    loads = load_all(
        (
            (normed_far, normed),
            (weight_far, weight),
            (cosine_far, cosine),
            (sine_far, sine),
            (query_far.at[0], query),
            (lengths_far, lengths),
        ),
        load,
    )
    spans = [pl.ds(part * per_part, per_part) for part in range(parts)]
    blocks = load_all([(cache_far.at[span], cache.at[span]) for span in spans], done)
    spread = (
        lax.broadcasted_iota(jnp.int32, (LANES, 2 * LANES), 1)
        == 2 * lax.broadcasted_iota(jnp.int32, (LANES, 2 * LANES), 0)
    ).astype(BF16)
    loads[0].wait()
    rows = normed[...]
    widened = jnp.concatenate(
        [dot(rows[:, c : c + LANES], spread) for c in range(0, rows.shape[1], LANES)], axis=1
    )
    both = jnp.concatenate([widened, pltpu.roll(widened, 1, 1)], axis=0).astype(BF16)
    for copy in loads[1:]:
        copy.wait()
    made = dot(both, weight[...])
    key_new = rotate(made[:tokens], cosine[...], sine[...]).astype(BF16)
    value_new = made[tokens:].astype(BF16)
    low = lane_iota((16, LANES)) < HEAD_DIM
    row_id = lax.broadcasted_iota(jnp.int32, (32, 1), 0)
    row_sample = (row_id % 8) // fresh_count
    row_fresh = row_id % fresh_count
    column = lane_iota((32, width))
    even = column % 2 == 0
    token_id = lane_iota((32, tokens))
    for part in range(parts):
        blocks[part].wait()
        wide = by_head(query[part * 16 : (part + 1) * 16, :], low)
        length = jnp.zeros((32, 1), jnp.int32)
        for a in range(per_part):
            length = jnp.where(row_sample == a, lengths[0, part * per_part + a], length)
        placed = [jnp.where(row_sample == a, wide, jnp.zeros_like(wide)) for a in range(per_part)]
        beside = [cache[part * per_part + a] for a in range(per_part)]
        scores = dot_t(jnp.concatenate(placed, axis=1), jnp.concatenate(beside, axis=1))
        scores = jnp.where(even & (column < 2 * length), scores, LOWEST)
        fresh = dot_t(wide, key_new)
        own_sample = row_sample + part * per_part
        fresh_seen = (token_id // fresh_count == own_sample) & (token_id % fresh_count <= row_fresh)
        fresh = jnp.where(fresh_seen, fresh, LOWEST)
        peak = jnp.maximum(
            jnp.max(scores, axis=1, keepdims=True), jnp.max(fresh, axis=1, keepdims=True)
        )
        peak = peak.astype(BF16).astype(F32)
        weights = jnp.exp(scores - peak)
        fresh_weights = jnp.exp(fresh - peak)
        amount = jnp.sum(weights, axis=1, keepdims=True) + jnp.sum(
            fresh_weights, axis=1, keepdims=True
        )
        shifted = pltpu.roll(weights, 1, 1).astype(BF16)
        every = dot(shifted, jnp.concatenate(beside, axis=1))
        mixed = every[:, :LANES]
        for a in range(1, per_part):
            mixed = jnp.where(row_sample == a, every[:, a * LANES : (a + 1) * LANES], mixed)
        mixed = mixed + dot(fresh_weights.astype(BF16), value_new)
        out[part] = pack_message(
            jnp.where(low, mixed[:16], mixed[16:]),
            jnp.where(low, peak[:16], peak[16:]),
            jnp.where(low, amount[:16], amount[16:]),
        )


def page_kernel(slot_cap, homes, pages, lengths, query, cache, tail, out, slots, counts):
    requests = query.shape[0]
    parts = tail.shape[0]
    pool = cache.shape[0]
    page_size = cache.shape[1] // 2
    rows = parts * 16
    me = lax.axis_index("req")
    base = me * pool
    tail_numer, tail_top, tail_total = [
        kind.reshape(rows, LANES) for kind in unpack_message(tail[...])
    ]

    def clear(r, carry):
        counts[r] = 0
        for j in range(slot_cap):
            slots[r * slot_cap + j] = -1
        return carry

    lax.fori_loop(0, requests, clear, 0)

    def assign(v, carry):
        r = homes[base + v]
        rank = counts[r]
        slots[r * slot_cap + rank] = v
        counts[r] = rank + 1
        return carry

    lax.fori_loop(0, pool, assign, 0)

    low = lane_iota((rows, LANES)) < HEAD_DIM
    column = lane_iota((2 * rows, page_size))

    def finish(r, mixed, peak, amount):
        own = r == me
        top = jnp.where(low, peak[:rows], peak[rows:])
        joint = jnp.maximum(top, jnp.where(own, tail_top, FLOOR))
        here = jnp.exp(top - joint)
        there = jnp.where(own, jnp.exp(tail_top - joint), 0.0)
        numer = jnp.where(low, mixed[:rows], mixed[rows:]) * here + tail_numer * there
        total = jnp.where(low, amount[:rows], amount[rows:]) * here + tail_total * there
        for part in range(parts):
            span = slice(part * 16, (part + 1) * 16)
            out[r * parts + part] = pack_message(numer[span], joint[span], total[span])

    def several_requests(first, count):
        wides = []
        keys = []
        values = []
        limits = []
        for k in range(count):
            r = first + k
            wide = by_head(query[r, 0:rows, :], low)
            zero = jnp.zeros_like(wide)
            wides.append(jnp.concatenate([wide if c == k else zero for c in range(count)], axis=1))
            own_keys = []
            own_values = []
            own_limits = []
            for j in range(slot_cap):
                slot = slots[r * slot_cap + j]
                safe = jnp.maximum(slot, 0)
                own_limits.append(
                    jnp.where(slot >= 0, lengths[r] - pages[base + safe] * page_size, 0)
                )
                own_keys.append(cache[safe, :page_size, :])
                own_values.append(cache[safe, page_size:, :])
            keys.append(jnp.concatenate(own_keys, axis=0))
            values.append(jnp.concatenate(own_values, axis=0))
            limits.append(own_limits)
        scores = dot_t(jnp.concatenate(wides, axis=0), jnp.concatenate(keys, axis=1))
        all_weights = []
        stats = []
        for k in range(count):
            own = scores[k * 2 * rows : (k + 1) * 2 * rows]
            own = [
                jnp.where(
                    column < limits[k][j], own[:, j * page_size : (j + 1) * page_size], LOWEST
                )
                for j in range(slot_cap)
            ]
            peak = jnp.max(functools.reduce(jnp.maximum, own), axis=1, keepdims=True)
            peak = jnp.maximum(peak, FLOOR).astype(BF16).astype(F32)
            weights = [jnp.exp(one - peak) for one in own]
            amount = jnp.sum(functools.reduce(jnp.add, weights), axis=1, keepdims=True)
            all_weights.append(jnp.concatenate([one.astype(BF16) for one in weights], axis=1))
            stats.append((peak, amount))
        mixed = dot(jnp.concatenate(all_weights, axis=0), jnp.concatenate(values, axis=1))
        for k in range(count):
            finish(
                first + k,
                mixed[k * 2 * rows : (k + 1) * 2 * rows, k * LANES : (k + 1) * LANES],
                *stats[k],
            )

    pair = 2 if requests % 2 == 0 else 1
    step = 8 if requests % 8 == 0 else pair

    def several(g, carry):
        for k in range(0, step, pair):
            several_requests(g * step + k, pair)
        return carry

    if requests == step:
        several(0, 0)
    else:
        lax.fori_loop(0, requests // step, several, 0)


def merge_kernel(arrived, tokens, gains, *refs):
    parts = arrived.shape[1]
    weights = refs[:parts]
    out, residual, columns = refs[parts:]
    part = my_part()
    for t in range(parts):
        numer, top, total = unpack_message(arrived[:, t])
        factor = jnp.exp(top - jnp.max(top, axis=0, keepdims=True))
        attended = jnp.sum(factor * numer, axis=0) / jnp.sum(factor * total, axis=0)
        columns[t] = jnp.concatenate(swap_halves(attended[0:8], attended[8:16]), axis=1)
    projected = None
    for flip in range(parts):
        one = dot(columns[part ^ flip].astype(BF16), weights[flip][...])
        projected = one if projected is None else projected + one
    rows = (tokens[part].astype(F32) + projected).astype(BF16).astype(F32)
    residual[...] = rows
    normed = normalize(rows, gains[1:2, :])
    half = normed.shape[1] // 2
    message = jnp.concatenate([normed[:, :half], normed[:, half:]], axis=0).astype(BF16)
    for n in range(out.shape[0]):
        out[n] = message


def prepare_kernel(first_far, out, near, wide, done):
    local, double, _ = near.shape
    depth = double // 2
    loads = load_all([(first_far.at[e], near.at[e]) for e in range(local)], done)

    for e in range(local):
        loads[e].wait()
        buffer = wide.at[e % 2]
        buffer[...] = near[e].astype(F32)
        out[e, :, :LANES] = buffer[pl.ds(0, depth, stride=2), :].astype(BF16)
        out[e, :, LANES:] = buffer[pl.ds(1, depth, stride=2), :].astype(BF16)


def names_kernel(part_rows, fresh_count, packed, out):
    requests, span, _ = packed.shape
    experts = out.shape[1]
    halves = out.shape[0] // (requests * part_rows)
    top = span // fresh_count
    row = lax.broadcasted_iota(jnp.int32, (halves * part_rows, LANES), 0)
    token = (row // part_rows) * 2 * part_rows + lax.axis_index("tp_side") * part_rows + row % part_rows
    pick = (lane_iota(row.shape) == token // fresh_count).astype(BF16)
    found = jnp.concatenate([dot_t(pick, packed[r]) for r in range(requests)], axis=0)
    fresh = lax.broadcasted_iota(jnp.int32, (found.shape[0], 1), 0) % fresh_count
    chosen = found[:, :top]
    for i in range(1, fresh_count):
        chosen = jnp.where(fresh == i, found[:, i * top : (i + 1) * top], chosen)
    lanes = lane_iota(out.shape).astype(F32)
    mask = jnp.zeros(out.shape, F32)
    for k in range(top):
        mask = jnp.where(chosen[:, k : k + 1] == lanes, 1.0, mask)
    out[...] = mask


def expert_kernel(
    copies,
    part_rows,
    group,
    arrived,
    mask,
    router,
    first,
    first_other,
    second,
    second_other,
    out,
):
    team, _, half = arrived.shape
    local = first.shape[0]
    expert_count = router.shape[0]
    count = group * part_rows
    me = lax.axis_index("req")

    def one_block(block):
        here = pl.ds(block * group, group)
        states = arrived[here].astype(F32)
        states = jnp.concatenate(
            [
                states[:, :part_rows].reshape(count, half),
                states[:, part_rows:].reshape(count, half),
            ],
            axis=1,
        ).astype(BF16)
        logits = dot_t(states, router[...])
        span = pl.ds(pl.multiple_of(block * count, count), count)
        chosen = jnp.where(mask[span, :] > 0.5, logits, LOWEST)
        shares = jnp.exp(chosen - jnp.max(chosen, axis=1, keepdims=True))
        gates = shares / jnp.sum(shares, axis=1, keepdims=True)
        lanes = lane_iota(gates.shape)
        row = lax.broadcasted_iota(jnp.int32, (count, 1), 0)
        row_request = (block * group + row // part_rows) // 2
        weights = []
        for e in range(local):
            slot = me * local + e
            gate = jnp.sum(
                jnp.where(lanes == lax.rem(slot, expert_count), gates, 0.0), axis=1, keepdims=True
            )
            if copies > 1:
                copy = lax.div(slot, expert_count)
                gate = jnp.where(lax.rem(row_request, copies) == copy, gate, 0.0)
            weights.append(gate)
        mixed = None
        for up, down in ((first, second), (first_other, second_other)):
            pieces = []
            for e in range(local):
                wide = dot(states, up[e])
                value = wide[:, :LANES]
                other = wide[:, LANES:]
                hidden = (value / (1.0 + jnp.exp(-value)) * other).astype(BF16).astype(F32)
                pieces.append((hidden * weights[e]).astype(BF16))
            part = dot(jnp.concatenate(pieces, axis=1), down[...])
            mixed = part if mixed is None else mixed + part
        out[here] = jnp.concatenate(
            [
                mixed[:, :half].reshape(group, part_rows, half),
                mixed[:, half:].reshape(group, part_rows, half),
            ],
            axis=1,
        ).astype(BF16)

    if team == group:
        one_block(0)
    else:

        def body(block, carry):
            one_block(block)
            return carry

        lax.fori_loop(0, team // group, body, 0)


def finish_kernel(arrived, residual, out):
    mixed = jnp.sum(arrived[...].astype(F32), axis=0)
    half = mixed.shape[1]
    kept = residual[...]
    message = jnp.concatenate([kept[:, :half], kept[:, half:]], axis=0) + mixed
    out[...] = message.astype(BF16)


def score_kernel(fresh_count, *refs):
    *arrived, gains, weight, layer, score, ordered, wide = refs
    double, half = arrived[0].shape
    rows = double // 2
    blocks, tokens, _ = ordered.shape
    samples = tokens // fresh_count
    for step, block in enumerate(arrived):
        state = block[...].astype(F32)
        spot = pl.ds(pl.multiple_of((my_part() ^ step) * rows, rows), rows)
        for c in range(blocks // 2):
            ordered[c, spot, :] = state[:rows, c * LANES : (c + 1) * LANES]
            ordered[blocks // 2 + c, spot, :] = state[rows:, c * LANES : (c + 1) * LANES]
    for c in range(blocks):
        for i in range(fresh_count):
            wide[pl.ds(fresh_count * c + i, samples, stride=fresh_count * blocks), :] = ordered[
                c, pl.ds(i, samples, stride=fresh_count), :
            ]
    layer[...] = wide[...].astype(BF16)
    states = jnp.concatenate([ordered[c] for c in range(blocks)], axis=1)
    final = normalize(states, gains[2:3, :])
    scored = jnp.sum(final * weight[...], axis=1, keepdims=True)
    row = lax.broadcasted_iota(jnp.int32, (tokens, samples), 0)
    here = row // fresh_count == lane_iota(row.shape)
    for i in range(fresh_count):
        score[i : i + 1, :] = jnp.sum(
            jnp.where(here & (row % fresh_count == i), scored, 0.0), axis=0, keepdims=True
        )


def shards(
    tokens_new,
    prefix_len,
    tail_len,
    pool_home,
    pool_page,
    slot_page_cache,
    tail_cache,
    routes,
    norm_gains,
    query_weight,
    key_value_weight,
    out_weight,
    router,
    expert_in,
    expert_out,
    score_weight,
):
    req_count = lax.axis_size("req")
    pairs = lax.axis_size("tp_pair")
    parts = 2 * pairs
    _, samples, fresh_count, model = tokens_new.shape
    tokens = samples * fresh_count
    part_rows = tokens // parts
    pool = slot_page_cache.shape[0]
    page_size = slot_page_cache.shape[1]
    slot_cap = max(1, pool // req_count)
    tail_count = tail_cache.shape[2]
    local = expert_in.shape[0]
    expert_count = router.shape[1]
    copies = local * req_count // expert_count
    everyone = req_count * parts
    rows = 2 * tokens
    blocks = model // LANES
    top = routes.shape[3]
    half = model // 2
    team = req_count * pairs

    whole = ("tp_pair", "tp_side")
    flips = [[(t, t ^ flip) for t in range(parts)] for flip in range(parts)]
    first_raw = expert_in.reshape(local, 2 * model, LANES)
    second_raw = expert_out.reshape(local * LANES, model)


    token_bytes = tokens_new.reshape(samples, fresh_count, blocks, LANES)
    token_bytes = token_bytes.transpose(0, 2, 1, 3).reshape(tokens * blocks, LANES)
    route_bytes = routes[0].transpose(1, 2, 0).reshape(fresh_count * top, samples)

    message, flat, normed, cosine, sine = pl.pallas_call(
        functools.partial(query_kernel, fresh_count),
        out_shape=(
            jax.ShapeDtypeStruct((req_count, rows + fresh_count * top, LANES), BF16),
            jax.ShapeDtypeStruct((parts, part_rows, model), BF16),
            jax.ShapeDtypeStruct((tokens, model), BF16),
            jax.ShapeDtypeStruct((tokens, LANES), F32),
            jax.ShapeDtypeStruct((tokens, LANES), F32),
        ),
        in_specs=[HBM] * 6,
        out_specs=(VMEM,) * 5,
        scratch_shapes=[
            pltpu.SMEM(prefix_len.shape, jnp.int32),
            pltpu.SMEM(tail_len.shape, jnp.int32),
            pltpu.VMEM(token_bytes.shape, BF16),
            pltpu.VMEM(route_bytes.shape, jnp.int32),
            pltpu.VMEM(norm_gains.shape, F32),
            pltpu.VMEM(query_weight.shape, BF16),
            pltpu.VMEM((tokens * blocks, LANES), F32),
            pltpu.VMEM((blocks, tokens, LANES), F32),
            pltpu.SemaphoreType.DMA((6,)),
        ],
        compiler_params=params(HOLD_MIB),
        name="query",
    )(prefix_len, tail_len, token_bytes, route_bytes, norm_gains, query_weight)

    later, message = lax.optimization_barrier((out_weight, message))
    across = [lax.ppermute(later, whole, flips[flip]) for flip in range(2, parts, 2)]
    first_all = lax.all_to_all(message, "req", split_axis=0, concat_axis=0, tiled=True)

    key_value_rows = key_value_weight.reshape(2 * model, LANES)
    tail_rows = tail_cache.reshape(samples, 2 * tail_count, LANES)
    tail = pl.pallas_call(
        functools.partial(tail_kernel, fresh_count),
        out_shape=jax.ShapeDtypeStruct((parts, 24, LANES), BF16),
        in_specs=[HBM] * 7,
        out_specs=VMEM,
        scratch_shapes=[
            pltpu.SMEM(tail_len.shape, jnp.int32),
            pltpu.VMEM(message.shape[1:], BF16),
            pltpu.VMEM(normed.shape, BF16),
            pltpu.VMEM(cosine.shape, F32),
            pltpu.VMEM(sine.shape, F32),
            pltpu.VMEM(key_value_rows.shape, BF16),
            pltpu.VMEM(tail_rows.shape, BF16),
            pltpu.SemaphoreType.DMA((6,)),
            pltpu.SemaphoreType.DMA((parts,)),
        ],
        compiler_params=params(HOLD_MIB),
        cost_estimate=cost(2e9, 5e6),
        name="tail",
    )(tail_len, message, normed, cosine, sine, key_value_rows, tail_rows)
    beside = lax.ppermute(later, whole, flips[1])
    page_rows, tail, across, beside = lax.optimization_barrier(
        (slot_page_cache.reshape(pool, 2 * page_size, LANES), tail, across, beside)
    )
    projects = [out_weight, beside]
    for block in across:
        projects += [block, lax.ppermute(block, whole, flips[1])]

    step = 8 if pool % 8 == 0 else 1
    split_pages = pl.pallas_call(
        split_pages_kernel,
        grid=(pool // step,),
        out_shape=jax.ShapeDtypeStruct((pool, 2 * page_size, LANES), BF16),
        in_specs=[pl.BlockSpec((step, 2 * page_size, LANES), lambda v: (v, 0, 0))],
        out_specs=pl.BlockSpec((step, 2 * page_size, LANES), lambda v: (v, 0, 0)),
        scratch_shapes=[pltpu.VMEM((step * 2 * page_size, LANES), F32)],
        compiler_params=params(8),
        cost_estimate=cost(1e6, 4e6),
        name="split_pages",
    )(page_rows)

    partial = pl.pallas_call(
        functools.partial(page_kernel, slot_cap),
        out_shape=jax.ShapeDtypeStruct((everyone, 24, LANES), BF16),
        in_specs=[SMEM] * 3 + [VMEM] * 3,
        out_specs=VMEM,
        scratch_shapes=[
            pltpu.SMEM((req_count * slot_cap,), jnp.int32),
            pltpu.SMEM((req_count,), jnp.int32),
        ],
        compiler_params=params(12),
        cost_estimate=cost(2e9, 5e6),
        name="pages",
    )(pool_home, pool_page, prefix_len, first_all, split_pages, tail)
    arrived = lax.all_to_all(partial, ("req",) + whole, split_axis=0, concat_axis=0, tiled=True)

    first_raw, projects, _ = lax.optimization_barrier((first_raw, projects, partial))
    first = pl.pallas_call(
        prepare_kernel,
        out_shape=jax.ShapeDtypeStruct((local, model, 2 * LANES), BF16),
        in_specs=[HBM],
        out_specs=VMEM,
        scratch_shapes=[
            pltpu.VMEM(first_raw.shape, BF16),
            pltpu.VMEM((2, 2 * model, LANES), F32),
            pltpu.SemaphoreType.DMA((local,)),
        ],
        compiler_params=params(HOLD_MIB),
        cost_estimate=cost(2e9, 8e6),
        name="prepare",
    )(first_raw)
    mask = pl.pallas_call(
        functools.partial(names_kernel, part_rows, fresh_count),
        grid=(1,),
        out_shape=jax.ShapeDtypeStruct((team * part_rows, expert_count), F32),
        in_specs=[
            pl.BlockSpec(
                (req_count, fresh_count * top, LANES),
                lambda b: (0, rows // (fresh_count * top), 0),
            ),
        ],
        out_specs=pl.BlockSpec((team * part_rows, expert_count), lambda b: (0, 0)),
        compiler_params=params(8),
        cost_estimate=cost(1e6, 1e6),
        name="names",
    )(first_all)
    arrived, first, second_sent, mask = lax.optimization_barrier(
        (arrived, first, second_raw, mask)
    )
    first_other = lax.ppermute(first, whole, flips[1])
    second_other = lax.ppermute(second_sent, whole, flips[1])

    message, residual = pl.pallas_call(
        merge_kernel,
        out_shape=(
            jax.ShapeDtypeStruct((team, 2 * part_rows, half), BF16),
            jax.ShapeDtypeStruct((part_rows, model), F32),
        ),
        in_specs=[VMEM] * (3 + parts),
        out_specs=(VMEM, VMEM),
        scratch_shapes=[pltpu.VMEM((parts, part_rows, model // parts), F32)],
        compiler_params=params(12),
        name="merge",
    )(arrived.reshape(req_count, parts, 24, LANES), flat, norm_gains, *projects)
    states = lax.all_to_all(message, ("req", "tp_pair"), split_axis=0, concat_axis=0, tiled=True)

    expert_inputs = (
        states,
        mask,
        router.T,
        first,
        first_other,
        second_raw,
        second_other,
    )
    mixed = pl.pallas_call(
        functools.partial(expert_kernel, copies, part_rows, min(req_count, 8) * pairs),
        out_shape=jax.ShapeDtypeStruct((team, 2 * part_rows, half), BF16),
        in_specs=[VMEM] * 7,
        out_specs=VMEM,
        compiler_params=params(16),
        name="experts",
    )(*expert_inputs)
    mixed = lax.all_to_all(mixed, ("req", "tp_pair"), split_axis=0, concat_axis=0, tiled=True)

    finished = pl.pallas_call(
        finish_kernel,
        out_shape=jax.ShapeDtypeStruct((2 * part_rows, half), BF16),
        in_specs=[VMEM, VMEM],
        out_specs=VMEM,
        compiler_params=params(8),
        name="finish",
    )(mixed, residual)
    gathered = [finished] + [
        lax.ppermute(finished, whole, flips[flip]) for flip in range(1, parts)
    ]

    layer, score = pl.pallas_call(
        functools.partial(score_kernel, fresh_count),
        out_shape=(
            jax.ShapeDtypeStruct((tokens * blocks, LANES), BF16),
            jax.ShapeDtypeStruct((fresh_count, samples), F32),
        ),
        in_specs=[VMEM] * (parts + 2),
        out_specs=(VMEM, VMEM),
        scratch_shapes=[
            pltpu.VMEM((blocks, tokens, LANES), F32),
            pltpu.VMEM((tokens * blocks, LANES), F32),
        ],
        compiler_params=params(8),
        name="score",
    )(*gathered, norm_gains, score_weight.reshape(1, model))
    layer = layer.reshape(samples, blocks, fresh_count, LANES).transpose(0, 2, 1, 3)
    return (
        layer.reshape(1, samples, fresh_count, model),
        score.T.reshape(1, samples, fresh_count),
    )


def solution(mesh):
    tp = ("tp_pair", "tp_side")
    req_count, parts = mesh.devices.shape
    mesh = jax.sharding.Mesh(
        mesh.devices.reshape(req_count, parts // 2, 2), ("req", "tp_pair", "tp_side")
    )
    placed = (
        P("req", None, None, None),
        P(),
        P("req", None),
        P(),
        P(),
        P("req", None, None, tp),
        P("req", None, None, None, tp),
        P("req", None, None, None),
        P(),
        P(None, tp),
        P(None, None, tp),
        P(tp, None),
        P(),
        P("req", None, None, tp),
        P("req", tp, None),
        P(),
    )
    return jax.shard_map(
        shards,
        mesh=mesh,
        in_specs=placed,
        out_specs=(P("req", None, None, None), P("req", None, None)),
        check_vma=False,
    )
```

```python
import functools
import math

import jax
import jax.numpy as jnp
from jax import lax
from jax.experimental import pallas as pl
from jax.experimental.pallas import tpu as pltpu
from jax.sharding import PartitionSpec as P

HEAD_DIM = 64
LANES = 128
EPSILON = 1e-05
ROPE_BASE = 10000.0
LOWEST = -1e30
FLOOR = -1e28
F32 = jnp.float32
BF16 = jnp.bfloat16
MIB = 1024 * 1024
HOLD_MIB = 56

VMEM = pl.BlockSpec(memory_space=pltpu.VMEM)
SMEM = pl.BlockSpec(memory_space=pltpu.SMEM)
HBM = pl.BlockSpec(memory_space=pltpu.HBM)
ANY = pl.BlockSpec(memory_space=pl.ANY)


def params(mib):
    return pltpu.CompilerParams(vmem_limit_bytes=mib * MIB)


def cost(flops, moved):
    return pl.CostEstimate(flops=int(flops), bytes_accessed=int(moved), transcendentals=0)


def dot(left, right):
    return jnp.dot(left, right, preferred_element_type=F32)


def dot_t(left, right):
    return lax.dot_general(left, right, (((1,), (1,)), ((), ())), preferred_element_type=F32)


def my_part():
    return lax.axis_index("tp_pair") * 2 + lax.axis_index("tp_side")


def load_all(pairs, done):
    copies = [pltpu.make_async_copy(far, near, done.at[k]) for k, (far, near) in enumerate(pairs)]
    for copy in copies:
        copy.start()
    return copies


def lane_iota(shape):
    return lax.broadcasted_iota(jnp.int32, shape, len(shape) - 1)


def normalize(x, gain):
    return x * lax.rsqrt(jnp.mean(x * x, axis=-1, keepdims=True) + EPSILON) * gain


def rotate(x, cosine, sine):
    lanes = lane_iota(x.shape)
    partner = jnp.where(lanes % HEAD_DIM < HEAD_DIM // 2, pltpu.roll(x, 96, 1), pltpu.roll(x, 32, 1))
    return x * cosine + partner * sine


def by_head(packed, low):
    zero = jnp.zeros_like(packed)
    return jnp.concatenate([jnp.where(low, packed, zero), jnp.where(low, zero, packed)], axis=0)


def swap_halves(first, second):
    low = lane_iota(first.shape) < HEAD_DIM
    return (
        jnp.where(low, first, pltpu.roll(second, HEAD_DIM, 1)),
        jnp.where(low, pltpu.roll(first, HEAD_DIM, 1), second),
    )


def query_kernel(
    fresh_count,
    prefix_far,
    lengths_far,
    tokens_far,
    named_far,
    gains_far,
    weight_far,
    message,
    flat,
    normed,
    cosine,
    sine,
    prefix,
    lengths,
    tokens,
    named,
    gains,
    weight,
    wide,
    ordered,
    done,
):
    loads = load_all(
        (
            (tokens_far, tokens),
            (gains_far, gains),
            (lengths_far, lengths),
            (prefix_far, prefix),
            (weight_far, weight),
            (named_far, named),
        ),
        done,
    )
    count, model = normed.shape
    samples = count // fresh_count
    parts, part_rows, _ = flat.shape
    blocks = model // LANES
    loads[0].wait()
    wide[...] = tokens[...].astype(F32)
    for c in range(blocks):
        for i in range(fresh_count):
            ordered[c, pl.ds(i, samples, stride=fresh_count), :] = wide[
                pl.ds(fresh_count * c + i, samples, stride=fresh_count * blocks), :
            ]
    states = jnp.concatenate([ordered[c] for c in range(blocks)], axis=1)
    for part in range(parts):
        flat[part] = states[part * part_rows : (part + 1) * part_rows].astype(BF16)
    loads[1].wait()
    rows = normalize(states, gains[0:1, :]).astype(BF16)
    normed[...] = rows
    loads[2].wait()
    loads[3].wait()
    row_id = lax.broadcasted_iota(jnp.int32, (count, 1), 0)
    position = row_id % fresh_count + prefix[lax.axis_index("req")]
    for sample in range(samples):
        position = position + jnp.where(row_id // fresh_count == sample, lengths[0, sample], 0)
    within = lane_iota((1, LANES)) % HEAD_DIM
    pair = (within % (HEAD_DIM // 2)).astype(F32)
    frequency = jnp.exp(pair * (-math.log(ROPE_BASE) / (HEAD_DIM // 2)))
    angles = position.astype(F32) * frequency
    cosine[...] = jnp.cos(angles)
    turn = jnp.sin(angles)
    sine[...] = jnp.where(within < HEAD_DIM // 2, -turn, turn)
    loads[4].wait()
    made = dot(rows, weight[...])
    pieces = []
    for group in swap_halves(made[:, :LANES], made[:, LANES:]):
        pieces.append(rotate(group, cosine[...], sine[...]).astype(BF16).astype(F32) * 0.125)
    packed = []
    for part in range(parts):
        for piece in pieces:
            packed.append(piece[part * part_rows : (part + 1) * part_rows])
    loads[5].wait()
    routed = named[...].astype(F32)
    packed.append(
        jnp.concatenate(
            [routed, jnp.zeros((routed.shape[0], LANES - routed.shape[1]), F32)], axis=1
        )
    )
    packed = jnp.concatenate(packed, axis=0).astype(BF16)
    message[...] = packed


def split_pages_kernel(source, out, wide):
    count, double, _ = source.shape
    half = double // 2
    wide[...] = source[...].astype(F32).reshape(count * double, LANES)
    keys = wide[pl.ds(0, count * half, stride=2), :].astype(BF16)
    values = wide[pl.ds(1, count * half, stride=2), :].astype(BF16)
    out[:, :half, :] = keys.reshape(count, half, LANES)
    out[:, half:, :] = values.reshape(count, half, LANES)


def pack_message(numer, top, total):
    high = total.astype(BF16).astype(F32)
    section = (lane_iota((8, LANES)) % HEAD_DIM) // 8
    stats = jnp.zeros((8, LANES), F32)
    for group in range(2):
        span = slice(group * 8, (group + 1) * 8)
        for k, kind in enumerate((top, high, total - high)):
            stats = jnp.where(section == 3 * group + k, kind[span], stats)
    return jnp.concatenate([numer, stats], axis=0).astype(BF16)


def unpack_message(block):
    block = block.astype(F32)
    stats = block[..., 16:24, :]
    low = lane_iota(stats.shape) < HEAD_DIM

    def pick(section):
        lane = section * 8
        return jnp.where(
            low, stats[..., lane : lane + 1], stats[..., HEAD_DIM + lane : HEAD_DIM + lane + 1]
        )

    top = jnp.concatenate([pick(0), pick(3)], axis=-2)
    total = jnp.concatenate([pick(1) + pick(2), pick(4) + pick(5)], axis=-2)
    return block[..., 0:16, :], top, total


def tail_kernel(
    fresh_count,
    first_part,
    lengths_far,
    query_far,
    normed_far,
    cosine_far,
    sine_far,
    weight_far,
    cache_far,
    out,
    lengths,
    query,
    normed,
    cosine,
    sine,
    weight,
    cache,
    load,
    done,
):
    tokens = normed.shape[0]
    samples, width, _ = cache.shape
    parts = out.shape[0]
    per_part = samples // parts
    first_sample = first_part * per_part
    some = pl.ds(first_part * (tokens // parts), tokens)
    loads = load_all(
        (
            (normed_far.at[some], normed),
            (weight_far, weight),
            (cosine_far.at[some], cosine),
            (sine_far.at[some], sine),
            (query_far.at[pl.ds(first_part * 16, parts * 16)], query),
            (lengths_far, lengths),
        ),
        load,
    )
    blocks = []
    for part in range(parts):
        far = cache_far.at[pl.ds(first_sample + part * per_part, per_part)]
        near = cache.at[pl.ds(part * per_part, per_part)]
        blocks.append(pltpu.make_async_copy(far, near, done.at[part]))
        blocks[-1].start()
    spread = (
        lax.broadcasted_iota(jnp.int32, (LANES, 2 * LANES), 1)
        == 2 * lax.broadcasted_iota(jnp.int32, (LANES, 2 * LANES), 0)
    ).astype(BF16)
    loads[0].wait()
    rows = normed[...]
    widened = jnp.concatenate(
        [dot(rows[:, c : c + LANES], spread) for c in range(0, rows.shape[1], LANES)], axis=1
    )
    both = jnp.concatenate([widened, pltpu.roll(widened, 1, 1)], axis=0).astype(BF16)
    for copy in loads[1:]:
        copy.wait()
    made = dot(both, weight[...])
    key_new = rotate(made[:tokens], cosine[...], sine[...]).astype(BF16)
    value_new = made[tokens:].astype(BF16)
    low = lane_iota((16, LANES)) < HEAD_DIM
    row_id = lax.broadcasted_iota(jnp.int32, (32, 1), 0)
    row_sample = (row_id % 8) // fresh_count
    row_fresh = row_id % fresh_count
    column_id = lane_iota((1, 32))
    column_sample = (column_id % 8) // fresh_count
    position = lax.broadcasted_iota(jnp.int32, (width, 32), 0)
    even = position % 2 == 0
    token_id = lane_iota((32, tokens))
    for part in range(parts):
        blocks[part].wait()
        wide = by_head(query[part * 16 : (part + 1) * 16, :], low)
        length = jnp.zeros((1, 32), jnp.int32)
        for a in range(per_part):
            sample = first_sample + part * per_part + a
            length = jnp.where(column_sample == a, lengths[0, sample], length)
        placed = [jnp.where(row_sample == a, wide, jnp.zeros_like(wide)) for a in range(per_part)]
        beside = jnp.concatenate([cache[part * per_part + a] for a in range(per_part)], axis=1)
        scores = dot_t(beside, jnp.concatenate(placed, axis=1))
        scores = jnp.where(even & (position < 2 * length), scores, LOWEST).T
        fresh = dot_t(wide, key_new)
        own_sample = row_sample + part * per_part
        fresh_seen = (token_id // fresh_count == own_sample) & (token_id % fresh_count <= row_fresh)
        fresh = jnp.where(fresh_seen, fresh, LOWEST)
        peak = jnp.maximum(
            jnp.max(scores, axis=1, keepdims=True), jnp.max(fresh, axis=1, keepdims=True)
        )
        peak = peak.astype(BF16).astype(F32)
        weights = jnp.exp(scores - peak)
        fresh_weights = jnp.exp(fresh - peak)
        amount = jnp.sum(weights, axis=1, keepdims=True) + jnp.sum(
            fresh_weights, axis=1, keepdims=True
        )
        shifted = pltpu.roll(weights, 1, 1).astype(BF16)
        every = dot(shifted, beside)
        mixed = every[:, :LANES]
        for a in range(1, per_part):
            mixed = jnp.where(row_sample == a, every[:, a * LANES : (a + 1) * LANES], mixed)
        mixed = mixed + dot(fresh_weights.astype(BF16), value_new)
        out[part] = pack_message(
            jnp.where(low, mixed[:16], mixed[16:]),
            jnp.where(low, peak[:16], peak[16:]),
            jnp.where(low, amount[:16], amount[16:]),
        )


def stack_kernel(*refs):
    *blocks, out = refs
    for k, block in enumerate(blocks):
        out[k] = block[...]


def page_kernel(
    slot_cap, homes, pages, lengths, cache, first_tail, last_tail, *refs
):
    *blocks, out, named, query, slots, counts = refs
    requests = query.shape[0]
    parts = 2 * first_tail.shape[0]
    pool = cache.shape[0]
    page_size = cache.shape[1] // 2
    rows = parts * 16
    me = lax.axis_index("req")
    base = me * pool
    tail = jnp.concatenate([first_tail[...].astype(F32), last_tail[...].astype(F32)], axis=0)
    tail_numer, tail_top, tail_total = [
        kind.reshape(rows, LANES) for kind in unpack_message(tail)
    ]
    if len(blocks) == 1:
        query[...] = blocks[0][...]
    else:
        for far, block in enumerate(blocks):
            for k in range(block.shape[0]):
                query[me ^ (2 * k + far)] = block[k]
    named[...] = query[:, rows:, :]

    def clear(r, carry):
        counts[r] = 0
        for j in range(slot_cap):
            slots[r * slot_cap + j] = -1
        return carry

    lax.fori_loop(0, requests, clear, 0)

    def assign(v, carry):
        r = homes[base + v]
        rank = counts[r]
        slots[r * slot_cap + rank] = v
        counts[r] = rank + 1
        return carry

    lax.fori_loop(0, pool, assign, 0)

    low = lane_iota((rows, LANES)) < HEAD_DIM
    column = lane_iota((2 * rows, page_size))

    def finish(r, mixed, peak, amount):
        own = r == me
        top = jnp.where(low, peak[:rows], peak[rows:])
        joint = jnp.maximum(top, jnp.where(own, tail_top, FLOOR))
        here = jnp.exp(top - joint)
        there = jnp.where(own, jnp.exp(tail_top - joint), 0.0)
        numer = jnp.where(low, mixed[:rows], mixed[rows:]) * here + tail_numer * there
        total = jnp.where(low, amount[:rows], amount[rows:]) * here + tail_total * there
        for part in range(parts):
            span = slice(part * 16, (part + 1) * 16)
            out[r * parts + part] = pack_message(numer[span], joint[span], total[span])

    def several_requests(first, count):
        wides = []
        keys = []
        values = []
        limits = []
        for k in range(count):
            r = first + k
            wide = by_head(query[r, 0:rows, :], low)
            zero = jnp.zeros_like(wide)
            wides.append(jnp.concatenate([wide if c == k else zero for c in range(count)], axis=1))
            own_keys = []
            own_values = []
            own_limits = []
            for j in range(slot_cap):
                slot = slots[r * slot_cap + j]
                safe = jnp.maximum(slot, 0)
                own_limits.append(
                    jnp.where(slot >= 0, lengths[r] - pages[base + safe] * page_size, 0)
                )
                own_keys.append(cache[safe, :page_size, :])
                own_values.append(cache[safe, page_size:, :])
            keys.append(jnp.concatenate(own_keys, axis=0))
            values.append(jnp.concatenate(own_values, axis=0))
            limits.append(own_limits)
        scores = dot_t(jnp.concatenate(wides, axis=0), jnp.concatenate(keys, axis=1))
        all_weights = []
        stats = []
        for k in range(count):
            own = scores[k * 2 * rows : (k + 1) * 2 * rows]
            own = [
                jnp.where(
                    column < limits[k][j], own[:, j * page_size : (j + 1) * page_size], LOWEST
                )
                for j in range(slot_cap)
            ]
            peak = jnp.max(functools.reduce(jnp.maximum, own), axis=1, keepdims=True)
            peak = jnp.maximum(peak, FLOOR).astype(BF16).astype(F32)
            weights = [jnp.exp(one - peak) for one in own]
            amount = jnp.sum(functools.reduce(jnp.add, weights), axis=1, keepdims=True)
            all_weights.append(jnp.concatenate([one.astype(BF16) for one in weights], axis=1))
            stats.append((peak, amount))
        mixed = dot(jnp.concatenate(all_weights, axis=0), jnp.concatenate(values, axis=1))
        for k in range(count):
            finish(
                first + k,
                mixed[k * 2 * rows : (k + 1) * 2 * rows, k * LANES : (k + 1) * LANES],
                *stats[k],
            )

    pair = 2 if requests % 2 == 0 else 1
    step = 8 if requests % 8 == 0 else pair

    def several(g, carry):
        for k in range(0, step, pair):
            several_requests(g * step + k, pair)
        return carry

    if requests == step:
        several(0, 0)
    else:
        lax.fori_loop(0, requests // step, several, 0)


def merge_kernel(arrived_far, tokens_far, gains_far, *refs):
    parts = arrived_far.shape[1]
    weights_far = refs[:parts]
    out, residual, arrived, tokens, gains, weights, columns, done = refs[parts:]
    part = my_part()
    first_load, *loads = load_all(
        [(arrived_far, arrived), (tokens_far.at[part], tokens), (gains_far, gains)]
        + [(weights_far[flip], weights.at[flip]) for flip in range(parts)],
        done,
    )
    first_load.wait()
    for t in range(parts):
        numer, top, total = unpack_message(arrived[:, t])
        factor = jnp.exp(top - jnp.max(top, axis=0, keepdims=True))
        attended = jnp.sum(factor * numer, axis=0) / jnp.sum(factor * total, axis=0)
        columns[t] = jnp.concatenate(swap_halves(attended[0:8], attended[8:16]), axis=1)
    for copy in loads:
        copy.wait()
    projected = None
    for flip in range(parts):
        one = dot(columns[part ^ flip].astype(BF16), weights[flip])
        projected = one if projected is None else projected + one
    rows = (tokens[...].astype(F32) + projected).astype(BF16).astype(F32)
    residual[...] = rows
    normed = normalize(rows, gains[1:2, :])
    half = normed.shape[1] // 2
    message = jnp.concatenate([normed[:, :half], normed[:, half:]], axis=0).astype(BF16)
    for n in range(out.shape[0]):
        out[n] = message


def prepare_kernel(first_far, out, near, wide, done):
    local, double, _ = near.shape
    depth = double // 2
    loads = load_all([(first_far.at[e], near.at[e]) for e in range(local)], done)

    for e in range(local):
        loads[e].wait()
        buffer = wide.at[e % 2]
        buffer[...] = near[e].astype(F32)
        out[e, :, :LANES] = buffer[pl.ds(0, depth, stride=2), :].astype(BF16)
        out[e, :, LANES:] = buffer[pl.ds(1, depth, stride=2), :].astype(BF16)


def names_kernel(part_rows, fresh_count, packed, out):
    requests, span, _ = packed.shape
    experts = out.shape[1]
    halves = out.shape[0] // (requests * part_rows)
    top = span // fresh_count
    row = lax.broadcasted_iota(jnp.int32, (halves * part_rows, LANES), 0)
    token = (row // part_rows) * 2 * part_rows + lax.axis_index("tp_side") * part_rows + row % part_rows
    pick = (lane_iota(row.shape) == token // fresh_count).astype(BF16)
    found = jnp.concatenate([dot_t(pick, packed[r]) for r in range(requests)], axis=0)
    fresh = lax.broadcasted_iota(jnp.int32, (found.shape[0], 1), 0) % fresh_count
    chosen = found[:, :top]
    for i in range(1, fresh_count):
        chosen = jnp.where(fresh == i, found[:, i * top : (i + 1) * top], chosen)
    lanes = lane_iota(out.shape).astype(F32)
    mask = jnp.zeros(out.shape, F32)
    for k in range(top):
        mask = jnp.where(chosen[:, k : k + 1] == lanes, 1.0, mask)
    out[...] = mask


def expert_kernel(
    copies,
    part_rows,
    group,
    arrived,
    mask,
    router,
    first,
    first_other,
    second,
    second_other,
    out,
):
    team, _, half = arrived.shape
    local = first.shape[0]
    expert_count = router.shape[0]
    count = group * part_rows
    me = lax.axis_index("req")

    def one_block(block):
        here = pl.ds(block * group, group)
        states = arrived[here].astype(F32)
        states = jnp.concatenate(
            [
                states[:, :part_rows].reshape(count, half),
                states[:, part_rows:].reshape(count, half),
            ],
            axis=1,
        ).astype(BF16)
        logits = dot_t(states, router[...])
        span = pl.ds(pl.multiple_of(block * count, count), count)
        chosen = jnp.where(mask[span, :] > 0.5, logits, LOWEST)
        shares = jnp.exp(chosen - jnp.max(chosen, axis=1, keepdims=True))
        gates = shares / jnp.sum(shares, axis=1, keepdims=True)
        lanes = lane_iota(gates.shape)
        row = lax.broadcasted_iota(jnp.int32, (count, 1), 0)
        row_request = (block * group + row // part_rows) // 2
        weights = []
        for e in range(local):
            slot = me * local + e
            gate = jnp.sum(
                jnp.where(lanes == lax.rem(slot, expert_count), gates, 0.0), axis=1, keepdims=True
            )
            if copies > 1:
                copy = lax.div(slot, expert_count)
                gate = jnp.where(lax.rem(row_request, copies) == copy, gate, 0.0)
            weights.append(gate)
        mixed = None
        for up, down in ((first, second), (first_other, second_other)):
            pieces = []
            for e in range(local):
                wide = dot(states, up[e])
                value = wide[:, :LANES]
                other = wide[:, LANES:]
                hidden = (value / (1.0 + jnp.exp(-value)) * other).astype(BF16).astype(F32)
                pieces.append((hidden * weights[e]).astype(BF16))
            part = dot(jnp.concatenate(pieces, axis=1), down[...])
            mixed = part if mixed is None else mixed + part
        out[here] = jnp.concatenate(
            [
                mixed[:, :half].reshape(group, part_rows, half),
                mixed[:, half:].reshape(group, part_rows, half),
            ],
            axis=1,
        ).astype(BF16)

    if team == group:
        one_block(0)
    else:

        def body(block, carry):
            one_block(block)
            return carry

        lax.fori_loop(0, team // group, body, 0)


def finish_kernel(arrived, residual, out):
    mixed = jnp.sum(arrived[...].astype(F32), axis=0)
    half = mixed.shape[1]
    kept = residual[...]
    message = jnp.concatenate([kept[:, :half], kept[:, half:]], axis=0) + mixed
    out[...] = message.astype(BF16)


def score_kernel(fresh_count, *refs):
    *arrived, gains, weight, layer, score, ordered, wide = refs
    double, half = arrived[0].shape
    rows = double // 2
    blocks, tokens, _ = ordered.shape
    samples = tokens // fresh_count
    for step, block in enumerate(arrived):
        state = block[...].astype(F32)
        spot = pl.ds(pl.multiple_of((my_part() ^ step) * rows, rows), rows)
        for c in range(blocks // 2):
            ordered[c, spot, :] = state[:rows, c * LANES : (c + 1) * LANES]
            ordered[blocks // 2 + c, spot, :] = state[rows:, c * LANES : (c + 1) * LANES]
    for c in range(blocks):
        for i in range(fresh_count):
            wide[pl.ds(fresh_count * c + i, samples, stride=fresh_count * blocks), :] = ordered[
                c, pl.ds(i, samples, stride=fresh_count), :
            ]
    layer[...] = wide[...].astype(BF16)
    states = jnp.concatenate([ordered[c] for c in range(blocks)], axis=1)
    final = normalize(states, gains[2:3, :])
    scored = jnp.sum(final * weight[...], axis=1, keepdims=True)
    row = lax.broadcasted_iota(jnp.int32, (tokens, samples), 0)
    here = row // fresh_count == lane_iota(row.shape)
    for i in range(fresh_count):
        score[i : i + 1, :] = jnp.sum(
            jnp.where(here & (row % fresh_count == i), scored, 0.0), axis=0, keepdims=True
        )


def shards(
    tokens_new,
    prefix_len,
    tail_len,
    pool_home,
    pool_page,
    slot_page_cache,
    tail_cache,
    routes,
    norm_gains,
    query_weight,
    key_value_weight,
    out_weight,
    router,
    expert_in,
    expert_out,
    score_weight,
):
    req_count = lax.axis_size("req")
    pairs = lax.axis_size("tp_pair")
    parts = 2 * pairs
    _, samples, fresh_count, model = tokens_new.shape
    tokens = samples * fresh_count
    part_rows = tokens // parts
    pool = slot_page_cache.shape[0]
    page_size = slot_page_cache.shape[1]
    slot_cap = max(1, pool // req_count)
    tail_count = tail_cache.shape[2]
    local = expert_in.shape[0]
    expert_count = router.shape[1]
    copies = local * req_count // expert_count
    everyone = req_count * parts
    rows = 2 * tokens
    blocks = model // LANES
    top = routes.shape[3]
    half = model // 2
    team = req_count * pairs

    whole = ("tp_pair", "tp_side")
    flips = [[(t, t ^ flip) for t in range(parts)] for flip in range(parts)]
    first_raw = expert_in.reshape(local, 2 * model, LANES)
    second_raw = expert_out.reshape(local * LANES, model)


    token_bytes = tokens_new.reshape(samples, fresh_count, blocks, LANES)
    token_bytes = token_bytes.transpose(0, 2, 1, 3).reshape(tokens * blocks, LANES)
    route_bytes = routes[0].transpose(1, 2, 0).reshape(fresh_count * top, samples)

    message, flat, normed, cosine, sine = pl.pallas_call(
        functools.partial(query_kernel, fresh_count),
        out_shape=(
            jax.ShapeDtypeStruct((rows + fresh_count * top, LANES), BF16),
            jax.ShapeDtypeStruct((parts, part_rows, model), BF16),
            jax.ShapeDtypeStruct((tokens, model), BF16),
            jax.ShapeDtypeStruct((tokens, LANES), F32),
            jax.ShapeDtypeStruct((tokens, LANES), F32),
        ),
        in_specs=[HBM] * 6,
        out_specs=(VMEM,) * 5,
        scratch_shapes=[
            pltpu.SMEM(prefix_len.shape, jnp.int32),
            pltpu.SMEM(tail_len.shape, jnp.int32),
            pltpu.VMEM(token_bytes.shape, BF16),
            pltpu.VMEM(route_bytes.shape, jnp.int32),
            pltpu.VMEM(norm_gains.shape, F32),
            pltpu.VMEM(query_weight.shape, BF16),
            pltpu.VMEM((tokens * blocks, LANES), F32),
            pltpu.VMEM((blocks, tokens, LANES), F32),
            pltpu.SemaphoreType.DMA((6,)),
        ],
        compiler_params=params(HOLD_MIB),
        name="query",
    )(prefix_len, tail_len, token_bytes, route_bytes, norm_gains, query_weight)

    key_value_rows = key_value_weight.reshape(2 * model, LANES)
    tail_rows = tail_cache.reshape(samples, 2 * tail_count, LANES)
    some = parts // 2

    def tail_half(first_part, inputs):
        name = "tail_first" if first_part == 0 else "tail_last"
        return pl.pallas_call(
            functools.partial(tail_kernel, fresh_count, first_part),
            out_shape=jax.ShapeDtypeStruct((some, 24, LANES), BF16),
            in_specs=[HBM] * 7,
            out_specs=VMEM,
            scratch_shapes=[
                pltpu.SMEM(tail_len.shape, jnp.int32),
                pltpu.VMEM((some * 16, LANES), BF16),
                pltpu.VMEM((tokens // 2, model), BF16),
                pltpu.VMEM((tokens // 2, LANES), F32),
                pltpu.VMEM((tokens // 2, LANES), F32),
                pltpu.VMEM(key_value_rows.shape, BF16),
                pltpu.VMEM((samples // 2,) + tail_rows.shape[1:], BF16),
                pltpu.SemaphoreType.DMA((6,)),
                pltpu.SemaphoreType.DMA((some,)),
            ],
            compiler_params=params(HOLD_MIB),
            cost_estimate=cost(1e9, 3e6),
            name=name,
        )(tail_len, *inputs, key_value_rows, tail_rows)

    inputs = (message, normed, cosine, sine)
    page_rows = slot_page_cache.reshape(pool, 2 * page_size, LANES)
    later, message = lax.optimization_barrier((out_weight, message))
    across = [lax.ppermute(later, whole, flips[flip]) for flip in range(2, parts, 2)]
    if req_count == 8:
        near = [
            lax.ppermute(message, "req", [(d, d ^ flip) for d in range(req_count)])
            for flip in (2, 4, 6)
        ]
        first_tail = tail_half(0, inputs)
        first_tail, near = lax.optimization_barrier((first_tail, near))
        stacked = pl.pallas_call(
            stack_kernel,
            out_shape=jax.ShapeDtypeStruct((4,) + message.shape, BF16),
            in_specs=[VMEM] * 4,
            out_specs=VMEM,
            compiler_params=params(8),
            name="stack",
        )(message, *near)
        inputs, page_rows, later, stacked = lax.optimization_barrier(
            (inputs, page_rows, later, stacked)
        )
        other = lax.ppermute(stacked, "req", [(d, d ^ 1) for d in range(req_count)])
        first_all = [stacked, other]
    else:
        copies_out = jnp.broadcast_to(message[None], (req_count,) + message.shape)
        first_all = [
            lax.all_to_all(copies_out, "req", split_axis=0, concat_axis=0, tiled=True)
        ]
        first_tail = tail_half(0, inputs)
    last_tail = tail_half(some, inputs)
    page_rows, last_tail, across, later = lax.optimization_barrier(
        (page_rows, last_tail, across, later)
    )
    projects = [out_weight, lax.ppermute(later, whole, flips[1])]
    for block in across:
        projects += [block, lax.ppermute(block, whole, flips[1])]

    step = 8 if pool % 8 == 0 else 1
    split_pages = pl.pallas_call(
        split_pages_kernel,
        grid=(pool // step,),
        out_shape=jax.ShapeDtypeStruct((pool, 2 * page_size, LANES), BF16),
        in_specs=[pl.BlockSpec((step, 2 * page_size, LANES), lambda v: (v, 0, 0))],
        out_specs=pl.BlockSpec((step, 2 * page_size, LANES), lambda v: (v, 0, 0)),
        scratch_shapes=[pltpu.VMEM((step * 2 * page_size, LANES), F32)],
        compiler_params=params(8),
        cost_estimate=cost(1e6, 4e6),
        name="split_pages",
    )(page_rows)

    partial, named = pl.pallas_call(
        functools.partial(page_kernel, slot_cap),
        out_shape=(
            jax.ShapeDtypeStruct((everyone, 24, LANES), BF16),
            jax.ShapeDtypeStruct((req_count, fresh_count * top, LANES), BF16),
        ),
        in_specs=[SMEM] * 3 + [VMEM] * (3 + len(first_all)),
        out_specs=(VMEM, VMEM),
        scratch_shapes=[
            pltpu.VMEM((req_count,) + message.shape, BF16),
            pltpu.SMEM((req_count * slot_cap,), jnp.int32),
            pltpu.SMEM((req_count,), jnp.int32),
        ],
        compiler_params=params(12),
        cost_estimate=cost(2e9, 5e6),
        name="pages",
    )(pool_home, pool_page, prefix_len, split_pages, first_tail, last_tail, *first_all)
    arrived = lax.all_to_all(partial, ("req",) + whole, split_axis=0, concat_axis=0, tiled=True)

    first_raw, _ = lax.optimization_barrier((first_raw, partial))
    first = pl.pallas_call(
        prepare_kernel,
        out_shape=jax.ShapeDtypeStruct((local, model, 2 * LANES), BF16),
        in_specs=[HBM],
        out_specs=VMEM,
        scratch_shapes=[
            pltpu.VMEM(first_raw.shape, BF16),
            pltpu.VMEM((2, 2 * model, LANES), F32),
            pltpu.SemaphoreType.DMA((local,)),
        ],
        compiler_params=params(HOLD_MIB),
        cost_estimate=cost(2e9, 8e6),
        name="prepare",
    )(first_raw)
    named, first, projects = lax.optimization_barrier((named, first, projects))
    mask = pl.pallas_call(
        functools.partial(names_kernel, part_rows, fresh_count),
        out_shape=jax.ShapeDtypeStruct((team * part_rows, expert_count), F32),
        in_specs=[VMEM],
        out_specs=VMEM,
        compiler_params=params(8),
        cost_estimate=cost(1e6, 1e6),
        name="names",
    )(named)
    arrived, first, second_sent, mask = lax.optimization_barrier(
        (arrived, first, second_raw, mask)
    )
    first_other = lax.ppermute(first, whole, flips[1])
    second_other = lax.ppermute(second_sent, whole, flips[1])

    message, residual = pl.pallas_call(
        merge_kernel,
        out_shape=(
            jax.ShapeDtypeStruct((team, 2 * part_rows, half), BF16),
            jax.ShapeDtypeStruct((part_rows, model), F32),
        ),
        in_specs=[HBM] * (3 + parts),
        out_specs=(VMEM, VMEM),
        scratch_shapes=[
            pltpu.VMEM((req_count, parts, 24, LANES), BF16),
            pltpu.VMEM((part_rows, model), BF16),
            pltpu.VMEM(norm_gains.shape, F32),
            pltpu.VMEM((parts,) + out_weight.shape, BF16),
            pltpu.VMEM((parts, part_rows, model // parts), F32),
            pltpu.SemaphoreType.DMA((3 + parts,)),
        ],
        compiler_params=params(HOLD_MIB),
        name="merge",
    )(arrived.reshape(req_count, parts, 24, LANES), flat, norm_gains, *projects)
    message, first, second_raw, router = lax.optimization_barrier(
        (message, first, second_raw, router)
    )
    states = lax.all_to_all(message, ("req", "tp_pair"), split_axis=0, concat_axis=0, tiled=True)

    expert_inputs = (
        states,
        mask,
        router.T,
        first,
        first_other,
        second_raw,
        second_other,
    )
    mixed = pl.pallas_call(
        functools.partial(expert_kernel, copies, part_rows, min(req_count, 8) * pairs),
        out_shape=jax.ShapeDtypeStruct((team, 2 * part_rows, half), BF16),
        in_specs=[VMEM] * 7,
        out_specs=VMEM,
        compiler_params=params(16),
        name="experts",
    )(*expert_inputs)
    mixed = lax.all_to_all(mixed, ("req", "tp_pair"), split_axis=0, concat_axis=0, tiled=True)

    finished = pl.pallas_call(
        finish_kernel,
        out_shape=jax.ShapeDtypeStruct((2 * part_rows, half), BF16),
        in_specs=[VMEM, VMEM],
        out_specs=VMEM,
        compiler_params=params(8),
        name="finish",
    )(mixed, residual)
    gathered = [finished] + [
        lax.ppermute(finished, whole, flips[flip]) for flip in range(1, parts)
    ]

    layer, score = pl.pallas_call(
        functools.partial(score_kernel, fresh_count),
        out_shape=(
            jax.ShapeDtypeStruct((tokens * blocks, LANES), BF16),
            jax.ShapeDtypeStruct((fresh_count, samples), F32),
        ),
        in_specs=[VMEM] * (parts + 2),
        out_specs=(VMEM, VMEM),
        scratch_shapes=[
            pltpu.VMEM((blocks, tokens, LANES), F32),
            pltpu.VMEM((tokens * blocks, LANES), F32),
        ],
        compiler_params=params(8),
        name="score",
    )(*gathered, norm_gains, score_weight.reshape(1, model))
    layer = layer.reshape(samples, blocks, fresh_count, LANES).transpose(0, 2, 1, 3)
    return (
        layer.reshape(1, samples, fresh_count, model),
        score.T.reshape(1, samples, fresh_count),
    )


def solution(mesh):
    tp = ("tp_pair", "tp_side")
    req_count, parts = mesh.devices.shape
    mesh = jax.sharding.Mesh(
        mesh.devices.reshape(req_count, parts // 2, 2), ("req", "tp_pair", "tp_side")
    )
    placed = (
        P("req", None, None, None),
        P(),
        P("req", None),
        P(),
        P(),
        P("req", None, None, tp),
        P("req", None, None, None, tp),
        P("req", None, None, None),
        P(),
        P(None, tp),
        P(None, None, tp),
        P(tp, None),
        P(),
        P("req", None, None, tp),
        P("req", tp, None),
        P(),
    )
    return jax.shard_map(
        shards,
        mesh=mesh,
        in_specs=placed,
        out_specs=(P("req", None, None, None), P("req", None, None)),
        check_vma=False,
    )
```

```python
import functools
import math

import jax
import jax.numpy as jnp
from jax import lax
from jax.experimental import pallas as pl
from jax.experimental.pallas import tpu as pltpu
from jax.sharding import PartitionSpec as P

HEAD_DIM = 64
LANES = 128
EPSILON = 1e-05
ROPE_BASE = 10000.0
LOWEST = -1e30
FLOOR = -1e28
F32 = jnp.float32
BF16 = jnp.bfloat16
MIB = 1024 * 1024
HOLD_MIB = 56

VMEM = pl.BlockSpec(memory_space=pltpu.VMEM)
SMEM = pl.BlockSpec(memory_space=pltpu.SMEM)
HBM = pl.BlockSpec(memory_space=pltpu.HBM)
ANY = pl.BlockSpec(memory_space=pl.ANY)


def params(mib):
    return pltpu.CompilerParams(vmem_limit_bytes=mib * MIB)


def cost(flops, moved):
    return pl.CostEstimate(flops=int(flops), bytes_accessed=int(moved), transcendentals=0)


def dot(left, right):
    return jnp.dot(left, right, preferred_element_type=F32)


def dot_t(left, right):
    return lax.dot_general(left, right, (((1,), (1,)), ((), ())), preferred_element_type=F32)


def my_part():
    return lax.axis_index("tp_pair") * 2 + lax.axis_index("tp_side")


def load_all(pairs, done):
    copies = [pltpu.make_async_copy(far, near, done.at[k]) for k, (far, near) in enumerate(pairs)]
    for copy in copies:
        copy.start()
    return copies


def lane_iota(shape):
    return lax.broadcasted_iota(jnp.int32, shape, len(shape) - 1)


def normalize(x, gain):
    return x * lax.rsqrt(jnp.mean(x * x, axis=-1, keepdims=True) + EPSILON) * gain


def rotate(x, cosine, sine):
    lanes = lane_iota(x.shape)
    partner = jnp.where(lanes % HEAD_DIM < HEAD_DIM // 2, pltpu.roll(x, 96, 1), pltpu.roll(x, 32, 1))
    return x * cosine + partner * sine


def by_head(packed, low):
    zero = jnp.zeros_like(packed)
    return jnp.concatenate([jnp.where(low, packed, zero), jnp.where(low, zero, packed)], axis=0)


def swap_halves(first, second):
    low = lane_iota(first.shape) < HEAD_DIM
    return (
        jnp.where(low, first, pltpu.roll(second, HEAD_DIM, 1)),
        jnp.where(low, pltpu.roll(first, HEAD_DIM, 1), second),
    )


def query_kernel(
    fresh_count,
    prefix_far,
    lengths_far,
    tokens_far,
    named_far,
    gains_far,
    weight_far,
    message,
    flat,
    normed,
    cosine,
    sine,
    prefix,
    lengths,
    tokens,
    named,
    gains,
    weight,
    wide,
    ordered,
    done,
):
    loads = load_all(
        (
            (tokens_far, tokens),
            (gains_far, gains),
            (lengths_far, lengths),
            (prefix_far, prefix),
            (weight_far, weight),
            (named_far, named),
        ),
        done,
    )
    count, model = normed.shape
    samples = count // fresh_count
    parts, part_rows, _ = flat.shape
    blocks = model // LANES
    loads[0].wait()
    wide[...] = tokens[...].astype(F32)
    for c in range(blocks):
        for i in range(fresh_count):
            ordered[c, pl.ds(i, samples, stride=fresh_count), :] = wide[
                pl.ds(fresh_count * c + i, samples, stride=fresh_count * blocks), :
            ]
    states = jnp.concatenate([ordered[c] for c in range(blocks)], axis=1)
    for part in range(parts):
        flat[part] = states[part * part_rows : (part + 1) * part_rows].astype(BF16)
    loads[1].wait()
    rows = normalize(states, gains[0:1, :]).astype(BF16)
    normed[...] = rows
    loads[2].wait()
    loads[3].wait()
    row_id = lax.broadcasted_iota(jnp.int32, (count, 1), 0)
    position = row_id % fresh_count + prefix[lax.axis_index("req")]
    for sample in range(samples):
        position = position + jnp.where(row_id // fresh_count == sample, lengths[0, sample], 0)
    within = lane_iota((1, LANES)) % HEAD_DIM
    pair = (within % (HEAD_DIM // 2)).astype(F32)
    frequency = jnp.exp(pair * (-math.log(ROPE_BASE) / (HEAD_DIM // 2)))
    angles = position.astype(F32) * frequency
    cosine[...] = jnp.cos(angles)
    turn = jnp.sin(angles)
    sine[...] = jnp.where(within < HEAD_DIM // 2, -turn, turn)
    loads[4].wait()
    made = dot(rows, weight[...])
    pieces = []
    for group in swap_halves(made[:, :LANES], made[:, LANES:]):
        pieces.append(rotate(group, cosine[...], sine[...]).astype(BF16).astype(F32) * 0.125)
    packed = []
    for part in range(parts):
        for piece in pieces:
            packed.append(piece[part * part_rows : (part + 1) * part_rows])
    loads[5].wait()
    routed = named[...].astype(F32)
    packed.append(
        jnp.concatenate(
            [routed, jnp.zeros((routed.shape[0], LANES - routed.shape[1]), F32)], axis=1
        )
    )
    packed = jnp.concatenate(packed, axis=0).astype(BF16)
    message[...] = packed


def split_pages_kernel(source, out, wide):
    count, double, _ = source.shape
    half = double // 2
    wide[...] = source[...].astype(F32).reshape(count * double, LANES)
    keys = wide[pl.ds(0, count * half, stride=2), :].astype(BF16)
    values = wide[pl.ds(1, count * half, stride=2), :].astype(BF16)
    out[:, :half, :] = keys.reshape(count, half, LANES)
    out[:, half:, :] = values.reshape(count, half, LANES)


def pack_message(numer, top, total):
    high = total.astype(BF16).astype(F32)
    section = (lane_iota((8, LANES)) % HEAD_DIM) // 8
    stats = jnp.zeros((8, LANES), F32)
    for group in range(2):
        span = slice(group * 8, (group + 1) * 8)
        for k, kind in enumerate((top, high, total - high)):
            stats = jnp.where(section == 3 * group + k, kind[span], stats)
    return jnp.concatenate([numer, stats], axis=0).astype(BF16)


def unpack_message(block):
    block = block.astype(F32)
    stats = block[..., 16:24, :]
    low = lane_iota(stats.shape) < HEAD_DIM

    def pick(section):
        lane = section * 8
        return jnp.where(
            low, stats[..., lane : lane + 1], stats[..., HEAD_DIM + lane : HEAD_DIM + lane + 1]
        )

    top = jnp.concatenate([pick(0), pick(3)], axis=-2)
    total = jnp.concatenate([pick(1) + pick(2), pick(4) + pick(5)], axis=-2)
    return block[..., 0:16, :], top, total


def tail_kernel(
    fresh_count,
    lengths_far,
    query_far,
    normed_far,
    cosine_far,
    sine_far,
    weight_far,
    cache_far,
    out,
    lengths,
    query,
    normed,
    cosine,
    sine,
    weight,
    cache,
    load,
    done,
):
    tokens = normed.shape[0]
    samples, width, _ = cache.shape
    parts = out.shape[0]
    per_part = samples // parts
    loads = load_all(
        (
            (normed_far, normed),
            (weight_far, weight),
            (cosine_far, cosine),
            (sine_far, sine),
            (query_far.at[pl.ds(0, parts * 16)], query),
            (lengths_far, lengths),
        ),
        load,
    )
    spans = [pl.ds(part * per_part, per_part) for part in range(parts)]
    blocks = load_all([(cache_far.at[span], cache.at[span]) for span in spans], done)
    spread = (
        lax.broadcasted_iota(jnp.int32, (LANES, 2 * LANES), 1)
        == 2 * lax.broadcasted_iota(jnp.int32, (LANES, 2 * LANES), 0)
    ).astype(BF16)
    loads[0].wait()
    rows = normed[...]
    widened = jnp.concatenate(
        [dot(rows[:, c : c + LANES], spread) for c in range(0, rows.shape[1], LANES)], axis=1
    )
    both = jnp.concatenate([widened, pltpu.roll(widened, 1, 1)], axis=0).astype(BF16)
    for copy in loads[1:] + blocks:
        copy.wait()
    made = dot(both, weight[...])
    key_new = rotate(made[:tokens], cosine[...], sine[...]).astype(BF16)
    value_new = made[tokens:].astype(BF16)
    low = lane_iota((16, LANES)) < HEAD_DIM
    row_id = lax.broadcasted_iota(jnp.int32, (32, 1), 0)
    row_sample = (row_id % 8) // fresh_count
    row_fresh = row_id % fresh_count
    column_id = lane_iota((1, 32))
    column_sample = (column_id % 8) // fresh_count
    position = lax.broadcasted_iota(jnp.int32, (width, 32), 0)
    even = position % 2 == 0
    token_id = lane_iota((32, tokens))
    for part in range(parts):
        wide = by_head(query[part * 16 : (part + 1) * 16, :], low)
        length = jnp.zeros((1, 32), jnp.int32)
        for a in range(per_part):
            sample = part * per_part + a
            length = jnp.where(column_sample == a, lengths[0, sample], length)
        placed = [jnp.where(row_sample == a, wide, jnp.zeros_like(wide)) for a in range(per_part)]
        beside = jnp.concatenate([cache[part * per_part + a] for a in range(per_part)], axis=1)
        scores = dot_t(beside, jnp.concatenate(placed, axis=1))
        scores = jnp.where(even & (position < 2 * length), scores, LOWEST).T
        fresh = dot_t(wide, key_new)
        own_sample = row_sample + part * per_part
        fresh_seen = (token_id // fresh_count == own_sample) & (token_id % fresh_count <= row_fresh)
        fresh = jnp.where(fresh_seen, fresh, LOWEST)
        peak = jnp.maximum(
            jnp.max(scores, axis=1, keepdims=True), jnp.max(fresh, axis=1, keepdims=True)
        )
        peak = peak.astype(BF16).astype(F32)
        weights = jnp.exp(scores - peak)
        fresh_weights = jnp.exp(fresh - peak)
        amount = jnp.sum(weights, axis=1, keepdims=True) + jnp.sum(
            fresh_weights, axis=1, keepdims=True
        )
        shifted = pltpu.roll(weights, 1, 1).astype(BF16)
        every = dot(shifted, beside)
        mixed = every[:, :LANES]
        for a in range(1, per_part):
            mixed = jnp.where(row_sample == a, every[:, a * LANES : (a + 1) * LANES], mixed)
        mixed = mixed + dot(fresh_weights.astype(BF16), value_new)
        out[part] = pack_message(
            jnp.where(low, mixed[:16], mixed[16:]),
            jnp.where(low, peak[:16], peak[16:]),
            jnp.where(low, amount[:16], amount[16:]),
        )


def stack_kernel(*refs):
    *blocks, out = refs
    for k, block in enumerate(blocks):
        out[k] = block[...]


def page_kernel(
    slot_cap, homes, pages, lengths, cache, tail, *refs
):
    *blocks, out, named, query, slots, counts = refs
    requests = query.shape[0]
    parts = tail.shape[0]
    pool = cache.shape[0]
    page_size = cache.shape[1] // 2
    rows = parts * 16
    me = lax.axis_index("req")
    base = me * pool
    tail_numer, tail_top, tail_total = [
        kind.reshape(rows, LANES) for kind in unpack_message(tail[...])
    ]
    if len(blocks) == 1:
        query[...] = blocks[0][...]
    else:
        for far, block in enumerate(blocks):
            for k in range(block.shape[0]):
                query[me ^ (2 * k + far)] = block[k]
    named[...] = query[:, rows:, :]

    def clear(r, carry):
        counts[r] = 0
        for j in range(slot_cap):
            slots[r * slot_cap + j] = -1
        return carry

    lax.fori_loop(0, requests, clear, 0)

    def assign(v, carry):
        r = homes[base + v]
        rank = counts[r]
        slots[r * slot_cap + rank] = v
        counts[r] = rank + 1
        return carry

    lax.fori_loop(0, pool, assign, 0)

    low = lane_iota((rows, LANES)) < HEAD_DIM
    column = lane_iota((2 * rows, page_size))

    def finish(r, mixed, peak, amount):
        own = r == me
        top = jnp.where(low, peak[:rows], peak[rows:])
        joint = jnp.maximum(top, jnp.where(own, tail_top, FLOOR))
        here = jnp.exp(top - joint)
        there = jnp.where(own, jnp.exp(tail_top - joint), 0.0)
        numer = jnp.where(low, mixed[:rows], mixed[rows:]) * here + tail_numer * there
        total = jnp.where(low, amount[:rows], amount[rows:]) * here + tail_total * there
        for part in range(parts):
            span = slice(part * 16, (part + 1) * 16)
            out[r * parts + part] = pack_message(numer[span], joint[span], total[span])

    def several_requests(first, count):
        wides = []
        keys = []
        values = []
        limits = []
        for k in range(count):
            r = first + k
            wide = by_head(query[r, 0:rows, :], low)
            zero = jnp.zeros_like(wide)
            wides.append(jnp.concatenate([wide if c == k else zero for c in range(count)], axis=1))
            own_keys = []
            own_values = []
            own_limits = []
            for j in range(slot_cap):
                slot = slots[r * slot_cap + j]
                safe = jnp.maximum(slot, 0)
                own_limits.append(
                    jnp.where(slot >= 0, lengths[r] - pages[base + safe] * page_size, 0)
                )
                own_keys.append(cache[safe, :page_size, :])
                own_values.append(cache[safe, page_size:, :])
            keys.append(jnp.concatenate(own_keys, axis=0))
            values.append(jnp.concatenate(own_values, axis=0))
            limits.append(own_limits)
        scores = dot_t(jnp.concatenate(wides, axis=0), jnp.concatenate(keys, axis=1))
        all_weights = []
        stats = []
        for k in range(count):
            own = scores[k * 2 * rows : (k + 1) * 2 * rows]
            own = [
                jnp.where(
                    column < limits[k][j], own[:, j * page_size : (j + 1) * page_size], LOWEST
                )
                for j in range(slot_cap)
            ]
            peak = jnp.max(functools.reduce(jnp.maximum, own), axis=1, keepdims=True)
            peak = jnp.maximum(peak, FLOOR).astype(BF16).astype(F32)
            weights = [jnp.exp(one - peak) for one in own]
            amount = jnp.sum(functools.reduce(jnp.add, weights), axis=1, keepdims=True)
            all_weights.append(jnp.concatenate([one.astype(BF16) for one in weights], axis=1))
            stats.append((peak, amount))
        mixed = dot(jnp.concatenate(all_weights, axis=0), jnp.concatenate(values, axis=1))
        for k in range(count):
            finish(
                first + k,
                mixed[k * 2 * rows : (k + 1) * 2 * rows, k * LANES : (k + 1) * LANES],
                *stats[k],
            )

    pair = 2 if requests % 2 == 0 else 1
    step = 8 if requests % 8 == 0 else pair

    def several(g, carry):
        for k in range(0, step, pair):
            several_requests(g * step + k, pair)
        return carry

    if requests == step:
        several(0, 0)
    else:
        lax.fori_loop(0, requests // step, several, 0)


def merge_kernel(arrived, tokens, gains, *refs):
    parts = arrived.shape[1]
    weights = refs[:parts]
    out, residual, columns = refs[parts:]
    part = my_part()
    for t in range(parts):
        numer, top, total = unpack_message(arrived[:, t])
        factor = jnp.exp(top - jnp.max(top, axis=0, keepdims=True))
        attended = jnp.sum(factor * numer, axis=0) / jnp.sum(factor * total, axis=0)
        columns[t] = jnp.concatenate(swap_halves(attended[0:8], attended[8:16]), axis=1)
    projected = None
    for flip in range(parts):
        one = dot(columns[part ^ flip].astype(BF16), weights[flip][...])
        projected = one if projected is None else projected + one
    rows = (tokens[part].astype(F32) + projected).astype(BF16).astype(F32)
    residual[...] = rows
    normed = normalize(rows, gains[1:2, :])
    half = normed.shape[1] // 2
    message = jnp.concatenate([normed[:, :half], normed[:, half:]], axis=0).astype(BF16)
    for n in range(out.shape[0]):
        out[n] = message


def prepare_kernel(first_far, out, near, wide, done):
    local, double, _ = near.shape
    depth = double // 2
    loads = load_all([(first_far.at[e], near.at[e]) for e in range(local)], done)

    for e in range(local):
        loads[e].wait()
        buffer = wide.at[e % 2]
        buffer[...] = near[e].astype(F32)
        out[e, :, :LANES] = buffer[pl.ds(0, depth, stride=2), :].astype(BF16)
        out[e, :, LANES:] = buffer[pl.ds(1, depth, stride=2), :].astype(BF16)


def keep_kernel(table, out):
    del table, out


def names_kernel(part_rows, fresh_count, packed, out):
    requests, span, _ = packed.shape
    experts = out.shape[1]
    halves = out.shape[0] // (requests * part_rows)
    top = span // fresh_count
    row = lax.broadcasted_iota(jnp.int32, (halves * part_rows, LANES), 0)
    token = (row // part_rows) * 2 * part_rows + lax.axis_index("tp_side") * part_rows + row % part_rows
    pick = (lane_iota(row.shape) == token // fresh_count).astype(BF16)
    found = jnp.concatenate([dot_t(pick, packed[r]) for r in range(requests)], axis=0)
    fresh = lax.broadcasted_iota(jnp.int32, (found.shape[0], 1), 0) % fresh_count
    chosen = found[:, :top]
    for i in range(1, fresh_count):
        chosen = jnp.where(fresh == i, found[:, i * top : (i + 1) * top], chosen)
    lanes = lane_iota(out.shape).astype(F32)
    mask = jnp.zeros(out.shape, F32)
    for k in range(top):
        mask = jnp.where(chosen[:, k : k + 1] == lanes, 1.0, mask)
    out[...] = mask


def expert_kernel(
    copies,
    part_rows,
    group,
    arrived,
    mask,
    router,
    first,
    first_other,
    second,
    second_other,
    out,
):
    team, _, half = arrived.shape
    local = first.shape[0]
    expert_count = router.shape[0]
    count = group * part_rows
    me = lax.axis_index("req")

    def one_block(block):
        here = pl.ds(block * group, group)
        states = arrived[here].astype(F32)
        states = jnp.concatenate(
            [
                states[:, :part_rows].reshape(count, half),
                states[:, part_rows:].reshape(count, half),
            ],
            axis=1,
        ).astype(BF16)
        logits = dot_t(states, router[...])
        span = pl.ds(pl.multiple_of(block * count, count), count)
        chosen = jnp.where(mask[span, :] > 0.5, logits, LOWEST)
        shares = jnp.exp(chosen - jnp.max(chosen, axis=1, keepdims=True))
        gates = shares / jnp.sum(shares, axis=1, keepdims=True)
        lanes = lane_iota(gates.shape)
        row = lax.broadcasted_iota(jnp.int32, (count, 1), 0)
        row_request = (block * group + row // part_rows) // 2
        weights = []
        for e in range(local):
            slot = me * local + e
            gate = jnp.sum(
                jnp.where(lanes == lax.rem(slot, expert_count), gates, 0.0), axis=1, keepdims=True
            )
            if copies > 1:
                copy = lax.div(slot, expert_count)
                gate = jnp.where(lax.rem(row_request, copies) == copy, gate, 0.0)
            weights.append(gate)
        mixed = None
        for up, down in ((first, second), (first_other, second_other)):
            pieces = []
            for e in range(local):
                wide = dot(states, up[e])
                value = wide[:, :LANES]
                other = wide[:, LANES:]
                hidden = (value / (1.0 + jnp.exp(-value)) * other).astype(BF16).astype(F32)
                pieces.append((hidden * weights[e]).astype(BF16))
            part = dot(jnp.concatenate(pieces, axis=1), down[...])
            mixed = part if mixed is None else mixed + part
        out[here] = jnp.concatenate(
            [
                mixed[:, :half].reshape(group, part_rows, half),
                mixed[:, half:].reshape(group, part_rows, half),
            ],
            axis=1,
        ).astype(BF16)

    if team == group:
        one_block(0)
    else:

        def body(block, carry):
            one_block(block)
            return carry

        lax.fori_loop(0, team // group, body, 0)


def finish_kernel(arrived, residual, out):
    mixed = jnp.sum(arrived[...].astype(F32), axis=0)
    half = mixed.shape[1]
    kept = residual[...]
    message = jnp.concatenate([kept[:, :half], kept[:, half:]], axis=0) + mixed
    out[...] = message.astype(BF16)


def score_kernel(fresh_count, *refs):
    *arrived, gains, weight, layer, score, ordered, wide = refs
    double, half = arrived[0].shape
    rows = double // 2
    blocks, tokens, _ = ordered.shape
    samples = tokens // fresh_count
    for step, block in enumerate(arrived):
        state = block[...].astype(F32)
        spot = pl.ds(pl.multiple_of((my_part() ^ step) * rows, rows), rows)
        for c in range(blocks // 2):
            ordered[c, spot, :] = state[:rows, c * LANES : (c + 1) * LANES]
            ordered[blocks // 2 + c, spot, :] = state[rows:, c * LANES : (c + 1) * LANES]
    for c in range(blocks):
        for i in range(fresh_count):
            wide[pl.ds(fresh_count * c + i, samples, stride=fresh_count * blocks), :] = ordered[
                c, pl.ds(i, samples, stride=fresh_count), :
            ]
    layer[...] = wide[...].astype(BF16)
    states = jnp.concatenate([ordered[c] for c in range(blocks)], axis=1)
    final = normalize(states, gains[2:3, :])
    scored = jnp.sum(final * weight[...], axis=1, keepdims=True)
    row = lax.broadcasted_iota(jnp.int32, (tokens, samples), 0)
    here = row // fresh_count == lane_iota(row.shape)
    for i in range(fresh_count):
        score[i : i + 1, :] = jnp.sum(
            jnp.where(here & (row % fresh_count == i), scored, 0.0), axis=0, keepdims=True
        )


def shards(
    tokens_new,
    prefix_len,
    tail_len,
    pool_home,
    pool_page,
    slot_page_cache,
    tail_cache,
    routes,
    norm_gains,
    query_weight,
    key_value_weight,
    out_weight,
    router,
    expert_in,
    expert_out,
    score_weight,
):
    req_count = lax.axis_size("req")
    pairs = lax.axis_size("tp_pair")
    parts = 2 * pairs
    _, samples, fresh_count, model = tokens_new.shape
    tokens = samples * fresh_count
    part_rows = tokens // parts
    pool = slot_page_cache.shape[0]
    page_size = slot_page_cache.shape[1]
    slot_cap = max(1, pool // req_count)
    tail_count = tail_cache.shape[2]
    local = expert_in.shape[0]
    expert_count = router.shape[1]
    copies = local * req_count // expert_count
    everyone = req_count * parts
    rows = 2 * tokens
    blocks = model // LANES
    top = routes.shape[3]
    half = model // 2
    team = req_count * pairs

    whole = ("tp_pair", "tp_side")
    flips = [[(t, t ^ flip) for t in range(parts)] for flip in range(parts)]
    first_raw = expert_in.reshape(local, 2 * model, LANES)
    second_raw = expert_out.reshape(local * LANES, model)


    token_bytes = tokens_new.reshape(samples, fresh_count, blocks, LANES)
    token_bytes = token_bytes.transpose(0, 2, 1, 3).reshape(tokens * blocks, LANES)
    route_bytes = routes[0].transpose(1, 2, 0).reshape(fresh_count * top, samples)

    message, flat, normed, cosine, sine = pl.pallas_call(
        functools.partial(query_kernel, fresh_count),
        out_shape=(
            jax.ShapeDtypeStruct((rows + fresh_count * top, LANES), BF16),
            jax.ShapeDtypeStruct((parts, part_rows, model), BF16),
            jax.ShapeDtypeStruct((tokens, model), BF16),
            jax.ShapeDtypeStruct((tokens, LANES), F32),
            jax.ShapeDtypeStruct((tokens, LANES), F32),
        ),
        in_specs=[HBM] * 6,
        out_specs=(VMEM,) * 5,
        scratch_shapes=[
            pltpu.SMEM(prefix_len.shape, jnp.int32),
            pltpu.SMEM(tail_len.shape, jnp.int32),
            pltpu.VMEM(token_bytes.shape, BF16),
            pltpu.VMEM(route_bytes.shape, jnp.int32),
            pltpu.VMEM(norm_gains.shape, F32),
            pltpu.VMEM(query_weight.shape, BF16),
            pltpu.VMEM((tokens * blocks, LANES), F32),
            pltpu.VMEM((blocks, tokens, LANES), F32),
            pltpu.SemaphoreType.DMA((6,)),
        ],
        compiler_params=params(HOLD_MIB),
        name="query",
    )(prefix_len, tail_len, token_bytes, route_bytes, norm_gains, query_weight)

    key_value_rows = key_value_weight.reshape(2 * model, LANES)
    tail_rows = tail_cache.reshape(samples, 2 * tail_count, LANES)
    tail_inputs = (message, normed, cosine, sine)
    tail = pl.pallas_call(
        functools.partial(tail_kernel, fresh_count),
        out_shape=jax.ShapeDtypeStruct((parts, 24, LANES), BF16),
        in_specs=[HBM] * 7,
        out_specs=VMEM,
        scratch_shapes=[
            pltpu.SMEM(tail_len.shape, jnp.int32),
            pltpu.VMEM((rows, LANES), BF16),
            pltpu.VMEM(normed.shape, BF16),
            pltpu.VMEM(cosine.shape, F32),
            pltpu.VMEM(sine.shape, F32),
            pltpu.VMEM(key_value_rows.shape, BF16),
            pltpu.VMEM(tail_rows.shape, BF16),
            pltpu.SemaphoreType.DMA((6,)),
            pltpu.SemaphoreType.DMA((parts,)),
        ],
        compiler_params=params(HOLD_MIB),
        cost_estimate=cost(2e9, 5e6),
        name="tail",
    )(tail_len, *tail_inputs, key_value_rows, tail_rows)

    page_rows = slot_page_cache.reshape(pool, 2 * page_size, LANES)
    later, message = lax.optimization_barrier((out_weight, message))
    across = [lax.ppermute(later, whole, flips[flip]) for flip in range(2, parts, 2)]
    if req_count == 8:
        near = [
            lax.ppermute(message, "req", [(d, d ^ flip) for d in range(req_count)])
            for flip in (2, 4, 6)
        ]
        tail, near = lax.optimization_barrier((tail, near))
        stacked = pl.pallas_call(
            stack_kernel,
            out_shape=jax.ShapeDtypeStruct((4,) + message.shape, BF16),
            in_specs=[VMEM] * 4,
            out_specs=VMEM,
            compiler_params=params(8),
            name="stack",
        )(message, *near)
        page_rows, stacked = lax.optimization_barrier((page_rows, stacked))
        other = lax.ppermute(stacked, "req", [(d, d ^ 1) for d in range(req_count)])
        first_all = [stacked, other]
    else:
        copies_out = jnp.broadcast_to(message[None], (req_count,) + message.shape)
        first_all = [
            lax.all_to_all(copies_out, "req", split_axis=0, concat_axis=0, tiled=True)
        ]
    page_rows, tail, across, later = lax.optimization_barrier((page_rows, tail, across, later))
    projects = [out_weight, lax.ppermute(later, whole, flips[1])]
    for block in across:
        projects += [block, lax.ppermute(block, whole, flips[1])]

    step = 8 if pool % 8 == 0 else 1
    split_pages = pl.pallas_call(
        split_pages_kernel,
        grid=(pool // step,),
        out_shape=jax.ShapeDtypeStruct((pool, 2 * page_size, LANES), BF16),
        in_specs=[pl.BlockSpec((step, 2 * page_size, LANES), lambda v: (v, 0, 0))],
        out_specs=pl.BlockSpec((step, 2 * page_size, LANES), lambda v: (v, 0, 0)),
        scratch_shapes=[pltpu.VMEM((step * 2 * page_size, LANES), F32)],
        compiler_params=params(8),
        cost_estimate=cost(1e6, 4e6),
        name="split_pages",
    )(page_rows)

    partial, named = pl.pallas_call(
        functools.partial(page_kernel, slot_cap),
        out_shape=(
            jax.ShapeDtypeStruct((everyone, 24, LANES), BF16),
            jax.ShapeDtypeStruct((req_count, fresh_count * top, LANES), BF16),
        ),
        in_specs=[SMEM] * 3 + [VMEM] * (2 + len(first_all)),
        out_specs=(VMEM, VMEM),
        scratch_shapes=[
            pltpu.VMEM((req_count,) + message.shape, BF16),
            pltpu.SMEM((req_count * slot_cap,), jnp.int32),
            pltpu.SMEM((req_count,), jnp.int32),
        ],
        compiler_params=params(12),
        cost_estimate=cost(2e9, 5e6),
        name="pages",
    )(pool_home, pool_page, prefix_len, split_pages, tail, *first_all)
    arrived = lax.all_to_all(partial, ("req",) + whole, split_axis=0, concat_axis=0, tiled=True)

    first_raw, _ = lax.optimization_barrier((first_raw, partial))
    first = pl.pallas_call(
        prepare_kernel,
        out_shape=jax.ShapeDtypeStruct((local, model, 2 * LANES), BF16),
        in_specs=[HBM],
        out_specs=VMEM,
        scratch_shapes=[
            pltpu.VMEM(first_raw.shape, BF16),
            pltpu.VMEM((2, 2 * model, LANES), F32),
            pltpu.SemaphoreType.DMA((local,)),
        ],
        compiler_params=params(HOLD_MIB),
        cost_estimate=cost(2e9, 8e6),
        name="prepare",
    )(first_raw)
    named, first, projects = lax.optimization_barrier((named, first, projects))
    mask = pl.pallas_call(
        functools.partial(names_kernel, part_rows, fresh_count),
        out_shape=jax.ShapeDtypeStruct((team * part_rows, expert_count), F32),
        in_specs=[VMEM],
        out_specs=VMEM,
        compiler_params=params(8),
        cost_estimate=cost(1e6, 1e6),
        name="names",
    )(named)
    arrived, first, second_sent, mask = lax.optimization_barrier(
        (arrived, first, second_raw, mask)
    )
    first = pl.pallas_call(
        keep_kernel,
        out_shape=jax.ShapeDtypeStruct(first.shape, BF16),
        in_specs=[HBM],
        out_specs=HBM,
        input_output_aliases={0: 0},
        compiler_params=params(HOLD_MIB),
        name="keep",
    )(first)
    first_other = lax.ppermute(first, whole, flips[1])
    second_other = lax.ppermute(second_sent, whole, flips[1])

    message, residual = pl.pallas_call(
        merge_kernel,
        out_shape=(
            jax.ShapeDtypeStruct((team, 2 * part_rows, half), BF16),
            jax.ShapeDtypeStruct((part_rows, model), F32),
        ),
        in_specs=[VMEM] * (3 + parts),
        out_specs=(VMEM, VMEM),
        scratch_shapes=[pltpu.VMEM((parts, part_rows, model // parts), F32)],
        compiler_params=params(12),
        name="merge",
    )(arrived.reshape(req_count, parts, 24, LANES), flat, norm_gains, *projects)
    states = lax.all_to_all(message, ("req", "tp_pair"), split_axis=0, concat_axis=0, tiled=True)

    expert_inputs = (
        states,
        mask,
        router.T,
        first,
        first_other,
        second_raw,
        second_other,
    )
    mixed = pl.pallas_call(
        functools.partial(expert_kernel, copies, part_rows, min(req_count, 8) * pairs),
        out_shape=jax.ShapeDtypeStruct((team, 2 * part_rows, half), BF16),
        in_specs=[VMEM] * 7,
        out_specs=VMEM,
        compiler_params=params(16),
        name="experts",
    )(*expert_inputs)
    mixed = lax.all_to_all(mixed, ("req", "tp_pair"), split_axis=0, concat_axis=0, tiled=True)

    finished = pl.pallas_call(
        finish_kernel,
        out_shape=jax.ShapeDtypeStruct((2 * part_rows, half), BF16),
        in_specs=[VMEM, VMEM],
        out_specs=VMEM,
        compiler_params=params(8),
        name="finish",
    )(mixed, residual)
    gathered = [finished] + [
        lax.ppermute(finished, whole, flips[flip]) for flip in range(1, parts)
    ]

    layer, score = pl.pallas_call(
        functools.partial(score_kernel, fresh_count),
        out_shape=(
            jax.ShapeDtypeStruct((tokens * blocks, LANES), BF16),
            jax.ShapeDtypeStruct((fresh_count, samples), F32),
        ),
        in_specs=[VMEM] * (parts + 2),
        out_specs=(VMEM, VMEM),
        scratch_shapes=[
            pltpu.VMEM((blocks, tokens, LANES), F32),
            pltpu.VMEM((tokens * blocks, LANES), F32),
        ],
        compiler_params=params(8),
        name="score",
    )(*gathered, norm_gains, score_weight.reshape(1, model))
    layer = layer.reshape(samples, blocks, fresh_count, LANES).transpose(0, 2, 1, 3)
    return (
        layer.reshape(1, samples, fresh_count, model),
        score.T.reshape(1, samples, fresh_count),
    )


def solution(mesh):
    tp = ("tp_pair", "tp_side")
    req_count, parts = mesh.devices.shape
    mesh = jax.sharding.Mesh(
        mesh.devices.reshape(req_count, parts // 2, 2), ("req", "tp_pair", "tp_side")
    )
    placed = (
        P("req", None, None, None),
        P(),
        P("req", None),
        P(),
        P(),
        P("req", None, None, tp),
        P("req", None, None, None, tp),
        P("req", None, None, None),
        P(),
        P(None, tp),
        P(None, None, tp),
        P(tp, None),
        P(),
        P("req", None, None, tp),
        P("req", tp, None),
        P(),
    )
    return jax.shard_map(
        shards,
        mesh=mesh,
        in_specs=placed,
        out_specs=(P("req", None, None, None), P("req", None, None)),
        check_vma=False,
    )
```

```python
import functools
import math

import jax
import jax.numpy as jnp
from jax import lax
from jax.experimental import pallas as pl
from jax.experimental.pallas import tpu as pltpu
from jax.sharding import PartitionSpec as P

HEAD_DIM = 64
LANES = 128
EPSILON = 1e-05
ROPE_BASE = 10000.0
LOWEST = -1e30
FLOOR = -1e28
F32 = jnp.float32
BF16 = jnp.bfloat16
MIB = 1024 * 1024
HOLD_MIB = 56

VMEM = pl.BlockSpec(memory_space=pltpu.VMEM)
SMEM = pl.BlockSpec(memory_space=pltpu.SMEM)
HBM = pl.BlockSpec(memory_space=pltpu.HBM)
ANY = pl.BlockSpec(memory_space=pl.ANY)


def params(mib):
    return pltpu.CompilerParams(vmem_limit_bytes=mib * MIB)


def cost(flops, moved):
    return pl.CostEstimate(flops=int(flops), bytes_accessed=int(moved), transcendentals=0)


def dot(left, right):
    return jnp.dot(left, right, preferred_element_type=F32)


def dot_t(left, right):
    return lax.dot_general(left, right, (((1,), (1,)), ((), ())), preferred_element_type=F32)


def my_part():
    return lax.axis_index("tp_pair") * 2 + lax.axis_index("tp_side")


def load_all(pairs, done):
    copies = [pltpu.make_async_copy(far, near, done.at[k]) for k, (far, near) in enumerate(pairs)]
    for copy in copies:
        copy.start()
    return copies


def lane_iota(shape):
    return lax.broadcasted_iota(jnp.int32, shape, len(shape) - 1)


def normalize(x, gain):
    return x * lax.rsqrt(jnp.mean(x * x, axis=-1, keepdims=True) + EPSILON) * gain


def rotate(x, cosine, sine):
    lanes = lane_iota(x.shape)
    partner = jnp.where(lanes % HEAD_DIM < HEAD_DIM // 2, pltpu.roll(x, 96, 1), pltpu.roll(x, 32, 1))
    return x * cosine + partner * sine


def by_head(packed, low):
    zero = jnp.zeros_like(packed)
    return jnp.concatenate([jnp.where(low, packed, zero), jnp.where(low, zero, packed)], axis=0)


def swap_halves(first, second):
    low = lane_iota(first.shape) < HEAD_DIM
    return (
        jnp.where(low, first, pltpu.roll(second, HEAD_DIM, 1)),
        jnp.where(low, pltpu.roll(first, HEAD_DIM, 1), second),
    )


def query_kernel(
    fresh_count,
    prefix_far,
    lengths_far,
    tokens_far,
    named_far,
    gains_far,
    weight_far,
    message,
    flat,
    normed,
    cosine,
    sine,
    prefix,
    lengths,
    tokens,
    named,
    gains,
    weight,
    wide,
    ordered,
    done,
):
    loads = load_all(
        (
            (tokens_far, tokens),
            (gains_far, gains),
            (lengths_far, lengths),
            (prefix_far, prefix),
            (weight_far, weight),
            (named_far, named),
        ),
        done,
    )
    count, model = normed.shape
    samples = count // fresh_count
    parts, part_rows, _ = flat.shape
    blocks = model // LANES
    loads[0].wait()
    wide[...] = tokens[...].astype(F32)
    for c in range(blocks):
        for i in range(fresh_count):
            ordered[c, pl.ds(i, samples, stride=fresh_count), :] = wide[
                pl.ds(fresh_count * c + i, samples, stride=fresh_count * blocks), :
            ]
    states = jnp.concatenate([ordered[c] for c in range(blocks)], axis=1)
    for part in range(parts):
        flat[part] = states[part * part_rows : (part + 1) * part_rows].astype(BF16)
    loads[1].wait()
    rows = normalize(states, gains[0:1, :]).astype(BF16)
    normed[...] = rows
    loads[2].wait()
    loads[3].wait()
    row_id = lax.broadcasted_iota(jnp.int32, (count, 1), 0)
    position = row_id % fresh_count + prefix[lax.axis_index("req")]
    for sample in range(samples):
        position = position + jnp.where(row_id // fresh_count == sample, lengths[0, sample], 0)
    within = lane_iota((1, LANES)) % HEAD_DIM
    pair = (within % (HEAD_DIM // 2)).astype(F32)
    frequency = jnp.exp(pair * (-math.log(ROPE_BASE) / (HEAD_DIM // 2)))
    angles = position.astype(F32) * frequency
    cosine[...] = jnp.cos(angles)
    turn = jnp.sin(angles)
    sine[...] = jnp.where(within < HEAD_DIM // 2, -turn, turn)
    loads[4].wait()
    made = dot(rows, weight[...])
    pieces = []
    for group in swap_halves(made[:, :LANES], made[:, LANES:]):
        pieces.append(rotate(group, cosine[...], sine[...]).astype(BF16).astype(F32) * 0.125)
    packed = []
    for part in range(parts):
        for piece in pieces:
            packed.append(piece[part * part_rows : (part + 1) * part_rows])
    loads[5].wait()
    routed = named[...].astype(F32)
    packed.append(
        jnp.concatenate(
            [routed, jnp.zeros((routed.shape[0], LANES - routed.shape[1]), F32)], axis=1
        )
    )
    packed = jnp.concatenate(packed, axis=0).astype(BF16)
    for n in range(message.shape[0]):
        message[n] = packed


def split_pages_kernel(source, out, wide):
    count, double, _ = source.shape
    half = double // 2
    wide[...] = source[...].astype(F32).reshape(count * double, LANES)
    keys = wide[pl.ds(0, count * half, stride=2), :].astype(BF16)
    values = wide[pl.ds(1, count * half, stride=2), :].astype(BF16)
    out[:, :half, :] = keys.reshape(count, half, LANES)
    out[:, half:, :] = values.reshape(count, half, LANES)


def pack_message(numer, top, total):
    high = total.astype(BF16).astype(F32)
    section = (lane_iota((8, LANES)) % HEAD_DIM) // 8
    stats = jnp.zeros((8, LANES), F32)
    for group in range(2):
        span = slice(group * 8, (group + 1) * 8)
        for k, kind in enumerate((top, high, total - high)):
            stats = jnp.where(section == 3 * group + k, kind[span], stats)
    return jnp.concatenate([numer, stats], axis=0).astype(BF16)


def unpack_message(block):
    block = block.astype(F32)
    stats = block[..., 16:24, :]
    low = lane_iota(stats.shape) < HEAD_DIM

    def pick(section):
        lane = section * 8
        return jnp.where(
            low, stats[..., lane : lane + 1], stats[..., HEAD_DIM + lane : HEAD_DIM + lane + 1]
        )

    top = jnp.concatenate([pick(0), pick(3)], axis=-2)
    total = jnp.concatenate([pick(1) + pick(2), pick(4) + pick(5)], axis=-2)
    return block[..., 0:16, :], top, total


def tail_kernel(
    fresh_count,
    lengths_far,
    query_far,
    normed_far,
    cosine_far,
    sine_far,
    weight_far,
    cache_far,
    out,
    lengths,
    query,
    normed,
    cosine,
    sine,
    weight,
    cache,
    load,
    done,
):
    tokens = normed.shape[0]
    samples, width, _ = cache.shape
    parts = out.shape[0]
    per_part = samples // parts
    loads = load_all(
        (
            (normed_far, normed),
            (weight_far, weight),
            (cosine_far, cosine),
            (sine_far, sine),
            (query_far.at[0, pl.ds(0, parts * 16)], query),
            (lengths_far, lengths),
        ),
        load,
    )
    spans = [pl.ds(part * per_part, per_part) for part in range(parts)]
    blocks = load_all([(cache_far.at[span], cache.at[span]) for span in spans], done)
    spread = (
        lax.broadcasted_iota(jnp.int32, (LANES, 2 * LANES), 1)
        == 2 * lax.broadcasted_iota(jnp.int32, (LANES, 2 * LANES), 0)
    ).astype(BF16)
    loads[0].wait()
    rows = normed[...]
    widened = jnp.concatenate(
        [dot(rows[:, c : c + LANES], spread) for c in range(0, rows.shape[1], LANES)], axis=1
    )
    both = jnp.concatenate([widened, pltpu.roll(widened, 1, 1)], axis=0).astype(BF16)
    for copy in loads[1:]:
        copy.wait()
    made = dot(both, weight[...])
    key_new = rotate(made[:tokens], cosine[...], sine[...]).astype(BF16)
    value_new = made[tokens:].astype(BF16)
    low = lane_iota((16, LANES)) < HEAD_DIM
    row_id = lax.broadcasted_iota(jnp.int32, (32, 1), 0)
    row_sample = (row_id % 8) // fresh_count
    row_fresh = row_id % fresh_count
    column = lane_iota((32, width))
    even = column % 2 == 0
    token_id = lane_iota((32, tokens))
    for part in range(parts):
        if part % 2 == 0:
            for copy in blocks[part : part + 2]:
                copy.wait()
        wide = by_head(query[part * 16 : (part + 1) * 16, :], low)
        length = jnp.zeros((32, 1), jnp.int32)
        for a in range(per_part):
            length = jnp.where(row_sample == a, lengths[0, part * per_part + a], length)
        placed = [jnp.where(row_sample == a, wide, jnp.zeros_like(wide)) for a in range(per_part)]
        beside = jnp.concatenate([cache[part * per_part + a] for a in range(per_part)], axis=1)
        scores = dot_t(jnp.concatenate(placed, axis=1), beside)
        scores = jnp.where(even & (column < 2 * length), scores, LOWEST)
        fresh = dot_t(wide, key_new)
        own_sample = row_sample + part * per_part
        fresh_seen = (token_id // fresh_count == own_sample) & (token_id % fresh_count <= row_fresh)
        fresh = jnp.where(fresh_seen, fresh, LOWEST)
        peak = jnp.maximum(
            jnp.max(scores, axis=1, keepdims=True), jnp.max(fresh, axis=1, keepdims=True)
        )
        peak = peak.astype(BF16).astype(F32)
        weights = jnp.exp(scores - peak)
        fresh_weights = jnp.exp(fresh - peak)
        amount = jnp.sum(weights, axis=1, keepdims=True) + jnp.sum(
            fresh_weights, axis=1, keepdims=True
        )
        shifted = pltpu.roll(weights, 1, 1).astype(BF16)
        every = dot(shifted, beside)
        mixed = every[:, :LANES]
        for a in range(1, per_part):
            mixed = jnp.where(row_sample == a, every[:, a * LANES : (a + 1) * LANES], mixed)
        mixed = mixed + dot(fresh_weights.astype(BF16), value_new)
        out[part] = pack_message(
            jnp.where(low, mixed[:16], mixed[16:]),
            jnp.where(low, peak[:16], peak[16:]),
            jnp.where(low, amount[:16], amount[16:]),
        )


def page_kernel(
    slot_cap, homes, pages, lengths, cache, tail, query, out, named, slots, counts
):
    requests = query.shape[0]
    parts = tail.shape[0]
    pool = cache.shape[0]
    page_size = cache.shape[1] // 2
    rows = parts * 16
    me = lax.axis_index("req")
    base = me * pool
    tail_numer, tail_top, tail_total = [
        kind.reshape(rows, LANES) for kind in unpack_message(tail[...])
    ]
    named[...] = query[:, rows:, :]

    def clear(r, carry):
        counts[r] = 0
        for j in range(slot_cap):
            slots[r * slot_cap + j] = -1
        return carry

    lax.fori_loop(0, requests, clear, 0)

    def assign(v, carry):
        r = homes[base + v]
        rank = counts[r]
        slots[r * slot_cap + rank] = v
        counts[r] = rank + 1
        return carry

    lax.fori_loop(0, pool, assign, 0)

    low = lane_iota((rows, LANES)) < HEAD_DIM
    column = lane_iota((2 * rows, page_size))

    def finish(r, mixed, peak, amount):
        own = r == me
        top = jnp.where(low, peak[:rows], peak[rows:])
        joint = jnp.maximum(top, jnp.where(own, tail_top, FLOOR))
        here = jnp.exp(top - joint)
        there = jnp.where(own, jnp.exp(tail_top - joint), 0.0)
        numer = jnp.where(low, mixed[:rows], mixed[rows:]) * here + tail_numer * there
        total = jnp.where(low, amount[:rows], amount[rows:]) * here + tail_total * there
        for part in range(parts):
            span = slice(part * 16, (part + 1) * 16)
            out[r * parts + part] = pack_message(numer[span], joint[span], total[span])

    def several_requests(first, count):
        wides = []
        keys = []
        values = []
        limits = []
        for k in range(count):
            r = first + k
            wide = by_head(query[r, 0:rows, :], low)
            zero = jnp.zeros_like(wide)
            wides.append(jnp.concatenate([wide if c == k else zero for c in range(count)], axis=1))
            own_keys = []
            own_values = []
            own_limits = []
            for j in range(slot_cap):
                slot = slots[r * slot_cap + j]
                safe = jnp.maximum(slot, 0)
                own_limits.append(
                    jnp.where(slot >= 0, lengths[r] - pages[base + safe] * page_size, 0)
                )
                own_keys.append(cache[safe, :page_size, :])
                own_values.append(cache[safe, page_size:, :])
            keys.append(jnp.concatenate(own_keys, axis=0))
            values.append(jnp.concatenate(own_values, axis=0))
            limits.append(own_limits)
        scores = dot_t(jnp.concatenate(wides, axis=0), jnp.concatenate(keys, axis=1))
        all_weights = []
        stats = []
        for k in range(count):
            own = scores[k * 2 * rows : (k + 1) * 2 * rows]
            own = [
                jnp.where(
                    column < limits[k][j], own[:, j * page_size : (j + 1) * page_size], LOWEST
                )
                for j in range(slot_cap)
            ]
            peak = jnp.max(functools.reduce(jnp.maximum, own), axis=1, keepdims=True)
            peak = jnp.maximum(peak, FLOOR).astype(BF16).astype(F32)
            weights = [jnp.exp(one - peak) for one in own]
            amount = jnp.sum(functools.reduce(jnp.add, weights), axis=1, keepdims=True)
            all_weights.append(jnp.concatenate([one.astype(BF16) for one in weights], axis=1))
            stats.append((peak, amount))
        mixed = dot(jnp.concatenate(all_weights, axis=0), jnp.concatenate(values, axis=1))
        for k in range(count):
            finish(
                first + k,
                mixed[k * 2 * rows : (k + 1) * 2 * rows, k * LANES : (k + 1) * LANES],
                *stats[k],
            )

    pair = 2 if requests % 2 == 0 else 1
    step = 8 if requests % 8 == 0 else pair

    def several(g, carry):
        for k in range(0, step, pair):
            several_requests(g * step + k, pair)
        return carry

    if requests == step:
        several(0, 0)
    else:
        lax.fori_loop(0, requests // step, several, 0)


def merge_kernel(arrived, tokens, gains, *refs):
    parts = arrived.shape[1]
    weights = refs[:parts]
    out, residual, columns = refs[parts:]
    part = my_part()
    for t in range(parts):
        numer, top, total = unpack_message(arrived[:, t])
        factor = jnp.exp(top - jnp.max(top, axis=0, keepdims=True))
        attended = jnp.sum(factor * numer, axis=0) / jnp.sum(factor * total, axis=0)
        columns[t] = jnp.concatenate(swap_halves(attended[0:8], attended[8:16]), axis=1)
    projected = None
    for flip in range(parts):
        one = dot(columns[part ^ flip].astype(BF16), weights[flip][...])
        projected = one if projected is None else projected + one
    rows = (tokens[part].astype(F32) + projected).astype(BF16).astype(F32)
    residual[...] = rows
    normed = normalize(rows, gains[1:2, :])
    half = normed.shape[1] // 2
    message = jnp.concatenate([normed[:, :half], normed[:, half:]], axis=0).astype(BF16)
    for n in range(out.shape[0]):
        out[n] = message


def prepare_kernel(first_far, out, near, wide, done):
    local, double, _ = near.shape
    depth = double // 2
    loads = load_all([(first_far.at[e], near.at[e]) for e in range(local)], done)

    for e in range(local):
        loads[e].wait()
        buffer = wide.at[e % 2]
        buffer[...] = near[e].astype(F32)
        out[e, :, :LANES] = buffer[pl.ds(0, depth, stride=2), :].astype(BF16)
        out[e, :, LANES:] = buffer[pl.ds(1, depth, stride=2), :].astype(BF16)


def keep_kernel(table, out):
    del table, out


def names_kernel(part_rows, fresh_count, packed, out):
    requests, span, _ = packed.shape
    experts = out.shape[1]
    halves = out.shape[0] // (requests * part_rows)
    top = span // fresh_count
    row = lax.broadcasted_iota(jnp.int32, (halves * part_rows, LANES), 0)
    token = (row // part_rows) * 2 * part_rows + lax.axis_index("tp_side") * part_rows + row % part_rows
    pick = (lane_iota(row.shape) == token // fresh_count).astype(BF16)
    found = jnp.concatenate([dot_t(pick, packed[r]) for r in range(requests)], axis=0)
    fresh = lax.broadcasted_iota(jnp.int32, (found.shape[0], 1), 0) % fresh_count
    chosen = found[:, :top]
    for i in range(1, fresh_count):
        chosen = jnp.where(fresh == i, found[:, i * top : (i + 1) * top], chosen)
    lanes = lane_iota(out.shape).astype(F32)
    mask = jnp.zeros(out.shape, F32)
    for k in range(top):
        mask = jnp.where(chosen[:, k : k + 1] == lanes, 1.0, mask)
    out[...] = mask


def expert_kernel(
    copies,
    part_rows,
    group,
    arrived,
    mask,
    router,
    first,
    first_other,
    second,
    second_other,
    out,
):
    team, _, half = arrived.shape
    local = first.shape[0]
    expert_count = router.shape[0]
    count = group * part_rows
    me = lax.axis_index("req")

    def one_block(block):
        here = pl.ds(block * group, group)
        states = arrived[here].astype(F32)
        states = jnp.concatenate(
            [
                states[:, :part_rows].reshape(count, half),
                states[:, part_rows:].reshape(count, half),
            ],
            axis=1,
        ).astype(BF16)
        logits = dot_t(states, router[...])
        span = pl.ds(pl.multiple_of(block * count, count), count)
        chosen = jnp.where(mask[span, :] > 0.5, logits, LOWEST)
        shares = jnp.exp(chosen - jnp.max(chosen, axis=1, keepdims=True))
        gates = shares / jnp.sum(shares, axis=1, keepdims=True)
        lanes = lane_iota(gates.shape)
        row = lax.broadcasted_iota(jnp.int32, (count, 1), 0)
        row_request = (block * group + row // part_rows) // 2
        weights = []
        for e in range(local):
            slot = me * local + e
            gate = jnp.sum(
                jnp.where(lanes == lax.rem(slot, expert_count), gates, 0.0), axis=1, keepdims=True
            )
            if copies > 1:
                copy = lax.div(slot, expert_count)
                gate = jnp.where(lax.rem(row_request, copies) == copy, gate, 0.0)
            weights.append(gate)
        mixed = None
        for up, down in ((first, second), (first_other, second_other)):
            pieces = []
            for e in range(local):
                wide = dot(states, up[e])
                value = wide[:, :LANES]
                other = wide[:, LANES:]
                hidden = (value / (1.0 + jnp.exp(-value)) * other).astype(BF16).astype(F32)
                pieces.append((hidden * weights[e]).astype(BF16))
            part = dot(jnp.concatenate(pieces, axis=1), down[...])
            mixed = part if mixed is None else mixed + part
        out[here] = jnp.concatenate(
            [
                mixed[:, :half].reshape(group, part_rows, half),
                mixed[:, half:].reshape(group, part_rows, half),
            ],
            axis=1,
        ).astype(BF16)

    if team == group:
        one_block(0)
    else:

        def body(block, carry):
            one_block(block)
            return carry

        lax.fori_loop(0, team // group, body, 0)


def finish_kernel(arrived, residual, out):
    mixed = jnp.sum(arrived[...].astype(F32), axis=0)
    half = mixed.shape[1]
    kept = residual[...]
    message = jnp.concatenate([kept[:, :half], kept[:, half:]], axis=0) + mixed
    out[...] = message.astype(BF16)


def score_kernel(fresh_count, *refs):
    *arrived, gains, weight, layer, score, ordered, wide = refs
    double, half = arrived[0].shape
    rows = double // 2
    blocks, tokens, _ = ordered.shape
    samples = tokens // fresh_count
    for step, block in enumerate(arrived):
        state = block[...].astype(F32)
        spot = pl.ds(pl.multiple_of((my_part() ^ step) * rows, rows), rows)
        for c in range(blocks // 2):
            ordered[c, spot, :] = state[:rows, c * LANES : (c + 1) * LANES]
            ordered[blocks // 2 + c, spot, :] = state[rows:, c * LANES : (c + 1) * LANES]
    for c in range(blocks):
        for i in range(fresh_count):
            wide[pl.ds(fresh_count * c + i, samples, stride=fresh_count * blocks), :] = ordered[
                c, pl.ds(i, samples, stride=fresh_count), :
            ]
    layer[...] = wide[...].astype(BF16)
    states = jnp.concatenate([ordered[c] for c in range(blocks)], axis=1)
    final = normalize(states, gains[2:3, :])
    scored = jnp.sum(final * weight[...], axis=1, keepdims=True)
    row = lax.broadcasted_iota(jnp.int32, (tokens, samples), 0)
    here = row // fresh_count == lane_iota(row.shape)
    for i in range(fresh_count):
        score[i : i + 1, :] = jnp.sum(
            jnp.where(here & (row % fresh_count == i), scored, 0.0), axis=0, keepdims=True
        )


def shards(
    tokens_new,
    prefix_len,
    tail_len,
    pool_home,
    pool_page,
    slot_page_cache,
    tail_cache,
    routes,
    norm_gains,
    query_weight,
    key_value_weight,
    out_weight,
    router,
    expert_in,
    expert_out,
    score_weight,
):
    req_count = lax.axis_size("req")
    pairs = lax.axis_size("tp_pair")
    parts = 2 * pairs
    _, samples, fresh_count, model = tokens_new.shape
    tokens = samples * fresh_count
    part_rows = tokens // parts
    pool = slot_page_cache.shape[0]
    page_size = slot_page_cache.shape[1]
    slot_cap = max(1, pool // req_count)
    tail_count = tail_cache.shape[2]
    local = expert_in.shape[0]
    expert_count = router.shape[1]
    copies = local * req_count // expert_count
    everyone = req_count * parts
    rows = 2 * tokens
    blocks = model // LANES
    top = routes.shape[3]
    half = model // 2
    team = req_count * pairs

    whole = ("tp_pair", "tp_side")
    flips = [[(t, t ^ flip) for t in range(parts)] for flip in range(parts)]
    first_raw = expert_in.reshape(local, 2 * model, LANES)
    second_raw = expert_out.reshape(local * LANES, model)


    token_bytes = tokens_new.reshape(samples, fresh_count, blocks, LANES)
    token_bytes = token_bytes.transpose(0, 2, 1, 3).reshape(tokens * blocks, LANES)
    route_bytes = routes[0].transpose(1, 2, 0).reshape(fresh_count * top, samples)

    message, flat, normed, cosine, sine = pl.pallas_call(
        functools.partial(query_kernel, fresh_count),
        out_shape=(
            jax.ShapeDtypeStruct((req_count, rows + fresh_count * top, LANES), BF16),
            jax.ShapeDtypeStruct((parts, part_rows, model), BF16),
            jax.ShapeDtypeStruct((tokens, model), BF16),
            jax.ShapeDtypeStruct((tokens, LANES), F32),
            jax.ShapeDtypeStruct((tokens, LANES), F32),
        ),
        in_specs=[HBM] * 6,
        out_specs=(VMEM,) * 5,
        scratch_shapes=[
            pltpu.SMEM(prefix_len.shape, jnp.int32),
            pltpu.SMEM(tail_len.shape, jnp.int32),
            pltpu.VMEM(token_bytes.shape, BF16),
            pltpu.VMEM(route_bytes.shape, jnp.int32),
            pltpu.VMEM(norm_gains.shape, F32),
            pltpu.VMEM(query_weight.shape, BF16),
            pltpu.VMEM((tokens * blocks, LANES), F32),
            pltpu.VMEM((blocks, tokens, LANES), F32),
            pltpu.SemaphoreType.DMA((6,)),
        ],
        compiler_params=params(HOLD_MIB),
        name="query",
    )(prefix_len, tail_len, token_bytes, route_bytes, norm_gains, query_weight)

    key_value_rows = key_value_weight.reshape(2 * model, LANES)
    tail_rows = tail_cache.reshape(samples, 2 * tail_count, LANES)
    tail_inputs = (message, normed, cosine, sine)
    tail = pl.pallas_call(
        functools.partial(tail_kernel, fresh_count),
        out_shape=jax.ShapeDtypeStruct((parts, 24, LANES), BF16),
        in_specs=[HBM] * 7,
        out_specs=VMEM,
        scratch_shapes=[
            pltpu.SMEM(tail_len.shape, jnp.int32),
            pltpu.VMEM((rows, LANES), BF16),
            pltpu.VMEM(normed.shape, BF16),
            pltpu.VMEM(cosine.shape, F32),
            pltpu.VMEM(sine.shape, F32),
            pltpu.VMEM(key_value_rows.shape, BF16),
            pltpu.VMEM(tail_rows.shape, BF16),
            pltpu.SemaphoreType.DMA((6,)),
            pltpu.SemaphoreType.DMA((parts,)),
        ],
        compiler_params=params(HOLD_MIB),
        cost_estimate=cost(2e9, 5e6),
        name="tail",
    )(tail_len, *tail_inputs, key_value_rows, tail_rows)

    page_rows = slot_page_cache.reshape(pool, 2 * page_size, LANES)
    later, message = lax.optimization_barrier((out_weight, message))
    across = [lax.ppermute(later, whole, flips[flip]) for flip in range(2, parts, 2)]
    beside = lax.ppermute(later, whole, flips[1])
    first_all = lax.all_to_all(message, "req", split_axis=0, concat_axis=0, tiled=True)
    page_rows, tail, beside = lax.optimization_barrier((page_rows, tail, beside))

    step = 8 if pool % 8 == 0 else 1
    split_pages = pl.pallas_call(
        split_pages_kernel,
        grid=(pool // step,),
        out_shape=jax.ShapeDtypeStruct((pool, 2 * page_size, LANES), BF16),
        in_specs=[pl.BlockSpec((step, 2 * page_size, LANES), lambda v: (v, 0, 0))],
        out_specs=pl.BlockSpec((step, 2 * page_size, LANES), lambda v: (v, 0, 0)),
        scratch_shapes=[pltpu.VMEM((step * 2 * page_size, LANES), F32)],
        compiler_params=params(8),
        cost_estimate=cost(1e6, 4e6),
        name="split_pages",
    )(page_rows)

    partial, named = pl.pallas_call(
        functools.partial(page_kernel, slot_cap),
        out_shape=(
            jax.ShapeDtypeStruct((everyone, 24, LANES), BF16),
            jax.ShapeDtypeStruct((req_count, fresh_count * top, LANES), BF16),
        ),
        in_specs=[SMEM] * 3 + [VMEM] * 3,
        out_specs=(VMEM, VMEM),
        scratch_shapes=[
            pltpu.SMEM((req_count * slot_cap,), jnp.int32),
            pltpu.SMEM((req_count,), jnp.int32),
        ],
        compiler_params=params(12),
        cost_estimate=cost(2e9, 5e6),
        name="pages",
    )(pool_home, pool_page, prefix_len, split_pages, tail, first_all)
    arrived = lax.all_to_all(partial, ("req",) + whole, split_axis=0, concat_axis=0, tiled=True)

    mask = pl.pallas_call(
        functools.partial(names_kernel, part_rows, fresh_count),
        out_shape=jax.ShapeDtypeStruct((team * part_rows, expert_count), F32),
        in_specs=[VMEM],
        out_specs=VMEM,
        compiler_params=params(8),
        cost_estimate=cost(1e6, 1e6),
        name="names",
    )(named)
    first_raw, across, mask = lax.optimization_barrier((first_raw, across, mask))
    projects = [out_weight, beside]
    for block in across:
        projects += [block, lax.ppermute(block, whole, flips[1])]
    first = pl.pallas_call(
        prepare_kernel,
        out_shape=jax.ShapeDtypeStruct((local, model, 2 * LANES), BF16),
        in_specs=[HBM],
        out_specs=VMEM,
        scratch_shapes=[
            pltpu.VMEM(first_raw.shape, BF16),
            pltpu.VMEM((2, 2 * model, LANES), F32),
            pltpu.SemaphoreType.DMA((local,)),
        ],
        compiler_params=params(HOLD_MIB),
        cost_estimate=cost(2e9, 8e6),
        name="prepare",
    )(first_raw)
    arrived, projects = lax.optimization_barrier((arrived, projects))
    arrived, first, second_sent, mask = lax.optimization_barrier(
        (arrived, first, second_raw, mask)
    )
    first = pl.pallas_call(
        keep_kernel,
        out_shape=jax.ShapeDtypeStruct(first.shape, BF16),
        in_specs=[HBM],
        out_specs=HBM,
        input_output_aliases={0: 0},
        compiler_params=params(HOLD_MIB),
        name="keep",
    )(first)
    first_other = lax.ppermute(first, whole, flips[1])
    second_other = lax.ppermute(second_sent, whole, flips[1])

    message, residual = pl.pallas_call(
        merge_kernel,
        out_shape=(
            jax.ShapeDtypeStruct((team, 2 * part_rows, half), BF16),
            jax.ShapeDtypeStruct((part_rows, model), F32),
        ),
        in_specs=[VMEM] * (3 + parts),
        out_specs=(VMEM, VMEM),
        scratch_shapes=[pltpu.VMEM((parts, part_rows, model // parts), F32)],
        compiler_params=params(12),
        name="merge",
    )(arrived.reshape(req_count, parts, 24, LANES), flat, norm_gains, *projects)
    states = lax.all_to_all(message, ("req", "tp_pair"), split_axis=0, concat_axis=0, tiled=True)

    expert_inputs = (
        states,
        mask,
        router.T,
        first,
        first_other,
        second_raw,
        second_other,
    )
    mixed = pl.pallas_call(
        functools.partial(expert_kernel, copies, part_rows, min(req_count, 8) * pairs),
        out_shape=jax.ShapeDtypeStruct((team, 2 * part_rows, half), BF16),
        in_specs=[VMEM] * 7,
        out_specs=VMEM,
        compiler_params=params(16),
        name="experts",
    )(*expert_inputs)
    mixed = lax.all_to_all(mixed, ("req", "tp_pair"), split_axis=0, concat_axis=0, tiled=True)

    finished = pl.pallas_call(
        finish_kernel,
        out_shape=jax.ShapeDtypeStruct((2 * part_rows, half), BF16),
        in_specs=[VMEM, VMEM],
        out_specs=VMEM,
        compiler_params=params(8),
        name="finish",
    )(mixed, residual)
    gathered = [finished] + [
        lax.ppermute(finished, whole, flips[flip]) for flip in range(1, parts)
    ]

    layer, score = pl.pallas_call(
        functools.partial(score_kernel, fresh_count),
        out_shape=(
            jax.ShapeDtypeStruct((tokens * blocks, LANES), BF16),
            jax.ShapeDtypeStruct((fresh_count, samples), F32),
        ),
        in_specs=[VMEM] * (parts + 2),
        out_specs=(VMEM, VMEM),
        scratch_shapes=[
            pltpu.VMEM((blocks, tokens, LANES), F32),
            pltpu.VMEM((tokens * blocks, LANES), F32),
        ],
        compiler_params=params(8),
        name="score",
    )(*gathered, norm_gains, score_weight.reshape(1, model))
    layer = layer.reshape(samples, blocks, fresh_count, LANES).transpose(0, 2, 1, 3)
    return (
        layer.reshape(1, samples, fresh_count, model),
        score.T.reshape(1, samples, fresh_count),
    )


def solution(mesh):
    tp = ("tp_pair", "tp_side")
    req_count, parts = mesh.devices.shape
    mesh = jax.sharding.Mesh(
        mesh.devices.reshape(req_count, parts // 2, 2), ("req", "tp_pair", "tp_side")
    )
    placed = (
        P("req", None, None, None),
        P(),
        P("req", None),
        P(),
        P(),
        P("req", None, None, tp),
        P("req", None, None, None, tp),
        P("req", None, None, None),
        P(),
        P(None, tp),
        P(None, None, tp),
        P(tp, None),
        P(),
        P("req", None, None, tp),
        P("req", tp, None),
        P(),
    )
    return jax.shard_map(
        shards,
        mesh=mesh,
        in_specs=placed,
        out_specs=(P("req", None, None, None), P("req", None, None)),
        check_vma=False,
    )
```

```python
import functools
import math

import jax
import jax.numpy as jnp
from jax import lax
from jax.experimental import pallas as pl
from jax.experimental.pallas import tpu as pltpu
from jax.sharding import PartitionSpec as P

HEAD_DIM = 64
LANES = 128
EPSILON = 1e-05
ROPE_BASE = 10000.0
LOWEST = -1e30
FLOOR = -1e28
F32 = jnp.float32
BF16 = jnp.bfloat16
MIB = 1024 * 1024
HOLD_MIB = 56

VMEM = pl.BlockSpec(memory_space=pltpu.VMEM)
SMEM = pl.BlockSpec(memory_space=pltpu.SMEM)
HBM = pl.BlockSpec(memory_space=pltpu.HBM)
ANY = pl.BlockSpec(memory_space=pl.ANY)


def params(mib):
    return pltpu.CompilerParams(vmem_limit_bytes=mib * MIB)


def cost(flops, moved):
    return pl.CostEstimate(flops=int(flops), bytes_accessed=int(moved), transcendentals=0)


def dot(left, right):
    return jnp.dot(left, right, preferred_element_type=F32)


def dot_t(left, right):
    return lax.dot_general(left, right, (((1,), (1,)), ((), ())), preferred_element_type=F32)


def my_part():
    return lax.axis_index("tp_pair") * 2 + lax.axis_index("tp_side")


def load_all(pairs, done):
    copies = [pltpu.make_async_copy(far, near, done.at[k]) for k, (far, near) in enumerate(pairs)]
    for copy in copies:
        copy.start()
    return copies


def lane_iota(shape):
    return lax.broadcasted_iota(jnp.int32, shape, len(shape) - 1)


def normalize(x, gain):
    return x * lax.rsqrt(jnp.mean(x * x, axis=-1, keepdims=True) + EPSILON) * gain


def rotate(x, cosine, sine):
    lanes = lane_iota(x.shape)
    partner = jnp.where(lanes % HEAD_DIM < HEAD_DIM // 2, pltpu.roll(x, 96, 1), pltpu.roll(x, 32, 1))
    return x * cosine + partner * sine


def by_head(packed, low):
    zero = jnp.zeros_like(packed)
    return jnp.concatenate([jnp.where(low, packed, zero), jnp.where(low, zero, packed)], axis=0)


def swap_halves(first, second):
    low = lane_iota(first.shape) < HEAD_DIM
    return (
        jnp.where(low, first, pltpu.roll(second, HEAD_DIM, 1)),
        jnp.where(low, pltpu.roll(first, HEAD_DIM, 1), second),
    )


def query_kernel(
    fresh_count,
    prefix_far,
    lengths_far,
    tokens_far,
    named_far,
    gains_far,
    weight_far,
    message,
    flat,
    normed,
    cosine,
    sine,
    prefix,
    lengths,
    tokens,
    named,
    gains,
    weight,
    wide,
    ordered,
    done,
):
    loads = load_all(
        (
            (tokens_far, tokens),
            (gains_far, gains),
            (lengths_far, lengths),
            (prefix_far, prefix),
            (weight_far, weight),
            (named_far, named),
        ),
        done,
    )
    count, model = normed.shape
    samples = count // fresh_count
    parts, part_rows, _ = flat.shape
    blocks = model // LANES
    loads[0].wait()
    wide[...] = tokens[...].astype(F32)
    for c in range(blocks):
        for i in range(fresh_count):
            ordered[c, pl.ds(i, samples, stride=fresh_count), :] = wide[
                pl.ds(fresh_count * c + i, samples, stride=fresh_count * blocks), :
            ]
    states = jnp.concatenate([ordered[c] for c in range(blocks)], axis=1)
    for part in range(parts):
        flat[part] = states[part * part_rows : (part + 1) * part_rows].astype(BF16)
    loads[1].wait()
    rows = normalize(states, gains[0:1, :]).astype(BF16)
    normed[...] = rows
    loads[2].wait()
    loads[3].wait()
    row_id = lax.broadcasted_iota(jnp.int32, (count, 1), 0)
    position = row_id % fresh_count + prefix[lax.axis_index("req")]
    for sample in range(samples):
        position = position + jnp.where(row_id // fresh_count == sample, lengths[0, sample], 0)
    within = lane_iota((1, LANES)) % HEAD_DIM
    pair = (within % (HEAD_DIM // 2)).astype(F32)
    frequency = jnp.exp(pair * (-math.log(ROPE_BASE) / (HEAD_DIM // 2)))
    angles = position.astype(F32) * frequency
    cosine[...] = jnp.cos(angles)
    turn = jnp.sin(angles)
    sine[...] = jnp.where(within < HEAD_DIM // 2, -turn, turn)
    loads[4].wait()
    made = dot(rows, weight[...])
    pieces = []
    for group in swap_halves(made[:, :LANES], made[:, LANES:]):
        pieces.append(rotate(group, cosine[...], sine[...]).astype(BF16).astype(F32) * 0.125)
    packed = []
    for part in range(parts):
        for piece in pieces:
            packed.append(piece[part * part_rows : (part + 1) * part_rows])
    loads[5].wait()
    routed = named[...].astype(F32)
    packed.append(
        jnp.concatenate(
            [routed, jnp.zeros((routed.shape[0], LANES - routed.shape[1]), F32)], axis=1
        )
    )
    packed = jnp.concatenate(packed, axis=0).astype(BF16)
    for n in range(message.shape[0]):
        message[n] = packed


def split_pages_kernel(source, out, wide):
    count, double, _ = source.shape
    half = double // 2
    wide[...] = source[...].astype(F32).reshape(count * double, LANES)
    keys = wide[pl.ds(0, count * half, stride=2), :].astype(BF16)
    values = wide[pl.ds(1, count * half, stride=2), :].astype(BF16)
    out[:, :half, :] = keys.reshape(count, half, LANES)
    out[:, half:, :] = values.reshape(count, half, LANES)


def pack_message(numer, top, total):
    high = total.astype(BF16).astype(F32)
    section = (lane_iota((8, LANES)) % HEAD_DIM) // 8
    stats = jnp.zeros((8, LANES), F32)
    for group in range(2):
        span = slice(group * 8, (group + 1) * 8)
        for k, kind in enumerate((top, high, total - high)):
            stats = jnp.where(section == 3 * group + k, kind[span], stats)
    return jnp.concatenate([numer, stats], axis=0).astype(BF16)


def unpack_message(block):
    block = block.astype(F32)
    stats = block[..., 16:24, :]
    low = lane_iota(stats.shape) < HEAD_DIM

    def pick(section):
        lane = section * 8
        return jnp.where(
            low, stats[..., lane : lane + 1], stats[..., HEAD_DIM + lane : HEAD_DIM + lane + 1]
        )

    top = jnp.concatenate([pick(0), pick(3)], axis=-2)
    total = jnp.concatenate([pick(1) + pick(2), pick(4) + pick(5)], axis=-2)
    return block[..., 0:16, :], top, total


def tail_kernel(
    fresh_count,
    lengths_far,
    query_far,
    normed_far,
    cosine_far,
    sine_far,
    weight_far,
    cache_far,
    out,
    lengths,
    query,
    normed,
    cosine,
    sine,
    weight,
    cache,
    load,
    done,
):
    tokens = normed.shape[0]
    samples, width, _ = cache.shape
    parts = out.shape[0]
    per_part = samples // parts
    loads = load_all(
        (
            (normed_far, normed),
            (weight_far, weight),
            (cosine_far, cosine),
            (sine_far, sine),
            (query_far.at[0, pl.ds(0, parts * 16)], query),
            (lengths_far, lengths),
        ),
        load,
    )
    spans = [pl.ds(part * per_part, per_part) for part in range(parts)]
    blocks = load_all([(cache_far.at[span], cache.at[span]) for span in spans], done)
    spread = (
        lax.broadcasted_iota(jnp.int32, (LANES, 2 * LANES), 1)
        == 2 * lax.broadcasted_iota(jnp.int32, (LANES, 2 * LANES), 0)
    ).astype(BF16)
    loads[0].wait()
    rows = normed[...]
    widened = jnp.concatenate(
        [dot(rows[:, c : c + LANES], spread) for c in range(0, rows.shape[1], LANES)], axis=1
    )
    both = jnp.concatenate([widened, pltpu.roll(widened, 1, 1)], axis=0).astype(BF16)
    for copy in loads[1:]:
        copy.wait()
    made = dot(both, weight[...])
    key_new = rotate(made[:tokens], cosine[...], sine[...]).astype(BF16)
    value_new = made[tokens:].astype(BF16)
    low = lane_iota((16, LANES)) < HEAD_DIM
    row_id = lax.broadcasted_iota(jnp.int32, (32, 1), 0)
    row_sample = (row_id % 8) // fresh_count
    row_fresh = row_id % fresh_count
    column = lane_iota((32, width))
    even = column % 2 == 0
    token_id = lane_iota((32, tokens))
    for part in range(parts):
        if part % 2 == 0:
            for copy in blocks[part : part + 2]:
                copy.wait()
        wide = by_head(query[part * 16 : (part + 1) * 16, :], low)
        length = jnp.zeros((32, 1), jnp.int32)
        for a in range(per_part):
            length = jnp.where(row_sample == a, lengths[0, part * per_part + a], length)
        placed = [jnp.where(row_sample == a, wide, jnp.zeros_like(wide)) for a in range(per_part)]
        beside = jnp.concatenate([cache[part * per_part + a] for a in range(per_part)], axis=1)
        scores = dot_t(jnp.concatenate(placed, axis=1), beside)
        scores = jnp.where(even & (column < 2 * length), scores, LOWEST)
        fresh = dot_t(wide, key_new)
        own_sample = row_sample + part * per_part
        fresh_seen = (token_id // fresh_count == own_sample) & (token_id % fresh_count <= row_fresh)
        fresh = jnp.where(fresh_seen, fresh, LOWEST)
        peak = jnp.maximum(
            jnp.max(scores, axis=1, keepdims=True), jnp.max(fresh, axis=1, keepdims=True)
        )
        peak = peak.astype(BF16).astype(F32)
        weights = jnp.exp(scores - peak)
        fresh_weights = jnp.exp(fresh - peak)
        amount = jnp.sum(weights, axis=1, keepdims=True) + jnp.sum(
            fresh_weights, axis=1, keepdims=True
        )
        shifted = pltpu.roll(weights, 1, 1).astype(BF16)
        every = dot(shifted, beside)
        mixed = every[:, :LANES]
        for a in range(1, per_part):
            mixed = jnp.where(row_sample == a, every[:, a * LANES : (a + 1) * LANES], mixed)
        mixed = mixed + dot(fresh_weights.astype(BF16), value_new)
        out[part] = pack_message(
            jnp.where(low, mixed[:16], mixed[16:]),
            jnp.where(low, peak[:16], peak[16:]),
            jnp.where(low, amount[:16], amount[16:]),
        )


def page_kernel(
    slot_cap, homes, pages, lengths, cache, tail, query, out, named, slots, counts
):
    requests = query.shape[0]
    parts = tail.shape[0]
    pool = cache.shape[0]
    page_size = cache.shape[1] // 2
    rows = parts * 16
    me = lax.axis_index("req")
    base = me * pool
    tail_numer, tail_top, tail_total = [
        kind.reshape(rows, LANES) for kind in unpack_message(tail[...])
    ]
    named[...] = query[:, rows:, :]

    def clear(r, carry):
        counts[r] = 0
        for j in range(slot_cap):
            slots[r * slot_cap + j] = -1
        return carry

    lax.fori_loop(0, requests, clear, 0)

    def assign(v, carry):
        r = homes[base + v]
        rank = counts[r]
        slots[r * slot_cap + rank] = v
        counts[r] = rank + 1
        return carry

    lax.fori_loop(0, pool, assign, 0)

    low = lane_iota((rows, LANES)) < HEAD_DIM
    column = lane_iota((2 * rows, page_size))

    def finish(r, mixed, peak, amount):
        own = r == me
        top = jnp.where(low, peak[:rows], peak[rows:])
        joint = jnp.maximum(top, jnp.where(own, tail_top, FLOOR))
        here = jnp.exp(top - joint)
        there = jnp.where(own, jnp.exp(tail_top - joint), 0.0)
        numer = jnp.where(low, mixed[:rows], mixed[rows:]) * here + tail_numer * there
        total = jnp.where(low, amount[:rows], amount[rows:]) * here + tail_total * there
        for part in range(parts):
            span = slice(part * 16, (part + 1) * 16)
            out[r * parts + part] = pack_message(numer[span], joint[span], total[span])

    def several_requests(first, count):
        wides = []
        keys = []
        values = []
        limits = []
        for k in range(count):
            r = first + k
            wide = by_head(query[r, 0:rows, :], low)
            zero = jnp.zeros_like(wide)
            wides.append(jnp.concatenate([wide if c == k else zero for c in range(count)], axis=1))
            own_keys = []
            own_values = []
            own_limits = []
            for j in range(slot_cap):
                slot = slots[r * slot_cap + j]
                safe = jnp.maximum(slot, 0)
                own_limits.append(
                    jnp.where(slot >= 0, lengths[r] - pages[base + safe] * page_size, 0)
                )
                own_keys.append(cache[safe, :page_size, :])
                own_values.append(cache[safe, page_size:, :])
            keys.append(jnp.concatenate(own_keys, axis=0))
            values.append(jnp.concatenate(own_values, axis=0))
            limits.append(own_limits)
        scores = dot_t(jnp.concatenate(wides, axis=0), jnp.concatenate(keys, axis=1))
        all_weights = []
        stats = []
        for k in range(count):
            own = scores[k * 2 * rows : (k + 1) * 2 * rows]
            own = [
                jnp.where(
                    column < limits[k][j], own[:, j * page_size : (j + 1) * page_size], LOWEST
                )
                for j in range(slot_cap)
            ]
            peak = jnp.max(functools.reduce(jnp.maximum, own), axis=1, keepdims=True)
            peak = jnp.maximum(peak, FLOOR).astype(BF16).astype(F32)
            weights = [jnp.exp(one - peak) for one in own]
            amount = jnp.sum(functools.reduce(jnp.add, weights), axis=1, keepdims=True)
            all_weights.append(jnp.concatenate([one.astype(BF16) for one in weights], axis=1))
            stats.append((peak, amount))
        mixed = dot(jnp.concatenate(all_weights, axis=0), jnp.concatenate(values, axis=1))
        for k in range(count):
            finish(
                first + k,
                mixed[k * 2 * rows : (k + 1) * 2 * rows, k * LANES : (k + 1) * LANES],
                *stats[k],
            )

    pair = 2 if requests % 2 == 0 else 1
    step = 8 if requests % 8 == 0 else pair

    def several(g, carry):
        for k in range(0, step, pair):
            several_requests(g * step + k, pair)
        return carry

    if requests == step:
        several(0, 0)
    else:
        lax.fori_loop(0, requests // step, several, 0)


def merge_kernel(arrived, tokens, gains, *refs):
    parts = arrived.shape[1]
    weights = refs[:parts]
    out, residual, columns = refs[parts:]
    part = my_part()
    for t in range(parts):
        numer, top, total = unpack_message(arrived[:, t])
        factor = jnp.exp(top - jnp.max(top, axis=0, keepdims=True))
        attended = jnp.sum(factor * numer, axis=0) / jnp.sum(factor * total, axis=0)
        columns[t] = jnp.concatenate(swap_halves(attended[0:8], attended[8:16]), axis=1)
    projected = None
    for flip in range(parts):
        one = dot(columns[part ^ flip].astype(BF16), weights[flip][...])
        projected = one if projected is None else projected + one
    rows = (tokens[part].astype(F32) + projected).astype(BF16).astype(F32)
    residual[...] = rows
    normed = normalize(rows, gains[1:2, :])
    half = normed.shape[1] // 2
    message = jnp.concatenate([normed[:, :half], normed[:, half:]], axis=0).astype(BF16)
    for n in range(out.shape[0]):
        out[n] = message


def prepare_kernel(first_far, out, near, wide, done):
    local, double, _ = near.shape
    depth = double // 2
    loads = load_all([(first_far.at[e], near.at[e]) for e in range(local)], done)

    for e in range(local):
        loads[e].wait()
        buffer = wide.at[e % 2]
        buffer[...] = near[e].astype(F32)
        out[e, :, :LANES] = buffer[pl.ds(0, depth, stride=2), :].astype(BF16)
        out[e, :, LANES:] = buffer[pl.ds(1, depth, stride=2), :].astype(BF16)


def keep_kernel(*refs):
    del refs


def names_kernel(part_rows, fresh_count, packed, out):
    requests, span, _ = packed.shape
    experts = out.shape[1]
    halves = out.shape[0] // (requests * part_rows)
    top = span // fresh_count
    row = lax.broadcasted_iota(jnp.int32, (halves * part_rows, LANES), 0)
    token = (row // part_rows) * 2 * part_rows + lax.axis_index("tp_side") * part_rows + row % part_rows
    pick = (lane_iota(row.shape) == token // fresh_count).astype(BF16)
    found = jnp.concatenate([dot_t(pick, packed[r]) for r in range(requests)], axis=0)
    fresh = lax.broadcasted_iota(jnp.int32, (found.shape[0], 1), 0) % fresh_count
    chosen = found[:, :top]
    for i in range(1, fresh_count):
        chosen = jnp.where(fresh == i, found[:, i * top : (i + 1) * top], chosen)
    lanes = lane_iota(out.shape).astype(F32)
    mask = jnp.zeros(out.shape, F32)
    for k in range(top):
        mask = jnp.where(chosen[:, k : k + 1] == lanes, 1.0, mask)
    out[...] = mask


def expert_kernel(
    copies,
    part_rows,
    group,
    arrived,
    mask,
    router,
    first,
    first_other,
    second,
    second_other,
    out,
):
    team, _, half = arrived.shape
    local = first.shape[0]
    expert_count = router.shape[0]
    count = group * part_rows
    me = lax.axis_index("req")

    def one_block(block):
        here = pl.ds(block * group, group)
        states = arrived[here].astype(F32)
        states = jnp.concatenate(
            [
                states[:, :part_rows].reshape(count, half),
                states[:, part_rows:].reshape(count, half),
            ],
            axis=1,
        ).astype(BF16)
        logits = dot_t(states, router[...])
        span = pl.ds(pl.multiple_of(block * count, count), count)
        chosen = jnp.where(mask[span, :] > 0.5, logits, LOWEST)
        shares = jnp.exp(chosen - jnp.max(chosen, axis=1, keepdims=True))
        gates = shares / jnp.sum(shares, axis=1, keepdims=True)
        lanes = lane_iota(gates.shape)
        row = lax.broadcasted_iota(jnp.int32, (count, 1), 0)
        row_request = (block * group + row // part_rows) // 2
        weights = []
        for e in range(local):
            slot = me * local + e
            gate = jnp.sum(
                jnp.where(lanes == lax.rem(slot, expert_count), gates, 0.0), axis=1, keepdims=True
            )
            if copies > 1:
                copy = lax.div(slot, expert_count)
                gate = jnp.where(lax.rem(row_request, copies) == copy, gate, 0.0)
            weights.append(gate)
        mixed = None
        for up, down in ((first, second), (first_other, second_other)):
            pieces = []
            for e in range(local):
                wide = dot(states, up[e])
                value = wide[:, :LANES]
                other = wide[:, LANES:]
                hidden = (value / (1.0 + jnp.exp(-value)) * other).astype(BF16).astype(F32)
                pieces.append((hidden * weights[e]).astype(BF16))
            part = dot(jnp.concatenate(pieces, axis=1), down[...])
            mixed = part if mixed is None else mixed + part
        out[here] = jnp.concatenate(
            [
                mixed[:, :half].reshape(group, part_rows, half),
                mixed[:, half:].reshape(group, part_rows, half),
            ],
            axis=1,
        ).astype(BF16)

    if team == group:
        one_block(0)
    else:

        def body(block, carry):
            one_block(block)
            return carry

        lax.fori_loop(0, team // group, body, 0)


def finish_kernel(arrived, residual, out):
    pairs = arrived.shape[1]
    half = arrived.shape[3]
    kept = residual[...]
    kept = jnp.concatenate([kept[:, :half], kept[:, half:]], axis=0)
    mine = lax.axis_index("tp_pair")
    for pair in range(pairs):
        mixed = jnp.sum(arrived[:, pair].astype(F32), axis=0)
        out[pair] = (mixed + jnp.where(mine == pair, kept, 0.0)).astype(BF16)


def score_kernel(fresh_count, *refs):
    *arrived, gains, weight, layer, score, ordered, wide = refs
    pairs, double, _ = arrived[0].shape
    rows = double // 2
    blocks, tokens, _ = ordered.shape
    samples = tokens // fresh_count
    side = lax.axis_index("tp_side")
    for flip in range(2):
        for pair in range(pairs):
            state = arrived[flip][pair].astype(F32)
            for other in range(flip + 2, len(arrived), 2):
                state = state + arrived[other][pair].astype(F32)
            spot = pl.ds(pl.multiple_of((2 * pair + (side ^ flip)) * rows, rows), rows)
            for c in range(blocks // 2):
                ordered[c, spot, :] = state[:rows, c * LANES : (c + 1) * LANES]
                ordered[blocks // 2 + c, spot, :] = state[rows:, c * LANES : (c + 1) * LANES]
    for c in range(blocks):
        for i in range(fresh_count):
            wide[pl.ds(fresh_count * c + i, samples, stride=fresh_count * blocks), :] = ordered[
                c, pl.ds(i, samples, stride=fresh_count), :
            ]
    layer[...] = wide[...].astype(BF16)
    states = jnp.concatenate([ordered[c] for c in range(blocks)], axis=1)
    states = states.astype(BF16).astype(F32)
    final = normalize(states, gains[2:3, :])
    scored = jnp.sum(final * weight[...], axis=1, keepdims=True)
    row = lax.broadcasted_iota(jnp.int32, (tokens, samples), 0)
    here = row // fresh_count == lane_iota(row.shape)
    for i in range(fresh_count):
        score[i : i + 1, :] = jnp.sum(
            jnp.where(here & (row % fresh_count == i), scored, 0.0), axis=0, keepdims=True
        )


def shards(
    tokens_new,
    prefix_len,
    tail_len,
    pool_home,
    pool_page,
    slot_page_cache,
    tail_cache,
    routes,
    norm_gains,
    query_weight,
    key_value_weight,
    out_weight,
    router,
    expert_in,
    expert_out,
    score_weight,
):
    req_count = lax.axis_size("req")
    pairs = lax.axis_size("tp_pair")
    parts = 2 * pairs
    _, samples, fresh_count, model = tokens_new.shape
    tokens = samples * fresh_count
    part_rows = tokens // parts
    pool = slot_page_cache.shape[0]
    page_size = slot_page_cache.shape[1]
    slot_cap = max(1, pool // req_count)
    tail_count = tail_cache.shape[2]
    local = expert_in.shape[0]
    expert_count = router.shape[1]
    copies = local * req_count // expert_count
    everyone = req_count * parts
    rows = 2 * tokens
    blocks = model // LANES
    top = routes.shape[3]
    half = model // 2
    team = req_count * pairs

    whole = ("tp_pair", "tp_side")
    flips = [[(t, t ^ flip) for t in range(parts)] for flip in range(parts)]
    first_raw = expert_in.reshape(local, 2 * model, LANES)
    second_raw = expert_out.reshape(local * LANES, model)


    token_bytes = tokens_new.reshape(samples, fresh_count, blocks, LANES)
    token_bytes = token_bytes.transpose(0, 2, 1, 3).reshape(tokens * blocks, LANES)
    route_bytes = routes[0].transpose(1, 2, 0).reshape(fresh_count * top, samples)

    message, flat, normed, cosine, sine = pl.pallas_call(
        functools.partial(query_kernel, fresh_count),
        out_shape=(
            jax.ShapeDtypeStruct((req_count, rows + fresh_count * top, LANES), BF16),
            jax.ShapeDtypeStruct((parts, part_rows, model), BF16),
            jax.ShapeDtypeStruct((tokens, model), BF16),
            jax.ShapeDtypeStruct((tokens, LANES), F32),
            jax.ShapeDtypeStruct((tokens, LANES), F32),
        ),
        in_specs=[HBM] * 6,
        out_specs=(VMEM,) * 5,
        scratch_shapes=[
            pltpu.SMEM(prefix_len.shape, jnp.int32),
            pltpu.SMEM(tail_len.shape, jnp.int32),
            pltpu.VMEM(token_bytes.shape, BF16),
            pltpu.VMEM(route_bytes.shape, jnp.int32),
            pltpu.VMEM(norm_gains.shape, F32),
            pltpu.VMEM(query_weight.shape, BF16),
            pltpu.VMEM((tokens * blocks, LANES), F32),
            pltpu.VMEM((blocks, tokens, LANES), F32),
            pltpu.SemaphoreType.DMA((6,)),
        ],
        compiler_params=params(HOLD_MIB),
        name="query",
    )(prefix_len, tail_len, token_bytes, route_bytes, norm_gains, query_weight)

    key_value_rows = key_value_weight.reshape(2 * model, LANES)
    tail_rows = tail_cache.reshape(samples, 2 * tail_count, LANES)
    tail_inputs = (message, normed, cosine, sine)
    tail = pl.pallas_call(
        functools.partial(tail_kernel, fresh_count),
        out_shape=jax.ShapeDtypeStruct((parts, 24, LANES), BF16),
        in_specs=[HBM] * 7,
        out_specs=VMEM,
        scratch_shapes=[
            pltpu.SMEM(tail_len.shape, jnp.int32),
            pltpu.VMEM((rows, LANES), BF16),
            pltpu.VMEM(normed.shape, BF16),
            pltpu.VMEM(cosine.shape, F32),
            pltpu.VMEM(sine.shape, F32),
            pltpu.VMEM(key_value_rows.shape, BF16),
            pltpu.VMEM(tail_rows.shape, BF16),
            pltpu.SemaphoreType.DMA((6,)),
            pltpu.SemaphoreType.DMA((parts,)),
        ],
        compiler_params=params(HOLD_MIB),
        cost_estimate=cost(2e9, 5e6),
        name="tail",
    )(tail_len, *tail_inputs, key_value_rows, tail_rows)

    page_rows = slot_page_cache.reshape(pool, 2 * page_size, LANES)
    later, message = lax.optimization_barrier((out_weight, message))
    across = [lax.ppermute(later, whole, flips[flip]) for flip in range(2, parts, 2)]
    beside = lax.ppermute(later, whole, flips[1])
    first_all = lax.all_to_all(message, "req", split_axis=0, concat_axis=0, tiled=True)
    page_rows, tail, beside = lax.optimization_barrier((page_rows, tail, beside))

    step = 8 if pool % 8 == 0 else 1
    split_pages = pl.pallas_call(
        split_pages_kernel,
        grid=(pool // step,),
        out_shape=jax.ShapeDtypeStruct((pool, 2 * page_size, LANES), BF16),
        in_specs=[pl.BlockSpec((step, 2 * page_size, LANES), lambda v: (v, 0, 0))],
        out_specs=pl.BlockSpec((step, 2 * page_size, LANES), lambda v: (v, 0, 0)),
        scratch_shapes=[pltpu.VMEM((step * 2 * page_size, LANES), F32)],
        compiler_params=params(8),
        cost_estimate=cost(1e6, 4e6),
        name="split_pages",
    )(page_rows)

    partial, named = pl.pallas_call(
        functools.partial(page_kernel, slot_cap),
        out_shape=(
            jax.ShapeDtypeStruct((everyone, 24, LANES), BF16),
            jax.ShapeDtypeStruct((req_count, fresh_count * top, LANES), BF16),
        ),
        in_specs=[SMEM] * 3 + [VMEM] * 3,
        out_specs=(VMEM, VMEM),
        scratch_shapes=[
            pltpu.SMEM((req_count * slot_cap,), jnp.int32),
            pltpu.SMEM((req_count,), jnp.int32),
        ],
        compiler_params=params(12),
        cost_estimate=cost(2e9, 5e6),
        name="pages",
    )(pool_home, pool_page, prefix_len, split_pages, tail, first_all)
    arrived = lax.all_to_all(partial, ("req",) + whole, split_axis=0, concat_axis=0, tiled=True)

    first_raw, _ = lax.optimization_barrier((first_raw, partial))
    first = pl.pallas_call(
        prepare_kernel,
        out_shape=jax.ShapeDtypeStruct((local, model, 2 * LANES), BF16),
        in_specs=[HBM],
        out_specs=VMEM,
        scratch_shapes=[
            pltpu.VMEM(first_raw.shape, BF16),
            pltpu.VMEM((2, 2 * model, LANES), F32),
            pltpu.SemaphoreType.DMA((local,)),
        ],
        compiler_params=params(HOLD_MIB),
        cost_estimate=cost(2e9, 8e6),
        name="prepare",
    )(first_raw)
    named, first, across, second_sent = lax.optimization_barrier(
        (named, first, across, second_raw)
    )
    projects = [out_weight, beside]
    for block in across:
        projects += [block, lax.ppermute(block, whole, flips[1])]
    second_other = lax.ppermute(second_sent, whole, flips[1])
    mask = pl.pallas_call(
        functools.partial(names_kernel, part_rows, fresh_count),
        out_shape=jax.ShapeDtypeStruct((team * part_rows, expert_count), F32),
        in_specs=[VMEM],
        out_specs=VMEM,
        compiler_params=params(8),
        cost_estimate=cost(1e6, 1e6),
        name="names",
    )(named)
    arrived, first, projects, second_other, mask = lax.optimization_barrier(
        (arrived, first, projects, second_other, mask)
    )
    first = pl.pallas_call(
        keep_kernel,
        out_shape=jax.ShapeDtypeStruct(first.shape, BF16),
        in_specs=[HBM],
        out_specs=HBM,
        input_output_aliases={0: 0},
        compiler_params=params(HOLD_MIB),
        name="keep",
    )(first)
    first_other = lax.ppermute(first, whole, flips[1])

    message, residual = pl.pallas_call(
        merge_kernel,
        out_shape=(
            jax.ShapeDtypeStruct((team, 2 * part_rows, half), BF16),
            jax.ShapeDtypeStruct((part_rows, model), F32),
        ),
        in_specs=[VMEM] * (3 + parts),
        out_specs=(VMEM, VMEM),
        scratch_shapes=[pltpu.VMEM((parts, part_rows, model // parts), F32)],
        compiler_params=params(12),
        name="merge",
    )(arrived.reshape(req_count, parts, 24, LANES), flat, norm_gains, *projects)
    states = lax.all_to_all(message, ("req", "tp_pair"), split_axis=0, concat_axis=0, tiled=True)

    expert_inputs = (
        states,
        mask,
        router.T,
        first,
        first_other,
        second_raw,
        second_other,
    )
    mixed = pl.pallas_call(
        functools.partial(expert_kernel, copies, part_rows, min(req_count, 8) * pairs),
        out_shape=jax.ShapeDtypeStruct((team, 2 * part_rows, half), BF16),
        in_specs=[VMEM] * 7,
        out_specs=VMEM,
        compiler_params=params(16),
        name="experts",
    )(*expert_inputs)
    mixed = mixed.reshape(req_count, pairs, 2 * part_rows, half)
    mixed = lax.all_to_all(mixed, "req", split_axis=0, concat_axis=0, tiled=True)

    finished = pl.pallas_call(
        finish_kernel,
        out_shape=jax.ShapeDtypeStruct((pairs, 2 * part_rows, half), BF16),
        in_specs=[VMEM, VMEM],
        out_specs=VMEM,
        compiler_params=params(8),
        name="finish",
    )(mixed, residual)
    gathered = [finished] + [
        lax.ppermute(finished, whole, flips[flip]) for flip in range(1, parts)
    ]

    layer, score = pl.pallas_call(
        functools.partial(score_kernel, fresh_count),
        out_shape=(
            jax.ShapeDtypeStruct((tokens * blocks, LANES), BF16),
            jax.ShapeDtypeStruct((fresh_count, samples), F32),
        ),
        in_specs=[VMEM] * (parts + 2),
        out_specs=(VMEM, VMEM),
        scratch_shapes=[
            pltpu.VMEM((blocks, tokens, LANES), F32),
            pltpu.VMEM((tokens * blocks, LANES), F32),
        ],
        compiler_params=params(8),
        name="score",
    )(*gathered, norm_gains, score_weight.reshape(1, model))
    layer = layer.reshape(samples, blocks, fresh_count, LANES).transpose(0, 2, 1, 3)
    return (
        layer.reshape(1, samples, fresh_count, model),
        score.T.reshape(1, samples, fresh_count),
    )


def solution(mesh):
    tp = ("tp_pair", "tp_side")
    req_count, parts = mesh.devices.shape
    mesh = jax.sharding.Mesh(
        mesh.devices.reshape(req_count, parts // 2, 2), ("req", "tp_pair", "tp_side")
    )
    placed = (
        P("req", None, None, None),
        P(),
        P("req", None),
        P(),
        P(),
        P("req", None, None, tp),
        P("req", None, None, None, tp),
        P("req", None, None, None),
        P(),
        P(None, tp),
        P(None, None, tp),
        P(tp, None),
        P(),
        P("req", None, None, tp),
        P("req", tp, None),
        P(),
    )
    return jax.shard_map(
        shards,
        mesh=mesh,
        in_specs=placed,
        out_specs=(P("req", None, None, None), P("req", None, None)),
        check_vma=False,
    )
```

```python
import functools
import math

import jax
import jax.numpy as jnp
from jax import lax
from jax.experimental import pallas as pl
from jax.experimental.pallas import tpu as pltpu
from jax.sharding import PartitionSpec as P

HEAD_DIM = 64
LANES = 128
EPSILON = 1e-05
ROPE_BASE = 10000.0
LOWEST = -1e30
FLOOR = -1e28
F32 = jnp.float32
BF16 = jnp.bfloat16
MIB = 1024 * 1024
HOLD_MIB = 56

VMEM = pl.BlockSpec(memory_space=pltpu.VMEM)
SMEM = pl.BlockSpec(memory_space=pltpu.SMEM)
HBM = pl.BlockSpec(memory_space=pltpu.HBM)
ANY = pl.BlockSpec(memory_space=pl.ANY)


def params(mib):
    return pltpu.CompilerParams(vmem_limit_bytes=mib * MIB)


def cost(flops, moved):
    return pl.CostEstimate(flops=int(flops), bytes_accessed=int(moved), transcendentals=0)


def dot(left, right):
    return jnp.dot(left, right, preferred_element_type=F32)


def dot_t(left, right):
    return lax.dot_general(left, right, (((1,), (1,)), ((), ())), preferred_element_type=F32)


def my_part():
    return lax.axis_index("tp_pair") * 2 + lax.axis_index("tp_side")


def load_all(pairs, done):
    copies = [pltpu.make_async_copy(far, near, done.at[k]) for k, (far, near) in enumerate(pairs)]
    for copy in copies:
        copy.start()
    return copies


def lane_iota(shape):
    return lax.broadcasted_iota(jnp.int32, shape, len(shape) - 1)


def normalize(x, gain):
    return x * lax.rsqrt(jnp.mean(x * x, axis=-1, keepdims=True) + EPSILON) * gain


def rotate(x, cosine, sine):
    lanes = lane_iota(x.shape)
    partner = jnp.where(lanes % HEAD_DIM < HEAD_DIM // 2, pltpu.roll(x, 96, 1), pltpu.roll(x, 32, 1))
    return x * cosine + partner * sine


def by_head(packed, low):
    zero = jnp.zeros_like(packed)
    return jnp.concatenate([jnp.where(low, packed, zero), jnp.where(low, zero, packed)], axis=0)


def swap_halves(first, second):
    low = lane_iota(first.shape) < HEAD_DIM
    return (
        jnp.where(low, first, pltpu.roll(second, HEAD_DIM, 1)),
        jnp.where(low, pltpu.roll(first, HEAD_DIM, 1), second),
    )


def query_kernel(
    fresh_count,
    prefix_far,
    lengths_far,
    tokens_far,
    named_far,
    gains_far,
    weight_far,
    message,
    flat,
    normed,
    cosine,
    sine,
    prefix,
    lengths,
    tokens,
    named,
    gains,
    weight,
    wide,
    ordered,
    done,
):
    loads = load_all(
        (
            (tokens_far, tokens),
            (gains_far, gains),
            (lengths_far, lengths),
            (prefix_far, prefix),
            (weight_far, weight),
            (named_far, named),
        ),
        done,
    )
    count, model = normed.shape
    samples = count // fresh_count
    parts, part_rows, _ = flat.shape
    blocks = model // LANES
    loads[0].wait()
    wide[...] = tokens[...].astype(F32)
    for c in range(blocks):
        for i in range(fresh_count):
            ordered[c, pl.ds(i, samples, stride=fresh_count), :] = wide[
                pl.ds(fresh_count * c + i, samples, stride=fresh_count * blocks), :
            ]
    states = jnp.concatenate([ordered[c] for c in range(blocks)], axis=1)
    for part in range(parts):
        flat[part] = states[part * part_rows : (part + 1) * part_rows].astype(BF16)
    loads[1].wait()
    rows = normalize(states, gains[0:1, :]).astype(BF16)
    normed[...] = rows
    loads[2].wait()
    loads[3].wait()
    row_id = lax.broadcasted_iota(jnp.int32, (count, 1), 0)
    position = row_id % fresh_count + prefix[lax.axis_index("req")]
    for sample in range(samples):
        position = position + jnp.where(row_id // fresh_count == sample, lengths[0, sample], 0)
    within = lane_iota((1, LANES)) % HEAD_DIM
    pair = (within % (HEAD_DIM // 2)).astype(F32)
    frequency = jnp.exp(pair * (-math.log(ROPE_BASE) / (HEAD_DIM // 2)))
    angles = position.astype(F32) * frequency
    cosine[...] = jnp.cos(angles)
    turn = jnp.sin(angles)
    sine[...] = jnp.where(within < HEAD_DIM // 2, -turn, turn)
    loads[4].wait()
    made = dot(rows, weight[...])
    pieces = []
    for group in swap_halves(made[:, :LANES], made[:, LANES:]):
        pieces.append(rotate(group, cosine[...], sine[...]).astype(BF16).astype(F32) * 0.125)
    packed = []
    for part in range(parts):
        for piece in pieces:
            packed.append(piece[part * part_rows : (part + 1) * part_rows])
    loads[5].wait()
    routed = named[...].astype(F32)
    packed.append(
        jnp.concatenate(
            [routed, jnp.zeros((routed.shape[0], LANES - routed.shape[1]), F32)], axis=1
        )
    )
    packed = jnp.concatenate(packed, axis=0).astype(BF16)
    for n in range(message.shape[0]):
        message[n] = packed


def split_pages_kernel(source, out, wide):
    count, double, _ = source.shape
    half = double // 2
    wide[...] = source[...].astype(F32).reshape(count * double, LANES)
    keys = wide[pl.ds(0, count * half, stride=2), :].astype(BF16)
    values = wide[pl.ds(1, count * half, stride=2), :].astype(BF16)
    out[:, :half, :] = keys.reshape(count, half, LANES)
    out[:, half:, :] = values.reshape(count, half, LANES)


def pack_message(numer, top, total):
    high = total.astype(BF16).astype(F32)
    section = (lane_iota((8, LANES)) % HEAD_DIM) // 8
    stats = jnp.zeros((8, LANES), F32)
    for group in range(2):
        span = slice(group * 8, (group + 1) * 8)
        for k, kind in enumerate((top, high, total - high)):
            stats = jnp.where(section == 3 * group + k, kind[span], stats)
    return jnp.concatenate([numer, stats], axis=0).astype(BF16)


def unpack_message(block):
    block = block.astype(F32)
    stats = block[..., 16:24, :]
    low = lane_iota(stats.shape) < HEAD_DIM

    def pick(section):
        lane = section * 8
        return jnp.where(
            low, stats[..., lane : lane + 1], stats[..., HEAD_DIM + lane : HEAD_DIM + lane + 1]
        )

    top = jnp.concatenate([pick(0), pick(3)], axis=-2)
    total = jnp.concatenate([pick(1) + pick(2), pick(4) + pick(5)], axis=-2)
    return block[..., 0:16, :], top, total


def tail_kernel(
    fresh_count,
    lengths_far,
    query_far,
    normed_far,
    cosine_far,
    sine_far,
    weight_far,
    cache_far,
    out,
    lengths,
    query,
    normed,
    cosine,
    sine,
    weight,
    cache,
    load,
    done,
):
    tokens = normed.shape[0]
    samples, width, _ = cache.shape
    parts = out.shape[0]
    per_part = samples // parts
    loads = load_all(
        (
            (normed_far, normed),
            (weight_far, weight),
            (cosine_far, cosine),
            (sine_far, sine),
            (query_far.at[0, pl.ds(0, parts * 16)], query),
            (lengths_far, lengths),
        ),
        load,
    )
    spans = [pl.ds(part * per_part, per_part) for part in range(parts)]
    blocks = load_all([(cache_far.at[span], cache.at[span]) for span in spans], done)
    spread = (
        lax.broadcasted_iota(jnp.int32, (LANES, 2 * LANES), 1)
        == 2 * lax.broadcasted_iota(jnp.int32, (LANES, 2 * LANES), 0)
    ).astype(BF16)
    loads[0].wait()
    rows = normed[...]
    widened = jnp.concatenate(
        [dot(rows[:, c : c + LANES], spread) for c in range(0, rows.shape[1], LANES)], axis=1
    )
    both = jnp.concatenate([widened, pltpu.roll(widened, 1, 1)], axis=0).astype(BF16)
    for copy in loads[1:]:
        copy.wait()
    made = dot(both, weight[...])
    key_new = rotate(made[:tokens], cosine[...], sine[...]).astype(BF16)
    value_new = made[tokens:].astype(BF16)
    low = lane_iota((16, LANES)) < HEAD_DIM
    row_id = lax.broadcasted_iota(jnp.int32, (32, 1), 0)
    row_sample = (row_id % 8) // fresh_count
    row_fresh = row_id % fresh_count
    column = lane_iota((32, width))
    even = column % 2 == 0
    token_id = lane_iota((32, tokens))
    for part in range(parts):
        if part % 2 == 0:
            for copy in blocks[part : part + 2]:
                copy.wait()
        wide = by_head(query[part * 16 : (part + 1) * 16, :], low)
        length = jnp.zeros((32, 1), jnp.int32)
        for a in range(per_part):
            length = jnp.where(row_sample == a, lengths[0, part * per_part + a], length)
        placed = [jnp.where(row_sample == a, wide, jnp.zeros_like(wide)) for a in range(per_part)]
        beside = jnp.concatenate([cache[part * per_part + a] for a in range(per_part)], axis=1)
        scores = dot_t(jnp.concatenate(placed, axis=1), beside)
        scores = jnp.where(even & (column < 2 * length), scores, LOWEST)
        fresh = dot_t(wide, key_new)
        own_sample = row_sample + part * per_part
        fresh_seen = (token_id // fresh_count == own_sample) & (token_id % fresh_count <= row_fresh)
        fresh = jnp.where(fresh_seen, fresh, LOWEST)
        peak = jnp.maximum(
            jnp.max(scores, axis=1, keepdims=True), jnp.max(fresh, axis=1, keepdims=True)
        )
        peak = peak.astype(BF16).astype(F32)
        weights = jnp.exp(scores - peak)
        fresh_weights = jnp.exp(fresh - peak)
        amount = jnp.sum(weights, axis=1, keepdims=True) + jnp.sum(
            fresh_weights, axis=1, keepdims=True
        )
        shifted = pltpu.roll(weights, 1, 1).astype(BF16)
        every = dot(shifted, beside)
        mixed = every[:, :LANES]
        for a in range(1, per_part):
            mixed = jnp.where(row_sample == a, every[:, a * LANES : (a + 1) * LANES], mixed)
        mixed = mixed + dot(fresh_weights.astype(BF16), value_new)
        out[part] = pack_message(
            jnp.where(low, mixed[:16], mixed[16:]),
            jnp.where(low, peak[:16], peak[16:]),
            jnp.where(low, amount[:16], amount[16:]),
        )


def page_kernel(
    slot_cap, homes, pages, lengths, cache, tail, query, out, named, slots, counts
):
    requests = query.shape[0]
    parts = tail.shape[0]
    pool = cache.shape[0]
    page_size = cache.shape[1] // 2
    rows = parts * 16
    me = lax.axis_index("req")
    base = me * pool
    tail_numer, tail_top, tail_total = [
        kind.reshape(rows, LANES) for kind in unpack_message(tail[...])
    ]
    named[...] = query[:, rows:, :]

    def clear(r, carry):
        counts[r] = 0
        for j in range(slot_cap):
            slots[r * slot_cap + j] = -1
        return carry

    lax.fori_loop(0, requests, clear, 0)

    def assign(v, carry):
        r = homes[base + v]
        rank = counts[r]
        slots[r * slot_cap + rank] = v
        counts[r] = rank + 1
        return carry

    lax.fori_loop(0, pool, assign, 0)

    low = lane_iota((rows, LANES)) < HEAD_DIM
    column = lane_iota((2 * rows, page_size))

    def finish(r, mixed, peak, amount):
        own = r == me
        top = jnp.where(low, peak[:rows], peak[rows:])
        joint = jnp.maximum(top, jnp.where(own, tail_top, FLOOR))
        here = jnp.exp(top - joint)
        there = jnp.where(own, jnp.exp(tail_top - joint), 0.0)
        numer = jnp.where(low, mixed[:rows], mixed[rows:]) * here + tail_numer * there
        total = jnp.where(low, amount[:rows], amount[rows:]) * here + tail_total * there
        for part in range(parts):
            span = slice(part * 16, (part + 1) * 16)
            out[r * parts + part] = pack_message(numer[span], joint[span], total[span])

    def several_requests(first, count):
        wides = []
        keys = []
        values = []
        limits = []
        for k in range(count):
            r = first + k
            wide = by_head(query[r, 0:rows, :], low)
            zero = jnp.zeros_like(wide)
            wides.append(jnp.concatenate([wide if c == k else zero for c in range(count)], axis=1))
            own_keys = []
            own_values = []
            own_limits = []
            for j in range(slot_cap):
                slot = slots[r * slot_cap + j]
                safe = jnp.maximum(slot, 0)
                own_limits.append(
                    jnp.where(slot >= 0, lengths[r] - pages[base + safe] * page_size, 0)
                )
                own_keys.append(cache[safe, :page_size, :])
                own_values.append(cache[safe, page_size:, :])
            keys.append(jnp.concatenate(own_keys, axis=0))
            values.append(jnp.concatenate(own_values, axis=0))
            limits.append(own_limits)
        scores = dot_t(jnp.concatenate(wides, axis=0), jnp.concatenate(keys, axis=1))
        all_weights = []
        stats = []
        for k in range(count):
            own = scores[k * 2 * rows : (k + 1) * 2 * rows]
            own = [
                jnp.where(
                    column < limits[k][j], own[:, j * page_size : (j + 1) * page_size], LOWEST
                )
                for j in range(slot_cap)
            ]
            peak = jnp.max(functools.reduce(jnp.maximum, own), axis=1, keepdims=True)
            peak = jnp.maximum(peak, FLOOR).astype(BF16).astype(F32)
            weights = [jnp.exp(one - peak) for one in own]
            amount = jnp.sum(functools.reduce(jnp.add, weights), axis=1, keepdims=True)
            all_weights.append(jnp.concatenate([one.astype(BF16) for one in weights], axis=1))
            stats.append((peak, amount))
        mixed = dot(jnp.concatenate(all_weights, axis=0), jnp.concatenate(values, axis=1))
        for k in range(count):
            finish(
                first + k,
                mixed[k * 2 * rows : (k + 1) * 2 * rows, k * LANES : (k + 1) * LANES],
                *stats[k],
            )

    pair = 2 if requests % 2 == 0 else 1
    step = 8 if requests % 8 == 0 else pair

    def several(g, carry):
        for k in range(0, step, pair):
            several_requests(g * step + k, pair)
        return carry

    if requests == step:
        several(0, 0)
    else:
        lax.fori_loop(0, requests // step, several, 0)


def merge_kernel(arrived, tokens, gains, *refs):
    parts = arrived.shape[1]
    weights = refs[:parts]
    out, residual, columns = refs[parts:]
    part = my_part()
    for t in range(parts):
        numer, top, total = unpack_message(arrived[:, t])
        factor = jnp.exp(top - jnp.max(top, axis=0, keepdims=True))
        attended = jnp.sum(factor * numer, axis=0) / jnp.sum(factor * total, axis=0)
        columns[t] = jnp.concatenate(swap_halves(attended[0:8], attended[8:16]), axis=1)
    projected = None
    for flip in range(parts):
        one = dot(columns[part ^ flip].astype(BF16), weights[flip][...])
        projected = one if projected is None else projected + one
    rows = (tokens[part].astype(F32) + projected).astype(BF16).astype(F32)
    residual[...] = rows
    normed = normalize(rows, gains[1:2, :])
    half = normed.shape[1] // 2
    message = jnp.concatenate([normed[:, :half], normed[:, half:]], axis=0).astype(BF16)
    for n in range(out.shape[0]):
        out[n] = message


def prepare_kernel(first_far, out, near, wide, done):
    local, double, _ = near.shape
    depth = double // 2
    loads = load_all([(first_far.at[e], near.at[e]) for e in range(local)], done)

    for e in range(local):
        loads[e].wait()
        buffer = wide.at[e % 2]
        buffer[...] = near[e].astype(F32)
        out[e, :, :LANES] = buffer[pl.ds(0, depth, stride=2), :].astype(BF16)
        out[e, :, LANES:] = buffer[pl.ds(1, depth, stride=2), :].astype(BF16)


def keep_kernel(*refs):
    del refs


def names_kernel(part_rows, fresh_count, packed, out):
    requests, span, _ = packed.shape
    experts = out.shape[1]
    halves = out.shape[0] // (requests * part_rows)
    top = span // fresh_count
    row = lax.broadcasted_iota(jnp.int32, (halves * part_rows, LANES), 0)
    token = (row // part_rows) * 2 * part_rows + lax.axis_index("tp_side") * part_rows + row % part_rows
    pick = (lane_iota(row.shape) == token // fresh_count).astype(BF16)
    found = jnp.concatenate([dot_t(pick, packed[r]) for r in range(requests)], axis=0)
    fresh = lax.broadcasted_iota(jnp.int32, (found.shape[0], 1), 0) % fresh_count
    chosen = found[:, :top]
    for i in range(1, fresh_count):
        chosen = jnp.where(fresh == i, found[:, i * top : (i + 1) * top], chosen)
    lanes = lane_iota(out.shape).astype(F32)
    mask = jnp.zeros(out.shape, F32)
    for k in range(top):
        mask = jnp.where(chosen[:, k : k + 1] == lanes, 1.0, mask)
    out[...] = mask


def expert_kernel(
    copies,
    part_rows,
    group,
    arrived,
    mask,
    router,
    first,
    first_other,
    second,
    second_other,
    out,
):
    team, _, half = arrived.shape
    local = first.shape[0]
    expert_count = router.shape[0]
    count = group * part_rows
    me = lax.axis_index("req")

    def one_block(block):
        here = pl.ds(block * group, group)
        states = arrived[here].astype(F32)
        states = jnp.concatenate(
            [
                states[:, :part_rows].reshape(count, half),
                states[:, part_rows:].reshape(count, half),
            ],
            axis=1,
        ).astype(BF16)
        logits = dot_t(states, router[...])
        span = pl.ds(pl.multiple_of(block * count, count), count)
        chosen = jnp.where(mask[span, :] > 0.5, logits, LOWEST)
        shares = jnp.exp(chosen - jnp.max(chosen, axis=1, keepdims=True))
        gates = shares / jnp.sum(shares, axis=1, keepdims=True)
        lanes = lane_iota(gates.shape)
        row = lax.broadcasted_iota(jnp.int32, (count, 1), 0)
        row_request = (block * group + row // part_rows) // 2
        weights = []
        for e in range(local):
            slot = me * local + e
            gate = jnp.sum(
                jnp.where(lanes == lax.rem(slot, expert_count), gates, 0.0), axis=1, keepdims=True
            )
            if copies > 1:
                copy = lax.div(slot, expert_count)
                gate = jnp.where(lax.rem(row_request, copies) == copy, gate, 0.0)
            weights.append(gate)
        mixed = None
        for up, down in ((first, second), (first_other, second_other)):
            pieces = []
            for e in range(local):
                wide = dot(states, up[e])
                value = wide[:, :LANES]
                other = wide[:, LANES:]
                hidden = (value / (1.0 + jnp.exp(-value)) * other).astype(BF16).astype(F32)
                pieces.append((hidden * weights[e]).astype(BF16))
            part = dot(jnp.concatenate(pieces, axis=1), down[...])
            mixed = part if mixed is None else mixed + part
        out[here] = jnp.concatenate(
            [
                mixed[:, :half].reshape(group, part_rows, half),
                mixed[:, half:].reshape(group, part_rows, half),
            ],
            axis=1,
        ).astype(BF16)

    if team == group:
        one_block(0)
    else:

        def body(block, carry):
            one_block(block)
            return carry

        lax.fori_loop(0, team // group, body, 0)


def finish_kernel(arrived, residual, out):
    pairs = arrived.shape[1]
    half = arrived.shape[3]
    kept = residual[...]
    kept = jnp.concatenate([kept[:, :half], kept[:, half:]], axis=0)
    mine = lax.axis_index("tp_pair")
    for pair in range(pairs):
        mixed = jnp.sum(arrived[:, pair].astype(F32), axis=0)
        out[pair] = (mixed + jnp.where(mine == pair, kept, 0.0)).astype(BF16)


def score_kernel(fresh_count, *refs):
    *arrived, gains, weight, layer, score, ordered, wide = refs
    pairs, double, _ = arrived[0].shape
    rows = double // 2
    blocks, tokens, _ = ordered.shape
    samples = tokens // fresh_count
    side = lax.axis_index("tp_side")
    for flip in range(2):
        for pair in range(pairs):
            state = arrived[flip][pair].astype(F32)
            for other in range(flip + 2, len(arrived), 2):
                state = state + arrived[other][pair].astype(F32)
            spot = pl.ds(pl.multiple_of((2 * pair + (side ^ flip)) * rows, rows), rows)
            for c in range(blocks // 2):
                ordered[c, spot, :] = state[:rows, c * LANES : (c + 1) * LANES]
                ordered[blocks // 2 + c, spot, :] = state[rows:, c * LANES : (c + 1) * LANES]
    for c in range(blocks):
        for i in range(fresh_count):
            wide[pl.ds(fresh_count * c + i, samples, stride=fresh_count * blocks), :] = ordered[
                c, pl.ds(i, samples, stride=fresh_count), :
            ]
    layer[...] = wide[...].astype(BF16)
    states = jnp.concatenate([ordered[c] for c in range(blocks)], axis=1)
    states = states.astype(BF16).astype(F32)
    final = normalize(states, gains[2:3, :])
    scored = jnp.sum(final * weight[...], axis=1, keepdims=True)
    row = lax.broadcasted_iota(jnp.int32, (tokens, samples), 0)
    here = row // fresh_count == lane_iota(row.shape)
    for i in range(fresh_count):
        score[i : i + 1, :] = jnp.sum(
            jnp.where(here & (row % fresh_count == i), scored, 0.0), axis=0, keepdims=True
        )


def shards(
    tokens_new,
    prefix_len,
    tail_len,
    pool_home,
    pool_page,
    slot_page_cache,
    tail_cache,
    routes,
    norm_gains,
    query_weight,
    key_value_weight,
    out_weight,
    router,
    expert_in,
    expert_out,
    score_weight,
):
    req_count = lax.axis_size("req")
    pairs = lax.axis_size("tp_pair")
    parts = 2 * pairs
    _, samples, fresh_count, model = tokens_new.shape
    tokens = samples * fresh_count
    part_rows = tokens // parts
    pool = slot_page_cache.shape[0]
    page_size = slot_page_cache.shape[1]
    slot_cap = max(1, pool // req_count)
    tail_count = tail_cache.shape[2]
    local = expert_in.shape[0]
    expert_count = router.shape[1]
    copies = local * req_count // expert_count
    everyone = req_count * parts
    rows = 2 * tokens
    blocks = model // LANES
    top = routes.shape[3]
    half = model // 2
    team = req_count * pairs

    whole = ("tp_pair", "tp_side")
    flips = [[(t, t ^ flip) for t in range(parts)] for flip in range(parts)]
    first_raw = expert_in.reshape(local, 2 * model, LANES)
    second_raw = expert_out.reshape(local * LANES, model)


    token_bytes = tokens_new.reshape(samples, fresh_count, blocks, LANES)
    token_bytes = token_bytes.transpose(0, 2, 1, 3).reshape(tokens * blocks, LANES)
    route_bytes = routes[0].transpose(1, 2, 0).reshape(fresh_count * top, samples)

    message, flat, normed, cosine, sine = pl.pallas_call(
        functools.partial(query_kernel, fresh_count),
        out_shape=(
            jax.ShapeDtypeStruct((req_count, rows + fresh_count * top, LANES), BF16),
            jax.ShapeDtypeStruct((parts, part_rows, model), BF16),
            jax.ShapeDtypeStruct((tokens, model), BF16),
            jax.ShapeDtypeStruct((tokens, LANES), F32),
            jax.ShapeDtypeStruct((tokens, LANES), F32),
        ),
        in_specs=[HBM] * 6,
        out_specs=(VMEM,) * 5,
        scratch_shapes=[
            pltpu.SMEM(prefix_len.shape, jnp.int32),
            pltpu.SMEM(tail_len.shape, jnp.int32),
            pltpu.VMEM(token_bytes.shape, BF16),
            pltpu.VMEM(route_bytes.shape, jnp.int32),
            pltpu.VMEM(norm_gains.shape, F32),
            pltpu.VMEM(query_weight.shape, BF16),
            pltpu.VMEM((tokens * blocks, LANES), F32),
            pltpu.VMEM((blocks, tokens, LANES), F32),
            pltpu.SemaphoreType.DMA((6,)),
        ],
        compiler_params=params(HOLD_MIB),
        name="query",
    )(prefix_len, tail_len, token_bytes, route_bytes, norm_gains, query_weight)

    key_value_rows = key_value_weight.reshape(2 * model, LANES)
    tail_rows = tail_cache.reshape(samples, 2 * tail_count, LANES)
    tail_inputs = (message, normed, cosine, sine)
    tail = pl.pallas_call(
        functools.partial(tail_kernel, fresh_count),
        out_shape=jax.ShapeDtypeStruct((parts, 24, LANES), BF16),
        in_specs=[HBM] * 7,
        out_specs=VMEM,
        scratch_shapes=[
            pltpu.SMEM(tail_len.shape, jnp.int32),
            pltpu.VMEM((rows, LANES), BF16),
            pltpu.VMEM(normed.shape, BF16),
            pltpu.VMEM(cosine.shape, F32),
            pltpu.VMEM(sine.shape, F32),
            pltpu.VMEM(key_value_rows.shape, BF16),
            pltpu.VMEM(tail_rows.shape, BF16),
            pltpu.SemaphoreType.DMA((6,)),
            pltpu.SemaphoreType.DMA((parts,)),
        ],
        compiler_params=params(HOLD_MIB),
        cost_estimate=cost(2e9, 5e6),
        name="tail",
    )(tail_len, *tail_inputs, key_value_rows, tail_rows)

    page_rows = slot_page_cache.reshape(pool, 2 * page_size, LANES)
    later, message = lax.optimization_barrier((out_weight, message))
    across = [lax.ppermute(later, whole, flips[flip]) for flip in range(2, parts, 2)]
    beside = lax.ppermute(later, whole, flips[1])
    first_all = lax.all_to_all(message, "req", split_axis=0, concat_axis=0, tiled=True)
    page_rows, tail, beside = lax.optimization_barrier((page_rows, tail, beside))

    step = 8 if pool % 8 == 0 else 1
    split_pages = pl.pallas_call(
        split_pages_kernel,
        grid=(pool // step,),
        out_shape=jax.ShapeDtypeStruct((pool, 2 * page_size, LANES), BF16),
        in_specs=[pl.BlockSpec((step, 2 * page_size, LANES), lambda v: (v, 0, 0))],
        out_specs=pl.BlockSpec((step, 2 * page_size, LANES), lambda v: (v, 0, 0)),
        scratch_shapes=[pltpu.VMEM((step * 2 * page_size, LANES), F32)],
        compiler_params=params(8),
        cost_estimate=cost(1e6, 4e6),
        name="split_pages",
    )(page_rows)

    partial, named = pl.pallas_call(
        functools.partial(page_kernel, slot_cap),
        out_shape=(
            jax.ShapeDtypeStruct((everyone, 24, LANES), BF16),
            jax.ShapeDtypeStruct((req_count, fresh_count * top, LANES), BF16),
        ),
        in_specs=[SMEM] * 3 + [VMEM] * 3,
        out_specs=(VMEM, VMEM),
        scratch_shapes=[
            pltpu.SMEM((req_count * slot_cap,), jnp.int32),
            pltpu.SMEM((req_count,), jnp.int32),
        ],
        compiler_params=params(12),
        cost_estimate=cost(2e9, 5e6),
        name="pages",
    )(pool_home, pool_page, prefix_len, split_pages, tail, first_all)
    arrived = lax.all_to_all(partial, ("req",) + whole, split_axis=0, concat_axis=0, tiled=True)

    first_raw, across, _ = lax.optimization_barrier((first_raw, across, partial))
    projects = [out_weight, beside]
    for block in across:
        projects += [block, lax.ppermute(block, whole, flips[1])]
    first = pl.pallas_call(
        prepare_kernel,
        out_shape=jax.ShapeDtypeStruct((local, model, 2 * LANES), BF16),
        in_specs=[HBM],
        out_specs=VMEM,
        scratch_shapes=[
            pltpu.VMEM(first_raw.shape, BF16),
            pltpu.VMEM((2, 2 * model, LANES), F32),
            pltpu.SemaphoreType.DMA((local,)),
        ],
        compiler_params=params(HOLD_MIB),
        cost_estimate=cost(2e10, 8e6),
        name="prepare",
    )(first_raw)
    named, first, projects = lax.optimization_barrier((named, first, projects))
    mask = pl.pallas_call(
        functools.partial(names_kernel, part_rows, fresh_count),
        out_shape=jax.ShapeDtypeStruct((team * part_rows, expert_count), F32),
        in_specs=[VMEM],
        out_specs=VMEM,
        compiler_params=params(8),
        cost_estimate=cost(1e6, 1e6),
        name="names",
    )(named)
    arrived, first, mask = lax.optimization_barrier((arrived, first, mask))
    first = pl.pallas_call(
        keep_kernel,
        out_shape=jax.ShapeDtypeStruct(first.shape, BF16),
        in_specs=[HBM],
        out_specs=HBM,
        input_output_aliases={0: 0},
        compiler_params=params(HOLD_MIB),
        name="keep",
    )(first)
    first_other = lax.ppermute(first, whole, flips[1])

    message, residual = pl.pallas_call(
        merge_kernel,
        out_shape=(
            jax.ShapeDtypeStruct((team, 2 * part_rows, half), BF16),
            jax.ShapeDtypeStruct((part_rows, model), F32),
        ),
        in_specs=[VMEM] * (3 + parts),
        out_specs=(VMEM, VMEM),
        scratch_shapes=[pltpu.VMEM((parts, part_rows, model // parts), F32)],
        compiler_params=params(12),
        name="merge",
    )(arrived.reshape(req_count, parts, 24, LANES), flat, norm_gains, *projects)
    message, second_sent = lax.optimization_barrier((message, second_raw))
    second_other = lax.ppermute(second_sent, whole, flips[1])
    states = lax.all_to_all(message, ("req", "tp_pair"), split_axis=0, concat_axis=0, tiled=True)

    expert_inputs = (
        states,
        mask,
        router.T,
        first,
        first_other,
        second_raw,
        second_other,
    )
    mixed = pl.pallas_call(
        functools.partial(expert_kernel, copies, part_rows, min(req_count, 8) * pairs),
        out_shape=jax.ShapeDtypeStruct((team, 2 * part_rows, half), BF16),
        in_specs=[VMEM] * 7,
        out_specs=VMEM,
        compiler_params=params(16),
        name="experts",
    )(*expert_inputs)
    mixed = mixed.reshape(req_count, pairs, 2 * part_rows, half)
    mixed = lax.all_to_all(mixed, "req", split_axis=0, concat_axis=0, tiled=True)

    finished = pl.pallas_call(
        finish_kernel,
        out_shape=jax.ShapeDtypeStruct((pairs, 2 * part_rows, half), BF16),
        in_specs=[VMEM, VMEM],
        out_specs=VMEM,
        compiler_params=params(8),
        name="finish",
    )(mixed, residual)
    gathered = [finished] + [
        lax.ppermute(finished, whole, flips[flip]) for flip in range(1, parts)
    ]

    layer, score = pl.pallas_call(
        functools.partial(score_kernel, fresh_count),
        out_shape=(
            jax.ShapeDtypeStruct((tokens * blocks, LANES), BF16),
            jax.ShapeDtypeStruct((fresh_count, samples), F32),
        ),
        in_specs=[VMEM] * (parts + 2),
        out_specs=(VMEM, VMEM),
        scratch_shapes=[
            pltpu.VMEM((blocks, tokens, LANES), F32),
            pltpu.VMEM((tokens * blocks, LANES), F32),
        ],
        compiler_params=params(8),
        name="score",
    )(*gathered, norm_gains, score_weight.reshape(1, model))
    layer = layer.reshape(samples, blocks, fresh_count, LANES).transpose(0, 2, 1, 3)
    return (
        layer.reshape(1, samples, fresh_count, model),
        score.T.reshape(1, samples, fresh_count),
    )


def solution(mesh):
    tp = ("tp_pair", "tp_side")
    req_count, parts = mesh.devices.shape
    mesh = jax.sharding.Mesh(
        mesh.devices.reshape(req_count, parts // 2, 2), ("req", "tp_pair", "tp_side")
    )
    placed = (
        P("req", None, None, None),
        P(),
        P("req", None),
        P(),
        P(),
        P("req", None, None, tp),
        P("req", None, None, None, tp),
        P("req", None, None, None),
        P(),
        P(None, tp),
        P(None, None, tp),
        P(tp, None),
        P(),
        P("req", None, None, tp),
        P("req", tp, None),
        P(),
    )
    return jax.shard_map(
        shards,
        mesh=mesh,
        in_specs=placed,
        out_specs=(P("req", None, None, None), P("req", None, None)),
        check_vma=False,
    )
```

```python
import functools
import math

import jax
import jax.numpy as jnp
from jax import lax
from jax.experimental import pallas as pl
from jax.experimental.pallas import tpu as pltpu
from jax.sharding import PartitionSpec as P

HEAD_DIM = 64
LANES = 128
EPSILON = 1e-05
ROPE_BASE = 10000.0
LOWEST = -1e30
FLOOR = -1e28
F32 = jnp.float32
BF16 = jnp.bfloat16
MIB = 1024 * 1024
HOLD_MIB = 56

VMEM = pl.BlockSpec(memory_space=pltpu.VMEM)
SMEM = pl.BlockSpec(memory_space=pltpu.SMEM)
HBM = pl.BlockSpec(memory_space=pltpu.HBM)
ANY = pl.BlockSpec(memory_space=pl.ANY)


def params(mib):
    return pltpu.CompilerParams(vmem_limit_bytes=mib * MIB)


def cost(flops, moved):
    return pl.CostEstimate(flops=int(flops), bytes_accessed=int(moved), transcendentals=0)


def dot(left, right):
    return jnp.dot(left, right, preferred_element_type=F32)


def dot_t(left, right):
    return lax.dot_general(left, right, (((1,), (1,)), ((), ())), preferred_element_type=F32)


def my_part():
    return lax.axis_index("tp_pair") * 2 + lax.axis_index("tp_side")


def load_all(pairs, done):
    copies = [pltpu.make_async_copy(far, near, done.at[k]) for k, (far, near) in enumerate(pairs)]
    for copy in copies:
        copy.start()
    return copies


def lane_iota(shape):
    return lax.broadcasted_iota(jnp.int32, shape, len(shape) - 1)


def normalize(x, gain):
    return x * lax.rsqrt(jnp.mean(x * x, axis=-1, keepdims=True) + EPSILON) * gain


def rotate(x, cosine, sine):
    lanes = lane_iota(x.shape)
    partner = jnp.where(lanes % HEAD_DIM < HEAD_DIM // 2, pltpu.roll(x, 96, 1), pltpu.roll(x, 32, 1))
    return x * cosine + partner * sine


def by_head(packed, low):
    zero = jnp.zeros_like(packed)
    return jnp.concatenate([jnp.where(low, packed, zero), jnp.where(low, zero, packed)], axis=0)


def swap_halves(first, second):
    low = lane_iota(first.shape) < HEAD_DIM
    return (
        jnp.where(low, first, pltpu.roll(second, HEAD_DIM, 1)),
        jnp.where(low, pltpu.roll(first, HEAD_DIM, 1), second),
    )


def query_kernel(
    fresh_count,
    prefix_far,
    lengths_far,
    tokens_far,
    named_far,
    gains_far,
    weight_far,
    message,
    flat,
    normed,
    cosine,
    sine,
    prefix,
    lengths,
    tokens,
    named,
    gains,
    weight,
    wide,
    ordered,
    done,
):
    loads = load_all(
        (
            (tokens_far, tokens),
            (gains_far, gains),
            (lengths_far, lengths),
            (prefix_far, prefix),
            (weight_far, weight),
            (named_far, named),
        ),
        done,
    )
    count, model = normed.shape
    samples = count // fresh_count
    parts, part_rows, _ = flat.shape
    blocks = model // LANES
    loads[0].wait()
    wide[...] = tokens[...].astype(F32)
    for c in range(blocks):
        for i in range(fresh_count):
            ordered[c, pl.ds(i, samples, stride=fresh_count), :] = wide[
                pl.ds(fresh_count * c + i, samples, stride=fresh_count * blocks), :
            ]
    states = jnp.concatenate([ordered[c] for c in range(blocks)], axis=1)
    for part in range(parts):
        flat[part] = states[part * part_rows : (part + 1) * part_rows].astype(BF16)
    loads[1].wait()
    rows = normalize(states, gains[0:1, :]).astype(BF16)
    normed[...] = rows
    loads[2].wait()
    loads[3].wait()
    row_id = lax.broadcasted_iota(jnp.int32, (count, 1), 0)
    position = row_id % fresh_count + prefix[lax.axis_index("req")]
    for sample in range(samples):
        position = position + jnp.where(row_id // fresh_count == sample, lengths[0, sample], 0)
    within = lane_iota((1, LANES)) % HEAD_DIM
    pair = (within % (HEAD_DIM // 2)).astype(F32)
    frequency = jnp.exp(pair * (-math.log(ROPE_BASE) / (HEAD_DIM // 2)))
    angles = position.astype(F32) * frequency
    cosine[...] = jnp.cos(angles)
    turn = jnp.sin(angles)
    sine[...] = jnp.where(within < HEAD_DIM // 2, -turn, turn)
    loads[4].wait()
    made = dot(rows, weight[...])
    pieces = []
    for group in swap_halves(made[:, :LANES], made[:, LANES:]):
        pieces.append(rotate(group, cosine[...], sine[...]).astype(BF16).astype(F32) * 0.125)
    packed = []
    for part in range(parts):
        for piece in pieces:
            packed.append(piece[part * part_rows : (part + 1) * part_rows])
    loads[5].wait()
    routed = named[...].astype(F32)
    packed.append(
        jnp.concatenate(
            [routed, jnp.zeros((routed.shape[0], LANES - routed.shape[1]), F32)], axis=1
        )
    )
    packed = jnp.concatenate(packed, axis=0).astype(BF16)
    for n in range(message.shape[0]):
        message[n] = packed


def split_pages_kernel(source, out, wide):
    count, double, _ = source.shape
    half = double // 2
    wide[...] = source[...].astype(F32).reshape(count * double, LANES)
    keys = wide[pl.ds(0, count * half, stride=2), :].astype(BF16)
    values = wide[pl.ds(1, count * half, stride=2), :].astype(BF16)
    out[:, :half, :] = keys.reshape(count, half, LANES)
    out[:, half:, :] = values.reshape(count, half, LANES)


def pack_message(numer, top, total):
    high = total.astype(BF16).astype(F32)
    section = (lane_iota((8, LANES)) % HEAD_DIM) // 8
    stats = jnp.zeros((8, LANES), F32)
    for group in range(2):
        span = slice(group * 8, (group + 1) * 8)
        for k, kind in enumerate((top, high, total - high)):
            stats = jnp.where(section == 3 * group + k, kind[span], stats)
    return jnp.concatenate([numer, stats], axis=0).astype(BF16)


def unpack_message(block):
    block = block.astype(F32)
    stats = block[..., 16:24, :]
    low = lane_iota(stats.shape) < HEAD_DIM

    def pick(section):
        lane = section * 8
        return jnp.where(
            low, stats[..., lane : lane + 1], stats[..., HEAD_DIM + lane : HEAD_DIM + lane + 1]
        )

    top = jnp.concatenate([pick(0), pick(3)], axis=-2)
    total = jnp.concatenate([pick(1) + pick(2), pick(4) + pick(5)], axis=-2)
    return block[..., 0:16, :], top, total


def tail_kernel(
    fresh_count,
    lengths_far,
    query_far,
    normed_far,
    cosine_far,
    sine_far,
    weight_far,
    cache_far,
    out,
    lengths,
    query,
    normed,
    cosine,
    sine,
    weight,
    cache,
    load,
    done,
):
    tokens = normed.shape[0]
    samples, width, _ = cache.shape
    parts = out.shape[0]
    per_part = samples // parts
    loads = load_all(
        (
            (normed_far, normed),
            (weight_far, weight),
            (cosine_far, cosine),
            (sine_far, sine),
            (query_far.at[0, pl.ds(0, parts * 16)], query),
            (lengths_far, lengths),
        ),
        load,
    )
    spans = [pl.ds(part * per_part, per_part) for part in range(parts)]
    blocks = load_all([(cache_far.at[span], cache.at[span]) for span in spans], done)
    spread = (
        lax.broadcasted_iota(jnp.int32, (LANES, 2 * LANES), 1)
        == 2 * lax.broadcasted_iota(jnp.int32, (LANES, 2 * LANES), 0)
    ).astype(BF16)
    loads[0].wait()
    rows = normed[...]
    widened = jnp.concatenate(
        [dot(rows[:, c : c + LANES], spread) for c in range(0, rows.shape[1], LANES)], axis=1
    )
    both = jnp.concatenate([widened, pltpu.roll(widened, 1, 1)], axis=0).astype(BF16)
    for copy in loads[1:]:
        copy.wait()
    made = dot(both, weight[...])
    key_new = rotate(made[:tokens], cosine[...], sine[...]).astype(BF16)
    value_new = made[tokens:].astype(BF16)
    low = lane_iota((16, LANES)) < HEAD_DIM
    row_id = lax.broadcasted_iota(jnp.int32, (parts * 32, 1), 0)
    row_sample = (row_id // 32) * per_part + (row_id % 8) // fresh_count
    row_fresh = row_id % fresh_count
    part_sample = row_sample[:32]
    wide = [by_head(query[part * 16 : (part + 1) * 16, :], low) for part in range(parts)]
    length = jnp.zeros((parts * 32, 1), jnp.int32)
    for sample in range(samples):
        length = jnp.where(row_sample == sample, lengths[0, sample], length)
    fresh = dot_t(jnp.concatenate(wide, axis=0), key_new)
    token_id = lane_iota(fresh.shape)
    fresh_seen = (token_id // fresh_count == row_sample) & (token_id % fresh_count <= row_fresh)
    fresh = jnp.where(fresh_seen, fresh, LOWEST)
    for copy in blocks:
        copy.wait()
    beside = []
    scores = []
    for part in range(parts):
        placed = [
            jnp.where(part_sample == a, wide[part], jnp.zeros_like(wide[part]))
            for a in range(per_part)
        ]
        beside.append(
            jnp.concatenate([cache[part * per_part + a] for a in range(per_part)], axis=1)
        )
        scores.append(dot_t(jnp.concatenate(placed, axis=1), beside[part]))
    scores = jnp.concatenate(scores, axis=0)
    column = lane_iota(scores.shape)
    scores = jnp.where((column % 2 == 0) & (column < 2 * length), scores, LOWEST)
    peak = jnp.maximum(
        jnp.max(scores, axis=1, keepdims=True), jnp.max(fresh, axis=1, keepdims=True)
    )
    peak = peak.astype(BF16).astype(F32)
    weights = jnp.exp(scores - peak)
    fresh_weights = jnp.exp(fresh - peak)
    amount = jnp.sum(weights, axis=1, keepdims=True) + jnp.sum(fresh_weights, axis=1, keepdims=True)
    shifted = pltpu.roll(weights, 1, 1).astype(BF16)
    fresh_part = dot(fresh_weights.astype(BF16), value_new)
    every = [dot(shifted[part * 32 : (part + 1) * 32], beside[part]) for part in range(parts)]
    for part in range(parts):
        mixed = every[part][:, :LANES]
        for a in range(1, per_part):
            mixed = jnp.where(part_sample == a, every[part][:, a * LANES : (a + 1) * LANES], mixed)
        first = slice(part * 32, part * 32 + 16)
        second = slice(part * 32 + 16, part * 32 + 32)
        mixed = mixed + fresh_part[part * 32 : (part + 1) * 32]
        out[part] = pack_message(
            jnp.where(low, mixed[:16], mixed[16:]),
            jnp.where(low, peak[first], peak[second]),
            jnp.where(low, amount[first], amount[second]),
        )


def page_kernel(
    slot_cap, homes, pages, lengths, cache, tail, query, out, named, slots, counts
):
    requests = query.shape[0]
    parts = tail.shape[0]
    pool = cache.shape[0]
    page_size = cache.shape[1] // 2
    rows = parts * 16
    me = lax.axis_index("req")
    base = me * pool
    tail_numer, tail_top, tail_total = [
        kind.reshape(rows, LANES) for kind in unpack_message(tail[...])
    ]
    named[...] = query[:, rows:, :]

    def clear(r, carry):
        counts[r] = 0
        for j in range(slot_cap):
            slots[r * slot_cap + j] = -1
        return carry

    lax.fori_loop(0, requests, clear, 0)

    def assign(v, carry):
        r = homes[base + v]
        rank = counts[r]
        slots[r * slot_cap + rank] = v
        counts[r] = rank + 1
        return carry

    lax.fori_loop(0, pool, assign, 0)

    low = lane_iota((rows, LANES)) < HEAD_DIM
    column = lane_iota((2 * rows, page_size))

    def finish(r, mixed, peak, amount):
        own = r == me
        top = jnp.where(low, peak[:rows], peak[rows:])
        joint = jnp.maximum(top, jnp.where(own, tail_top, FLOOR))
        here = jnp.exp(top - joint)
        there = jnp.where(own, jnp.exp(tail_top - joint), 0.0)
        numer = jnp.where(low, mixed[:rows], mixed[rows:]) * here + tail_numer * there
        total = jnp.where(low, amount[:rows], amount[rows:]) * here + tail_total * there
        for part in range(parts):
            span = slice(part * 16, (part + 1) * 16)
            out[r * parts + part] = pack_message(numer[span], joint[span], total[span])

    def gather(first, count):
        wides = []
        keys = []
        values = []
        limits = []
        for k in range(count):
            r = first + k
            wide = by_head(query[r, 0:rows, :], low)
            zero = jnp.zeros_like(wide)
            wides.append(jnp.concatenate([wide if c == k else zero for c in range(count)], axis=1))
            own_keys = []
            own_values = []
            own_limits = []
            for j in range(slot_cap):
                slot = slots[r * slot_cap + j]
                safe = jnp.maximum(slot, 0)
                own_limits.append(
                    jnp.where(slot >= 0, lengths[r] - pages[base + safe] * page_size, 0)
                )
                own_keys.append(cache[safe, :page_size, :])
                own_values.append(cache[safe, page_size:, :])
            keys.append(jnp.concatenate(own_keys, axis=0))
            values.append(jnp.concatenate(own_values, axis=0))
            limits.append(own_limits)
        scores = dot_t(jnp.concatenate(wides, axis=0), jnp.concatenate(keys, axis=1))
        return scores, jnp.concatenate(values, axis=1), limits

    def weigh(scores, limits):
        all_weights = []
        stats = []
        for k in range(len(limits)):
            own = scores[k * 2 * rows : (k + 1) * 2 * rows]
            own = [
                jnp.where(
                    column < limits[k][j], own[:, j * page_size : (j + 1) * page_size], LOWEST
                )
                for j in range(slot_cap)
            ]
            peak = jnp.max(functools.reduce(jnp.maximum, own), axis=1, keepdims=True)
            peak = jnp.maximum(peak, FLOOR).astype(BF16).astype(F32)
            weights = [jnp.exp(one - peak) for one in own]
            amount = jnp.sum(functools.reduce(jnp.add, weights), axis=1, keepdims=True)
            all_weights.append(jnp.concatenate([one.astype(BF16) for one in weights], axis=1))
            stats.append((peak, amount))
        return jnp.concatenate(all_weights, axis=0), stats

    pair = 2 if requests % 2 == 0 else 1
    step = 8 if requests % 8 == 0 else pair

    def several(g, carry):
        firsts = [g * step + k for k in range(0, step, pair)]
        gathered = [gather(first, pair) for first in firsts]
        weighed = [weigh(scores, limits) for scores, _, limits in gathered]
        mixed = [dot(weighed[n][0], gathered[n][1]) for n in range(len(firsts))]
        for n, first in enumerate(firsts):
            for k in range(pair):
                own = mixed[n][k * 2 * rows : (k + 1) * 2 * rows, k * LANES : (k + 1) * LANES]
                finish(first + k, own, *weighed[n][1][k])
        return carry

    if requests == step:
        several(0, 0)
    else:
        lax.fori_loop(0, requests // step, several, 0)


def merge_kernel(arrived, tokens, gains, *refs):
    parts = arrived.shape[1]
    weights = refs[:parts]
    out, residual, columns = refs[parts:]
    part = my_part()
    for t in range(parts):
        numer, top, total = unpack_message(arrived[:, t])
        factor = jnp.exp(top - jnp.max(top, axis=0, keepdims=True))
        attended = jnp.sum(factor * numer, axis=0) / jnp.sum(factor * total, axis=0)
        columns[t] = jnp.concatenate(swap_halves(attended[0:8], attended[8:16]), axis=1)
    projected = None
    for flip in range(parts):
        one = dot(columns[part ^ flip].astype(BF16), weights[flip][...])
        projected = one if projected is None else projected + one
    rows = (tokens[part].astype(F32) + projected).astype(BF16).astype(F32)
    residual[...] = rows
    normed = normalize(rows, gains[1:2, :])
    half = normed.shape[1] // 2
    message = jnp.concatenate([normed[:, :half], normed[:, half:]], axis=0).astype(BF16)
    for n in range(out.shape[0]):
        out[n] = message


def prepare_kernel(first_far, out, near, wide, done):
    local, double, _ = near.shape
    depth = double // 2
    loads = load_all([(first_far.at[e], near.at[e]) for e in range(local)], done)

    for e in range(local):
        loads[e].wait()
        buffer = wide.at[e % 2]
        buffer[...] = near[e].astype(F32)
        out[e, :, :LANES] = buffer[pl.ds(0, depth, stride=2), :].astype(BF16)
        out[e, :, LANES:] = buffer[pl.ds(1, depth, stride=2), :].astype(BF16)


def keep_kernel(*refs):
    del refs


def names_kernel(part_rows, fresh_count, packed, out):
    requests, span, _ = packed.shape
    experts = out.shape[1]
    halves = out.shape[0] // (requests * part_rows)
    top = span // fresh_count
    row = lax.broadcasted_iota(jnp.int32, (halves * part_rows, LANES), 0)
    token = (row // part_rows) * 2 * part_rows + lax.axis_index("tp_side") * part_rows + row % part_rows
    pick = (lane_iota(row.shape) == token // fresh_count).astype(BF16)
    found = jnp.concatenate([dot_t(pick, packed[r]) for r in range(requests)], axis=0)
    fresh = lax.broadcasted_iota(jnp.int32, (found.shape[0], 1), 0) % fresh_count
    chosen = found[:, :top]
    for i in range(1, fresh_count):
        chosen = jnp.where(fresh == i, found[:, i * top : (i + 1) * top], chosen)
    lanes = lane_iota(out.shape).astype(F32)
    mask = jnp.zeros(out.shape, F32)
    for k in range(top):
        mask = jnp.where(chosen[:, k : k + 1] == lanes, 1.0, mask)
    out[...] = mask


def expert_kernel(
    copies,
    part_rows,
    group,
    arrived,
    mask,
    router,
    first,
    first_other,
    second,
    second_other,
    out,
):
    team, _, half = arrived.shape
    local = first.shape[0]
    expert_count = router.shape[0]
    count = group * part_rows
    me = lax.axis_index("req")

    def one_block(block):
        here = pl.ds(block * group, group)
        states = arrived[here].astype(F32)
        states = jnp.concatenate(
            [
                states[:, :part_rows].reshape(count, half),
                states[:, part_rows:].reshape(count, half),
            ],
            axis=1,
        ).astype(BF16)
        logits = dot_t(states, router[...])
        span = pl.ds(pl.multiple_of(block * count, count), count)
        chosen = jnp.where(mask[span, :] > 0.5, logits, LOWEST)
        shares = jnp.exp(chosen - jnp.max(chosen, axis=1, keepdims=True))
        gates = shares / jnp.sum(shares, axis=1, keepdims=True)
        lanes = lane_iota(gates.shape)
        row = lax.broadcasted_iota(jnp.int32, (count, 1), 0)
        row_request = (block * group + row // part_rows) // 2
        weights = []
        for e in range(local):
            slot = me * local + e
            gate = jnp.sum(
                jnp.where(lanes == lax.rem(slot, expert_count), gates, 0.0), axis=1, keepdims=True
            )
            if copies > 1:
                copy = lax.div(slot, expert_count)
                gate = jnp.where(lax.rem(row_request, copies) == copy, gate, 0.0)
            weights.append(gate)
        mixed = None
        for up, down in ((first, second), (first_other, second_other)):
            pieces = []
            for e in range(local):
                wide = dot(states, up[e])
                value = wide[:, :LANES]
                other = wide[:, LANES:]
                hidden = (value / (1.0 + jnp.exp(-value)) * other).astype(BF16).astype(F32)
                pieces.append((hidden * weights[e]).astype(BF16))
            part = dot(jnp.concatenate(pieces, axis=1), down[...])
            mixed = part if mixed is None else mixed + part
        out[here] = jnp.concatenate(
            [
                mixed[:, :half].reshape(group, part_rows, half),
                mixed[:, half:].reshape(group, part_rows, half),
            ],
            axis=1,
        ).astype(BF16)

    if team == group:
        one_block(0)
    else:

        def body(block, carry):
            one_block(block)
            return carry

        lax.fori_loop(0, team // group, body, 0)


def finish_kernel(arrived, residual, out):
    pairs = arrived.shape[1]
    half = arrived.shape[3]
    kept = residual[...]
    kept = jnp.concatenate([kept[:, :half], kept[:, half:]], axis=0)
    mine = lax.axis_index("tp_pair")
    for pair in range(pairs):
        mixed = jnp.sum(arrived[:, pair].astype(F32), axis=0)
        out[pair] = (mixed + jnp.where(mine == pair, kept, 0.0)).astype(BF16)


def score_kernel(fresh_count, *refs):
    *arrived, gains, weight, layer, score, ordered, wide = refs
    pairs, double, _ = arrived[0].shape
    rows = double // 2
    blocks, tokens, _ = ordered.shape
    samples = tokens // fresh_count
    side = lax.axis_index("tp_side")
    for flip in range(2):
        for pair in range(pairs):
            state = arrived[flip][pair].astype(F32)
            for other in range(flip + 2, len(arrived), 2):
                state = state + arrived[other][pair].astype(F32)
            spot = pl.ds(pl.multiple_of((2 * pair + (side ^ flip)) * rows, rows), rows)
            for c in range(blocks // 2):
                ordered[c, spot, :] = state[:rows, c * LANES : (c + 1) * LANES]
                ordered[blocks // 2 + c, spot, :] = state[rows:, c * LANES : (c + 1) * LANES]
    for c in range(blocks):
        for i in range(fresh_count):
            wide[pl.ds(fresh_count * c + i, samples, stride=fresh_count * blocks), :] = ordered[
                c, pl.ds(i, samples, stride=fresh_count), :
            ]
    layer[...] = wide[...].astype(BF16)
    states = jnp.concatenate([ordered[c] for c in range(blocks)], axis=1)
    states = states.astype(BF16).astype(F32)
    final = normalize(states, gains[2:3, :])
    scored = jnp.sum(final * weight[...], axis=1, keepdims=True)
    row = lax.broadcasted_iota(jnp.int32, (tokens, samples), 0)
    here = row // fresh_count == lane_iota(row.shape)
    for i in range(fresh_count):
        score[i : i + 1, :] = jnp.sum(
            jnp.where(here & (row % fresh_count == i), scored, 0.0), axis=0, keepdims=True
        )


def shards(
    tokens_new,
    prefix_len,
    tail_len,
    pool_home,
    pool_page,
    slot_page_cache,
    tail_cache,
    routes,
    norm_gains,
    query_weight,
    key_value_weight,
    out_weight,
    router,
    expert_in,
    expert_out,
    score_weight,
):
    req_count = lax.axis_size("req")
    pairs = lax.axis_size("tp_pair")
    parts = 2 * pairs
    _, samples, fresh_count, model = tokens_new.shape
    tokens = samples * fresh_count
    part_rows = tokens // parts
    pool = slot_page_cache.shape[0]
    page_size = slot_page_cache.shape[1]
    slot_cap = max(1, pool // req_count)
    tail_count = tail_cache.shape[2]
    local = expert_in.shape[0]
    expert_count = router.shape[1]
    copies = local * req_count // expert_count
    everyone = req_count * parts
    rows = 2 * tokens
    blocks = model // LANES
    top = routes.shape[3]
    half = model // 2
    team = req_count * pairs

    whole = ("tp_pair", "tp_side")
    flips = [[(t, t ^ flip) for t in range(parts)] for flip in range(parts)]
    first_raw = expert_in.reshape(local, 2 * model, LANES)
    second_raw = expert_out.reshape(local * LANES, model)


    token_bytes = tokens_new.reshape(samples, fresh_count, blocks, LANES)
    token_bytes = token_bytes.transpose(0, 2, 1, 3).reshape(tokens * blocks, LANES)
    route_bytes = routes[0].transpose(1, 2, 0).reshape(fresh_count * top, samples)

    message, flat, normed, cosine, sine = pl.pallas_call(
        functools.partial(query_kernel, fresh_count),
        out_shape=(
            jax.ShapeDtypeStruct((req_count, rows + fresh_count * top, LANES), BF16),
            jax.ShapeDtypeStruct((parts, part_rows, model), BF16),
            jax.ShapeDtypeStruct((tokens, model), BF16),
            jax.ShapeDtypeStruct((tokens, LANES), F32),
            jax.ShapeDtypeStruct((tokens, LANES), F32),
        ),
        in_specs=[HBM] * 6,
        out_specs=(VMEM,) * 5,
        scratch_shapes=[
            pltpu.SMEM(prefix_len.shape, jnp.int32),
            pltpu.SMEM(tail_len.shape, jnp.int32),
            pltpu.VMEM(token_bytes.shape, BF16),
            pltpu.VMEM(route_bytes.shape, jnp.int32),
            pltpu.VMEM(norm_gains.shape, F32),
            pltpu.VMEM(query_weight.shape, BF16),
            pltpu.VMEM((tokens * blocks, LANES), F32),
            pltpu.VMEM((blocks, tokens, LANES), F32),
            pltpu.SemaphoreType.DMA((6,)),
        ],
        compiler_params=params(HOLD_MIB),
        name="query",
    )(prefix_len, tail_len, token_bytes, route_bytes, norm_gains, query_weight)

    key_value_rows = key_value_weight.reshape(2 * model, LANES)
    tail_rows = tail_cache.reshape(samples, 2 * tail_count, LANES)
    tail_inputs = (message, normed, cosine, sine)
    tail = pl.pallas_call(
        functools.partial(tail_kernel, fresh_count),
        out_shape=jax.ShapeDtypeStruct((parts, 24, LANES), BF16),
        in_specs=[HBM] * 7,
        out_specs=VMEM,
        scratch_shapes=[
            pltpu.SMEM(tail_len.shape, jnp.int32),
            pltpu.VMEM((rows, LANES), BF16),
            pltpu.VMEM(normed.shape, BF16),
            pltpu.VMEM(cosine.shape, F32),
            pltpu.VMEM(sine.shape, F32),
            pltpu.VMEM(key_value_rows.shape, BF16),
            pltpu.VMEM(tail_rows.shape, BF16),
            pltpu.SemaphoreType.DMA((6,)),
            pltpu.SemaphoreType.DMA((parts,)),
        ],
        compiler_params=params(HOLD_MIB),
        cost_estimate=cost(2e9, 5e6),
        name="tail",
    )(tail_len, *tail_inputs, key_value_rows, tail_rows)

    page_rows = slot_page_cache.reshape(pool, 2 * page_size, LANES)
    later, message = lax.optimization_barrier((out_weight, message))
    across = [lax.ppermute(later, whole, flips[flip]) for flip in range(2, parts, 2)]
    beside = lax.ppermute(later, whole, flips[1])
    first_all = lax.all_to_all(message, "req", split_axis=0, concat_axis=0, tiled=True)
    page_rows, tail, beside = lax.optimization_barrier((page_rows, tail, beside))

    step = 8 if pool % 8 == 0 else 1
    split_pages = pl.pallas_call(
        split_pages_kernel,
        grid=(pool // step,),
        out_shape=jax.ShapeDtypeStruct((pool, 2 * page_size, LANES), BF16),
        in_specs=[pl.BlockSpec((step, 2 * page_size, LANES), lambda v: (v, 0, 0))],
        out_specs=pl.BlockSpec((step, 2 * page_size, LANES), lambda v: (v, 0, 0)),
        scratch_shapes=[pltpu.VMEM((step * 2 * page_size, LANES), F32)],
        compiler_params=params(8),
        cost_estimate=cost(1e6, 4e6),
        name="split_pages",
    )(page_rows)

    partial, named = pl.pallas_call(
        functools.partial(page_kernel, slot_cap),
        out_shape=(
            jax.ShapeDtypeStruct((everyone, 24, LANES), BF16),
            jax.ShapeDtypeStruct((req_count, fresh_count * top, LANES), BF16),
        ),
        in_specs=[SMEM] * 3 + [VMEM] * 3,
        out_specs=(VMEM, VMEM),
        scratch_shapes=[
            pltpu.SMEM((req_count * slot_cap,), jnp.int32),
            pltpu.SMEM((req_count,), jnp.int32),
        ],
        compiler_params=params(12),
        cost_estimate=cost(2e9, 5e6),
        name="pages",
    )(pool_home, pool_page, prefix_len, split_pages, tail, first_all)
    arrived = lax.all_to_all(partial, ("req",) + whole, split_axis=0, concat_axis=0, tiled=True)

    first_raw, across, _ = lax.optimization_barrier((first_raw, across, partial))
    projects = [out_weight, beside]
    for block in across:
        projects += [block, lax.ppermute(block, whole, flips[1])]
    first = pl.pallas_call(
        prepare_kernel,
        out_shape=jax.ShapeDtypeStruct((local, model, 2 * LANES), BF16),
        in_specs=[HBM],
        out_specs=VMEM,
        scratch_shapes=[
            pltpu.VMEM(first_raw.shape, BF16),
            pltpu.VMEM((2, 2 * model, LANES), F32),
            pltpu.SemaphoreType.DMA((local,)),
        ],
        compiler_params=params(HOLD_MIB),
        cost_estimate=cost(2e10, 8e6),
        name="prepare",
    )(first_raw)
    named, first, projects = lax.optimization_barrier((named, first, projects))
    mask = pl.pallas_call(
        functools.partial(names_kernel, part_rows, fresh_count),
        out_shape=jax.ShapeDtypeStruct((team * part_rows, expert_count), F32),
        in_specs=[VMEM],
        out_specs=VMEM,
        compiler_params=params(8),
        cost_estimate=cost(1e6, 1e6),
        name="names",
    )(named)
    arrived, first, mask = lax.optimization_barrier((arrived, first, mask))
    first = pl.pallas_call(
        keep_kernel,
        out_shape=jax.ShapeDtypeStruct(first.shape, BF16),
        in_specs=[HBM],
        out_specs=HBM,
        input_output_aliases={0: 0},
        compiler_params=params(HOLD_MIB),
        name="keep",
    )(first)
    first_other = lax.ppermute(first, whole, flips[1])

    message, residual = pl.pallas_call(
        merge_kernel,
        out_shape=(
            jax.ShapeDtypeStruct((team, 2 * part_rows, half), BF16),
            jax.ShapeDtypeStruct((part_rows, model), F32),
        ),
        in_specs=[VMEM] * (3 + parts),
        out_specs=(VMEM, VMEM),
        scratch_shapes=[pltpu.VMEM((parts, part_rows, model // parts), F32)],
        compiler_params=params(12),
        name="merge",
    )(arrived.reshape(req_count, parts, 24, LANES), flat, norm_gains, *projects)
    message, second_sent = lax.optimization_barrier((message, second_raw))
    second_other = lax.ppermute(second_sent, whole, flips[1])
    states = lax.all_to_all(message, ("req", "tp_pair"), split_axis=0, concat_axis=0, tiled=True)

    expert_inputs = (
        states,
        mask,
        router.T,
        first,
        first_other,
        second_raw,
        second_other,
    )
    mixed = pl.pallas_call(
        functools.partial(expert_kernel, copies, part_rows, min(req_count, 8) * pairs),
        out_shape=jax.ShapeDtypeStruct((team, 2 * part_rows, half), BF16),
        in_specs=[VMEM] * 7,
        out_specs=VMEM,
        compiler_params=params(16),
        name="experts",
    )(*expert_inputs)
    mixed = mixed.reshape(req_count, pairs, 2 * part_rows, half)
    mixed = lax.all_to_all(mixed, "req", split_axis=0, concat_axis=0, tiled=True)

    finished = pl.pallas_call(
        finish_kernel,
        out_shape=jax.ShapeDtypeStruct((pairs, 2 * part_rows, half), BF16),
        in_specs=[VMEM, VMEM],
        out_specs=VMEM,
        compiler_params=params(8),
        name="finish",
    )(mixed, residual)
    gathered = [finished] + [
        lax.ppermute(finished, whole, flips[flip]) for flip in range(1, parts)
    ]

    layer, score = pl.pallas_call(
        functools.partial(score_kernel, fresh_count),
        out_shape=(
            jax.ShapeDtypeStruct((tokens * blocks, LANES), BF16),
            jax.ShapeDtypeStruct((fresh_count, samples), F32),
        ),
        in_specs=[VMEM] * (parts + 2),
        out_specs=(VMEM, VMEM),
        scratch_shapes=[
            pltpu.VMEM((blocks, tokens, LANES), F32),
            pltpu.VMEM((tokens * blocks, LANES), F32),
        ],
        compiler_params=params(8),
        name="score",
    )(*gathered, norm_gains, score_weight.reshape(1, model))
    layer = layer.reshape(samples, blocks, fresh_count, LANES).transpose(0, 2, 1, 3)
    return (
        layer.reshape(1, samples, fresh_count, model),
        score.T.reshape(1, samples, fresh_count),
    )


def solution(mesh):
    tp = ("tp_pair", "tp_side")
    req_count, parts = mesh.devices.shape
    mesh = jax.sharding.Mesh(
        mesh.devices.reshape(req_count, parts // 2, 2), ("req", "tp_pair", "tp_side")
    )
    placed = (
        P("req", None, None, None),
        P(),
        P("req", None),
        P(),
        P(),
        P("req", None, None, tp),
        P("req", None, None, None, tp),
        P("req", None, None, None),
        P(),
        P(None, tp),
        P(None, None, tp),
        P(tp, None),
        P(),
        P("req", None, None, tp),
        P("req", tp, None),
        P(),
    )
    return jax.shard_map(
        shards,
        mesh=mesh,
        in_specs=placed,
        out_specs=(P("req", None, None, None), P("req", None, None)),
        check_vma=False,
    )
```

```python
import functools
import math

import jax
import jax.numpy as jnp
from jax import lax
from jax.experimental import pallas as pl
from jax.experimental.pallas import tpu as pltpu
from jax.sharding import PartitionSpec as P

HEAD_DIM = 64
LANES = 128
EPSILON = 1e-05
ROPE_BASE = 10000.0
LOWEST = -1e30
FLOOR = -1e28
F32 = jnp.float32
BF16 = jnp.bfloat16
MIB = 1024 * 1024
HOLD_MIB = 56

VMEM = pl.BlockSpec(memory_space=pltpu.VMEM)
SMEM = pl.BlockSpec(memory_space=pltpu.SMEM)
HBM = pl.BlockSpec(memory_space=pltpu.HBM)
ANY = pl.BlockSpec(memory_space=pl.ANY)


def params(mib):
    return pltpu.CompilerParams(vmem_limit_bytes=mib * MIB)


def cost(flops, moved):
    return pl.CostEstimate(flops=int(flops), bytes_accessed=int(moved), transcendentals=0)


def dot(left, right):
    return jnp.dot(left, right, preferred_element_type=F32)


def dot_t(left, right):
    return lax.dot_general(left, right, (((1,), (1,)), ((), ())), preferred_element_type=F32)


def my_part():
    return lax.axis_index("tp_pair") * 2 + lax.axis_index("tp_side")


def load_all(pairs, done):
    copies = [pltpu.make_async_copy(far, near, done.at[k]) for k, (far, near) in enumerate(pairs)]
    for copy in copies:
        copy.start()
    return copies


def lane_iota(shape):
    return lax.broadcasted_iota(jnp.int32, shape, len(shape) - 1)


def normalize(x, gain):
    return x * lax.rsqrt(jnp.mean(x * x, axis=-1, keepdims=True) + EPSILON) * gain


def rotate(x, cosine, sine):
    lanes = lane_iota(x.shape)
    partner = jnp.where(lanes % HEAD_DIM < HEAD_DIM // 2, pltpu.roll(x, 96, 1), pltpu.roll(x, 32, 1))
    return x * cosine + partner * sine


def by_head(packed, low):
    zero = jnp.zeros_like(packed)
    return jnp.concatenate([jnp.where(low, packed, zero), jnp.where(low, zero, packed)], axis=0)


def swap_halves(first, second):
    low = lane_iota(first.shape) < HEAD_DIM
    return (
        jnp.where(low, first, pltpu.roll(second, HEAD_DIM, 1)),
        jnp.where(low, pltpu.roll(first, HEAD_DIM, 1), second),
    )


def query_kernel(
    fresh_count,
    prefix_far,
    lengths_far,
    tokens_far,
    named_far,
    gains_far,
    weight_far,
    message,
    flat,
    normed,
    cosine,
    sine,
    prefix,
    lengths,
    tokens,
    named,
    gains,
    weight,
    wide,
    ordered,
    done,
):
    loads = load_all(
        (
            (tokens_far, tokens),
            (gains_far, gains),
            (lengths_far, lengths),
            (prefix_far, prefix),
            (weight_far, weight),
            (named_far, named),
        ),
        done,
    )
    count, model = normed.shape
    samples = count // fresh_count
    parts, part_rows, _ = flat.shape
    blocks = model // LANES
    loads[0].wait()
    wide[...] = tokens[...].astype(F32)
    for c in range(blocks):
        for i in range(fresh_count):
            ordered[c, pl.ds(i, samples, stride=fresh_count), :] = wide[
                pl.ds(fresh_count * c + i, samples, stride=fresh_count * blocks), :
            ]
    states = jnp.concatenate([ordered[c] for c in range(blocks)], axis=1)
    for part in range(parts):
        flat[part] = states[part * part_rows : (part + 1) * part_rows].astype(BF16)
    loads[1].wait()
    rows = normalize(states, gains[0:1, :]).astype(BF16)
    normed[...] = rows
    loads[2].wait()
    loads[3].wait()
    row_id = lax.broadcasted_iota(jnp.int32, (count, 1), 0)
    position = row_id % fresh_count + prefix[lax.axis_index("req")]
    for sample in range(samples):
        position = position + jnp.where(row_id // fresh_count == sample, lengths[0, sample], 0)
    within = lane_iota((1, LANES)) % HEAD_DIM
    pair = (within % (HEAD_DIM // 2)).astype(F32)
    frequency = jnp.exp(pair * (-math.log(ROPE_BASE) / (HEAD_DIM // 2)))
    angles = position.astype(F32) * frequency
    cosine[...] = jnp.cos(angles)
    turn = jnp.sin(angles)
    sine[...] = jnp.where(within < HEAD_DIM // 2, -turn, turn)
    loads[4].wait()
    made = dot(rows, weight[...])
    pieces = []
    for group in swap_halves(made[:, :LANES], made[:, LANES:]):
        pieces.append(rotate(group, cosine[...], sine[...]).astype(BF16).astype(F32) * 0.125)
    packed = []
    for part in range(parts):
        for piece in pieces:
            packed.append(piece[part * part_rows : (part + 1) * part_rows])
    loads[5].wait()
    routed = named[...].astype(F32)
    packed.append(
        jnp.concatenate(
            [routed, jnp.zeros((routed.shape[0], LANES - routed.shape[1]), F32)], axis=1
        )
    )
    packed = jnp.concatenate(packed, axis=0).astype(BF16)
    message[...] = packed


def split_pages_kernel(source, out, wide):
    count, double, _ = source.shape
    half = double // 2
    wide[...] = source[...].astype(F32).reshape(count * double, LANES)
    keys = wide[pl.ds(0, count * half, stride=2), :].astype(BF16)
    values = wide[pl.ds(1, count * half, stride=2), :].astype(BF16)
    out[:, :half, :] = keys.reshape(count, half, LANES)
    out[:, half:, :] = values.reshape(count, half, LANES)


def pack_message(numer, top, total):
    high = total.astype(BF16).astype(F32)
    section = (lane_iota((8, LANES)) % HEAD_DIM) // 8
    stats = jnp.zeros((8, LANES), F32)
    for group in range(2):
        span = slice(group * 8, (group + 1) * 8)
        for k, kind in enumerate((top, high, total - high)):
            stats = jnp.where(section == 3 * group + k, kind[span], stats)
    return jnp.concatenate([numer, stats], axis=0).astype(BF16)


def unpack_message(block):
    block = block.astype(F32)
    stats = block[..., 16:24, :]
    low = lane_iota(stats.shape) < HEAD_DIM

    def pick(section):
        lane = section * 8
        return jnp.where(
            low, stats[..., lane : lane + 1], stats[..., HEAD_DIM + lane : HEAD_DIM + lane + 1]
        )

    top = jnp.concatenate([pick(0), pick(3)], axis=-2)
    total = jnp.concatenate([pick(1) + pick(2), pick(4) + pick(5)], axis=-2)
    return block[..., 0:16, :], top, total


def tail_kernel(
    fresh_count,
    lengths_far,
    query_far,
    normed_far,
    cosine_far,
    sine_far,
    weight_far,
    cache_far,
    out,
    lengths,
    query,
    normed,
    cosine,
    sine,
    weight,
    cache,
    load,
    done,
):
    tokens = normed.shape[0]
    samples, width, _ = cache.shape
    parts = out.shape[0]
    per_part = samples // parts
    loads = load_all(
        (
            (normed_far, normed),
            (weight_far, weight),
            (cosine_far, cosine),
            (sine_far, sine),
            (query_far.at[pl.ds(0, parts * 16)], query),
            (lengths_far, lengths),
        ),
        load,
    )
    spans = [pl.ds(part * per_part, per_part) for part in range(parts)]
    blocks = load_all([(cache_far.at[span], cache.at[span]) for span in spans], done)
    spread = (
        lax.broadcasted_iota(jnp.int32, (LANES, 2 * LANES), 1)
        == 2 * lax.broadcasted_iota(jnp.int32, (LANES, 2 * LANES), 0)
    ).astype(BF16)
    loads[0].wait()
    rows = normed[...]
    widened = jnp.concatenate(
        [dot(rows[:, c : c + LANES], spread) for c in range(0, rows.shape[1], LANES)], axis=1
    )
    both = jnp.concatenate([widened, pltpu.roll(widened, 1, 1)], axis=0).astype(BF16)
    for copy in loads[1:]:
        copy.wait()
    made = dot(both, weight[...])
    key_new = rotate(made[:tokens], cosine[...], sine[...]).astype(BF16)
    value_new = made[tokens:].astype(BF16)
    low = lane_iota((16, LANES)) < HEAD_DIM
    row_id = lax.broadcasted_iota(jnp.int32, (parts * 32, 1), 0)
    row_sample = (row_id // 32) * per_part + (row_id % 8) // fresh_count
    row_fresh = row_id % fresh_count
    part_sample = row_sample[:32]
    wide = [by_head(query[part * 16 : (part + 1) * 16, :], low) for part in range(parts)]
    length = jnp.zeros((parts * 32, 1), jnp.int32)
    for sample in range(samples):
        length = jnp.where(row_sample == sample, lengths[0, sample], length)
    fresh = dot_t(jnp.concatenate(wide, axis=0), key_new)
    token_id = lane_iota(fresh.shape)
    fresh_seen = (token_id // fresh_count == row_sample) & (token_id % fresh_count <= row_fresh)
    fresh = jnp.where(fresh_seen, fresh, LOWEST)
    for copy in blocks:
        copy.wait()
    beside = []
    scores = []
    for part in range(parts):
        placed = [
            jnp.where(part_sample == a, wide[part], jnp.zeros_like(wide[part]))
            for a in range(per_part)
        ]
        beside.append(
            jnp.concatenate([cache[part * per_part + a] for a in range(per_part)], axis=1)
        )
        scores.append(dot_t(jnp.concatenate(placed, axis=1), beside[part]))
    scores = jnp.concatenate(scores, axis=0)
    column = lane_iota(scores.shape)
    scores = jnp.where((column % 2 == 0) & (column < 2 * length), scores, LOWEST)
    peak = jnp.maximum(
        jnp.max(scores, axis=1, keepdims=True), jnp.max(fresh, axis=1, keepdims=True)
    )
    peak = peak.astype(BF16).astype(F32)
    weights = jnp.exp(scores - peak)
    fresh_weights = jnp.exp(fresh - peak)
    amount = jnp.sum(weights, axis=1, keepdims=True) + jnp.sum(fresh_weights, axis=1, keepdims=True)
    shifted = pltpu.roll(weights, 1, 1).astype(BF16)
    fresh_part = dot(fresh_weights.astype(BF16), value_new)
    every = [dot(shifted[part * 32 : (part + 1) * 32], beside[part]) for part in range(parts)]
    for part in range(parts):
        mixed = every[part][:, :LANES]
        for a in range(1, per_part):
            mixed = jnp.where(part_sample == a, every[part][:, a * LANES : (a + 1) * LANES], mixed)
        first = slice(part * 32, part * 32 + 16)
        second = slice(part * 32 + 16, part * 32 + 32)
        mixed = mixed + fresh_part[part * 32 : (part + 1) * 32]
        out[part] = pack_message(
            jnp.where(low, mixed[:16], mixed[16:]),
            jnp.where(low, peak[first], peak[second]),
            jnp.where(low, amount[first], amount[second]),
        )


def stack_kernel(*refs):
    *blocks, out = refs
    for k, block in enumerate(blocks):
        out[k] = block[...]


def page_kernel(
    slot_cap, homes, pages, lengths, cache, tail, *refs
):
    *blocks, out, named, query, slots, counts = refs
    requests = query.shape[0]
    parts = tail.shape[0]
    pool = cache.shape[0]
    page_size = cache.shape[1] // 2
    rows = parts * 16
    me = lax.axis_index("req")
    base = me * pool
    tail_numer, tail_top, tail_total = [
        kind.reshape(rows, LANES) for kind in unpack_message(tail[...])
    ]
    if len(blocks) == 1:
        query[...] = blocks[0][...]
    else:
        for n, block in enumerate(blocks):
            for k in range(block.shape[0]):
                query[me ^ (block.shape[0] * n + k)] = block[k]
    named[...] = query[:, rows:, :]

    def clear(r, carry):
        counts[r] = 0
        for j in range(slot_cap):
            slots[r * slot_cap + j] = -1
        return carry

    lax.fori_loop(0, requests, clear, 0)

    def assign(v, carry):
        r = homes[base + v]
        rank = counts[r]
        slots[r * slot_cap + rank] = v
        counts[r] = rank + 1
        return carry

    lax.fori_loop(0, pool, assign, 0)

    low = lane_iota((rows, LANES)) < HEAD_DIM
    column = lane_iota((2 * rows, page_size))

    def finish(r, mixed, peak, amount):
        own = r == me
        top = jnp.where(low, peak[:rows], peak[rows:])
        joint = jnp.maximum(top, jnp.where(own, tail_top, FLOOR))
        here = jnp.exp(top - joint)
        there = jnp.where(own, jnp.exp(tail_top - joint), 0.0)
        numer = jnp.where(low, mixed[:rows], mixed[rows:]) * here + tail_numer * there
        total = jnp.where(low, amount[:rows], amount[rows:]) * here + tail_total * there
        for part in range(parts):
            span = slice(part * 16, (part + 1) * 16)
            out[r * parts + part] = pack_message(numer[span], joint[span], total[span])

    def gather(first, count):
        wides = []
        keys = []
        values = []
        limits = []
        for k in range(count):
            r = first + k
            wide = by_head(query[r, 0:rows, :], low)
            zero = jnp.zeros_like(wide)
            wides.append(jnp.concatenate([wide if c == k else zero for c in range(count)], axis=1))
            own_keys = []
            own_values = []
            own_limits = []
            for j in range(slot_cap):
                slot = slots[r * slot_cap + j]
                safe = jnp.maximum(slot, 0)
                own_limits.append(
                    jnp.where(slot >= 0, lengths[r] - pages[base + safe] * page_size, 0)
                )
                own_keys.append(cache[safe, :page_size, :])
                own_values.append(cache[safe, page_size:, :])
            keys.append(jnp.concatenate(own_keys, axis=0))
            values.append(jnp.concatenate(own_values, axis=0))
            limits.append(own_limits)
        scores = dot_t(jnp.concatenate(wides, axis=0), jnp.concatenate(keys, axis=1))
        return scores, jnp.concatenate(values, axis=1), limits

    def weigh(scores, limits):
        all_weights = []
        stats = []
        for k in range(len(limits)):
            own = scores[k * 2 * rows : (k + 1) * 2 * rows]
            own = [
                jnp.where(
                    column < limits[k][j], own[:, j * page_size : (j + 1) * page_size], LOWEST
                )
                for j in range(slot_cap)
            ]
            peak = jnp.max(functools.reduce(jnp.maximum, own), axis=1, keepdims=True)
            peak = jnp.maximum(peak, FLOOR).astype(BF16).astype(F32)
            weights = [jnp.exp(one - peak) for one in own]
            amount = jnp.sum(functools.reduce(jnp.add, weights), axis=1, keepdims=True)
            all_weights.append(jnp.concatenate([one.astype(BF16) for one in weights], axis=1))
            stats.append((peak, amount))
        return jnp.concatenate(all_weights, axis=0), stats

    pair = 2 if requests % 2 == 0 else 1
    step = 8 if requests % 8 == 0 else pair

    def several(g, carry):
        firsts = [g * step + k for k in range(0, step, pair)]
        gathered = [gather(first, pair) for first in firsts]
        weighed = [weigh(scores, limits) for scores, _, limits in gathered]
        mixed = [dot(weighed[n][0], gathered[n][1]) for n in range(len(firsts))]
        for n, first in enumerate(firsts):
            for k in range(pair):
                own = mixed[n][k * 2 * rows : (k + 1) * 2 * rows, k * LANES : (k + 1) * LANES]
                finish(first + k, own, *weighed[n][1][k])
        return carry

    if requests == step:
        several(0, 0)
    else:
        lax.fori_loop(0, requests // step, several, 0)


def merge_kernel(arrived, tokens, gains, *refs):
    parts = arrived.shape[1]
    weights = refs[:parts]
    out, residual, columns = refs[parts:]
    part = my_part()
    for t in range(parts):
        numer, top, total = unpack_message(arrived[:, t])
        factor = jnp.exp(top - jnp.max(top, axis=0, keepdims=True))
        attended = jnp.sum(factor * numer, axis=0) / jnp.sum(factor * total, axis=0)
        columns[t] = jnp.concatenate(swap_halves(attended[0:8], attended[8:16]), axis=1)
    projected = None
    for flip in range(parts):
        one = dot(columns[part ^ flip].astype(BF16), weights[flip][...])
        projected = one if projected is None else projected + one
    rows = (tokens[part].astype(F32) + projected).astype(BF16).astype(F32)
    residual[...] = rows
    normed = normalize(rows, gains[1:2, :])
    half = normed.shape[1] // 2
    message = jnp.concatenate([normed[:, :half], normed[:, half:]], axis=0).astype(BF16)
    for n in range(out.shape[0]):
        out[n] = message


def prepare_kernel(first_far, out, near, wide, done):
    local, double, _ = near.shape
    depth = double // 2
    loads = load_all([(first_far.at[e], near.at[e]) for e in range(local)], done)

    for e in range(local):
        loads[e].wait()
        buffer = wide.at[e % 2]
        buffer[...] = near[e].astype(F32)
        out[e, :, :LANES] = buffer[pl.ds(0, depth, stride=2), :].astype(BF16)
        out[e, :, LANES:] = buffer[pl.ds(1, depth, stride=2), :].astype(BF16)


def keep_kernel(*refs):
    del refs


def names_kernel(part_rows, fresh_count, packed, out):
    requests, span, _ = packed.shape
    experts = out.shape[1]
    halves = out.shape[0] // (requests * part_rows)
    top = span // fresh_count
    row = lax.broadcasted_iota(jnp.int32, (halves * part_rows, LANES), 0)
    token = (row // part_rows) * 2 * part_rows + lax.axis_index("tp_side") * part_rows + row % part_rows
    pick = (lane_iota(row.shape) == token // fresh_count).astype(BF16)
    found = jnp.concatenate([dot_t(pick, packed[r]) for r in range(requests)], axis=0)
    fresh = lax.broadcasted_iota(jnp.int32, (found.shape[0], 1), 0) % fresh_count
    chosen = found[:, :top]
    for i in range(1, fresh_count):
        chosen = jnp.where(fresh == i, found[:, i * top : (i + 1) * top], chosen)
    lanes = lane_iota(out.shape).astype(F32)
    mask = jnp.zeros(out.shape, F32)
    for k in range(top):
        mask = jnp.where(chosen[:, k : k + 1] == lanes, 1.0, mask)
    out[...] = mask


def expert_kernel(
    copies,
    part_rows,
    group,
    arrived,
    mask,
    router,
    first,
    first_other,
    second,
    second_other,
    out,
):
    team, _, half = arrived.shape
    local = first.shape[0]
    expert_count = router.shape[0]
    count = group * part_rows
    me = lax.axis_index("req")

    def one_block(block):
        here = pl.ds(block * group, group)
        states = arrived[here].astype(F32)
        states = jnp.concatenate(
            [
                states[:, :part_rows].reshape(count, half),
                states[:, part_rows:].reshape(count, half),
            ],
            axis=1,
        ).astype(BF16)
        logits = dot_t(states, router[...])
        span = pl.ds(pl.multiple_of(block * count, count), count)
        chosen = jnp.where(mask[span, :] > 0.5, logits, LOWEST)
        shares = jnp.exp(chosen - jnp.max(chosen, axis=1, keepdims=True))
        gates = shares / jnp.sum(shares, axis=1, keepdims=True)
        lanes = lane_iota(gates.shape)
        row = lax.broadcasted_iota(jnp.int32, (count, 1), 0)
        row_request = (block * group + row // part_rows) // 2
        weights = []
        for e in range(local):
            slot = me * local + e
            gate = jnp.sum(
                jnp.where(lanes == lax.rem(slot, expert_count), gates, 0.0), axis=1, keepdims=True
            )
            if copies > 1:
                copy = lax.div(slot, expert_count)
                gate = jnp.where(lax.rem(row_request, copies) == copy, gate, 0.0)
            weights.append(gate)
        mixed = None
        for up, down in ((first, second), (first_other, second_other)):
            pieces = []
            for e in range(local):
                wide = dot(states, up[e])
                value = wide[:, :LANES]
                other = wide[:, LANES:]
                hidden = (value / (1.0 + jnp.exp(-value)) * other).astype(BF16).astype(F32)
                pieces.append((hidden * weights[e]).astype(BF16))
            part = dot(jnp.concatenate(pieces, axis=1), down[...])
            mixed = part if mixed is None else mixed + part
        out[here] = jnp.concatenate(
            [
                mixed[:, :half].reshape(group, part_rows, half),
                mixed[:, half:].reshape(group, part_rows, half),
            ],
            axis=1,
        ).astype(BF16)

    if team == group:
        one_block(0)
    else:

        def body(block, carry):
            one_block(block)
            return carry

        lax.fori_loop(0, team // group, body, 0)


def finish_kernel(arrived, residual, out):
    pairs = arrived.shape[1]
    half = arrived.shape[3]
    kept = residual[...]
    kept = jnp.concatenate([kept[:, :half], kept[:, half:]], axis=0)
    mine = lax.axis_index("tp_pair")
    for pair in range(pairs):
        mixed = jnp.sum(arrived[:, pair].astype(F32), axis=0)
        out[pair] = (mixed + jnp.where(mine == pair, kept, 0.0)).astype(BF16)


def score_kernel(fresh_count, *refs):
    *arrived, gains, weight, layer, score, ordered, wide = refs
    pairs, double, _ = arrived[0].shape
    rows = double // 2
    blocks, tokens, _ = ordered.shape
    samples = tokens // fresh_count
    side = lax.axis_index("tp_side")
    for flip in range(2):
        for pair in range(pairs):
            state = arrived[flip][pair].astype(F32)
            for other in range(flip + 2, len(arrived), 2):
                state = state + arrived[other][pair].astype(F32)
            spot = pl.ds(pl.multiple_of((2 * pair + (side ^ flip)) * rows, rows), rows)
            for c in range(blocks // 2):
                ordered[c, spot, :] = state[:rows, c * LANES : (c + 1) * LANES]
                ordered[blocks // 2 + c, spot, :] = state[rows:, c * LANES : (c + 1) * LANES]
    for c in range(blocks):
        for i in range(fresh_count):
            wide[pl.ds(fresh_count * c + i, samples, stride=fresh_count * blocks), :] = ordered[
                c, pl.ds(i, samples, stride=fresh_count), :
            ]
    layer[...] = wide[...].astype(BF16)
    states = jnp.concatenate([ordered[c] for c in range(blocks)], axis=1)
    states = states.astype(BF16).astype(F32)
    final = normalize(states, gains[2:3, :])
    scored = jnp.sum(final * weight[...], axis=1, keepdims=True)
    row = lax.broadcasted_iota(jnp.int32, (tokens, samples), 0)
    here = row // fresh_count == lane_iota(row.shape)
    for i in range(fresh_count):
        score[i : i + 1, :] = jnp.sum(
            jnp.where(here & (row % fresh_count == i), scored, 0.0), axis=0, keepdims=True
        )


def shards(
    tokens_new,
    prefix_len,
    tail_len,
    pool_home,
    pool_page,
    slot_page_cache,
    tail_cache,
    routes,
    norm_gains,
    query_weight,
    key_value_weight,
    out_weight,
    router,
    expert_in,
    expert_out,
    score_weight,
):
    req_count = lax.axis_size("req")
    pairs = lax.axis_size("tp_pair")
    parts = 2 * pairs
    _, samples, fresh_count, model = tokens_new.shape
    tokens = samples * fresh_count
    part_rows = tokens // parts
    pool = slot_page_cache.shape[0]
    page_size = slot_page_cache.shape[1]
    slot_cap = max(1, pool // req_count)
    tail_count = tail_cache.shape[2]
    local = expert_in.shape[0]
    expert_count = router.shape[1]
    copies = local * req_count // expert_count
    everyone = req_count * parts
    rows = 2 * tokens
    blocks = model // LANES
    top = routes.shape[3]
    half = model // 2
    team = req_count * pairs

    whole = ("tp_pair", "tp_side")
    flips = [[(t, t ^ flip) for t in range(parts)] for flip in range(parts)]
    first_raw = expert_in.reshape(local, 2 * model, LANES)
    second_raw = expert_out.reshape(local * LANES, model)


    token_bytes = tokens_new.reshape(samples, fresh_count, blocks, LANES)
    token_bytes = token_bytes.transpose(0, 2, 1, 3).reshape(tokens * blocks, LANES)
    route_bytes = routes[0].transpose(1, 2, 0).reshape(fresh_count * top, samples)

    message, flat, normed, cosine, sine = pl.pallas_call(
        functools.partial(query_kernel, fresh_count),
        out_shape=(
            jax.ShapeDtypeStruct((rows + fresh_count * top, LANES), BF16),
            jax.ShapeDtypeStruct((parts, part_rows, model), BF16),
            jax.ShapeDtypeStruct((tokens, model), BF16),
            jax.ShapeDtypeStruct((tokens, LANES), F32),
            jax.ShapeDtypeStruct((tokens, LANES), F32),
        ),
        in_specs=[HBM] * 6,
        out_specs=(VMEM,) * 5,
        scratch_shapes=[
            pltpu.SMEM(prefix_len.shape, jnp.int32),
            pltpu.SMEM(tail_len.shape, jnp.int32),
            pltpu.VMEM(token_bytes.shape, BF16),
            pltpu.VMEM(route_bytes.shape, jnp.int32),
            pltpu.VMEM(norm_gains.shape, F32),
            pltpu.VMEM(query_weight.shape, BF16),
            pltpu.VMEM((tokens * blocks, LANES), F32),
            pltpu.VMEM((blocks, tokens, LANES), F32),
            pltpu.SemaphoreType.DMA((6,)),
        ],
        compiler_params=params(HOLD_MIB),
        name="query",
    )(prefix_len, tail_len, token_bytes, route_bytes, norm_gains, query_weight)

    key_value_rows = key_value_weight.reshape(2 * model, LANES)
    tail_rows = tail_cache.reshape(samples, 2 * tail_count, LANES)
    page_rows = slot_page_cache.reshape(pool, 2 * page_size, LANES)
    later, message = lax.optimization_barrier((out_weight, message))
    across = [lax.ppermute(later, whole, flips[flip]) for flip in range(2, parts, 2)]
    beside = lax.ppermute(later, whole, flips[1])
    if req_count == 8:
        xor = [[(d, d ^ flip) for d in range(req_count)] for flip in range(req_count)]
        near = lax.ppermute(message, "req", xor[1])
        page_rows, message = lax.optimization_barrier((page_rows, message))
    step = 8 if pool % 8 == 0 else 1
    split_pages = pl.pallas_call(
        split_pages_kernel,
        grid=(pool // step,),
        out_shape=jax.ShapeDtypeStruct((pool, 2 * page_size, LANES), BF16),
        in_specs=[pl.BlockSpec((step, 2 * page_size, LANES), lambda v: (v, 0, 0))],
        out_specs=pl.BlockSpec((step, 2 * page_size, LANES), lambda v: (v, 0, 0)),
        scratch_shapes=[pltpu.VMEM((step * 2 * page_size, LANES), F32)],
        compiler_params=params(8),
        cost_estimate=cost(1e6, 4e6),
        name="split_pages",
    )(page_rows)

    if req_count == 8:
        split_pages, near = lax.optimization_barrier((split_pages, near))
        stacked = pl.pallas_call(
            stack_kernel,
            out_shape=jax.ShapeDtypeStruct((2,) + message.shape, BF16),
            in_specs=[VMEM] * 2,
            out_specs=VMEM,
            compiler_params=params(8),
            name="stack",
        )(message, near)
        normed, stacked = lax.optimization_barrier((normed, stacked))
        first_all = [stacked] + [lax.ppermute(stacked, "req", xor[flip]) for flip in (2, 4, 6)]
    else:
        copies_out = jnp.broadcast_to(message[None], (req_count,) + message.shape)
        first_all = [
            lax.all_to_all(copies_out, "req", split_axis=0, concat_axis=0, tiled=True)
        ]
    tail_inputs = (message, normed, cosine, sine)
    tail = pl.pallas_call(
        functools.partial(tail_kernel, fresh_count),
        out_shape=jax.ShapeDtypeStruct((parts, 24, LANES), BF16),
        in_specs=[HBM] * 7,
        out_specs=VMEM,
        scratch_shapes=[
            pltpu.SMEM(tail_len.shape, jnp.int32),
            pltpu.VMEM((rows, LANES), BF16),
            pltpu.VMEM(normed.shape, BF16),
            pltpu.VMEM(cosine.shape, F32),
            pltpu.VMEM(sine.shape, F32),
            pltpu.VMEM(key_value_rows.shape, BF16),
            pltpu.VMEM(tail_rows.shape, BF16),
            pltpu.SemaphoreType.DMA((6,)),
            pltpu.SemaphoreType.DMA((parts,)),
        ],
        compiler_params=params(HOLD_MIB),
        cost_estimate=cost(2e9, 5e6),
        name="tail",
    )(tail_len, *tail_inputs, key_value_rows, tail_rows)

    split_pages, beside, tail = lax.optimization_barrier((split_pages, beside, tail))

    partial, named = pl.pallas_call(
        functools.partial(page_kernel, slot_cap),
        out_shape=(
            jax.ShapeDtypeStruct((everyone, 24, LANES), BF16),
            jax.ShapeDtypeStruct((req_count, fresh_count * top, LANES), BF16),
        ),
        in_specs=[SMEM] * 3 + [VMEM] * (2 + len(first_all)),
        out_specs=(VMEM, VMEM),
        scratch_shapes=[
            pltpu.VMEM((req_count,) + message.shape, BF16),
            pltpu.SMEM((req_count * slot_cap,), jnp.int32),
            pltpu.SMEM((req_count,), jnp.int32),
        ],
        compiler_params=params(12),
        cost_estimate=cost(2e9, 5e6),
        name="pages",
    )(pool_home, pool_page, prefix_len, split_pages, tail, *first_all)
    arrived = lax.all_to_all(partial, ("req",) + whole, split_axis=0, concat_axis=0, tiled=True)

    first_raw, across, _ = lax.optimization_barrier((first_raw, across, partial))
    projects = [out_weight, beside]
    for block in across:
        projects += [block, lax.ppermute(block, whole, flips[1])]
    first = pl.pallas_call(
        prepare_kernel,
        out_shape=jax.ShapeDtypeStruct((local, model, 2 * LANES), BF16),
        in_specs=[HBM],
        out_specs=VMEM,
        scratch_shapes=[
            pltpu.VMEM(first_raw.shape, BF16),
            pltpu.VMEM((2, 2 * model, LANES), F32),
            pltpu.SemaphoreType.DMA((local,)),
        ],
        compiler_params=params(HOLD_MIB),
        cost_estimate=cost(2e10, 8e6),
        name="prepare",
    )(first_raw)
    named, first, projects = lax.optimization_barrier((named, first, projects))
    mask = pl.pallas_call(
        functools.partial(names_kernel, part_rows, fresh_count),
        out_shape=jax.ShapeDtypeStruct((team * part_rows, expert_count), F32),
        in_specs=[VMEM],
        out_specs=VMEM,
        compiler_params=params(8),
        cost_estimate=cost(1e6, 1e6),
        name="names",
    )(named)
    arrived, first, mask = lax.optimization_barrier((arrived, first, mask))
    first = pl.pallas_call(
        keep_kernel,
        out_shape=jax.ShapeDtypeStruct(first.shape, BF16),
        in_specs=[HBM],
        out_specs=HBM,
        input_output_aliases={0: 0},
        compiler_params=params(HOLD_MIB),
        name="keep",
    )(first)
    first_other = lax.ppermute(first, whole, flips[1])

    message, residual = pl.pallas_call(
        merge_kernel,
        out_shape=(
            jax.ShapeDtypeStruct((team, 2 * part_rows, half), BF16),
            jax.ShapeDtypeStruct((part_rows, model), F32),
        ),
        in_specs=[VMEM] * (3 + parts),
        out_specs=(VMEM, VMEM),
        scratch_shapes=[pltpu.VMEM((parts, part_rows, model // parts), F32)],
        compiler_params=params(12),
        name="merge",
    )(arrived.reshape(req_count, parts, 24, LANES), flat, norm_gains, *projects)
    message, second_sent = lax.optimization_barrier((message, second_raw))
    second_other = lax.ppermute(second_sent, whole, flips[1])
    states = lax.all_to_all(message, ("req", "tp_pair"), split_axis=0, concat_axis=0, tiled=True)

    expert_inputs = (
        states,
        mask,
        router.T,
        first,
        first_other,
        second_raw,
        second_other,
    )
    mixed = pl.pallas_call(
        functools.partial(expert_kernel, copies, part_rows, min(req_count, 8) * pairs),
        out_shape=jax.ShapeDtypeStruct((team, 2 * part_rows, half), BF16),
        in_specs=[VMEM] * 7,
        out_specs=VMEM,
        compiler_params=params(16),
        name="experts",
    )(*expert_inputs)
    mixed = mixed.reshape(req_count, pairs, 2 * part_rows, half)
    mixed = lax.all_to_all(mixed, "req", split_axis=0, concat_axis=0, tiled=True)

    finished = pl.pallas_call(
        finish_kernel,
        out_shape=jax.ShapeDtypeStruct((pairs, 2 * part_rows, half), BF16),
        in_specs=[VMEM, VMEM],
        out_specs=VMEM,
        compiler_params=params(8),
        name="finish",
    )(mixed, residual)
    gathered = [finished] + [
        lax.ppermute(finished, whole, flips[flip]) for flip in range(1, parts)
    ]

    layer, score = pl.pallas_call(
        functools.partial(score_kernel, fresh_count),
        out_shape=(
            jax.ShapeDtypeStruct((tokens * blocks, LANES), BF16),
            jax.ShapeDtypeStruct((fresh_count, samples), F32),
        ),
        in_specs=[VMEM] * (parts + 2),
        out_specs=(VMEM, VMEM),
        scratch_shapes=[
            pltpu.VMEM((blocks, tokens, LANES), F32),
            pltpu.VMEM((tokens * blocks, LANES), F32),
        ],
        compiler_params=params(8),
        name="score",
    )(*gathered, norm_gains, score_weight.reshape(1, model))
    layer = layer.reshape(samples, blocks, fresh_count, LANES).transpose(0, 2, 1, 3)
    return (
        layer.reshape(1, samples, fresh_count, model),
        score.T.reshape(1, samples, fresh_count),
    )


def solution(mesh):
    tp = ("tp_pair", "tp_side")
    req_count, parts = mesh.devices.shape
    mesh = jax.sharding.Mesh(
        mesh.devices.reshape(req_count, parts // 2, 2), ("req", "tp_pair", "tp_side")
    )
    placed = (
        P("req", None, None, None),
        P(),
        P("req", None),
        P(),
        P(),
        P("req", None, None, tp),
        P("req", None, None, None, tp),
        P("req", None, None, None),
        P(),
        P(None, tp),
        P(None, None, tp),
        P(tp, None),
        P(),
        P("req", None, None, tp),
        P("req", tp, None),
        P(),
    )
    return jax.shard_map(
        shards,
        mesh=mesh,
        in_specs=placed,
        out_specs=(P("req", None, None, None), P("req", None, None)),
        check_vma=False,
    )
```

```python
import functools
import math

import jax
import jax.numpy as jnp
from jax import lax
from jax.experimental import pallas as pl
from jax.experimental.pallas import tpu as pltpu
from jax.sharding import PartitionSpec as P

HEAD_DIM = 64
LANES = 128
EPSILON = 1e-05
ROPE_BASE = 10000.0
LOWEST = -1e30
FLOOR = -1e28
F32 = jnp.float32
BF16 = jnp.bfloat16
MIB = 1024 * 1024
HOLD_MIB = 56

VMEM = pl.BlockSpec(memory_space=pltpu.VMEM)
SMEM = pl.BlockSpec(memory_space=pltpu.SMEM)
HBM = pl.BlockSpec(memory_space=pltpu.HBM)
ANY = pl.BlockSpec(memory_space=pl.ANY)


def params(mib):
    return pltpu.CompilerParams(vmem_limit_bytes=mib * MIB)


def cost(flops, moved):
    return pl.CostEstimate(flops=int(flops), bytes_accessed=int(moved), transcendentals=0)


def dot(left, right):
    return jnp.dot(left, right, preferred_element_type=F32)


def dot_t(left, right):
    return lax.dot_general(left, right, (((1,), (1,)), ((), ())), preferred_element_type=F32)


def my_part():
    return lax.axis_index("tp_pair") * 2 + lax.axis_index("tp_side")


def load_all(pairs, done):
    copies = [pltpu.make_async_copy(far, near, done.at[k]) for k, (far, near) in enumerate(pairs)]
    for copy in copies:
        copy.start()
    return copies


def lane_iota(shape):
    return lax.broadcasted_iota(jnp.int32, shape, len(shape) - 1)


def normalize(x, gain):
    return x * lax.rsqrt(jnp.mean(x * x, axis=-1, keepdims=True) + EPSILON) * gain


def rotate(x, cosine, sine):
    lanes = lane_iota(x.shape)
    partner = jnp.where(lanes % HEAD_DIM < HEAD_DIM // 2, pltpu.roll(x, 96, 1), pltpu.roll(x, 32, 1))
    return x * cosine + partner * sine


def by_head(packed, low):
    zero = jnp.zeros_like(packed)
    return jnp.concatenate([jnp.where(low, packed, zero), jnp.where(low, zero, packed)], axis=0)


def swap_halves(first, second):
    low = lane_iota(first.shape) < HEAD_DIM
    return (
        jnp.where(low, first, pltpu.roll(second, HEAD_DIM, 1)),
        jnp.where(low, pltpu.roll(first, HEAD_DIM, 1), second),
    )


def query_kernel(
    fresh_count,
    prefix_far,
    lengths_far,
    tokens_far,
    named_far,
    gains_far,
    weight_far,
    message,
    flat,
    normed,
    cosine,
    sine,
    prefix,
    lengths,
    tokens,
    named,
    gains,
    weight,
    wide,
    ordered,
    done,
):
    loads = load_all(
        (
            (tokens_far, tokens),
            (gains_far, gains),
            (lengths_far, lengths),
            (prefix_far, prefix),
            (weight_far, weight),
            (named_far, named),
        ),
        done,
    )
    count, model = normed.shape
    samples = count // fresh_count
    parts, part_rows, _ = flat.shape
    blocks = model // LANES
    loads[0].wait()
    wide[...] = tokens[...].astype(F32)
    for c in range(blocks):
        for i in range(fresh_count):
            ordered[c, pl.ds(i, samples, stride=fresh_count), :] = wide[
                pl.ds(fresh_count * c + i, samples, stride=fresh_count * blocks), :
            ]
    states = jnp.concatenate([ordered[c] for c in range(blocks)], axis=1)
    for part in range(parts):
        flat[part] = states[part * part_rows : (part + 1) * part_rows].astype(BF16)
    loads[1].wait()
    rows = normalize(states, gains[0:1, :]).astype(BF16)
    normed[...] = rows
    loads[2].wait()
    loads[3].wait()
    row_id = lax.broadcasted_iota(jnp.int32, (count, 1), 0)
    position = row_id % fresh_count + prefix[lax.axis_index("req")]
    for sample in range(samples):
        position = position + jnp.where(row_id // fresh_count == sample, lengths[0, sample], 0)
    within = lane_iota((1, LANES)) % HEAD_DIM
    pair = (within % (HEAD_DIM // 2)).astype(F32)
    frequency = jnp.exp(pair * (-math.log(ROPE_BASE) / (HEAD_DIM // 2)))
    angles = position.astype(F32) * frequency
    cosine[...] = jnp.cos(angles)
    turn = jnp.sin(angles)
    sine[...] = jnp.where(within < HEAD_DIM // 2, -turn, turn)
    loads[4].wait()
    made = dot(rows, weight[...])
    pieces = []
    for group in swap_halves(made[:, :LANES], made[:, LANES:]):
        pieces.append(rotate(group, cosine[...], sine[...]).astype(BF16).astype(F32) * 0.125)
    packed = []
    for part in range(parts):
        for piece in pieces:
            packed.append(piece[part * part_rows : (part + 1) * part_rows])
    loads[5].wait()
    routed = named[...].astype(F32)
    packed.append(
        jnp.concatenate(
            [routed, jnp.zeros((routed.shape[0], LANES - routed.shape[1]), F32)], axis=1
        )
    )
    packed = jnp.concatenate(packed, axis=0).astype(BF16)
    for n in range(message.shape[0]):
        message[n] = packed


def split_pages_kernel(source, out, wide):
    count, double, _ = source.shape
    half = double // 2
    wide[...] = source[...].astype(F32).reshape(count * double, LANES)
    keys = wide[pl.ds(0, count * half, stride=2), :].astype(BF16)
    values = wide[pl.ds(1, count * half, stride=2), :].astype(BF16)
    out[:, :half, :] = keys.reshape(count, half, LANES)
    out[:, half:, :] = values.reshape(count, half, LANES)


def pack_message(numer, top, total):
    high = total.astype(BF16).astype(F32)
    section = (lane_iota((8, LANES)) % HEAD_DIM) // 8
    stats = jnp.zeros((8, LANES), F32)
    for group in range(2):
        span = slice(group * 8, (group + 1) * 8)
        for k, kind in enumerate((top, high, total - high)):
            stats = jnp.where(section == 3 * group + k, kind[span], stats)
    return jnp.concatenate([numer, stats], axis=0).astype(BF16)


def unpack_message(block):
    block = block.astype(F32)
    stats = block[..., 16:24, :]
    low = lane_iota(stats.shape) < HEAD_DIM

    def pick(section):
        lane = section * 8
        return jnp.where(
            low, stats[..., lane : lane + 1], stats[..., HEAD_DIM + lane : HEAD_DIM + lane + 1]
        )

    top = jnp.concatenate([pick(0), pick(3)], axis=-2)
    total = jnp.concatenate([pick(1) + pick(2), pick(4) + pick(5)], axis=-2)
    return block[..., 0:16, :], top, total


def tail_kernel(
    fresh_count,
    lengths_far,
    query_far,
    normed_far,
    cosine_far,
    sine_far,
    weight_far,
    cache_far,
    out,
    lengths,
    query,
    normed,
    cosine,
    sine,
    weight,
    cache,
    load,
    done,
):
    tokens = normed.shape[0]
    samples, width, _ = cache.shape
    parts = out.shape[0]
    per_part = samples // parts
    loads = load_all(
        (
            (normed_far, normed),
            (weight_far, weight),
            (cosine_far, cosine),
            (sine_far, sine),
            (query_far.at[0, pl.ds(0, parts * 16)], query),
            (lengths_far, lengths),
        ),
        load,
    )
    spans = [pl.ds(part * per_part, per_part) for part in range(parts)]
    blocks = load_all([(cache_far.at[span], cache.at[span]) for span in spans], done)
    spread = (
        lax.broadcasted_iota(jnp.int32, (LANES, 2 * LANES), 1)
        == 2 * lax.broadcasted_iota(jnp.int32, (LANES, 2 * LANES), 0)
    ).astype(BF16)
    loads[0].wait()
    rows = normed[...]
    widened = jnp.concatenate(
        [dot(rows[:, c : c + LANES], spread) for c in range(0, rows.shape[1], LANES)], axis=1
    )
    both = jnp.concatenate([widened, pltpu.roll(widened, 1, 1)], axis=0).astype(BF16)
    for copy in loads[1:]:
        copy.wait()
    made = dot(both, weight[...])
    key_new = rotate(made[:tokens], cosine[...], sine[...]).astype(BF16)
    value_new = made[tokens:].astype(BF16)
    low = lane_iota((16, LANES)) < HEAD_DIM
    row_id = lax.broadcasted_iota(jnp.int32, (parts * 32, 1), 0)
    row_sample = (row_id // 32) * per_part + (row_id % 8) // fresh_count
    row_fresh = row_id % fresh_count
    part_sample = row_sample[:32]
    wide = [by_head(query[part * 16 : (part + 1) * 16, :], low) for part in range(parts)]
    length = jnp.zeros((parts * 32, 1), jnp.int32)
    for sample in range(samples):
        length = jnp.where(row_sample == sample, lengths[0, sample], length)
    fresh = dot_t(jnp.concatenate(wide, axis=0), key_new)
    token_id = lane_iota(fresh.shape)
    fresh_seen = (token_id // fresh_count == row_sample) & (token_id % fresh_count <= row_fresh)
    fresh = jnp.where(fresh_seen, fresh, LOWEST)
    beside = []
    scores = []
    for part in range(parts):
        blocks[part].wait()
        placed = [
            jnp.where(part_sample == a, wide[part], jnp.zeros_like(wide[part]))
            for a in range(per_part)
        ]
        beside.append(
            jnp.concatenate([cache[part * per_part + a] for a in range(per_part)], axis=1)
        )
        scores.append(dot_t(jnp.concatenate(placed, axis=1), beside[part]))
    scores = jnp.concatenate(scores, axis=0)
    column = lane_iota(scores.shape)
    scores = jnp.where((column % 2 == 0) & (column < 2 * length), scores, LOWEST)
    peak = jnp.maximum(
        jnp.max(scores, axis=1, keepdims=True), jnp.max(fresh, axis=1, keepdims=True)
    )
    peak = peak.astype(BF16).astype(F32)
    weights = jnp.exp(scores - peak)
    fresh_weights = jnp.exp(fresh - peak)
    amount = jnp.sum(weights, axis=1, keepdims=True) + jnp.sum(fresh_weights, axis=1, keepdims=True)
    shifted = pltpu.roll(weights, 1, 1).astype(BF16)
    fresh_part = dot(fresh_weights.astype(BF16), value_new)
    every = [dot(shifted[part * 32 : (part + 1) * 32], beside[part]) for part in range(parts)]
    for part in range(parts):
        mixed = every[part][:, :LANES]
        for a in range(1, per_part):
            mixed = jnp.where(part_sample == a, every[part][:, a * LANES : (a + 1) * LANES], mixed)
        first = slice(part * 32, part * 32 + 16)
        second = slice(part * 32 + 16, part * 32 + 32)
        mixed = mixed + fresh_part[part * 32 : (part + 1) * 32]
        out[part] = pack_message(
            jnp.where(low, mixed[:16], mixed[16:]),
            jnp.where(low, peak[first], peak[second]),
            jnp.where(low, amount[first], amount[second]),
        )


def page_kernel(
    slot_cap, homes, pages, lengths, cache, tail, query, out, named, slots, counts
):
    requests = query.shape[0]
    parts = tail.shape[0]
    pool = cache.shape[0]
    page_size = cache.shape[1] // 2
    rows = parts * 16
    me = lax.axis_index("req")
    base = me * pool
    tail_numer, tail_top, tail_total = [
        kind.reshape(rows, LANES) for kind in unpack_message(tail[...])
    ]
    named[...] = query[:, rows:, :]

    def clear(r, carry):
        counts[r] = 0
        for j in range(slot_cap):
            slots[r * slot_cap + j] = -1
        return carry

    lax.fori_loop(0, requests, clear, 0)

    def assign(v, carry):
        r = homes[base + v]
        rank = counts[r]
        slots[r * slot_cap + rank] = v
        counts[r] = rank + 1
        return carry

    lax.fori_loop(0, pool, assign, 0)

    low = lane_iota((rows, LANES)) < HEAD_DIM
    column = lane_iota((2 * rows, page_size))

    def finish(r, mixed, peak, amount):
        own = r == me
        top = jnp.where(low, peak[:rows], peak[rows:])
        joint = jnp.maximum(top, jnp.where(own, tail_top, FLOOR))
        here = jnp.exp(top - joint)
        there = jnp.where(own, jnp.exp(tail_top - joint), 0.0)
        numer = jnp.where(low, mixed[:rows], mixed[rows:]) * here + tail_numer * there
        total = jnp.where(low, amount[:rows], amount[rows:]) * here + tail_total * there
        for part in range(parts):
            span = slice(part * 16, (part + 1) * 16)
            out[r * parts + part] = pack_message(numer[span], joint[span], total[span])

    def gather(first, count):
        wides = []
        keys = []
        values = []
        limits = []
        for k in range(count):
            r = first + k
            wide = by_head(query[r, 0:rows, :], low)
            zero = jnp.zeros_like(wide)
            wides.append(jnp.concatenate([wide if c == k else zero for c in range(count)], axis=1))
            own_keys = []
            own_values = []
            own_limits = []
            for j in range(slot_cap):
                slot = slots[r * slot_cap + j]
                safe = jnp.maximum(slot, 0)
                own_limits.append(
                    jnp.where(slot >= 0, lengths[r] - pages[base + safe] * page_size, 0)
                )
                own_keys.append(cache[safe, :page_size, :])
                own_values.append(cache[safe, page_size:, :])
            keys.append(jnp.concatenate(own_keys, axis=0))
            values.append(jnp.concatenate(own_values, axis=0))
            limits.append(own_limits)
        scores = dot_t(jnp.concatenate(wides, axis=0), jnp.concatenate(keys, axis=1))
        return scores, jnp.concatenate(values, axis=1), limits

    def weigh(scores, limits):
        all_weights = []
        stats = []
        for k in range(len(limits)):
            own = scores[k * 2 * rows : (k + 1) * 2 * rows]
            own = [
                jnp.where(
                    column < limits[k][j], own[:, j * page_size : (j + 1) * page_size], LOWEST
                )
                for j in range(slot_cap)
            ]
            peak = jnp.max(functools.reduce(jnp.maximum, own), axis=1, keepdims=True)
            peak = jnp.maximum(peak, FLOOR).astype(BF16).astype(F32)
            weights = [jnp.exp(one - peak) for one in own]
            amount = jnp.sum(functools.reduce(jnp.add, weights), axis=1, keepdims=True)
            all_weights.append(jnp.concatenate([one.astype(BF16) for one in weights], axis=1))
            stats.append((peak, amount))
        return jnp.concatenate(all_weights, axis=0), stats

    pair = 2 if requests % 2 == 0 else 1
    step = 8 if requests % 8 == 0 else pair

    def several(g, carry):
        firsts = [g * step + k for k in range(0, step, pair)]
        gathered = [gather(first, pair) for first in firsts]
        weighed = [weigh(scores, limits) for scores, _, limits in gathered]
        mixed = [dot(weighed[n][0], gathered[n][1]) for n in range(len(firsts))]
        for n, first in enumerate(firsts):
            for k in range(pair):
                own = mixed[n][k * 2 * rows : (k + 1) * 2 * rows, k * LANES : (k + 1) * LANES]
                finish(first + k, own, *weighed[n][1][k])
        return carry

    if requests == step:
        several(0, 0)
    else:
        lax.fori_loop(0, requests // step, several, 0)


def merge_kernel(arrived, tokens, gains, *refs):
    parts = arrived.shape[1]
    weights = refs[:parts]
    out, residual, columns = refs[parts:]
    part = my_part()
    for t in range(parts):
        numer, top, total = unpack_message(arrived[:, t])
        factor = jnp.exp(top - jnp.max(top, axis=0, keepdims=True))
        attended = jnp.sum(factor * numer, axis=0) / jnp.sum(factor * total, axis=0)
        columns[t] = jnp.concatenate(swap_halves(attended[0:8], attended[8:16]), axis=1)
    projected = None
    for flip in range(parts):
        one = dot(columns[part ^ flip].astype(BF16), weights[flip][...])
        projected = one if projected is None else projected + one
    rows = (tokens[part].astype(F32) + projected).astype(BF16).astype(F32)
    residual[...] = rows
    normed = normalize(rows, gains[1:2, :])
    half = normed.shape[1] // 2
    message = jnp.concatenate([normed[:, :half], normed[:, half:]], axis=0).astype(BF16)
    for n in range(out.shape[0]):
        out[n] = message


def prepare_kernel(first_far, out, near, wide, done):
    local, double, _ = near.shape
    depth = double // 2
    loads = load_all([(first_far.at[e], near.at[e]) for e in range(local)], done)

    for e in range(local):
        loads[e].wait()
        buffer = wide.at[e % 2]
        buffer[...] = near[e].astype(F32)
        out[e, :, :LANES] = buffer[pl.ds(0, depth, stride=2), :].astype(BF16)
        out[e, :, LANES:] = buffer[pl.ds(1, depth, stride=2), :].astype(BF16)


def keep_kernel(*refs):
    del refs


def names_kernel(part_rows, fresh_count, packed, out):
    requests, span, _ = packed.shape
    experts = out.shape[1]
    halves = out.shape[0] // (requests * part_rows)
    top = span // fresh_count
    row = lax.broadcasted_iota(jnp.int32, (halves * part_rows, LANES), 0)
    token = (row // part_rows) * 2 * part_rows + lax.axis_index("tp_side") * part_rows + row % part_rows
    pick = (lane_iota(row.shape) == token // fresh_count).astype(BF16)
    found = jnp.concatenate([dot_t(pick, packed[r]) for r in range(requests)], axis=0)
    fresh = lax.broadcasted_iota(jnp.int32, (found.shape[0], 1), 0) % fresh_count
    chosen = found[:, :top]
    for i in range(1, fresh_count):
        chosen = jnp.where(fresh == i, found[:, i * top : (i + 1) * top], chosen)
    lanes = lane_iota(out.shape).astype(F32)
    mask = jnp.zeros(out.shape, F32)
    for k in range(top):
        mask = jnp.where(chosen[:, k : k + 1] == lanes, 1.0, mask)
    out[...] = mask


def expert_kernel(
    copies,
    part_rows,
    group,
    arrived,
    mask,
    router,
    first,
    first_other,
    second,
    second_other,
    out,
):
    team, _, half = arrived.shape
    local = first.shape[0]
    expert_count = router.shape[0]
    count = group * part_rows
    me = lax.axis_index("req")

    def one_block(block):
        here = pl.ds(block * group, group)
        states = arrived[here].astype(F32)
        states = jnp.concatenate(
            [
                states[:, :part_rows].reshape(count, half),
                states[:, part_rows:].reshape(count, half),
            ],
            axis=1,
        ).astype(BF16)
        logits = dot_t(states, router[...])
        span = pl.ds(pl.multiple_of(block * count, count), count)
        chosen = jnp.where(mask[span, :] > 0.5, logits, LOWEST)
        shares = jnp.exp(chosen - jnp.max(chosen, axis=1, keepdims=True))
        gates = shares / jnp.sum(shares, axis=1, keepdims=True)
        lanes = lane_iota(gates.shape)
        row = lax.broadcasted_iota(jnp.int32, (count, 1), 0)
        row_request = (block * group + row // part_rows) // 2
        weights = []
        for e in range(local):
            slot = me * local + e
            gate = jnp.sum(
                jnp.where(lanes == lax.rem(slot, expert_count), gates, 0.0), axis=1, keepdims=True
            )
            if copies > 1:
                copy = lax.div(slot, expert_count)
                gate = jnp.where(lax.rem(row_request, copies) == copy, gate, 0.0)
            weights.append(gate)
        mixed = None
        for up, down in ((first, second), (first_other, second_other)):
            pieces = []
            for e in range(local):
                wide = dot(states, up[e])
                value = wide[:, :LANES]
                other = wide[:, LANES:]
                hidden = (value / (1.0 + jnp.exp(-value)) * other).astype(BF16).astype(F32)
                pieces.append((hidden * weights[e]).astype(BF16))
            part = dot(jnp.concatenate(pieces, axis=1), down[...])
            mixed = part if mixed is None else mixed + part
        out[here] = jnp.concatenate(
            [
                mixed[:, :half].reshape(group, part_rows, half),
                mixed[:, half:].reshape(group, part_rows, half),
            ],
            axis=1,
        ).astype(BF16)

    if team == group:
        one_block(0)
    else:

        def body(block, carry):
            one_block(block)
            return carry

        lax.fori_loop(0, team // group, body, 0)


def finish_kernel(arrived, residual, out):
    pairs = arrived.shape[1]
    half = arrived.shape[3]
    kept = residual[...]
    kept = jnp.concatenate([kept[:, :half], kept[:, half:]], axis=0)
    mine = lax.axis_index("tp_pair")
    for pair in range(pairs):
        mixed = jnp.sum(arrived[:, pair].astype(F32), axis=0)
        out[pair] = (mixed + jnp.where(mine == pair, kept, 0.0)).astype(BF16)


def add_kernel(*refs):
    *terms, out = refs
    total = terms[0][...].astype(F32)
    for term in terms[1:]:
        total = total + term[...].astype(F32)
    out[...] = total.astype(BF16)


def score_kernel(fresh_count, *refs):
    *arrived, gains, weight, layer, score, ordered, wide = refs
    pairs, double, _ = arrived[0].shape
    rows = double // 2
    blocks, tokens, _ = ordered.shape
    samples = tokens // fresh_count
    side = lax.axis_index("tp_side")
    for flip in range(2):
        for pair in range(pairs):
            state = arrived[flip][pair].astype(F32)
            spot = pl.ds(pl.multiple_of((2 * pair + (side ^ flip)) * rows, rows), rows)
            for c in range(blocks // 2):
                ordered[c, spot, :] = state[:rows, c * LANES : (c + 1) * LANES]
                ordered[blocks // 2 + c, spot, :] = state[rows:, c * LANES : (c + 1) * LANES]
    for c in range(blocks):
        for i in range(fresh_count):
            wide[pl.ds(fresh_count * c + i, samples, stride=fresh_count * blocks), :] = ordered[
                c, pl.ds(i, samples, stride=fresh_count), :
            ]
    layer[...] = wide[...].astype(BF16)
    states = jnp.concatenate([ordered[c] for c in range(blocks)], axis=1)
    final = normalize(states, gains[2:3, :])
    scored = jnp.sum(final * weight[...], axis=1, keepdims=True)
    row = lax.broadcasted_iota(jnp.int32, (tokens, samples), 0)
    here = row // fresh_count == lane_iota(row.shape)
    for i in range(fresh_count):
        score[i : i + 1, :] = jnp.sum(
            jnp.where(here & (row % fresh_count == i), scored, 0.0), axis=0, keepdims=True
        )


def shards(
    tokens_new,
    prefix_len,
    tail_len,
    pool_home,
    pool_page,
    slot_page_cache,
    tail_cache,
    routes,
    norm_gains,
    query_weight,
    key_value_weight,
    out_weight,
    router,
    expert_in,
    expert_out,
    score_weight,
):
    req_count = lax.axis_size("req")
    pairs = lax.axis_size("tp_pair")
    parts = 2 * pairs
    _, samples, fresh_count, model = tokens_new.shape
    tokens = samples * fresh_count
    part_rows = tokens // parts
    pool = slot_page_cache.shape[0]
    page_size = slot_page_cache.shape[1]
    slot_cap = max(1, pool // req_count)
    tail_count = tail_cache.shape[2]
    local = expert_in.shape[0]
    expert_count = router.shape[1]
    copies = local * req_count // expert_count
    everyone = req_count * parts
    rows = 2 * tokens
    blocks = model // LANES
    top = routes.shape[3]
    half = model // 2
    team = req_count * pairs

    whole = ("tp_pair", "tp_side")
    flips = [[(t, t ^ flip) for t in range(parts)] for flip in range(parts)]
    first_raw = expert_in.reshape(local, 2 * model, LANES)
    second_raw = expert_out.reshape(local * LANES, model)


    token_bytes = tokens_new.reshape(samples, fresh_count, blocks, LANES)
    token_bytes = token_bytes.transpose(0, 2, 1, 3).reshape(tokens * blocks, LANES)
    route_bytes = routes[0].transpose(1, 2, 0).reshape(fresh_count * top, samples)

    message, flat, normed, cosine, sine = pl.pallas_call(
        functools.partial(query_kernel, fresh_count),
        out_shape=(
            jax.ShapeDtypeStruct((req_count, rows + fresh_count * top, LANES), BF16),
            jax.ShapeDtypeStruct((parts, part_rows, model), BF16),
            jax.ShapeDtypeStruct((tokens, model), BF16),
            jax.ShapeDtypeStruct((tokens, LANES), F32),
            jax.ShapeDtypeStruct((tokens, LANES), F32),
        ),
        in_specs=[HBM] * 6,
        out_specs=(VMEM,) * 5,
        scratch_shapes=[
            pltpu.SMEM(prefix_len.shape, jnp.int32),
            pltpu.SMEM(tail_len.shape, jnp.int32),
            pltpu.VMEM(token_bytes.shape, BF16),
            pltpu.VMEM(route_bytes.shape, jnp.int32),
            pltpu.VMEM(norm_gains.shape, F32),
            pltpu.VMEM(query_weight.shape, BF16),
            pltpu.VMEM((tokens * blocks, LANES), F32),
            pltpu.VMEM((blocks, tokens, LANES), F32),
            pltpu.SemaphoreType.DMA((6,)),
        ],
        compiler_params=params(HOLD_MIB),
        name="query",
    )(prefix_len, tail_len, token_bytes, route_bytes, norm_gains, query_weight)

    key_value_rows = key_value_weight.reshape(2 * model, LANES)
    tail_rows = tail_cache.reshape(samples, 2 * tail_count, LANES)
    tail_inputs = (message, normed, cosine, sine)
    tail = pl.pallas_call(
        functools.partial(tail_kernel, fresh_count),
        out_shape=jax.ShapeDtypeStruct((parts, 24, LANES), BF16),
        in_specs=[HBM] * 7,
        out_specs=VMEM,
        scratch_shapes=[
            pltpu.SMEM(tail_len.shape, jnp.int32),
            pltpu.VMEM((rows, LANES), BF16),
            pltpu.VMEM(normed.shape, BF16),
            pltpu.VMEM(cosine.shape, F32),
            pltpu.VMEM(sine.shape, F32),
            pltpu.VMEM(key_value_rows.shape, BF16),
            pltpu.VMEM(tail_rows.shape, BF16),
            pltpu.SemaphoreType.DMA((6,)),
            pltpu.SemaphoreType.DMA((parts,)),
        ],
        compiler_params=params(HOLD_MIB),
        cost_estimate=cost(2e9, 5e6),
        name="tail",
    )(tail_len, *tail_inputs, key_value_rows, tail_rows)

    page_rows = slot_page_cache.reshape(pool, 2 * page_size, LANES)
    later, message = lax.optimization_barrier((out_weight, message))
    across = [lax.ppermute(later, whole, flips[flip]) for flip in range(2, parts, 2)]
    beside = lax.ppermute(later, whole, flips[1])
    first_all = lax.all_to_all(message, "req", split_axis=0, concat_axis=0, tiled=True)
    page_rows, tail, beside = lax.optimization_barrier((page_rows, tail, beside))

    step = 8 if pool % 8 == 0 else 1
    split_pages = pl.pallas_call(
        split_pages_kernel,
        grid=(pool // step,),
        out_shape=jax.ShapeDtypeStruct((pool, 2 * page_size, LANES), BF16),
        in_specs=[pl.BlockSpec((step, 2 * page_size, LANES), lambda v: (v, 0, 0))],
        out_specs=pl.BlockSpec((step, 2 * page_size, LANES), lambda v: (v, 0, 0)),
        scratch_shapes=[pltpu.VMEM((step * 2 * page_size, LANES), F32)],
        compiler_params=params(8),
        cost_estimate=cost(1e6, 4e6),
        name="split_pages",
    )(page_rows)

    partial, named = pl.pallas_call(
        functools.partial(page_kernel, slot_cap),
        out_shape=(
            jax.ShapeDtypeStruct((everyone, 24, LANES), BF16),
            jax.ShapeDtypeStruct((req_count, fresh_count * top, LANES), BF16),
        ),
        in_specs=[SMEM] * 3 + [VMEM] * 3,
        out_specs=(VMEM, VMEM),
        scratch_shapes=[
            pltpu.SMEM((req_count * slot_cap,), jnp.int32),
            pltpu.SMEM((req_count,), jnp.int32),
        ],
        compiler_params=params(12),
        cost_estimate=cost(2e9, 5e6),
        name="pages",
    )(pool_home, pool_page, prefix_len, split_pages, tail, first_all)
    arrived = lax.all_to_all(partial, ("req",) + whole, split_axis=0, concat_axis=0, tiled=True)

    first_raw, across, _ = lax.optimization_barrier((first_raw, across, partial))
    projects = [out_weight, beside]
    for block in across:
        projects += [block, lax.ppermute(block, whole, flips[1])]
    first = pl.pallas_call(
        prepare_kernel,
        out_shape=jax.ShapeDtypeStruct((local, model, 2 * LANES), BF16),
        in_specs=[HBM],
        out_specs=VMEM,
        scratch_shapes=[
            pltpu.VMEM(first_raw.shape, BF16),
            pltpu.VMEM((2, 2 * model, LANES), F32),
            pltpu.SemaphoreType.DMA((local,)),
        ],
        compiler_params=params(HOLD_MIB),
        cost_estimate=cost(2e10, 8e6),
        name="prepare",
    )(first_raw)
    named, first, projects = lax.optimization_barrier((named, first, projects))
    mask = pl.pallas_call(
        functools.partial(names_kernel, part_rows, fresh_count),
        out_shape=jax.ShapeDtypeStruct((team * part_rows, expert_count), F32),
        in_specs=[VMEM],
        out_specs=VMEM,
        compiler_params=params(8),
        cost_estimate=cost(1e6, 1e6),
        name="names",
    )(named)
    arrived, first, mask = lax.optimization_barrier((arrived, first, mask))
    first = pl.pallas_call(
        keep_kernel,
        out_shape=jax.ShapeDtypeStruct(first.shape, BF16),
        in_specs=[HBM],
        out_specs=HBM,
        input_output_aliases={0: 0},
        compiler_params=params(HOLD_MIB),
        name="keep",
    )(first)
    first_other = lax.ppermute(first, whole, flips[1])

    message, residual = pl.pallas_call(
        merge_kernel,
        out_shape=(
            jax.ShapeDtypeStruct((team, 2 * part_rows, half), BF16),
            jax.ShapeDtypeStruct((part_rows, model), F32),
        ),
        in_specs=[VMEM] * (3 + parts),
        out_specs=(VMEM, VMEM),
        scratch_shapes=[pltpu.VMEM((parts, part_rows, model // parts), F32)],
        compiler_params=params(12),
        name="merge",
    )(arrived.reshape(req_count, parts, 24, LANES), flat, norm_gains, *projects)
    message, second_sent = lax.optimization_barrier((message, second_raw))
    second_other = lax.ppermute(second_sent, whole, flips[1])
    states = lax.all_to_all(message, ("req", "tp_pair"), split_axis=0, concat_axis=0, tiled=True)

    expert_inputs = (
        states,
        mask,
        router.T,
        first,
        first_other,
        second_raw,
        second_other,
    )
    mixed = pl.pallas_call(
        functools.partial(expert_kernel, copies, part_rows, min(req_count, 8) * pairs),
        out_shape=jax.ShapeDtypeStruct((team, 2 * part_rows, half), BF16),
        in_specs=[VMEM] * 7,
        out_specs=VMEM,
        compiler_params=params(16),
        name="experts",
    )(*expert_inputs)
    mixed = mixed.reshape(req_count, pairs, 2 * part_rows, half)
    mixed = lax.all_to_all(mixed, "req", split_axis=0, concat_axis=0, tiled=True)

    finished = pl.pallas_call(
        finish_kernel,
        out_shape=jax.ShapeDtypeStruct((pairs, 2 * part_rows, half), BF16),
        in_specs=[VMEM, VMEM],
        out_specs=VMEM,
        compiler_params=params(8),
        name="finish",
    )(mixed, residual)
    terms = [finished] + [
        lax.ppermute(finished, whole, flips[flip]) for flip in range(2, parts, 2)
    ]
    finished = pl.pallas_call(
        add_kernel,
        out_shape=jax.ShapeDtypeStruct(finished.shape, BF16),
        in_specs=[VMEM] * len(terms),
        out_specs=VMEM,
        compiler_params=params(8),
        name="add",
    )(*terms)
    gathered = [finished, lax.ppermute(finished, whole, flips[1])]

    layer, score = pl.pallas_call(
        functools.partial(score_kernel, fresh_count),
        out_shape=(
            jax.ShapeDtypeStruct((tokens * blocks, LANES), BF16),
            jax.ShapeDtypeStruct((fresh_count, samples), F32),
        ),
        in_specs=[VMEM] * 4,
        out_specs=(VMEM, VMEM),
        scratch_shapes=[
            pltpu.VMEM((blocks, tokens, LANES), F32),
            pltpu.VMEM((tokens * blocks, LANES), F32),
        ],
        compiler_params=params(8),
        name="score",
    )(*gathered, norm_gains, score_weight.reshape(1, model))
    layer = layer.reshape(samples, blocks, fresh_count, LANES).transpose(0, 2, 1, 3)
    return (
        layer.reshape(1, samples, fresh_count, model),
        score.T.reshape(1, samples, fresh_count),
    )


def solution(mesh):
    tp = ("tp_pair", "tp_side")
    req_count, parts = mesh.devices.shape
    mesh = jax.sharding.Mesh(
        mesh.devices.reshape(req_count, parts // 2, 2), ("req", "tp_pair", "tp_side")
    )
    placed = (
        P("req", None, None, None),
        P(),
        P("req", None),
        P(),
        P(),
        P("req", None, None, tp),
        P("req", None, None, None, tp),
        P("req", None, None, None),
        P(),
        P(None, tp),
        P(None, None, tp),
        P(tp, None),
        P(),
        P("req", None, None, tp),
        P("req", tp, None),
        P(),
    )
    return jax.shard_map(
        shards,
        mesh=mesh,
        in_specs=placed,
        out_specs=(P("req", None, None, None), P("req", None, None)),
        check_vma=False,
    )
```

```python
import functools
import math

import jax
import jax.numpy as jnp
from jax import lax
from jax.experimental import pallas as pl
from jax.experimental.pallas import tpu as pltpu
from jax.sharding import PartitionSpec as P

HEAD_DIM = 64
LANES = 128
EPSILON = 1e-05
ROPE_BASE = 10000.0
LOWEST = -1e30
FLOOR = -1e28
F32 = jnp.float32
BF16 = jnp.bfloat16
MIB = 1024 * 1024
HOLD_MIB = 56

VMEM = pl.BlockSpec(memory_space=pltpu.VMEM)
SMEM = pl.BlockSpec(memory_space=pltpu.SMEM)
HBM = pl.BlockSpec(memory_space=pltpu.HBM)
ANY = pl.BlockSpec(memory_space=pl.ANY)


def params(mib):
    return pltpu.CompilerParams(vmem_limit_bytes=mib * MIB)


def cost(flops, moved):
    return pl.CostEstimate(flops=int(flops), bytes_accessed=int(moved), transcendentals=0)


def dot(left, right):
    return jnp.dot(left, right, preferred_element_type=F32)


def dot_t(left, right):
    return lax.dot_general(left, right, (((1,), (1,)), ((), ())), preferred_element_type=F32)


def my_part():
    return lax.axis_index("tp_pair") * 2 + lax.axis_index("tp_side")


def load_all(pairs, done):
    copies = [pltpu.make_async_copy(far, near, done.at[k]) for k, (far, near) in enumerate(pairs)]
    for copy in copies:
        copy.start()
    return copies


def lane_iota(shape):
    return lax.broadcasted_iota(jnp.int32, shape, len(shape) - 1)


def normalize(x, gain):
    return x * lax.rsqrt(jnp.mean(x * x, axis=-1, keepdims=True) + EPSILON) * gain


def rotate(x, cosine, sine):
    lanes = lane_iota(x.shape)
    partner = jnp.where(lanes % HEAD_DIM < HEAD_DIM // 2, pltpu.roll(x, 96, 1), pltpu.roll(x, 32, 1))
    return x * cosine + partner * sine


def by_head(packed, low):
    zero = jnp.zeros_like(packed)
    return jnp.concatenate([jnp.where(low, packed, zero), jnp.where(low, zero, packed)], axis=0)


def swap_halves(first, second):
    low = lane_iota(first.shape) < HEAD_DIM
    return (
        jnp.where(low, first, pltpu.roll(second, HEAD_DIM, 1)),
        jnp.where(low, pltpu.roll(first, HEAD_DIM, 1), second),
    )


def query_kernel(
    fresh_count,
    prefix_far,
    lengths_far,
    tokens_far,
    named_far,
    gains_far,
    weight_far,
    message,
    flat,
    normed,
    cosine,
    sine,
    prefix,
    lengths,
    tokens,
    named,
    gains,
    weight,
    wide,
    ordered,
    done,
):
    loads = load_all(
        (
            (tokens_far, tokens),
            (gains_far, gains),
            (lengths_far, lengths),
            (prefix_far, prefix),
            (weight_far, weight),
            (named_far, named),
        ),
        done,
    )
    count, model = normed.shape
    samples = count // fresh_count
    parts, part_rows, _ = flat.shape
    blocks = model // LANES
    loads[0].wait()
    wide[...] = tokens[...].astype(F32)
    for c in range(blocks):
        for i in range(fresh_count):
            ordered[c, pl.ds(i, samples, stride=fresh_count), :] = wide[
                pl.ds(fresh_count * c + i, samples, stride=fresh_count * blocks), :
            ]
    states = jnp.concatenate([ordered[c] for c in range(blocks)], axis=1)
    for part in range(parts):
        flat[part] = states[part * part_rows : (part + 1) * part_rows].astype(BF16)
    loads[1].wait()
    rows = normalize(states, gains[0:1, :]).astype(BF16)
    normed[...] = rows
    loads[2].wait()
    loads[3].wait()
    row_id = lax.broadcasted_iota(jnp.int32, (count, 1), 0)
    position = row_id % fresh_count + prefix[lax.axis_index("req")]
    for sample in range(samples):
        position = position + jnp.where(row_id // fresh_count == sample, lengths[0, sample], 0)
    within = lane_iota((1, LANES)) % HEAD_DIM
    pair = (within % (HEAD_DIM // 2)).astype(F32)
    frequency = jnp.exp(pair * (-math.log(ROPE_BASE) / (HEAD_DIM // 2)))
    angles = position.astype(F32) * frequency
    cosine[...] = jnp.cos(angles)
    turn = jnp.sin(angles)
    sine[...] = jnp.where(within < HEAD_DIM // 2, -turn, turn)
    loads[4].wait()
    made = dot(rows, weight[...])
    pieces = []
    for group in swap_halves(made[:, :LANES], made[:, LANES:]):
        pieces.append(rotate(group, cosine[...], sine[...]).astype(BF16).astype(F32) * 0.125)
    packed = []
    for part in range(parts):
        for piece in pieces:
            packed.append(piece[part * part_rows : (part + 1) * part_rows])
    loads[5].wait()
    routed = named[...].astype(F32)
    packed.append(
        jnp.concatenate(
            [routed, jnp.zeros((routed.shape[0], LANES - routed.shape[1]), F32)], axis=1
        )
    )
    packed = jnp.concatenate(packed, axis=0).astype(BF16)
    for n in range(message.shape[0]):
        message[n] = packed


def split_pages_kernel(source, out, wide):
    count, double, _ = source.shape
    half = double // 2
    wide[...] = source[...].astype(F32).reshape(count * double, LANES)
    keys = wide[pl.ds(0, count * half, stride=2), :].astype(BF16)
    values = wide[pl.ds(1, count * half, stride=2), :].astype(BF16)
    out[:, :half, :] = keys.reshape(count, half, LANES)
    out[:, half:, :] = values.reshape(count, half, LANES)


def pack_message(numer, top, total):
    high = total.astype(BF16).astype(F32)
    section = (lane_iota((8, LANES)) % HEAD_DIM) // 8
    stats = jnp.zeros((8, LANES), F32)
    for group in range(2):
        span = slice(group * 8, (group + 1) * 8)
        for k, kind in enumerate((top, high, total - high)):
            stats = jnp.where(section == 3 * group + k, kind[span], stats)
    return jnp.concatenate([numer, stats], axis=0).astype(BF16)


def unpack_message(block):
    block = block.astype(F32)
    stats = block[..., 16:24, :]
    low = lane_iota(stats.shape) < HEAD_DIM

    def pick(section):
        lane = section * 8
        return jnp.where(
            low, stats[..., lane : lane + 1], stats[..., HEAD_DIM + lane : HEAD_DIM + lane + 1]
        )

    top = jnp.concatenate([pick(0), pick(3)], axis=-2)
    total = jnp.concatenate([pick(1) + pick(2), pick(4) + pick(5)], axis=-2)
    return block[..., 0:16, :], top, total


def tail_kernel(
    fresh_count,
    lengths_far,
    query_far,
    normed_far,
    cosine_far,
    sine_far,
    weight_far,
    cache_far,
    out,
    lengths,
    query,
    normed,
    cosine,
    sine,
    weight,
    cache,
    load,
    done,
):
    tokens = normed.shape[0]
    samples, width, _ = cache.shape
    parts = out.shape[0]
    per_part = samples // parts
    loads = load_all(
        (
            (normed_far, normed),
            (weight_far, weight),
            (cosine_far, cosine),
            (sine_far, sine),
            (query_far.at[0, pl.ds(0, parts * 16)], query),
            (lengths_far, lengths),
        ),
        load,
    )
    spans = [pl.ds(part * per_part, per_part) for part in range(parts)]
    blocks = load_all([(cache_far.at[span], cache.at[span]) for span in spans], done)
    spread = (
        lax.broadcasted_iota(jnp.int32, (LANES, 2 * LANES), 1)
        == 2 * lax.broadcasted_iota(jnp.int32, (LANES, 2 * LANES), 0)
    ).astype(BF16)
    loads[0].wait()
    rows = normed[...]
    widened = jnp.concatenate(
        [dot(rows[:, c : c + LANES], spread) for c in range(0, rows.shape[1], LANES)], axis=1
    )
    both = jnp.concatenate([widened, pltpu.roll(widened, 1, 1)], axis=0).astype(BF16)
    for copy in loads[1:]:
        copy.wait()
    made = dot(both, weight[...])
    key_new = rotate(made[:tokens], cosine[...], sine[...]).astype(BF16)
    value_new = made[tokens:].astype(BF16)
    low = lane_iota((16, LANES)) < HEAD_DIM
    row_id = lax.broadcasted_iota(jnp.int32, (parts * 32, 1), 0)
    row_sample = (row_id // 32) * per_part + (row_id % 8) // fresh_count
    row_fresh = row_id % fresh_count
    part_sample = row_sample[:32]
    wide = [by_head(query[part * 16 : (part + 1) * 16, :], low) for part in range(parts)]
    length = jnp.zeros((parts * 32, 1), jnp.int32)
    for sample in range(samples):
        length = jnp.where(row_sample == sample, lengths[0, sample], length)
    fresh = dot_t(jnp.concatenate(wide, axis=0), key_new)
    token_id = lane_iota(fresh.shape)
    fresh_seen = (token_id // fresh_count == row_sample) & (token_id % fresh_count <= row_fresh)
    fresh = jnp.where(fresh_seen, fresh, LOWEST)
    beside = []
    scores = []
    for part in range(parts):
        blocks[part].wait()
        placed = [
            jnp.where(part_sample == a, wide[part], jnp.zeros_like(wide[part]))
            for a in range(per_part)
        ]
        beside.append(
            jnp.concatenate([cache[part * per_part + a] for a in range(per_part)], axis=1)
        )
        scores.append(dot_t(jnp.concatenate(placed, axis=1), beside[part]))
    scores = jnp.concatenate(scores, axis=0)
    column = lane_iota(scores.shape)
    scores = jnp.where((column % 2 == 0) & (column < 2 * length), scores, LOWEST)
    peak = jnp.maximum(
        jnp.max(scores, axis=1, keepdims=True), jnp.max(fresh, axis=1, keepdims=True)
    )
    peak = peak.astype(BF16).astype(F32)
    weights = jnp.exp(scores - peak)
    fresh_weights = jnp.exp(fresh - peak)
    amount = jnp.sum(weights, axis=1, keepdims=True) + jnp.sum(fresh_weights, axis=1, keepdims=True)
    shifted = pltpu.roll(weights, 1, 1).astype(BF16)
    fresh_part = dot(fresh_weights.astype(BF16), value_new)
    every = [dot(shifted[part * 32 : (part + 1) * 32], beside[part]) for part in range(parts)]
    for part in range(parts):
        mixed = every[part][:, :LANES]
        for a in range(1, per_part):
            mixed = jnp.where(part_sample == a, every[part][:, a * LANES : (a + 1) * LANES], mixed)
        first = slice(part * 32, part * 32 + 16)
        second = slice(part * 32 + 16, part * 32 + 32)
        mixed = mixed + fresh_part[part * 32 : (part + 1) * 32]
        out[part] = pack_message(
            jnp.where(low, mixed[:16], mixed[16:]),
            jnp.where(low, peak[first], peak[second]),
            jnp.where(low, amount[first], amount[second]),
        )


def page_kernel(
    slot_cap, homes, pages, lengths, cache, tail, query, out, named, slots, counts
):
    requests = query.shape[0]
    parts = tail.shape[0]
    pool = cache.shape[0]
    page_size = cache.shape[1] // 2
    rows = parts * 16
    me = lax.axis_index("req")
    base = me * pool
    tail_numer, tail_top, tail_total = [
        kind.reshape(rows, LANES) for kind in unpack_message(tail[...])
    ]
    named[...] = query[:, rows:, :]

    def clear(r, carry):
        counts[r] = 0
        for j in range(slot_cap):
            slots[r * slot_cap + j] = -1
        return carry

    lax.fori_loop(0, requests, clear, 0)

    def assign(v, carry):
        r = homes[base + v]
        rank = counts[r]
        slots[r * slot_cap + rank] = v
        counts[r] = rank + 1
        return carry

    lax.fori_loop(0, pool, assign, 0)

    low = lane_iota((rows, LANES)) < HEAD_DIM
    column = lane_iota((2 * rows, page_size))

    def finish(r, mixed, peak, amount):
        own = r == me
        top = jnp.where(low, peak[:rows], peak[rows:])
        joint = jnp.maximum(top, jnp.where(own, tail_top, FLOOR))
        here = jnp.exp(top - joint)
        there = jnp.where(own, jnp.exp(tail_top - joint), 0.0)
        numer = jnp.where(low, mixed[:rows], mixed[rows:]) * here + tail_numer * there
        total = jnp.where(low, amount[:rows], amount[rows:]) * here + tail_total * there
        for part in range(parts):
            span = slice(part * 16, (part + 1) * 16)
            out[r * parts + part] = pack_message(numer[span], joint[span], total[span])

    def gather(first, count):
        wides = []
        keys = []
        values = []
        limits = []
        for k in range(count):
            r = first + k
            wide = by_head(query[r, 0:rows, :], low)
            zero = jnp.zeros_like(wide)
            wides.append(jnp.concatenate([wide if c == k else zero for c in range(count)], axis=1))
            own_keys = []
            own_values = []
            own_limits = []
            for j in range(slot_cap):
                slot = slots[r * slot_cap + j]
                safe = jnp.maximum(slot, 0)
                own_limits.append(
                    jnp.where(slot >= 0, lengths[r] - pages[base + safe] * page_size, 0)
                )
                own_keys.append(cache[safe, :page_size, :])
                own_values.append(cache[safe, page_size:, :])
            keys.append(jnp.concatenate(own_keys, axis=0))
            values.append(jnp.concatenate(own_values, axis=0))
            limits.append(own_limits)
        scores = dot_t(jnp.concatenate(wides, axis=0), jnp.concatenate(keys, axis=1))
        return scores, jnp.concatenate(values, axis=1), limits

    def weigh(scores, limits):
        all_weights = []
        stats = []
        for k in range(len(limits)):
            own = scores[k * 2 * rows : (k + 1) * 2 * rows]
            own = [
                jnp.where(
                    column < limits[k][j], own[:, j * page_size : (j + 1) * page_size], LOWEST
                )
                for j in range(slot_cap)
            ]
            peak = jnp.max(functools.reduce(jnp.maximum, own), axis=1, keepdims=True)
            peak = jnp.maximum(peak, FLOOR).astype(BF16).astype(F32)
            weights = [jnp.exp(one - peak) for one in own]
            amount = jnp.sum(functools.reduce(jnp.add, weights), axis=1, keepdims=True)
            all_weights.append(jnp.concatenate([one.astype(BF16) for one in weights], axis=1))
            stats.append((peak, amount))
        return jnp.concatenate(all_weights, axis=0), stats

    pair = 2 if requests % 2 == 0 else 1
    step = 8 if requests % 8 == 0 else pair

    def several(g, carry):
        firsts = [g * step + k for k in range(0, step, pair)]
        gathered = [gather(first, pair) for first in firsts]
        weighed = [weigh(scores, limits) for scores, _, limits in gathered]
        mixed = [dot(weighed[n][0], gathered[n][1]) for n in range(len(firsts))]
        for n, first in enumerate(firsts):
            for k in range(pair):
                own = mixed[n][k * 2 * rows : (k + 1) * 2 * rows, k * LANES : (k + 1) * LANES]
                finish(first + k, own, *weighed[n][1][k])
        return carry

    if requests == step:
        several(0, 0)
    else:
        lax.fori_loop(0, requests // step, several, 0)


def merge_kernel(arrived, tokens, gains, *refs):
    parts = arrived.shape[1]
    weights = refs[:parts]
    out, residual, columns = refs[parts:]
    part = my_part()
    for t in range(parts):
        numer, top, total = unpack_message(arrived[:, t])
        factor = jnp.exp(top - jnp.max(top, axis=0, keepdims=True))
        attended = jnp.sum(factor * numer, axis=0) / jnp.sum(factor * total, axis=0)
        columns[t] = jnp.concatenate(swap_halves(attended[0:8], attended[8:16]), axis=1)
    projected = None
    for flip in range(parts):
        one = dot(columns[part ^ flip].astype(BF16), weights[flip][...])
        projected = one if projected is None else projected + one
    rows = (tokens[part].astype(F32) + projected).astype(BF16).astype(F32)
    residual[...] = rows
    normed = normalize(rows, gains[1:2, :])
    half = normed.shape[1] // 2
    message = jnp.concatenate([normed[:, :half], normed[:, half:]], axis=0).astype(BF16)
    for n in range(out.shape[0]):
        out[n] = message


def prepare_kernel(first_far, out, near, wide, done):
    local, double, _ = near.shape
    depth = double // 2
    loads = load_all([(first_far.at[e], near.at[e]) for e in range(local)], done)

    for e in range(local):
        loads[e].wait()
        buffer = wide.at[e % 2]
        buffer[...] = near[e].astype(F32)
        out[e, :, :LANES] = buffer[pl.ds(0, depth, stride=2), :].astype(BF16)
        out[e, :, LANES:] = buffer[pl.ds(1, depth, stride=2), :].astype(BF16)


def keep_kernel(*refs):
    del refs


def names_kernel(part_rows, fresh_count, packed, out):
    requests, span, _ = packed.shape
    experts = out.shape[1]
    halves = out.shape[0] // (requests * part_rows)
    top = span // fresh_count
    row = lax.broadcasted_iota(jnp.int32, (halves * part_rows, LANES), 0)
    token = (row // part_rows) * 2 * part_rows + lax.axis_index("tp_side") * part_rows + row % part_rows
    pick = (lane_iota(row.shape) == token // fresh_count).astype(BF16)
    found = jnp.concatenate([dot_t(pick, packed[r]) for r in range(requests)], axis=0)
    fresh = lax.broadcasted_iota(jnp.int32, (found.shape[0], 1), 0) % fresh_count
    chosen = found[:, :top]
    for i in range(1, fresh_count):
        chosen = jnp.where(fresh == i, found[:, i * top : (i + 1) * top], chosen)
    lanes = lane_iota(out.shape).astype(F32)
    mask = jnp.zeros(out.shape, F32)
    for k in range(top):
        mask = jnp.where(chosen[:, k : k + 1] == lanes, 1.0, mask)
    out[...] = mask


def expert_kernel(
    copies,
    part_rows,
    group,
    arrived,
    mask,
    router,
    first,
    first_other,
    second,
    second_other,
    out,
):
    team, _, half = arrived.shape
    local = first.shape[0]
    expert_count = router.shape[0]
    count = group * part_rows
    me = lax.axis_index("req")

    def one_block(block):
        here = pl.ds(block * group, group)
        states = arrived[here].astype(F32)
        states = jnp.concatenate(
            [
                states[:, :part_rows].reshape(count, half),
                states[:, part_rows:].reshape(count, half),
            ],
            axis=1,
        ).astype(BF16)
        logits = dot_t(states, router[...])
        span = pl.ds(pl.multiple_of(block * count, count), count)
        chosen = jnp.where(mask[span, :] > 0.5, logits, LOWEST)
        shares = jnp.exp(chosen - jnp.max(chosen, axis=1, keepdims=True))
        gates = shares / jnp.sum(shares, axis=1, keepdims=True)
        lanes = lane_iota(gates.shape)
        row = lax.broadcasted_iota(jnp.int32, (count, 1), 0)
        row_request = (block * group + row // part_rows) // 2
        weights = []
        for e in range(local):
            slot = me * local + e
            gate = jnp.sum(
                jnp.where(lanes == lax.rem(slot, expert_count), gates, 0.0), axis=1, keepdims=True
            )
            if copies > 1:
                copy = lax.div(slot, expert_count)
                gate = jnp.where(lax.rem(row_request, copies) == copy, gate, 0.0)
            weights.append(gate)
        mixed = None
        for up, down in ((first, second), (first_other, second_other)):
            pieces = []
            for e in range(local):
                wide = dot(states, up[e])
                value = wide[:, :LANES]
                other = wide[:, LANES:]
                hidden = (value / (1.0 + jnp.exp(-value)) * other).astype(BF16).astype(F32)
                pieces.append((hidden * weights[e]).astype(BF16))
            part = dot(jnp.concatenate(pieces, axis=1), down[...])
            mixed = part if mixed is None else mixed + part
        out[here] = jnp.concatenate(
            [
                mixed[:, :half].reshape(group, part_rows, half),
                mixed[:, half:].reshape(group, part_rows, half),
            ],
            axis=1,
        ).astype(BF16)

    if team == group:
        one_block(0)
    else:

        def body(block, carry):
            one_block(block)
            return carry

        lax.fori_loop(0, team // group, body, 0)


def finish_kernel(arrived, residual, out):
    pairs = arrived.shape[1]
    half = arrived.shape[3]
    kept = residual[...]
    kept = jnp.concatenate([kept[:, :half], kept[:, half:]], axis=0)
    mine = lax.axis_index("tp_pair")
    for pair in range(pairs):
        mixed = jnp.sum(arrived[:, pair].astype(F32), axis=0)
        out[pair] = (mixed + jnp.where(mine == pair, kept, 0.0)).astype(BF16)


def score_kernel(fresh_count, *refs):
    *arrived, gains, weight, layer, score, ordered, wide = refs
    pairs, double, _ = arrived[0].shape
    rows = double // 2
    blocks, tokens, _ = ordered.shape
    samples = tokens // fresh_count
    side = lax.axis_index("tp_side")
    for flip in range(2):
        for pair in range(pairs):
            state = arrived[flip][pair].astype(F32)
            for other in range(flip + 2, len(arrived), 2):
                state = state + arrived[other][pair].astype(F32)
            spot = pl.ds(pl.multiple_of((2 * pair + (side ^ flip)) * rows, rows), rows)
            for c in range(blocks // 2):
                ordered[c, spot, :] = state[:rows, c * LANES : (c + 1) * LANES]
                ordered[blocks // 2 + c, spot, :] = state[rows:, c * LANES : (c + 1) * LANES]
    for c in range(blocks):
        for i in range(fresh_count):
            wide[pl.ds(fresh_count * c + i, samples, stride=fresh_count * blocks), :] = ordered[
                c, pl.ds(i, samples, stride=fresh_count), :
            ]
    layer[...] = wide[...].astype(BF16)
    states = jnp.concatenate([ordered[c] for c in range(blocks)], axis=1)
    states = states.astype(BF16).astype(F32)
    final = normalize(states, gains[2:3, :])
    scored = jnp.sum(final * weight[...], axis=1, keepdims=True)
    row = lax.broadcasted_iota(jnp.int32, (tokens, samples), 0)
    here = row // fresh_count == lane_iota(row.shape)
    for i in range(fresh_count):
        score[i : i + 1, :] = jnp.sum(
            jnp.where(here & (row % fresh_count == i), scored, 0.0), axis=0, keepdims=True
        )


def shards(
    tokens_new,
    prefix_len,
    tail_len,
    pool_home,
    pool_page,
    slot_page_cache,
    tail_cache,
    routes,
    norm_gains,
    query_weight,
    key_value_weight,
    out_weight,
    router,
    expert_in,
    expert_out,
    score_weight,
):
    req_count = lax.axis_size("req")
    pairs = lax.axis_size("tp_pair")
    parts = 2 * pairs
    _, samples, fresh_count, model = tokens_new.shape
    tokens = samples * fresh_count
    part_rows = tokens // parts
    pool = slot_page_cache.shape[0]
    page_size = slot_page_cache.shape[1]
    slot_cap = max(1, pool // req_count)
    tail_count = tail_cache.shape[2]
    local = expert_in.shape[0]
    expert_count = router.shape[1]
    copies = local * req_count // expert_count
    everyone = req_count * parts
    rows = 2 * tokens
    blocks = model // LANES
    top = routes.shape[3]
    half = model // 2
    team = req_count * pairs

    whole = ("tp_pair", "tp_side")
    flips = [[(t, t ^ flip) for t in range(parts)] for flip in range(parts)]
    first_raw = expert_in.reshape(local, 2 * model, LANES)
    second_raw = expert_out.reshape(local * LANES, model)


    token_bytes = tokens_new.reshape(samples, fresh_count, blocks, LANES)
    token_bytes = token_bytes.transpose(0, 2, 1, 3).reshape(tokens * blocks, LANES)
    route_bytes = routes[0].transpose(1, 2, 0).reshape(fresh_count * top, samples)

    message, flat, normed, cosine, sine = pl.pallas_call(
        functools.partial(query_kernel, fresh_count),
        out_shape=(
            jax.ShapeDtypeStruct((req_count, rows + fresh_count * top, LANES), BF16),
            jax.ShapeDtypeStruct((parts, part_rows, model), BF16),
            jax.ShapeDtypeStruct((tokens, model), BF16),
            jax.ShapeDtypeStruct((tokens, LANES), F32),
            jax.ShapeDtypeStruct((tokens, LANES), F32),
        ),
        in_specs=[HBM] * 6,
        out_specs=(VMEM,) * 5,
        scratch_shapes=[
            pltpu.SMEM(prefix_len.shape, jnp.int32),
            pltpu.SMEM(tail_len.shape, jnp.int32),
            pltpu.VMEM(token_bytes.shape, BF16),
            pltpu.VMEM(route_bytes.shape, jnp.int32),
            pltpu.VMEM(norm_gains.shape, F32),
            pltpu.VMEM(query_weight.shape, BF16),
            pltpu.VMEM((tokens * blocks, LANES), F32),
            pltpu.VMEM((blocks, tokens, LANES), F32),
            pltpu.SemaphoreType.DMA((6,)),
        ],
        compiler_params=params(HOLD_MIB),
        name="query",
    )(prefix_len, tail_len, token_bytes, route_bytes, norm_gains, query_weight)

    key_value_rows = key_value_weight.reshape(2 * model, LANES)
    tail_rows = tail_cache.reshape(samples, 2 * tail_count, LANES)
    tail_inputs = (message, normed, cosine, sine)
    tail = pl.pallas_call(
        functools.partial(tail_kernel, fresh_count),
        out_shape=jax.ShapeDtypeStruct((parts, 24, LANES), BF16),
        in_specs=[HBM] * 7,
        out_specs=VMEM,
        scratch_shapes=[
            pltpu.SMEM(tail_len.shape, jnp.int32),
            pltpu.VMEM((rows, LANES), BF16),
            pltpu.VMEM(normed.shape, BF16),
            pltpu.VMEM(cosine.shape, F32),
            pltpu.VMEM(sine.shape, F32),
            pltpu.VMEM(key_value_rows.shape, BF16),
            pltpu.VMEM(tail_rows.shape, BF16),
            pltpu.SemaphoreType.DMA((6,)),
            pltpu.SemaphoreType.DMA((parts,)),
        ],
        compiler_params=params(HOLD_MIB),
        cost_estimate=cost(2e9, 5e6),
        name="tail",
    )(tail_len, *tail_inputs, key_value_rows, tail_rows)

    page_rows = slot_page_cache.reshape(pool, 2 * page_size, LANES)
    later, message = lax.optimization_barrier((out_weight, message))
    across = [lax.ppermute(later, whole, flips[flip]) for flip in range(2, parts, 2)]
    beside = lax.ppermute(later, whole, flips[1])
    first_all = lax.all_to_all(message, "req", split_axis=0, concat_axis=0, tiled=True)
    page_rows, tail = lax.optimization_barrier((page_rows, tail))

    step = 8 if pool % 8 == 0 else 1
    split_pages = pl.pallas_call(
        split_pages_kernel,
        grid=(pool // step,),
        out_shape=jax.ShapeDtypeStruct((pool, 2 * page_size, LANES), BF16),
        in_specs=[pl.BlockSpec((step, 2 * page_size, LANES), lambda v: (v, 0, 0))],
        out_specs=pl.BlockSpec((step, 2 * page_size, LANES), lambda v: (v, 0, 0)),
        scratch_shapes=[pltpu.VMEM((step * 2 * page_size, LANES), F32)],
        compiler_params=params(8),
        cost_estimate=cost(1e6, 4e6),
        name="split_pages",
    )(page_rows)

    partial, named = pl.pallas_call(
        functools.partial(page_kernel, slot_cap),
        out_shape=(
            jax.ShapeDtypeStruct((everyone, 24, LANES), BF16),
            jax.ShapeDtypeStruct((req_count, fresh_count * top, LANES), BF16),
        ),
        in_specs=[SMEM] * 3 + [VMEM] * 3,
        out_specs=(VMEM, VMEM),
        scratch_shapes=[
            pltpu.SMEM((req_count * slot_cap,), jnp.int32),
            pltpu.SMEM((req_count,), jnp.int32),
        ],
        compiler_params=params(12),
        cost_estimate=cost(2e9, 5e6),
        name="pages",
    )(pool_home, pool_page, prefix_len, split_pages, tail, first_all)
    arrived = lax.all_to_all(partial, ("req",) + whole, split_axis=0, concat_axis=0, tiled=True)

    first_raw, _ = lax.optimization_barrier((first_raw, partial))
    first = pl.pallas_call(
        prepare_kernel,
        out_shape=jax.ShapeDtypeStruct((local, model, 2 * LANES), BF16),
        in_specs=[HBM],
        out_specs=VMEM,
        scratch_shapes=[
            pltpu.VMEM(first_raw.shape, BF16),
            pltpu.VMEM((2, 2 * model, LANES), F32),
            pltpu.SemaphoreType.DMA((local,)),
        ],
        compiler_params=params(HOLD_MIB),
        cost_estimate=cost(2e10, 8e6),
        name="prepare",
    )(first_raw)
    first, across = lax.optimization_barrier((first, across))
    projects = [out_weight, beside]
    for block in across:
        projects += [block, lax.ppermute(block, whole, flips[1])]
    named, first, beside = lax.optimization_barrier((named, first, beside))
    mask = pl.pallas_call(
        functools.partial(names_kernel, part_rows, fresh_count),
        out_shape=jax.ShapeDtypeStruct((team * part_rows, expert_count), F32),
        in_specs=[VMEM],
        out_specs=VMEM,
        compiler_params=params(8),
        cost_estimate=cost(1e6, 1e6),
        name="names",
    )(named)
    arrived, first, mask, projects = lax.optimization_barrier((arrived, first, mask, projects))
    first = pl.pallas_call(
        keep_kernel,
        out_shape=jax.ShapeDtypeStruct(first.shape, BF16),
        in_specs=[HBM],
        out_specs=HBM,
        input_output_aliases={0: 0},
        compiler_params=params(HOLD_MIB),
        name="keep",
    )(first)
    first_other = lax.ppermute(first, whole, flips[1])

    message, residual = pl.pallas_call(
        merge_kernel,
        out_shape=(
            jax.ShapeDtypeStruct((team, 2 * part_rows, half), BF16),
            jax.ShapeDtypeStruct((part_rows, model), F32),
        ),
        in_specs=[VMEM] * (3 + parts),
        out_specs=(VMEM, VMEM),
        scratch_shapes=[pltpu.VMEM((parts, part_rows, model // parts), F32)],
        compiler_params=params(12),
        name="merge",
    )(arrived.reshape(req_count, parts, 24, LANES), flat, norm_gains, *projects)
    message, second_sent = lax.optimization_barrier((message, second_raw))
    second_other = lax.ppermute(second_sent, whole, flips[1])
    states = lax.all_to_all(message, ("req", "tp_pair"), split_axis=0, concat_axis=0, tiled=True)

    expert_inputs = (
        states,
        mask,
        router.T,
        first,
        first_other,
        second_raw,
        second_other,
    )
    mixed = pl.pallas_call(
        functools.partial(expert_kernel, copies, part_rows, min(req_count, 8) * pairs),
        out_shape=jax.ShapeDtypeStruct((team, 2 * part_rows, half), BF16),
        in_specs=[VMEM] * 7,
        out_specs=VMEM,
        compiler_params=params(16),
        name="experts",
    )(*expert_inputs)
    mixed = mixed.reshape(req_count, pairs, 2 * part_rows, half)
    mixed = lax.all_to_all(mixed, "req", split_axis=0, concat_axis=0, tiled=True)

    finished = pl.pallas_call(
        finish_kernel,
        out_shape=jax.ShapeDtypeStruct((pairs, 2 * part_rows, half), BF16),
        in_specs=[VMEM, VMEM],
        out_specs=VMEM,
        compiler_params=params(8),
        name="finish",
    )(mixed, residual)
    gathered = [finished] + [
        lax.ppermute(finished, whole, flips[flip]) for flip in range(1, parts)
    ]

    layer, score = pl.pallas_call(
        functools.partial(score_kernel, fresh_count),
        out_shape=(
            jax.ShapeDtypeStruct((tokens * blocks, LANES), BF16),
            jax.ShapeDtypeStruct((fresh_count, samples), F32),
        ),
        in_specs=[VMEM] * (parts + 2),
        out_specs=(VMEM, VMEM),
        scratch_shapes=[
            pltpu.VMEM((blocks, tokens, LANES), F32),
            pltpu.VMEM((tokens * blocks, LANES), F32),
        ],
        compiler_params=params(8),
        name="score",
    )(*gathered, norm_gains, score_weight.reshape(1, model))
    layer = layer.reshape(samples, blocks, fresh_count, LANES).transpose(0, 2, 1, 3)
    return (
        layer.reshape(1, samples, fresh_count, model),
        score.T.reshape(1, samples, fresh_count),
    )


def solution(mesh):
    tp = ("tp_pair", "tp_side")
    req_count, parts = mesh.devices.shape
    mesh = jax.sharding.Mesh(
        mesh.devices.reshape(req_count, parts // 2, 2), ("req", "tp_pair", "tp_side")
    )
    placed = (
        P("req", None, None, None),
        P(),
        P("req", None),
        P(),
        P(),
        P("req", None, None, tp),
        P("req", None, None, None, tp),
        P("req", None, None, None),
        P(),
        P(None, tp),
        P(None, None, tp),
        P(tp, None),
        P(),
        P("req", None, None, tp),
        P("req", tp, None),
        P(),
    )
    return jax.shard_map(
        shards,
        mesh=mesh,
        in_specs=placed,
        out_specs=(P("req", None, None, None), P("req", None, None)),
        check_vma=False,
    )
```

```python
import functools
import math

import jax
import jax.numpy as jnp
from jax import lax
from jax.experimental import pallas as pl
from jax.experimental.pallas import tpu as pltpu
from jax.sharding import PartitionSpec as P

HEAD_DIM = 64
LANES = 128
EPSILON = 1e-05
ROPE_BASE = 10000.0
LOWEST = -1e30
FLOOR = -1e28
F32 = jnp.float32
BF16 = jnp.bfloat16
MIB = 1024 * 1024
HOLD_MIB = 56

VMEM = pl.BlockSpec(memory_space=pltpu.VMEM)
SMEM = pl.BlockSpec(memory_space=pltpu.SMEM)
HBM = pl.BlockSpec(memory_space=pltpu.HBM)
ANY = pl.BlockSpec(memory_space=pl.ANY)


def params(mib):
    return pltpu.CompilerParams(vmem_limit_bytes=mib * MIB)


def cost(flops, moved):
    return pl.CostEstimate(flops=int(flops), bytes_accessed=int(moved), transcendentals=0)


def dot(left, right):
    return jnp.dot(left, right, preferred_element_type=F32)


def dot_t(left, right):
    return lax.dot_general(left, right, (((1,), (1,)), ((), ())), preferred_element_type=F32)


def my_part():
    return lax.axis_index("tp_pair") * 2 + lax.axis_index("tp_side")


def load_all(pairs, done):
    copies = [pltpu.make_async_copy(far, near, done.at[k]) for k, (far, near) in enumerate(pairs)]
    for copy in copies:
        copy.start()
    return copies


def lane_iota(shape):
    return lax.broadcasted_iota(jnp.int32, shape, len(shape) - 1)


def normalize(x, gain):
    return x * lax.rsqrt(jnp.mean(x * x, axis=-1, keepdims=True) + EPSILON) * gain


def rotate(x, cosine, sine):
    lanes = lane_iota(x.shape)
    partner = jnp.where(lanes % HEAD_DIM < HEAD_DIM // 2, pltpu.roll(x, 96, 1), pltpu.roll(x, 32, 1))
    return x * cosine + partner * sine


def by_head(packed, low):
    zero = jnp.zeros_like(packed)
    return jnp.concatenate([jnp.where(low, packed, zero), jnp.where(low, zero, packed)], axis=0)


def swap_halves(first, second):
    low = lane_iota(first.shape) < HEAD_DIM
    return (
        jnp.where(low, first, pltpu.roll(second, HEAD_DIM, 1)),
        jnp.where(low, pltpu.roll(first, HEAD_DIM, 1), second),
    )


def query_kernel(
    fresh_count,
    prefix_far,
    lengths_far,
    tokens_far,
    named_far,
    gains_far,
    weight_far,
    message,
    flat,
    normed,
    cosine,
    sine,
    prefix,
    lengths,
    tokens,
    named,
    gains,
    weight,
    wide,
    ordered,
    done,
):
    loads = load_all(
        (
            (tokens_far, tokens),
            (gains_far, gains),
            (lengths_far, lengths),
            (prefix_far, prefix),
            (weight_far, weight),
            (named_far, named),
        ),
        done,
    )
    count, model = normed.shape
    samples = count // fresh_count
    parts, part_rows, _ = flat.shape
    blocks = model // LANES
    loads[0].wait()
    wide[...] = tokens[...].astype(F32)
    for c in range(blocks):
        for i in range(fresh_count):
            ordered[c, pl.ds(i, samples, stride=fresh_count), :] = wide[
                pl.ds(fresh_count * c + i, samples, stride=fresh_count * blocks), :
            ]
    states = jnp.concatenate([ordered[c] for c in range(blocks)], axis=1)
    for part in range(parts):
        flat[part] = states[part * part_rows : (part + 1) * part_rows].astype(BF16)
    loads[1].wait()
    rows = normalize(states, gains[0:1, :]).astype(BF16)
    normed[...] = rows
    loads[2].wait()
    loads[3].wait()
    row_id = lax.broadcasted_iota(jnp.int32, (count, 1), 0)
    position = row_id % fresh_count + prefix[lax.axis_index("req")]
    for sample in range(samples):
        position = position + jnp.where(row_id // fresh_count == sample, lengths[0, sample], 0)
    within = lane_iota((1, LANES)) % HEAD_DIM
    pair = (within % (HEAD_DIM // 2)).astype(F32)
    frequency = jnp.exp(pair * (-math.log(ROPE_BASE) / (HEAD_DIM // 2)))
    angles = position.astype(F32) * frequency
    cosine[...] = jnp.cos(angles)
    turn = jnp.sin(angles)
    sine[...] = jnp.where(within < HEAD_DIM // 2, -turn, turn)
    loads[4].wait()
    made = dot(rows, weight[...])
    pieces = []
    for group in swap_halves(made[:, :LANES], made[:, LANES:]):
        pieces.append(rotate(group, cosine[...], sine[...]).astype(BF16).astype(F32) * 0.125)
    packed = []
    for part in range(parts):
        for piece in pieces:
            packed.append(piece[part * part_rows : (part + 1) * part_rows])
    loads[5].wait()
    routed = named[...].astype(F32)
    packed.append(
        jnp.concatenate(
            [routed, jnp.zeros((routed.shape[0], LANES - routed.shape[1]), F32)], axis=1
        )
    )
    packed = jnp.concatenate(packed, axis=0).astype(BF16)
    for n in range(message.shape[0]):
        message[n] = packed


def split_pages_kernel(source, out, wide):
    count, double, _ = source.shape
    half = double // 2
    wide[...] = source[...].astype(F32).reshape(count * double, LANES)
    keys = wide[pl.ds(0, count * half, stride=2), :].astype(BF16)
    values = wide[pl.ds(1, count * half, stride=2), :].astype(BF16)
    out[:, :half, :] = keys.reshape(count, half, LANES)
    out[:, half:, :] = values.reshape(count, half, LANES)


def pack_message(numer, top, total):
    high = total.astype(BF16).astype(F32)
    section = (lane_iota((8, LANES)) % HEAD_DIM) // 8
    stats = jnp.zeros((8, LANES), F32)
    for group in range(2):
        span = slice(group * 8, (group + 1) * 8)
        for k, kind in enumerate((top, high, total - high)):
            stats = jnp.where(section == 3 * group + k, kind[span], stats)
    return jnp.concatenate([numer, stats], axis=0).astype(BF16)


def unpack_message(block):
    block = block.astype(F32)
    stats = block[..., 16:24, :]
    low = lane_iota(stats.shape) < HEAD_DIM

    def pick(section):
        lane = section * 8
        return jnp.where(
            low, stats[..., lane : lane + 1], stats[..., HEAD_DIM + lane : HEAD_DIM + lane + 1]
        )

    top = jnp.concatenate([pick(0), pick(3)], axis=-2)
    total = jnp.concatenate([pick(1) + pick(2), pick(4) + pick(5)], axis=-2)
    return block[..., 0:16, :], top, total


def tail_kernel(
    fresh_count,
    lengths_far,
    query_far,
    normed_far,
    cosine_far,
    sine_far,
    weight_far,
    cache_far,
    out,
    lengths,
    query,
    normed,
    cosine,
    sine,
    weight,
    cache,
    load,
    done,
):
    tokens = normed.shape[0]
    samples, width, _ = cache.shape
    parts = out.shape[0]
    per_part = samples // parts
    loads = load_all(
        (
            (normed_far, normed),
            (weight_far, weight),
            (cosine_far, cosine),
            (sine_far, sine),
            (query_far.at[0, pl.ds(0, parts * 16)], query),
            (lengths_far, lengths),
        ),
        load,
    )
    spans = [pl.ds(part * per_part, per_part) for part in range(parts)]
    blocks = load_all([(cache_far.at[span], cache.at[span]) for span in spans], done)
    spread = (
        lax.broadcasted_iota(jnp.int32, (LANES, 2 * LANES), 1)
        == 2 * lax.broadcasted_iota(jnp.int32, (LANES, 2 * LANES), 0)
    ).astype(BF16)
    loads[0].wait()
    rows = normed[...]
    widened = jnp.concatenate(
        [dot(rows[:, c : c + LANES], spread) for c in range(0, rows.shape[1], LANES)], axis=1
    )
    both = jnp.concatenate([widened, pltpu.roll(widened, 1, 1)], axis=0).astype(BF16)
    for copy in loads[1:]:
        copy.wait()
    made = dot(both, weight[...])
    key_new = rotate(made[:tokens], cosine[...], sine[...]).astype(BF16)
    value_new = made[tokens:].astype(BF16)
    low = lane_iota((16, LANES)) < HEAD_DIM
    row_id = lax.broadcasted_iota(jnp.int32, (parts * 32, 1), 0)
    row_sample = (row_id // 32) * per_part + (row_id % 8) // fresh_count
    row_fresh = row_id % fresh_count
    part_sample = row_sample[:32]
    wide = [by_head(query[part * 16 : (part + 1) * 16, :], low) for part in range(parts)]
    length = jnp.zeros((parts * 32, 1), jnp.int32)
    for sample in range(samples):
        length = jnp.where(row_sample == sample, lengths[0, sample], length)
    fresh = dot_t(jnp.concatenate(wide, axis=0), key_new)
    token_id = lane_iota(fresh.shape)
    fresh_seen = (token_id // fresh_count == row_sample) & (token_id % fresh_count <= row_fresh)
    fresh = jnp.where(fresh_seen, fresh, LOWEST)
    beside = []
    scores = []
    for part in range(parts):
        blocks[part].wait()
        placed = [
            jnp.where(part_sample == a, wide[part], jnp.zeros_like(wide[part]))
            for a in range(per_part)
        ]
        beside.append(
            jnp.concatenate([cache[part * per_part + a] for a in range(per_part)], axis=1)
        )
        scores.append(dot_t(jnp.concatenate(placed, axis=1), beside[part]))
    scores = jnp.concatenate(scores, axis=0)
    column = lane_iota(scores.shape)
    scores = jnp.where((column % 2 == 0) & (column < 2 * length), scores, LOWEST)
    peak = jnp.maximum(
        jnp.max(scores, axis=1, keepdims=True), jnp.max(fresh, axis=1, keepdims=True)
    )
    peak = peak.astype(BF16).astype(F32)
    weights = jnp.exp(scores - peak)
    fresh_weights = jnp.exp(fresh - peak)
    amount = jnp.sum(weights, axis=1, keepdims=True) + jnp.sum(fresh_weights, axis=1, keepdims=True)
    shifted = pltpu.roll(weights, 1, 1).astype(BF16)
    fresh_part = dot(fresh_weights.astype(BF16), value_new)
    every = [dot(shifted[part * 32 : (part + 1) * 32], beside[part]) for part in range(parts)]
    for part in range(parts):
        mixed = every[part][:, :LANES]
        for a in range(1, per_part):
            mixed = jnp.where(part_sample == a, every[part][:, a * LANES : (a + 1) * LANES], mixed)
        first = slice(part * 32, part * 32 + 16)
        second = slice(part * 32 + 16, part * 32 + 32)
        mixed = mixed + fresh_part[part * 32 : (part + 1) * 32]
        out[part] = pack_message(
            jnp.where(low, mixed[:16], mixed[16:]),
            jnp.where(low, peak[first], peak[second]),
            jnp.where(low, amount[first], amount[second]),
        )


def page_kernel(
    slot_cap, homes, pages, lengths, cache, tail, query, out, named, slots, counts
):
    requests = query.shape[0]
    parts = tail.shape[0]
    pool = cache.shape[0]
    page_size = cache.shape[1] // 2
    rows = parts * 16
    me = lax.axis_index("req")
    base = me * pool
    tail_numer, tail_top, tail_total = [
        kind.reshape(rows, LANES) for kind in unpack_message(tail[...])
    ]
    named[...] = query[:, rows:, :]

    def clear(r, carry):
        counts[r] = 0
        for j in range(slot_cap):
            slots[r * slot_cap + j] = -1
        return carry

    lax.fori_loop(0, requests, clear, 0)

    def assign(v, carry):
        r = homes[base + v]
        rank = counts[r]
        slots[r * slot_cap + rank] = v
        counts[r] = rank + 1
        return carry

    lax.fori_loop(0, pool, assign, 0)

    low = lane_iota((rows, LANES)) < HEAD_DIM
    column = lane_iota((2 * rows, page_size))

    def finish(r, mixed, peak, amount):
        own = r == me
        top = jnp.where(low, peak[:rows], peak[rows:])
        joint = jnp.maximum(top, jnp.where(own, tail_top, FLOOR))
        here = jnp.exp(top - joint)
        there = jnp.where(own, jnp.exp(tail_top - joint), 0.0)
        numer = jnp.where(low, mixed[:rows], mixed[rows:]) * here + tail_numer * there
        total = jnp.where(low, amount[:rows], amount[rows:]) * here + tail_total * there
        for part in range(parts):
            span = slice(part * 16, (part + 1) * 16)
            out[r * parts + part] = pack_message(numer[span], joint[span], total[span])

    def gather(first, count):
        wides = []
        keys = []
        values = []
        limits = []
        for k in range(count):
            r = first + k
            wide = by_head(query[r, 0:rows, :], low)
            zero = jnp.zeros_like(wide)
            wides.append(jnp.concatenate([wide if c == k else zero for c in range(count)], axis=1))
            own_keys = []
            own_values = []
            own_limits = []
            for j in range(slot_cap):
                slot = slots[r * slot_cap + j]
                safe = jnp.maximum(slot, 0)
                own_limits.append(
                    jnp.where(slot >= 0, lengths[r] - pages[base + safe] * page_size, 0)
                )
                own_keys.append(cache[safe, :page_size, :])
                own_values.append(cache[safe, page_size:, :])
            keys.append(jnp.concatenate(own_keys, axis=0))
            values.append(jnp.concatenate(own_values, axis=0))
            limits.append(own_limits)
        scores = dot_t(jnp.concatenate(wides, axis=0), jnp.concatenate(keys, axis=1))
        return scores, jnp.concatenate(values, axis=1), limits

    def weigh(scores, limits):
        all_weights = []
        stats = []
        for k in range(len(limits)):
            own = scores[k * 2 * rows : (k + 1) * 2 * rows]
            own = [
                jnp.where(
                    column < limits[k][j], own[:, j * page_size : (j + 1) * page_size], LOWEST
                )
                for j in range(slot_cap)
            ]
            peak = jnp.max(functools.reduce(jnp.maximum, own), axis=1, keepdims=True)
            peak = jnp.maximum(peak, FLOOR).astype(BF16).astype(F32)
            weights = [jnp.exp(one - peak) for one in own]
            amount = jnp.sum(functools.reduce(jnp.add, weights), axis=1, keepdims=True)
            all_weights.append(jnp.concatenate([one.astype(BF16) for one in weights], axis=1))
            stats.append((peak, amount))
        return jnp.concatenate(all_weights, axis=0), stats

    pair = 2 if requests % 2 == 0 else 1
    step = 8 if requests % 8 == 0 else pair

    def several(g, carry):
        firsts = [g * step + k for k in range(0, step, pair)]
        gathered = [gather(first, pair) for first in firsts]
        weighed = [weigh(scores, limits) for scores, _, limits in gathered]
        mixed = [dot(weighed[n][0], gathered[n][1]) for n in range(len(firsts))]
        for n, first in enumerate(firsts):
            for k in range(pair):
                own = mixed[n][k * 2 * rows : (k + 1) * 2 * rows, k * LANES : (k + 1) * LANES]
                finish(first + k, own, *weighed[n][1][k])
        return carry

    if requests == step:
        several(0, 0)
    else:
        lax.fori_loop(0, requests // step, several, 0)


def merge_kernel(arrived, tokens, gains, *refs):
    parts = arrived.shape[1]
    weights = refs[:parts]
    out, residual, columns = refs[parts:]
    part = my_part()
    for t in range(parts):
        numer, top, total = unpack_message(arrived[:, t])
        factor = jnp.exp(top - jnp.max(top, axis=0, keepdims=True))
        attended = jnp.sum(factor * numer, axis=0) / jnp.sum(factor * total, axis=0)
        columns[t] = jnp.concatenate(swap_halves(attended[0:8], attended[8:16]), axis=1)
    projected = None
    for flip in range(parts):
        one = dot(columns[part ^ flip].astype(BF16), weights[flip][...])
        projected = one if projected is None else projected + one
    rows = (tokens[part].astype(F32) + projected).astype(BF16).astype(F32)
    residual[...] = rows
    normed = normalize(rows, gains[1:2, :])
    half = normed.shape[1] // 2
    message = jnp.concatenate([normed[:, :half], normed[:, half:]], axis=0).astype(BF16)
    for n in range(out.shape[0]):
        out[n] = message


def prepare_kernel(first_far, out, near, wide, done):
    local, double, _ = near.shape
    depth = double // 2
    loads = load_all([(first_far.at[e], near.at[e]) for e in range(local)], done)

    for e in range(local):
        loads[e].wait()
        buffer = wide.at[e % 2]
        buffer[...] = near[e].astype(F32)
        out[e, :, :LANES] = buffer[pl.ds(0, depth, stride=2), :].astype(BF16)
        out[e, :, LANES:] = buffer[pl.ds(1, depth, stride=2), :].astype(BF16)


def keep_kernel(*refs):
    del refs


def names_kernel(part_rows, fresh_count, packed, out):
    requests, span, _ = packed.shape
    experts = out.shape[1]
    halves = out.shape[0] // (requests * part_rows)
    top = span // fresh_count
    row = lax.broadcasted_iota(jnp.int32, (halves * part_rows, LANES), 0)
    token = (row // part_rows) * 2 * part_rows + lax.axis_index("tp_side") * part_rows + row % part_rows
    pick = (lane_iota(row.shape) == token // fresh_count).astype(BF16)
    found = jnp.concatenate([dot_t(pick, packed[r]) for r in range(requests)], axis=0)
    fresh = lax.broadcasted_iota(jnp.int32, (found.shape[0], 1), 0) % fresh_count
    chosen = found[:, :top]
    for i in range(1, fresh_count):
        chosen = jnp.where(fresh == i, found[:, i * top : (i + 1) * top], chosen)
    lanes = lane_iota(out.shape).astype(F32)
    mask = jnp.zeros(out.shape, F32)
    for k in range(top):
        mask = jnp.where(chosen[:, k : k + 1] == lanes, 1.0, mask)
    out[...] = mask


def expert_kernel(
    copies,
    part_rows,
    group,
    arrived,
    mask,
    router,
    first,
    first_other,
    second,
    second_other,
    out,
):
    team, _, half = arrived.shape
    local = first.shape[0]
    expert_count = router.shape[0]
    count = group * part_rows
    me = lax.axis_index("req")

    def one_block(block):
        here = pl.ds(block * group, group)
        states = arrived[here].astype(F32)
        states = jnp.concatenate(
            [
                states[:, :part_rows].reshape(count, half),
                states[:, part_rows:].reshape(count, half),
            ],
            axis=1,
        ).astype(BF16)
        logits = dot_t(states, router[...])
        span = pl.ds(pl.multiple_of(block * count, count), count)
        chosen = jnp.where(mask[span, :] > 0.5, logits, LOWEST)
        shares = jnp.exp(chosen - jnp.max(chosen, axis=1, keepdims=True))
        gates = shares / jnp.sum(shares, axis=1, keepdims=True)
        lanes = lane_iota(gates.shape)
        row = lax.broadcasted_iota(jnp.int32, (count, 1), 0)
        row_request = (block * group + row // part_rows) // 2
        weights = []
        for e in range(local):
            slot = me * local + e
            gate = jnp.sum(
                jnp.where(lanes == lax.rem(slot, expert_count), gates, 0.0), axis=1, keepdims=True
            )
            if copies > 1:
                copy = lax.div(slot, expert_count)
                gate = jnp.where(lax.rem(row_request, copies) == copy, gate, 0.0)
            weights.append(gate)
        mixed = None
        for up, down in ((first, second), (first_other, second_other)):
            pieces = []
            for e in range(local):
                wide = dot(states, up[e])
                value = wide[:, :LANES]
                other = wide[:, LANES:]
                hidden = (value / (1.0 + jnp.exp(-value)) * other).astype(BF16).astype(F32)
                pieces.append((hidden * weights[e]).astype(BF16))
            part = dot(jnp.concatenate(pieces, axis=1), down[...])
            mixed = part if mixed is None else mixed + part
        out[here] = jnp.concatenate(
            [
                mixed[:, :half].reshape(group, part_rows, half),
                mixed[:, half:].reshape(group, part_rows, half),
            ],
            axis=1,
        ).astype(BF16)

    if team == group:
        one_block(0)
    else:

        def body(block, carry):
            one_block(block)
            return carry

        lax.fori_loop(0, team // group, body, 0)


def finish_kernel(arrived, residual, out):
    pairs = arrived.shape[1]
    half = arrived.shape[3]
    kept = residual[...]
    kept = jnp.concatenate([kept[:, :half], kept[:, half:]], axis=0)
    mine = lax.axis_index("tp_pair")
    for pair in range(pairs):
        mixed = jnp.sum(arrived[:, pair].astype(F32), axis=0)
        out[pair] = (mixed + jnp.where(mine == pair, kept, 0.0)).astype(BF16)


def score_kernel(fresh_count, *refs):
    *arrived, gains, weight, layer, score, ordered, wide = refs
    pairs, double, _ = arrived[0].shape
    rows = double // 2
    blocks, tokens, _ = ordered.shape
    samples = tokens // fresh_count
    side = lax.axis_index("tp_side")
    for flip in range(2):
        for pair in range(pairs):
            state = arrived[flip][pair].astype(F32)
            for other in range(flip + 2, len(arrived), 2):
                state = state + arrived[other][pair].astype(F32)
            spot = pl.ds(pl.multiple_of((2 * pair + (side ^ flip)) * rows, rows), rows)
            for c in range(blocks // 2):
                ordered[c, spot, :] = state[:rows, c * LANES : (c + 1) * LANES]
                ordered[blocks // 2 + c, spot, :] = state[rows:, c * LANES : (c + 1) * LANES]
    for c in range(blocks):
        for i in range(fresh_count):
            wide[pl.ds(fresh_count * c + i, samples, stride=fresh_count * blocks), :] = ordered[
                c, pl.ds(i, samples, stride=fresh_count), :
            ]
    layer[...] = wide[...].astype(BF16)
    states = jnp.concatenate([ordered[c] for c in range(blocks)], axis=1)
    states = states.astype(BF16).astype(F32)
    final = normalize(states, gains[2:3, :])
    scored = jnp.sum(final * weight[...], axis=1, keepdims=True)
    row = lax.broadcasted_iota(jnp.int32, (tokens, samples), 0)
    here = row // fresh_count == lane_iota(row.shape)
    for i in range(fresh_count):
        score[i : i + 1, :] = jnp.sum(
            jnp.where(here & (row % fresh_count == i), scored, 0.0), axis=0, keepdims=True
        )


def shards(
    tokens_new,
    prefix_len,
    tail_len,
    pool_home,
    pool_page,
    slot_page_cache,
    tail_cache,
    routes,
    norm_gains,
    query_weight,
    key_value_weight,
    out_weight,
    router,
    expert_in,
    expert_out,
    score_weight,
):
    req_count = lax.axis_size("req")
    pairs = lax.axis_size("tp_pair")
    parts = 2 * pairs
    _, samples, fresh_count, model = tokens_new.shape
    tokens = samples * fresh_count
    part_rows = tokens // parts
    pool = slot_page_cache.shape[0]
    page_size = slot_page_cache.shape[1]
    slot_cap = max(1, pool // req_count)
    tail_count = tail_cache.shape[2]
    local = expert_in.shape[0]
    expert_count = router.shape[1]
    copies = local * req_count // expert_count
    everyone = req_count * parts
    rows = 2 * tokens
    blocks = model // LANES
    top = routes.shape[3]
    half = model // 2
    team = req_count * pairs

    whole = ("tp_pair", "tp_side")
    flips = [[(t, t ^ flip) for t in range(parts)] for flip in range(parts)]
    first_raw = expert_in.reshape(local, 2 * model, LANES)
    second_raw = expert_out.reshape(local * LANES, model)


    token_bytes = tokens_new.reshape(samples, fresh_count, blocks, LANES)
    token_bytes = token_bytes.transpose(0, 2, 1, 3).reshape(tokens * blocks, LANES)
    route_bytes = routes[0].transpose(1, 2, 0).reshape(fresh_count * top, samples)

    message, flat, normed, cosine, sine = pl.pallas_call(
        functools.partial(query_kernel, fresh_count),
        out_shape=(
            jax.ShapeDtypeStruct((req_count, rows + fresh_count * top, LANES), BF16),
            jax.ShapeDtypeStruct((parts, part_rows, model), BF16),
            jax.ShapeDtypeStruct((tokens, model), BF16),
            jax.ShapeDtypeStruct((tokens, LANES), F32),
            jax.ShapeDtypeStruct((tokens, LANES), F32),
        ),
        in_specs=[HBM] * 6,
        out_specs=(VMEM,) * 5,
        scratch_shapes=[
            pltpu.SMEM(prefix_len.shape, jnp.int32),
            pltpu.SMEM(tail_len.shape, jnp.int32),
            pltpu.VMEM(token_bytes.shape, BF16),
            pltpu.VMEM(route_bytes.shape, jnp.int32),
            pltpu.VMEM(norm_gains.shape, F32),
            pltpu.VMEM(query_weight.shape, BF16),
            pltpu.VMEM((tokens * blocks, LANES), F32),
            pltpu.VMEM((blocks, tokens, LANES), F32),
            pltpu.SemaphoreType.DMA((6,)),
        ],
        compiler_params=params(HOLD_MIB),
        name="query",
    )(prefix_len, tail_len, token_bytes, route_bytes, norm_gains, query_weight)

    key_value_rows = key_value_weight.reshape(2 * model, LANES)
    tail_rows = tail_cache.reshape(samples, 2 * tail_count, LANES)
    tail_inputs = (message, normed, cosine, sine)
    tail = pl.pallas_call(
        functools.partial(tail_kernel, fresh_count),
        out_shape=jax.ShapeDtypeStruct((parts, 24, LANES), BF16),
        in_specs=[HBM] * 7,
        out_specs=VMEM,
        scratch_shapes=[
            pltpu.SMEM(tail_len.shape, jnp.int32),
            pltpu.VMEM((rows, LANES), BF16),
            pltpu.VMEM(normed.shape, BF16),
            pltpu.VMEM(cosine.shape, F32),
            pltpu.VMEM(sine.shape, F32),
            pltpu.VMEM(key_value_rows.shape, BF16),
            pltpu.VMEM(tail_rows.shape, BF16),
            pltpu.SemaphoreType.DMA((6,)),
            pltpu.SemaphoreType.DMA((parts,)),
        ],
        compiler_params=params(HOLD_MIB),
        cost_estimate=cost(2e9, 5e6),
        name="tail",
    )(tail_len, *tail_inputs, key_value_rows, tail_rows)

    page_rows = slot_page_cache.reshape(pool, 2 * page_size, LANES)
    later, message = lax.optimization_barrier((out_weight, message))
    across = [lax.ppermute(later, whole, flips[flip]) for flip in range(2, parts, 2)]
    beside = lax.ppermute(later, whole, flips[1])
    first_all = lax.all_to_all(message, "req", split_axis=0, concat_axis=0, tiled=True)
    page_rows, tail = lax.optimization_barrier((page_rows, tail))

    step = 8 if pool % 8 == 0 else 1
    split_pages = pl.pallas_call(
        split_pages_kernel,
        grid=(pool // step,),
        out_shape=jax.ShapeDtypeStruct((pool, 2 * page_size, LANES), BF16),
        in_specs=[pl.BlockSpec((step, 2 * page_size, LANES), lambda v: (v, 0, 0))],
        out_specs=pl.BlockSpec((step, 2 * page_size, LANES), lambda v: (v, 0, 0)),
        scratch_shapes=[pltpu.VMEM((step * 2 * page_size, LANES), F32)],
        compiler_params=params(8),
        cost_estimate=cost(1e6, 4e6),
        name="split_pages",
    )(page_rows)

    partial, named = pl.pallas_call(
        functools.partial(page_kernel, slot_cap),
        out_shape=(
            jax.ShapeDtypeStruct((everyone, 24, LANES), BF16),
            jax.ShapeDtypeStruct((req_count, fresh_count * top, LANES), BF16),
        ),
        in_specs=[SMEM] * 3 + [VMEM] * 3,
        out_specs=(VMEM, VMEM),
        scratch_shapes=[
            pltpu.SMEM((req_count * slot_cap,), jnp.int32),
            pltpu.SMEM((req_count,), jnp.int32),
        ],
        compiler_params=params(12),
        cost_estimate=cost(2e9, 5e6),
        name="pages",
    )(pool_home, pool_page, prefix_len, split_pages, tail, first_all)
    arrived = lax.all_to_all(partial, ("req",) + whole, split_axis=0, concat_axis=0, tiled=True)

    first_raw, across, _ = lax.optimization_barrier((first_raw, across, partial))
    projects = [out_weight, beside]
    for block in across:
        projects += [block, lax.ppermute(block, whole, flips[1])]
    first = pl.pallas_call(
        prepare_kernel,
        out_shape=jax.ShapeDtypeStruct((local, model, 2 * LANES), BF16),
        in_specs=[HBM],
        out_specs=VMEM,
        scratch_shapes=[
            pltpu.VMEM(first_raw.shape, BF16),
            pltpu.VMEM((2, 2 * model, LANES), F32),
            pltpu.SemaphoreType.DMA((local,)),
        ],
        compiler_params=params(HOLD_MIB),
        cost_estimate=cost(2e10, 8e6),
        name="prepare",
    )(first_raw)
    named, first, projects = lax.optimization_barrier((named, first, projects))
    mask = pl.pallas_call(
        functools.partial(names_kernel, part_rows, fresh_count),
        out_shape=jax.ShapeDtypeStruct((team * part_rows, expert_count), F32),
        in_specs=[VMEM],
        out_specs=VMEM,
        compiler_params=params(8),
        cost_estimate=cost(1e6, 1e6),
        name="names",
    )(named)
    arrived, first, mask = lax.optimization_barrier((arrived, first, mask))
    first = pl.pallas_call(
        keep_kernel,
        out_shape=jax.ShapeDtypeStruct(first.shape, BF16),
        in_specs=[HBM],
        out_specs=HBM,
        input_output_aliases={0: 0},
        compiler_params=params(HOLD_MIB),
        name="keep",
    )(first)
    first_other = lax.ppermute(first, whole, flips[1])

    message, residual = pl.pallas_call(
        merge_kernel,
        out_shape=(
            jax.ShapeDtypeStruct((team, 2 * part_rows, half), BF16),
            jax.ShapeDtypeStruct((part_rows, model), F32),
        ),
        in_specs=[VMEM] * (3 + parts),
        out_specs=(VMEM, VMEM),
        scratch_shapes=[pltpu.VMEM((parts, part_rows, model // parts), F32)],
        compiler_params=params(12),
        name="merge",
    )(arrived.reshape(req_count, parts, 24, LANES), flat, norm_gains, *projects)
    message, second_sent = lax.optimization_barrier((message, second_raw))
    second_other = lax.ppermute(second_sent, whole, flips[1])
    states = lax.all_to_all(message, ("req", "tp_pair"), split_axis=0, concat_axis=0, tiled=True)

    expert_inputs = (
        states,
        mask,
        router.T,
        first,
        first_other,
        second_raw,
        second_other,
    )
    mixed = pl.pallas_call(
        functools.partial(expert_kernel, copies, part_rows, min(req_count, 8) * pairs),
        out_shape=jax.ShapeDtypeStruct((team, 2 * part_rows, half), BF16),
        in_specs=[VMEM] * 7,
        out_specs=VMEM,
        compiler_params=params(16),
        name="experts",
    )(*expert_inputs)
    mixed = mixed.reshape(req_count, pairs, 2 * part_rows, half)
    mixed = lax.all_to_all(mixed, "req", split_axis=0, concat_axis=0, tiled=True)

    finished = pl.pallas_call(
        finish_kernel,
        out_shape=jax.ShapeDtypeStruct((pairs, 2 * part_rows, half), BF16),
        in_specs=[VMEM, VMEM],
        out_specs=VMEM,
        compiler_params=params(8),
        name="finish",
    )(mixed, residual)
    gathered = [finished] + [
        lax.ppermute(finished, whole, flips[flip]) for flip in range(1, parts)
    ]

    layer, score = pl.pallas_call(
        functools.partial(score_kernel, fresh_count),
        out_shape=(
            jax.ShapeDtypeStruct((tokens * blocks, LANES), BF16),
            jax.ShapeDtypeStruct((fresh_count, samples), F32),
        ),
        in_specs=[VMEM] * (parts + 2),
        out_specs=(VMEM, VMEM),
        scratch_shapes=[
            pltpu.VMEM((blocks, tokens, LANES), F32),
            pltpu.VMEM((tokens * blocks, LANES), F32),
        ],
        compiler_params=params(8),
        name="score",
    )(*gathered, norm_gains, score_weight.reshape(1, model))
    layer = layer.reshape(samples, blocks, fresh_count, LANES).transpose(0, 2, 1, 3)
    return (
        layer.reshape(1, samples, fresh_count, model),
        score.T.reshape(1, samples, fresh_count),
    )


def solution(mesh):
    tp = ("tp_pair", "tp_side")
    req_count, parts = mesh.devices.shape
    mesh = jax.sharding.Mesh(
        mesh.devices.reshape(req_count, parts // 2, 2), ("req", "tp_pair", "tp_side")
    )
    placed = (
        P("req", None, None, None),
        P(),
        P("req", None),
        P(),
        P(),
        P("req", None, None, tp),
        P("req", None, None, None, tp),
        P("req", None, None, None),
        P(),
        P(None, tp),
        P(None, None, tp),
        P(tp, None),
        P(),
        P("req", None, None, tp),
        P("req", tp, None),
        P(),
    )
    return jax.shard_map(
        shards,
        mesh=mesh,
        in_specs=placed,
        out_specs=(P("req", None, None, None), P("req", None, None)),
        check_vma=False,
    )
```

```python
import functools
import math

import jax
import jax.numpy as jnp
from jax import lax
from jax.experimental import pallas as pl
from jax.experimental.pallas import tpu as pltpu
from jax.sharding import PartitionSpec as P

HEAD_DIM = 64
LANES = 128
EPSILON = 1e-05
ROPE_BASE = 10000.0
LOWEST = -1e30
FLOOR = -1e28
F32 = jnp.float32
BF16 = jnp.bfloat16
MIB = 1024 * 1024
HOLD_MIB = 56

VMEM = pl.BlockSpec(memory_space=pltpu.VMEM)
SMEM = pl.BlockSpec(memory_space=pltpu.SMEM)
HBM = pl.BlockSpec(memory_space=pltpu.HBM)
ANY = pl.BlockSpec(memory_space=pl.ANY)


def params(mib):
    return pltpu.CompilerParams(vmem_limit_bytes=mib * MIB)


def cost(flops, moved):
    return pl.CostEstimate(flops=int(flops), bytes_accessed=int(moved), transcendentals=0)


def dot(left, right):
    return jnp.dot(left, right, preferred_element_type=F32)


def dot_t(left, right):
    return lax.dot_general(left, right, (((1,), (1,)), ((), ())), preferred_element_type=F32)


def my_part():
    return lax.axis_index("tp_pair") * 2 + lax.axis_index("tp_side")


def load_all(pairs, done):
    copies = [pltpu.make_async_copy(far, near, done.at[k]) for k, (far, near) in enumerate(pairs)]
    for copy in copies:
        copy.start()
    return copies


def lane_iota(shape):
    return lax.broadcasted_iota(jnp.int32, shape, len(shape) - 1)


def normalize(x, gain):
    return x * lax.rsqrt(jnp.mean(x * x, axis=-1, keepdims=True) + EPSILON) * gain


def rotate(x, cosine, sine):
    lanes = lane_iota(x.shape)
    partner = jnp.where(lanes % HEAD_DIM < HEAD_DIM // 2, pltpu.roll(x, 96, 1), pltpu.roll(x, 32, 1))
    return x * cosine + partner * sine


def by_head(packed, low):
    zero = jnp.zeros_like(packed)
    return jnp.concatenate([jnp.where(low, packed, zero), jnp.where(low, zero, packed)], axis=0)


def swap_halves(first, second):
    low = lane_iota(first.shape) < HEAD_DIM
    return (
        jnp.where(low, first, pltpu.roll(second, HEAD_DIM, 1)),
        jnp.where(low, pltpu.roll(first, HEAD_DIM, 1), second),
    )


def query_kernel(
    fresh_count,
    prefix_far,
    lengths_far,
    tokens_far,
    named_far,
    gains_far,
    weight_far,
    message,
    flat,
    normed,
    cosine,
    sine,
    prefix,
    lengths,
    tokens,
    named,
    gains,
    weight,
    wide,
    ordered,
    done,
):
    loads = load_all(
        (
            (tokens_far, tokens),
            (gains_far, gains),
            (lengths_far, lengths),
            (prefix_far, prefix),
            (weight_far, weight),
            (named_far, named),
        ),
        done,
    )
    count, model = normed.shape
    samples = count // fresh_count
    parts, part_rows, _ = flat.shape
    blocks = model // LANES
    loads[0].wait()
    wide[...] = tokens[...].astype(F32)
    for c in range(blocks):
        for i in range(fresh_count):
            ordered[c, pl.ds(i, samples, stride=fresh_count), :] = wide[
                pl.ds(fresh_count * c + i, samples, stride=fresh_count * blocks), :
            ]
    states = jnp.concatenate([ordered[c] for c in range(blocks)], axis=1)
    for part in range(parts):
        flat[part] = states[part * part_rows : (part + 1) * part_rows].astype(BF16)
    loads[1].wait()
    rows = normalize(states, gains[0:1, :]).astype(BF16)
    normed[...] = rows
    loads[2].wait()
    loads[3].wait()
    row_id = lax.broadcasted_iota(jnp.int32, (count, 1), 0)
    position = row_id % fresh_count + prefix[lax.axis_index("req")]
    for sample in range(samples):
        position = position + jnp.where(row_id // fresh_count == sample, lengths[0, sample], 0)
    within = lane_iota((1, LANES)) % HEAD_DIM
    pair = (within % (HEAD_DIM // 2)).astype(F32)
    frequency = jnp.exp(pair * (-math.log(ROPE_BASE) / (HEAD_DIM // 2)))
    angles = position.astype(F32) * frequency
    cosine[...] = jnp.cos(angles)
    turn = jnp.sin(angles)
    sine[...] = jnp.where(within < HEAD_DIM // 2, -turn, turn)
    loads[4].wait()
    made = dot(rows, weight[...])
    pieces = []
    for group in swap_halves(made[:, :LANES], made[:, LANES:]):
        pieces.append(rotate(group, cosine[...], sine[...]).astype(BF16).astype(F32) * 0.125)
    packed = []
    for part in range(parts):
        for piece in pieces:
            packed.append(piece[part * part_rows : (part + 1) * part_rows])
    loads[5].wait()
    routed = named[...].astype(F32)
    packed.append(
        jnp.concatenate(
            [routed, jnp.zeros((routed.shape[0], LANES - routed.shape[1]), F32)], axis=1
        )
    )
    packed = jnp.concatenate(packed, axis=0).astype(BF16)
    for n in range(message.shape[0]):
        message[n] = packed


def split_pages_kernel(source, out, wide):
    count, double, _ = source.shape
    half = double // 2
    wide[...] = source[...].astype(F32).reshape(count * double, LANES)
    keys = wide[pl.ds(0, count * half, stride=2), :].astype(BF16)
    values = wide[pl.ds(1, count * half, stride=2), :].astype(BF16)
    out[:, :half, :] = keys.reshape(count, half, LANES)
    out[:, half:, :] = values.reshape(count, half, LANES)


def pack_message(numer, top, total):
    high = total.astype(BF16).astype(F32)
    section = (lane_iota((8, LANES)) % HEAD_DIM) // 8
    stats = jnp.zeros((8, LANES), F32)
    for group in range(2):
        span = slice(group * 8, (group + 1) * 8)
        for k, kind in enumerate((top, high, total - high)):
            stats = jnp.where(section == 3 * group + k, kind[span], stats)
    return jnp.concatenate([numer, stats], axis=0).astype(BF16)


def unpack_message(block):
    block = block.astype(F32)
    stats = block[..., 16:24, :]
    low = lane_iota(stats.shape) < HEAD_DIM

    def pick(section):
        lane = section * 8
        return jnp.where(
            low, stats[..., lane : lane + 1], stats[..., HEAD_DIM + lane : HEAD_DIM + lane + 1]
        )

    top = jnp.concatenate([pick(0), pick(3)], axis=-2)
    total = jnp.concatenate([pick(1) + pick(2), pick(4) + pick(5)], axis=-2)
    return block[..., 0:16, :], top, total


def tail_kernel(
    fresh_count,
    lengths_far,
    query_far,
    normed_far,
    cosine_far,
    sine_far,
    weight_far,
    cache_far,
    out,
    lengths,
    query,
    normed,
    cosine,
    sine,
    weight,
    cache,
    load,
    done,
):
    tokens = normed.shape[0]
    samples, width, _ = cache.shape
    parts = out.shape[0]
    per_part = samples // parts
    loads = load_all(
        (
            (normed_far, normed),
            (weight_far, weight),
            (cosine_far, cosine),
            (sine_far, sine),
            (query_far.at[0, pl.ds(0, parts * 16)], query),
            (lengths_far, lengths),
        ),
        load,
    )
    spans = [pl.ds(part * per_part, per_part) for part in range(parts)]
    blocks = load_all([(cache_far.at[span], cache.at[span]) for span in spans], done)
    spread = (
        lax.broadcasted_iota(jnp.int32, (LANES, 2 * LANES), 1)
        == 2 * lax.broadcasted_iota(jnp.int32, (LANES, 2 * LANES), 0)
    ).astype(BF16)
    loads[0].wait()
    rows = normed[...]
    widened = jnp.concatenate(
        [dot(rows[:, c : c + LANES], spread) for c in range(0, rows.shape[1], LANES)], axis=1
    )
    both = jnp.concatenate([widened, pltpu.roll(widened, 1, 1)], axis=0).astype(BF16)
    for copy in loads[1:]:
        copy.wait()
    made = dot(both, weight[...])
    key_new = rotate(made[:tokens], cosine[...], sine[...]).astype(BF16)
    value_new = made[tokens:].astype(BF16)
    low = lane_iota((16, LANES)) < HEAD_DIM
    row_id = lax.broadcasted_iota(jnp.int32, (parts * 32, 1), 0)
    row_sample = (row_id // 32) * per_part + (row_id % 8) // fresh_count
    row_fresh = row_id % fresh_count
    part_sample = row_sample[:32]
    wide = [by_head(query[part * 16 : (part + 1) * 16, :], low) for part in range(parts)]
    length = jnp.zeros((parts * 32, 1), jnp.int32)
    for sample in range(samples):
        length = jnp.where(row_sample == sample, lengths[0, sample], length)
    fresh = dot_t(jnp.concatenate(wide, axis=0), key_new)
    token_id = lane_iota(fresh.shape)
    fresh_seen = (token_id // fresh_count == row_sample) & (token_id % fresh_count <= row_fresh)
    fresh = jnp.where(fresh_seen, fresh, LOWEST)
    beside = []
    scores = []
    for part in range(parts):
        blocks[part].wait()
        placed = [
            jnp.where(part_sample == a, wide[part], jnp.zeros_like(wide[part]))
            for a in range(per_part)
        ]
        beside.append(
            jnp.concatenate([cache[part * per_part + a] for a in range(per_part)], axis=1)
        )
        scores.append(dot_t(jnp.concatenate(placed, axis=1), beside[part]))
    scores = jnp.concatenate(scores, axis=0)
    column = lane_iota(scores.shape)
    scores = jnp.where((column % 2 == 0) & (column < 2 * length), scores, LOWEST)
    peak = jnp.maximum(
        jnp.max(scores, axis=1, keepdims=True), jnp.max(fresh, axis=1, keepdims=True)
    )
    peak = peak.astype(BF16).astype(F32)
    weights = jnp.exp(scores - peak)
    fresh_weights = jnp.exp(fresh - peak)
    amount = jnp.sum(weights, axis=1, keepdims=True) + jnp.sum(fresh_weights, axis=1, keepdims=True)
    shifted = pltpu.roll(weights, 1, 1).astype(BF16)
    fresh_part = dot(fresh_weights.astype(BF16), value_new)
    every = [dot(shifted[part * 32 : (part + 1) * 32], beside[part]) for part in range(parts)]
    for part in range(parts):
        mixed = every[part][:, :LANES]
        for a in range(1, per_part):
            mixed = jnp.where(part_sample == a, every[part][:, a * LANES : (a + 1) * LANES], mixed)
        first = slice(part * 32, part * 32 + 16)
        second = slice(part * 32 + 16, part * 32 + 32)
        mixed = mixed + fresh_part[part * 32 : (part + 1) * 32]
        out[part] = pack_message(
            jnp.where(low, mixed[:16], mixed[16:]),
            jnp.where(low, peak[first], peak[second]),
            jnp.where(low, amount[first], amount[second]),
        )


def page_kernel(
    slot_cap, homes, pages, lengths, cache, tail, query, out, named, slots, counts
):
    requests = query.shape[0]
    parts = tail.shape[0]
    pool = cache.shape[0]
    page_size = cache.shape[1] // 2
    rows = parts * 16
    me = lax.axis_index("req")
    base = me * pool
    tail_numer, tail_top, tail_total = [
        kind.reshape(rows, LANES) for kind in unpack_message(tail[...])
    ]
    named[...] = query[:, rows:, :]

    def clear(r, carry):
        counts[r] = 0
        for j in range(slot_cap):
            slots[r * slot_cap + j] = -1
        return carry

    lax.fori_loop(0, requests, clear, 0)

    def assign(v, carry):
        r = homes[base + v]
        rank = counts[r]
        slots[r * slot_cap + rank] = v
        counts[r] = rank + 1
        return carry

    lax.fori_loop(0, pool, assign, 0)

    low = lane_iota((rows, LANES)) < HEAD_DIM
    column = lane_iota((2 * rows, page_size))

    def finish(r, mixed, peak, amount):
        own = r == me
        top = jnp.where(low, peak[:rows], peak[rows:])
        joint = jnp.maximum(top, jnp.where(own, tail_top, FLOOR))
        here = jnp.exp(top - joint)
        there = jnp.where(own, jnp.exp(tail_top - joint), 0.0)
        numer = jnp.where(low, mixed[:rows], mixed[rows:]) * here + tail_numer * there
        total = jnp.where(low, amount[:rows], amount[rows:]) * here + tail_total * there
        for part in range(parts):
            span = slice(part * 16, (part + 1) * 16)
            out[r * parts + part] = pack_message(numer[span], joint[span], total[span])

    def gather(first, count):
        wides = []
        keys = []
        values = []
        limits = []
        for k in range(count):
            r = first + k
            wide = by_head(query[r, 0:rows, :], low)
            zero = jnp.zeros_like(wide)
            wides.append(jnp.concatenate([wide if c == k else zero for c in range(count)], axis=1))
            own_keys = []
            own_values = []
            own_limits = []
            for j in range(slot_cap):
                slot = slots[r * slot_cap + j]
                safe = jnp.maximum(slot, 0)
                own_limits.append(
                    jnp.where(slot >= 0, lengths[r] - pages[base + safe] * page_size, 0)
                )
                own_keys.append(cache[safe, :page_size, :])
                own_values.append(cache[safe, page_size:, :])
            keys.append(jnp.concatenate(own_keys, axis=0))
            values.append(jnp.concatenate(own_values, axis=0))
            limits.append(own_limits)
        scores = dot_t(jnp.concatenate(wides, axis=0), jnp.concatenate(keys, axis=1))
        return scores, jnp.concatenate(values, axis=1), limits

    def weigh(scores, limits):
        all_weights = []
        stats = []
        for k in range(len(limits)):
            own = scores[k * 2 * rows : (k + 1) * 2 * rows]
            own = [
                jnp.where(
                    column < limits[k][j], own[:, j * page_size : (j + 1) * page_size], LOWEST
                )
                for j in range(slot_cap)
            ]
            peak = jnp.max(functools.reduce(jnp.maximum, own), axis=1, keepdims=True)
            peak = jnp.maximum(peak, FLOOR).astype(BF16).astype(F32)
            weights = [jnp.exp(one - peak) for one in own]
            amount = jnp.sum(functools.reduce(jnp.add, weights), axis=1, keepdims=True)
            all_weights.append(jnp.concatenate([one.astype(BF16) for one in weights], axis=1))
            stats.append((peak, amount))
        return jnp.concatenate(all_weights, axis=0), stats

    pair = 2 if requests % 2 == 0 else 1
    step = 8 if requests % 8 == 0 else pair

    def several(g, carry):
        firsts = [g * step + k for k in range(0, step, pair)]
        gathered = [gather(first, pair) for first in firsts]
        weighed = [weigh(scores, limits) for scores, _, limits in gathered]
        mixed = [dot(weighed[n][0], gathered[n][1]) for n in range(len(firsts))]
        for n, first in enumerate(firsts):
            for k in range(pair):
                own = mixed[n][k * 2 * rows : (k + 1) * 2 * rows, k * LANES : (k + 1) * LANES]
                finish(first + k, own, *weighed[n][1][k])
        return carry

    if requests == step:
        several(0, 0)
    else:
        lax.fori_loop(0, requests // step, several, 0)


def merge_kernel(arrived, tokens, gains, *refs):
    parts = arrived.shape[1]
    weights = refs[:parts]
    out, residual, columns = refs[parts:]
    part = my_part()
    for t in range(parts):
        numer, top, total = unpack_message(arrived[:, t])
        factor = jnp.exp(top - jnp.max(top, axis=0, keepdims=True))
        attended = jnp.sum(factor * numer, axis=0) / jnp.sum(factor * total, axis=0)
        columns[t] = jnp.concatenate(swap_halves(attended[0:8], attended[8:16]), axis=1)
    projected = None
    for flip in range(parts):
        one = dot(columns[part ^ flip].astype(BF16), weights[flip][...])
        projected = one if projected is None else projected + one
    rows = (tokens[part].astype(F32) + projected).astype(BF16).astype(F32)
    residual[...] = rows
    normed = normalize(rows, gains[1:2, :])
    half = normed.shape[1] // 2
    message = jnp.concatenate([normed[:, :half], normed[:, half:]], axis=0).astype(BF16)
    for n in range(out.shape[0]):
        out[n] = message


def prepare_kernel(first_far, out, near, wide, done):
    local, double, _ = near.shape
    depth = double // 2
    loads = load_all([(first_far.at[e], near.at[e]) for e in range(local)], done)

    for e in range(local):
        loads[e].wait()
        buffer = wide.at[e % 2]
        buffer[...] = near[e].astype(F32)
        out[e, :, :LANES] = buffer[pl.ds(0, depth, stride=2), :].astype(BF16)
        out[e, :, LANES:] = buffer[pl.ds(1, depth, stride=2), :].astype(BF16)


def keep_kernel(*refs):
    del refs


def names_kernel(part_rows, fresh_count, packed, out):
    requests, span, _ = packed.shape
    experts = out.shape[1]
    halves = out.shape[0] // (requests * part_rows)
    top = span // fresh_count
    row = lax.broadcasted_iota(jnp.int32, (halves * part_rows, LANES), 0)
    token = (row // part_rows) * 2 * part_rows + lax.axis_index("tp_side") * part_rows + row % part_rows
    pick = (lane_iota(row.shape) == token // fresh_count).astype(BF16)
    found = jnp.concatenate([dot_t(pick, packed[r]) for r in range(requests)], axis=0)
    fresh = lax.broadcasted_iota(jnp.int32, (found.shape[0], 1), 0) % fresh_count
    chosen = found[:, :top]
    for i in range(1, fresh_count):
        chosen = jnp.where(fresh == i, found[:, i * top : (i + 1) * top], chosen)
    lanes = lane_iota(out.shape).astype(F32)
    mask = jnp.zeros(out.shape, F32)
    for k in range(top):
        mask = jnp.where(chosen[:, k : k + 1] == lanes, 1.0, mask)
    out[...] = mask


def expert_kernel(
    copies,
    part_rows,
    group,
    arrived,
    mask,
    router,
    first,
    first_other,
    second,
    second_other,
    out,
):
    team, _, half = arrived.shape
    local = first.shape[0]
    expert_count = router.shape[0]
    count = group * part_rows
    me = lax.axis_index("req")

    def one_block(block):
        here = pl.ds(block * group, group)
        states = arrived[here].astype(F32)
        states = jnp.concatenate(
            [
                states[:, :part_rows].reshape(count, half),
                states[:, part_rows:].reshape(count, half),
            ],
            axis=1,
        ).astype(BF16)
        logits = dot_t(states, router[...])
        span = pl.ds(pl.multiple_of(block * count, count), count)
        chosen = jnp.where(mask[span, :] > 0.5, logits, LOWEST)
        shares = jnp.exp(chosen - jnp.max(chosen, axis=1, keepdims=True))
        gates = shares / jnp.sum(shares, axis=1, keepdims=True)
        lanes = lane_iota(gates.shape)
        row = lax.broadcasted_iota(jnp.int32, (count, 1), 0)
        row_request = (block * group + row // part_rows) // 2
        weights = []
        for e in range(local):
            slot = me * local + e
            gate = jnp.sum(
                jnp.where(lanes == lax.rem(slot, expert_count), gates, 0.0), axis=1, keepdims=True
            )
            if copies > 1:
                copy = lax.div(slot, expert_count)
                gate = jnp.where(lax.rem(row_request, copies) == copy, gate, 0.0)
            weights.append(gate)
        mixed = None
        for up, down in ((first, second), (first_other, second_other)):
            pieces = []
            for e in range(local):
                wide = dot(states, up[e])
                value = wide[:, :LANES]
                other = wide[:, LANES:]
                hidden = (value / (1.0 + jnp.exp(-value)) * other).astype(BF16).astype(F32)
                pieces.append((hidden * weights[e]).astype(BF16))
            part = dot(jnp.concatenate(pieces, axis=1), down[...])
            mixed = part if mixed is None else mixed + part
        out[here] = jnp.concatenate(
            [
                mixed[:, :half].reshape(group, part_rows, half),
                mixed[:, half:].reshape(group, part_rows, half),
            ],
            axis=1,
        ).astype(BF16)

    if team == group:
        one_block(0)
    else:

        def body(block, carry):
            one_block(block)
            return carry

        lax.fori_loop(0, team // group, body, 0)


def finish_kernel(arrived, residual, out):
    pairs = arrived.shape[1]
    half = arrived.shape[3]
    kept = residual[...]
    kept = jnp.concatenate([kept[:, :half], kept[:, half:]], axis=0)
    mine = lax.axis_index("tp_pair")
    for pair in range(pairs):
        mixed = jnp.sum(arrived[:, pair].astype(F32), axis=0)
        out[pair] = (mixed + jnp.where(mine == pair, kept, 0.0)).astype(BF16)


def score_kernel(fresh_count, *refs):
    *arrived, gains, weight, layer, score, ordered, wide = refs
    pairs, double, _ = arrived[0].shape
    rows = double // 2
    blocks, tokens, _ = ordered.shape
    samples = tokens // fresh_count
    side = lax.axis_index("tp_side")
    for flip in range(2):
        for pair in range(pairs):
            state = arrived[flip][pair].astype(F32)
            for other in range(flip + 2, len(arrived), 2):
                state = state + arrived[other][pair].astype(F32)
            spot = pl.ds(pl.multiple_of((2 * pair + (side ^ flip)) * rows, rows), rows)
            for c in range(blocks // 2):
                ordered[c, spot, :] = state[:rows, c * LANES : (c + 1) * LANES]
                ordered[blocks // 2 + c, spot, :] = state[rows:, c * LANES : (c + 1) * LANES]
    for c in range(blocks):
        for i in range(fresh_count):
            wide[pl.ds(fresh_count * c + i, samples, stride=fresh_count * blocks), :] = ordered[
                c, pl.ds(i, samples, stride=fresh_count), :
            ]
    layer[...] = wide[...].astype(BF16)
    states = jnp.concatenate([ordered[c] for c in range(blocks)], axis=1)
    states = states.astype(BF16).astype(F32)
    final = normalize(states, gains[2:3, :])
    scored = jnp.sum(final * weight[...], axis=1, keepdims=True)
    row = lax.broadcasted_iota(jnp.int32, (tokens, samples), 0)
    here = row // fresh_count == lane_iota(row.shape)
    for i in range(fresh_count):
        score[i : i + 1, :] = jnp.sum(
            jnp.where(here & (row % fresh_count == i), scored, 0.0), axis=0, keepdims=True
        )


def shards(
    tokens_new,
    prefix_len,
    tail_len,
    pool_home,
    pool_page,
    slot_page_cache,
    tail_cache,
    routes,
    norm_gains,
    query_weight,
    key_value_weight,
    out_weight,
    router,
    expert_in,
    expert_out,
    score_weight,
):
    req_count = lax.axis_size("req")
    pairs = lax.axis_size("tp_pair")
    parts = 2 * pairs
    _, samples, fresh_count, model = tokens_new.shape
    tokens = samples * fresh_count
    part_rows = tokens // parts
    pool = slot_page_cache.shape[0]
    page_size = slot_page_cache.shape[1]
    slot_cap = max(1, pool // req_count)
    tail_count = tail_cache.shape[2]
    local = expert_in.shape[0]
    expert_count = router.shape[1]
    copies = local * req_count // expert_count
    everyone = req_count * parts
    rows = 2 * tokens
    blocks = model // LANES
    top = routes.shape[3]
    half = model // 2
    team = req_count * pairs

    whole = ("tp_pair", "tp_side")
    flips = [[(t, t ^ flip) for t in range(parts)] for flip in range(parts)]
    first_raw = expert_in.reshape(local, 2 * model, LANES)
    second_raw = expert_out.reshape(local * LANES, model)


    token_bytes = tokens_new.reshape(samples, fresh_count, blocks, LANES)
    token_bytes = token_bytes.transpose(0, 2, 1, 3).reshape(tokens * blocks, LANES)
    route_bytes = routes[0].transpose(1, 2, 0).reshape(fresh_count * top, samples)

    message, flat, normed, cosine, sine = pl.pallas_call(
        functools.partial(query_kernel, fresh_count),
        out_shape=(
            jax.ShapeDtypeStruct((req_count, rows + fresh_count * top, LANES), BF16),
            jax.ShapeDtypeStruct((parts, part_rows, model), BF16),
            jax.ShapeDtypeStruct((tokens, model), BF16),
            jax.ShapeDtypeStruct((tokens, LANES), F32),
            jax.ShapeDtypeStruct((tokens, LANES), F32),
        ),
        in_specs=[HBM] * 6,
        out_specs=(VMEM,) * 5,
        scratch_shapes=[
            pltpu.SMEM(prefix_len.shape, jnp.int32),
            pltpu.SMEM(tail_len.shape, jnp.int32),
            pltpu.VMEM(token_bytes.shape, BF16),
            pltpu.VMEM(route_bytes.shape, jnp.int32),
            pltpu.VMEM(norm_gains.shape, F32),
            pltpu.VMEM(query_weight.shape, BF16),
            pltpu.VMEM((tokens * blocks, LANES), F32),
            pltpu.VMEM((blocks, tokens, LANES), F32),
            pltpu.SemaphoreType.DMA((6,)),
        ],
        compiler_params=params(HOLD_MIB),
        name="query",
    )(prefix_len, tail_len, token_bytes, route_bytes, norm_gains, query_weight)

    key_value_rows = key_value_weight.reshape(2 * model, LANES)
    tail_rows = tail_cache.reshape(samples, 2 * tail_count, LANES)
    tail_inputs = (message, normed, cosine, sine)
    tail = pl.pallas_call(
        functools.partial(tail_kernel, fresh_count),
        out_shape=jax.ShapeDtypeStruct((parts, 24, LANES), BF16),
        in_specs=[HBM] * 7,
        out_specs=VMEM,
        scratch_shapes=[
            pltpu.SMEM(tail_len.shape, jnp.int32),
            pltpu.VMEM((rows, LANES), BF16),
            pltpu.VMEM(normed.shape, BF16),
            pltpu.VMEM(cosine.shape, F32),
            pltpu.VMEM(sine.shape, F32),
            pltpu.VMEM(key_value_rows.shape, BF16),
            pltpu.VMEM(tail_rows.shape, BF16),
            pltpu.SemaphoreType.DMA((6,)),
            pltpu.SemaphoreType.DMA((parts,)),
        ],
        compiler_params=params(HOLD_MIB),
        cost_estimate=cost(2e10, 5e6),
        name="tail",
    )(tail_len, *tail_inputs, key_value_rows, tail_rows)

    page_rows = slot_page_cache.reshape(pool, 2 * page_size, LANES)
    later, message = lax.optimization_barrier((out_weight, message))
    across = [lax.ppermute(later, whole, flips[flip]) for flip in range(2, parts, 2)]
    beside = lax.ppermute(later, whole, flips[1])
    first_all = lax.all_to_all(message, "req", split_axis=0, concat_axis=0, tiled=True)
    page_rows, tail = lax.optimization_barrier((page_rows, tail))

    step = 8 if pool % 8 == 0 else 1
    split_pages = pl.pallas_call(
        split_pages_kernel,
        grid=(pool // step,),
        out_shape=jax.ShapeDtypeStruct((pool, 2 * page_size, LANES), BF16),
        in_specs=[pl.BlockSpec((step, 2 * page_size, LANES), lambda v: (v, 0, 0))],
        out_specs=pl.BlockSpec((step, 2 * page_size, LANES), lambda v: (v, 0, 0)),
        scratch_shapes=[pltpu.VMEM((step * 2 * page_size, LANES), F32)],
        compiler_params=params(8),
        cost_estimate=cost(1e6, 4e6),
        name="split_pages",
    )(page_rows)

    partial, named = pl.pallas_call(
        functools.partial(page_kernel, slot_cap),
        out_shape=(
            jax.ShapeDtypeStruct((everyone, 24, LANES), BF16),
            jax.ShapeDtypeStruct((req_count, fresh_count * top, LANES), BF16),
        ),
        in_specs=[SMEM] * 3 + [VMEM] * 3,
        out_specs=(VMEM, VMEM),
        scratch_shapes=[
            pltpu.SMEM((req_count * slot_cap,), jnp.int32),
            pltpu.SMEM((req_count,), jnp.int32),
        ],
        compiler_params=params(12),
        cost_estimate=cost(2e9, 5e6),
        name="pages",
    )(pool_home, pool_page, prefix_len, split_pages, tail, first_all)
    arrived = lax.all_to_all(partial, ("req",) + whole, split_axis=0, concat_axis=0, tiled=True)

    first_raw, across, _ = lax.optimization_barrier((first_raw, across, partial))
    projects = [out_weight, beside]
    for block in across:
        projects += [block, lax.ppermute(block, whole, flips[1])]
    first = pl.pallas_call(
        prepare_kernel,
        out_shape=jax.ShapeDtypeStruct((local, model, 2 * LANES), BF16),
        in_specs=[HBM],
        out_specs=VMEM,
        scratch_shapes=[
            pltpu.VMEM(first_raw.shape, BF16),
            pltpu.VMEM((2, 2 * model, LANES), F32),
            pltpu.SemaphoreType.DMA((local,)),
        ],
        compiler_params=params(HOLD_MIB),
        cost_estimate=cost(2e10, 8e6),
        name="prepare",
    )(first_raw)
    named, first, projects = lax.optimization_barrier((named, first, projects))
    mask = pl.pallas_call(
        functools.partial(names_kernel, part_rows, fresh_count),
        out_shape=jax.ShapeDtypeStruct((team * part_rows, expert_count), F32),
        in_specs=[VMEM],
        out_specs=VMEM,
        compiler_params=params(8),
        cost_estimate=cost(1e6, 1e6),
        name="names",
    )(named)
    arrived, first, mask = lax.optimization_barrier((arrived, first, mask))
    first = pl.pallas_call(
        keep_kernel,
        out_shape=jax.ShapeDtypeStruct(first.shape, BF16),
        in_specs=[HBM],
        out_specs=HBM,
        input_output_aliases={0: 0},
        compiler_params=params(HOLD_MIB),
        name="keep",
    )(first)
    first_other = lax.ppermute(first, whole, flips[1])

    message, residual = pl.pallas_call(
        merge_kernel,
        out_shape=(
            jax.ShapeDtypeStruct((team, 2 * part_rows, half), BF16),
            jax.ShapeDtypeStruct((part_rows, model), F32),
        ),
        in_specs=[VMEM] * (3 + parts),
        out_specs=(VMEM, VMEM),
        scratch_shapes=[pltpu.VMEM((parts, part_rows, model // parts), F32)],
        compiler_params=params(12),
        name="merge",
    )(arrived.reshape(req_count, parts, 24, LANES), flat, norm_gains, *projects)
    message, second_sent = lax.optimization_barrier((message, second_raw))
    second_other = lax.ppermute(second_sent, whole, flips[1])
    states = lax.all_to_all(message, ("req", "tp_pair"), split_axis=0, concat_axis=0, tiled=True)

    expert_inputs = (
        states,
        mask,
        router.T,
        first,
        first_other,
        second_raw,
        second_other,
    )
    mixed = pl.pallas_call(
        functools.partial(expert_kernel, copies, part_rows, min(req_count, 8) * pairs),
        out_shape=jax.ShapeDtypeStruct((team, 2 * part_rows, half), BF16),
        in_specs=[VMEM] * 7,
        out_specs=VMEM,
        compiler_params=params(16),
        name="experts",
    )(*expert_inputs)
    mixed = mixed.reshape(req_count, pairs, 2 * part_rows, half)
    mixed = lax.all_to_all(mixed, "req", split_axis=0, concat_axis=0, tiled=True)

    finished = pl.pallas_call(
        finish_kernel,
        out_shape=jax.ShapeDtypeStruct((pairs, 2 * part_rows, half), BF16),
        in_specs=[VMEM, VMEM],
        out_specs=VMEM,
        compiler_params=params(8),
        name="finish",
    )(mixed, residual)
    gathered = [finished] + [
        lax.ppermute(finished, whole, flips[flip]) for flip in range(1, parts)
    ]

    layer, score = pl.pallas_call(
        functools.partial(score_kernel, fresh_count),
        out_shape=(
            jax.ShapeDtypeStruct((tokens * blocks, LANES), BF16),
            jax.ShapeDtypeStruct((fresh_count, samples), F32),
        ),
        in_specs=[VMEM] * (parts + 2),
        out_specs=(VMEM, VMEM),
        scratch_shapes=[
            pltpu.VMEM((blocks, tokens, LANES), F32),
            pltpu.VMEM((tokens * blocks, LANES), F32),
        ],
        compiler_params=params(8),
        name="score",
    )(*gathered, norm_gains, score_weight.reshape(1, model))
    layer = layer.reshape(samples, blocks, fresh_count, LANES).transpose(0, 2, 1, 3)
    return (
        layer.reshape(1, samples, fresh_count, model),
        score.T.reshape(1, samples, fresh_count),
    )


def solution(mesh):
    tp = ("tp_pair", "tp_side")
    req_count, parts = mesh.devices.shape
    mesh = jax.sharding.Mesh(
        mesh.devices.reshape(req_count, parts // 2, 2), ("req", "tp_pair", "tp_side")
    )
    placed = (
        P("req", None, None, None),
        P(),
        P("req", None),
        P(),
        P(),
        P("req", None, None, tp),
        P("req", None, None, None, tp),
        P("req", None, None, None),
        P(),
        P(None, tp),
        P(None, None, tp),
        P(tp, None),
        P(),
        P("req", None, None, tp),
        P("req", tp, None),
        P(),
    )
    return jax.shard_map(
        shards,
        mesh=mesh,
        in_specs=placed,
        out_specs=(P("req", None, None, None), P("req", None, None)),
        check_vma=False,
    )
```
